32 devices in a mesh: seq: 16 (over z, y, x), head: 2 (over core).
Axes of the slice: x: 2, y: 2, z: 4, core: 2. Of those that a mesh axis runs over, the one named last changes fastest.
Arguments:
- token_values: bfloat16 [6144, 4096], P('seq', 'head'), may hold values from -6 to 6
- b_inputs: bfloat16 [6144, 128], P('seq'), may hold values from -6 to 6
- c_inputs: bfloat16 [6144, 128], P('seq'), may hold values from -6 to 6
- log_decay: float32 [64, 6144], P('head', 'seq'), may hold values from -1 to 0
- grad_out: bfloat16 [6144, 4096], P('seq', 'head'), may hold values from -0.005859375 to 0.005859375
Outputs:
- grad_values: bfloat16 [6144, 4096], P('seq', 'head')
- grad_b: bfloat16 [6144, 128], P('seq')
- grad_c: bfloat16 [6144, 128], P('seq')
The draws below stay inside these ranges and needn't reach their ends.
All inputs are finite; a program needn't handle non-finite values.
Results may differ from the reference program's by a relative error of at most 0.014.
Values may be sent and summed in bfloat16 or wider, within the bound.
No kernel may reach another device: no remote copies, remote signals or barrier semaphores. Data moves between devices by JAX's collectives and lax.ppermute only.
A program may use at most 128 MiB of HBM per device.

```python
import math
import jax
import jax.numpy as jnp
from jax import lax

HEADS = 64
HEAD_DIM = 64
STATE = 128
TOK_DEV = 384
HEADS_DEV = 32
WIDTH = 4096
WIDTH_DEV = 2048
STEP_TOTAL = 6144
N_HEAD = 2


def draw_log_decay(key, part):
    derived_prng_seeds = jax.random.split(key, 7)
    fast_share = 0.5
    halving = math.log(2.0)
    quick_heads = jax.random.uniform(derived_prng_seeds[0], (HEADS, 1)) < fast_share
    fast_rate = jnp.exp(jax.random.uniform(derived_prng_seeds[1], (HEADS, 1), minval=math.log(1.0 / 50.0), maxval=math.log(1.0 / 30.0)))
    slow_rate = jnp.exp(jax.random.uniform(derived_prng_seeds[2], (HEADS, 1), minval=math.log(0.02), maxval=math.log(0.17))) / STEP_TOTAL
    floor_intensity = jnp.where(quick_heads, fast_rate, slow_rate)
    jaggedness_level = jnp.exp(jax.random.uniform(derived_prng_seeds[3], (HEADS, STEP_TOTAL), minval=-halving, maxval=halving))
    number_within_segment = jnp.exp(jax.random.uniform(derived_prng_seeds[4], (HEADS, STEP_TOTAL // TOK_DEV), minval=-halving, maxval=halving))
    number_within_segment = jnp.repeat(number_within_segment, TOK_DEV, axis=1)
    spike_places = jax.random.randint(derived_prng_seeds[5], (3,), 0, STEP_TOTAL)
    kept_indicator = jax.random.uniform(derived_prng_seeds[6], (HEADS, 3), minval=0.6, maxval=0.8)
    entry_indices = jnp.arange(STEP_TOTAL, dtype=jnp.int32)
    hit_entries = entry_indices[:, None] == spike_places[None, :]
    spike_happenings = jnp.sum(jnp.where(hit_entries[None, :, :], jnp.log(kept_indicator)[:, None, :], 0.0), axis=2)
    return -(floor_intensity * jaggedness_level * number_within_segment) + spike_happenings


def block_scale(rng, extent, pieces, smallest, top_value):
    factor_of = 1.0
    for position, blocks in pieces:
        steps = jax.random.uniform(jax.random.fold_in(jax.random.fold_in(rng, 6), position), (blocks,), jnp.float32, smallest / len(pieces), top_value / len(pieces))
        factor_of = factor_of * jnp.repeat(jnp.exp(steps), extent[position] // blocks).reshape((-1,) + (1,) * (len(extent) - 1 - position))
    return factor_of


def centred(rng, shape, deviation, reach, cuts=(), kind=jnp.bfloat16):
    entries = jax.random.normal(rng, shape, jnp.float32) * deviation
    if len(cuts) > 0:
        entries = block_scale(rng, shape, cuts, -0.22, 0.18) * entries
    return jnp.clip(entries, min=-reach, max=reach).astype(kind)


def setup_inputs(seed: int = 0) -> dict:
    arg_keys = jax.random.split(jax.random.key(seed), 6)
    return {
        "token_values": centred(arg_keys[0], (STEP_TOTAL, WIDTH), 1.0, 6.0, ((0, 16), (1, 2))),
        "b_inputs": centred(arg_keys[1], (STEP_TOTAL, STATE), 1.0, 6.0, ((0, 16),)),
        "c_inputs": centred(arg_keys[2], (STEP_TOTAL, STATE), 1.0, 6.0, ((0, 16),)),
        "log_decay": draw_log_decay(jax.random.fold_in(arg_keys[5], 71), 0),
        "grad_out": centred(arg_keys[4], (STEP_TOTAL, WIDTH), 0.001, 0.005859375, ((0, 16), (1, 2))),
    }


PRECISE = lax.Precision.HIGHEST


def rounded(value):
    return lax.optimization_barrier(value.astype(jnp.bfloat16)).astype(jnp.float32)


def block_decays(decay_block):
    cumulative = jnp.cumsum(decay_block, axis=1)
    block_log = cumulative[:, -1]
    into_end = jnp.exp(block_log[:, None] - cumulative)
    from_start = jnp.exp(cumulative)
    return cumulative, into_end, from_start, jnp.exp(block_log)


def block_states(block_data):
    x_block, b_block, c_block, decay_block, dy_block = block_data
    cumulative, into_end, from_start, block_decay = block_decays(decay_block)
    b_float = b_block.astype(jnp.float32)
    c_float = c_block.astype(jnp.float32)
    decayed_b = rounded(into_end[:, :, None] * b_float[None])
    decayed_c = rounded(from_start[:, :, None] * c_float[None])
    x_heads = x_block.astype(jnp.float32).reshape(TOK_DEV, HEADS, HEAD_DIM)
    dy_heads = dy_block.astype(jnp.float32).reshape(TOK_DEV, HEADS, HEAD_DIM)
    state_local = jnp.einsum("htn,thp->nhp", decayed_b, x_heads, precision=PRECISE).reshape(STATE, WIDTH)
    adjoint_local = jnp.einsum("hsn,shp->nhp", decayed_c, dy_heads, precision=PRECISE).reshape(STATE, WIDTH)
    return state_local, adjoint_local, block_decay


def block_grads(block_data):
    x_block, b_block, c_block, decay_block, dy_block, state_in, adjoint_out = block_data
    cumulative, into_end, from_start, block_decay = block_decays(decay_block)
    b_float = b_block.astype(jnp.float32)
    c_float = c_block.astype(jnp.float32)
    x_float = x_block.astype(jnp.float32)
    dy_float = dy_block.astype(jnp.float32)
    scores = jnp.dot(c_float, b_float.T, precision=PRECISE)
    entry_indices = jnp.arange(TOK_DEV, dtype=jnp.int32)
    causal = entry_indices[:, None] >= entry_indices[None, :]
    to_end_cols = jnp.repeat(into_end.T, HEAD_DIM, axis=1)
    from_start_cols = jnp.repeat(from_start.T, HEAD_DIM, axis=1)
    x_scaled = x_float * to_end_cols
    dy_scaled = dy_float * from_start_cols

    def group_terms(group_idx):
        def head_step(running, offset):
            head_idx = group_idx * HEADS_DEV + offset
            cum_head = lax.dynamic_index_in_dim(cumulative, head_idx, 0, keepdims=False)
            log_gaps = cum_head[:, None] - cum_head[None, :]
            decays = jnp.where(causal, jnp.exp(jnp.where(causal, log_gaps, 0.0)), 0.0)
            mixing = rounded(scores * decays)
            x_head = lax.dynamic_slice_in_dim(x_float, head_idx * HEAD_DIM, HEAD_DIM, 1)
            dy_head = lax.dynamic_slice_in_dim(dy_float, head_idx * HEAD_DIM, HEAD_DIM, 1)
            dx_head = jnp.dot(mixing.T, dy_head, precision=PRECISE)
            dot_pairs = jnp.dot(dy_head, x_head.T, precision=PRECISE)
            return running + decays * dot_pairs, dx_head

        running, dx_heads = lax.scan(head_step, jnp.zeros((TOK_DEV, TOK_DEV), jnp.float32), jnp.arange(HEADS_DEV, dtype=jnp.int32))
        weighted = rounded(running)
        first_col = group_idx * WIDTH_DEV
        x_group = lax.dynamic_slice_in_dim(x_scaled, first_col, WIDTH_DEV, 1)
        dy_group = lax.dynamic_slice_in_dim(dy_scaled, first_col, WIDTH_DEV, 1)
        adj_group = lax.dynamic_slice_in_dim(adjoint_out, first_col, WIDTH_DEV, 1)
        state_group = lax.dynamic_slice_in_dim(state_in, first_col, WIDTH_DEV, 1)
        part_b = jnp.dot(weighted.T, c_float, precision=PRECISE) + jnp.dot(x_group, adj_group.T, precision=PRECISE)
        part_c = jnp.dot(weighted, b_float, precision=PRECISE) + jnp.dot(dy_group, state_group.T, precision=PRECISE)
        return dx_heads, rounded(part_b), rounded(part_c)

    dx_heads, db_groups, dc_groups = lax.map(group_terms, jnp.arange(N_HEAD, dtype=jnp.int32))
    dx_local = jnp.transpose(dx_heads.reshape(HEADS, TOK_DEV, HEAD_DIM), (1, 0, 2)).reshape(TOK_DEV, WIDTH)
    grad_values = dx_local + to_end_cols * jnp.dot(b_float, adjoint_out, precision=PRECISE)
    grad_b = jnp.sum(db_groups, axis=0)
    grad_c = jnp.sum(dc_groups, axis=0)
    return grad_values.astype(jnp.bfloat16), grad_b.astype(jnp.bfloat16), grad_c.astype(jnp.bfloat16)


def reference(token_values, b_inputs, c_inputs, log_decay, grad_out):
    blocks = STEP_TOTAL // TOK_DEV
    x_blocks = token_values.reshape(blocks, TOK_DEV, WIDTH)
    b_blocks = b_inputs.reshape(blocks, TOK_DEV, STATE)
    c_blocks = c_inputs.reshape(blocks, TOK_DEV, STATE)
    decay_blocks = jnp.transpose(log_decay.reshape(HEADS, blocks, TOK_DEV), (1, 0, 2))
    dy_blocks = grad_out.reshape(blocks, TOK_DEV, WIDTH)
    state_local, adjoint_local, block_decay = lax.map(block_states, (x_blocks, b_blocks, c_blocks, decay_blocks, dy_blocks))
    spread = jnp.repeat(block_decay, HEAD_DIM, axis=1)[:, None, :]

    def forward(carried, inputs):
        local_part, factor = inputs
        return factor * carried + local_part, carried

    def backward(carried, inputs):
        local_part, factor = inputs
        return local_part + factor * carried, carried

    start = jnp.zeros((STATE, WIDTH), jnp.float32)
    final_state, state_in = lax.scan(forward, start, (state_local, spread))
    final_adjoint, adjoint_out = lax.scan(backward, start, (adjoint_local, spread), reverse=True)
    grad_values, grad_b, grad_c = lax.map(block_grads, (x_blocks, b_blocks, c_blocks, decay_blocks, dy_blocks, state_in, adjoint_out))
    return grad_values.reshape(STEP_TOTAL, WIDTH), grad_b.reshape(STEP_TOTAL, STATE), grad_c.reshape(STEP_TOTAL, STATE)
```

```python
import functools

import jax
import jax.numpy as jnp
from jax import lax
from jax.experimental import pallas as pl
from jax.experimental.pallas import tpu as pltpu
from jax.sharding import PartitionSpec as P

BF16 = jnp.bfloat16
F32 = jnp.float32
GROUP = 4
LANES = 128
TAIL = 16
LOG2E = 1.4426950408889634
MIB = 1024 * 1024

NN = (((1,), (0,)), ((), ()))
NT = (((1,), (1,)), ((), ()))
TN = (((0,), (0,)), ((), ()))


def dot(a, b, dims):
    return lax.dot_general(a, b, dims, preferred_element_type=F32)


def iota(shape, dim):
    return lax.broadcasted_iota(jnp.int32, shape, dim)


def three(values):
    high = values.astype(BF16)
    rest = values - high.astype(F32)
    mid = rest.astype(BF16)
    return high, mid, (rest - mid.astype(F32)).astype(BF16)


def summed(mask, terms, copies=1):
    return sum(dot(mask, jnp.concatenate([t] * copies, axis=0), NT) for t in terms)


def head_of_lane(heads, head_dim, width, first, copies=1):
    shape = (copies * heads, width)
    rows = iota(shape, 0)
    if copies > 1:
        rows = lax.rem(rows, heads)
    return jnp.where(rows == first + iota(shape, 1) // head_dim, 1.0, 0.0).astype(BF16)


def whole(count):
    return [pl.BlockSpec(memory_space=pltpu.VMEM)] * count


SMEM = pl.BlockSpec(memory_space=pltpu.SMEM)


def params(mib):
    return pltpu.CompilerParams(vmem_limit_bytes=mib * MIB)


def local_kernel(forward, head_dim, place, ld, proj, cols, *outs):
    heads, length = ld.shape
    state, part = proj.shape[1], cols.shape[1] // GROUP
    scaled, decay = outs[0], outs[1]
    sends = outs[2:]
    terms = three(ld[...])
    rows, other = iota((length, length), 0), iota((length, length), 1)
    mask = jnp.where(other > rows if forward else other <= rows, 1.0, 0.0).astype(BF16)
    factors = jnp.exp(summed(mask, terms)).astype(BF16)
    decay[...] = factors
    if forward:
        total = jnp.exp(summed(jnp.ones((TAIL, length), BF16), terms))
        high = total.astype(BF16)
        low = (total - high.astype(F32)).astype(BF16)
        halves = jnp.where(iota(total.shape, 0) < TAIL // 2, high.astype(F32), low.astype(F32))
        halves = halves.astype(BF16)
    for k in range(GROUP):
        owner = place[0] ^ k
        where = pl.ds(pl.multiple_of(owner * part, part), part)
        hot = head_of_lane(heads, head_dim, part, owner * (heads // GROUP))
        spread = dot(factors, hot, NN).astype(BF16)
        piece = cols[:, where] * spread
        scaled[:, where] = piece
        sends[k][:state, :] = dot(proj[...], piece, TN).astype(BF16)
        if forward:
            sends[k][state:, :] = dot(halves, hot, NN).astype(BF16)


def local_states(forward, head_dim, place, ld, proj, cols):
    heads, length = ld.shape
    state, width = proj.shape[1], cols.shape[1]
    rows = state + (TAIL if forward else 0)
    return pl.pallas_call(
        functools.partial(local_kernel, forward, head_dim),
        out_shape=[
            jax.ShapeDtypeStruct(cols.shape, BF16),
            jax.ShapeDtypeStruct((length, heads), BF16),
        ]
        + [jax.ShapeDtypeStruct((rows, width // GROUP), BF16)] * GROUP,
        in_specs=[SMEM] + whole(3),
        out_specs=whole(2 + GROUP),
        compiler_params=params(16),
        cost_estimate=pl.CostEstimate(
            flops=2 * length * width * (state + heads),
            bytes_accessed=4 * length * width + 2 * state * width,
            transcendentals=length * heads,
        ),
        name="states_forward" if forward else "states_backward",
    )(place, ld, proj, cols)


def decay_row(ref, state):
    tail = ref[state:, :].astype(F32)
    return tail[:1, :] + tail[TAIL // 2 : TAIL // 2 + 1, :]


def put(ref, state, value, factor):
    ref[:state, :] = value.astype(BF16)
    high = factor.astype(BF16).astype(F32)
    shape = (TAIL, factor.shape[1])
    both = jnp.where(iota(shape, 0) < TAIL // 2, high, factor - high)
    ref[state:, :] = both.astype(BF16)


def entering_group(state, received):
    value = received[0][:state, :].astype(F32)
    factor = decay_row(received[0], state)
    for r in received[1:]:
        value = value + factor * r[:state, :].astype(F32)
        factor = factor * decay_row(r, state)
    return value, factor


def in_order(forward):
    return range(GROUP) if forward else range(GROUP - 1, -1, -1)


def total_kernel(forward, state, place, *refs):
    blocks, tails, out = refs[:GROUP], refs[-1 - GROUP : -1], refs[-1]
    for here in range(GROUP):

        @pl.when(place[0] == here)
        def _(here=here):
            value, factor = None, None
            for q in in_order(forward):
                piece = blocks[q ^ here][:state, :].astype(F32)
                d = decay_row(tails[q ^ here], state)
                value = piece if value is None else d * value + piece
                factor = d if factor is None else factor * d
            put(out, state, value, factor)


def group_total(forward, state, place, blocks, tails):
    operands = list(blocks) if forward else list(blocks) + list(tails)
    width = blocks[0].shape[1]
    return pl.pallas_call(
        functools.partial(total_kernel, forward, state),
        out_shape=jax.ShapeDtypeStruct((state + TAIL, width), BF16),
        in_specs=[SMEM] + whole(len(operands)),
        out_specs=whole(1)[0],
        compiler_params=params(8),
        cost_estimate=pl.CostEstimate(
            flops=8 * state * width, bytes_accessed=10 * state * width, transcendentals=0
        ),
        name="group_total",
    )(place, *operands)


def onward_kernel(state, own, *refs):
    received, out = refs[:-1], refs[-1]
    value, factor = entering_group(state, received)
    d = decay_row(own, state)
    put(out, state, own[:state, :].astype(F32) + d * value, d * factor)


def onward(state, own, received):
    return pl.pallas_call(
        functools.partial(onward_kernel, state),
        out_shape=jax.ShapeDtypeStruct(own.shape, BF16),
        in_specs=whole(1 + len(received)),
        out_specs=whole(1)[0],
        compiler_params=params(8),
        cost_estimate=pl.CostEstimate(flops=4 * own.size, bytes_accessed=6 * own.size, transcendentals=0),
        name="onward",
    )(own, *received)


def members_kernel(forward, state, n_received, place, *refs):
    received, refs = refs[:n_received], refs[n_received:]
    blocks, tails, outs = refs[:GROUP], refs[-2 * GROUP : -GROUP], refs[-GROUP:]
    entry, _ = entering_group(state, received)
    for here in range(GROUP):

        @pl.when(place[0] == here)
        def _(here=here):
            value = entry
            order = list(in_order(forward))
            for q in order:
                outs[q ^ here][...] = value.astype(BF16)
                if q != order[-1]:
                    d = decay_row(tails[q ^ here], state)
                    value = d * value + blocks[q ^ here][:state, :].astype(F32)


def member_entries(forward, state, place, received, blocks, tails):
    operands = list(received) + list(blocks) + ([] if forward else list(tails))
    width = blocks[0].shape[1]
    return pl.pallas_call(
        functools.partial(members_kernel, forward, state, len(received)),
        out_shape=[jax.ShapeDtypeStruct((state, width), BF16)] * GROUP,
        in_specs=[SMEM] + whole(len(operands)),
        out_specs=whole(GROUP),
        compiler_params=params(8),
        cost_estimate=pl.CostEstimate(
            flops=10 * state * width, bytes_accessed=20 * state * width, transcendentals=0
        ),
        name="member_entries",
    )(place, *operands)


def carried(forward, state, place, sends, tails=None):
    count = lax.axis_size("seq")
    groups = count // GROUP

    def to_member(block, k):
        return lax.ppermute(block, "seq", [(s, s ^ k) for s in range(count)])

    blocks = [sends[0]] + [to_member(sends[k], k) for k in range(1, GROUP)]
    tails = blocks if forward else tails
    own = group_total(forward, state, place, blocks, tails)
    received, sent, step = [], own, 1
    while step < groups:
        jump = step * GROUP if forward else -step * GROUP
        pairs = [(s, s + jump) for s in range(count) if 0 <= s + jump < count]
        received.append(lax.ppermute(sent, "seq", pairs))
        step *= 2
        if step < groups:
            sent = onward(state, own, received)
    entries = member_entries(forward, state, place, received, blocks, tails)
    return [entries[0]] + [to_member(entries[k], k) for k in range(1, GROUP)], blocks


def split_pairs(first, count):
    if count == 1:
        return []
    middle = first + count // 2
    return (
        [(first, middle, first + count)]
        + split_pairs(first, middle - first)
        + split_pairs(middle, first + count - middle)
    )


def inner_kernel(head_dim, ld, b, c, x, dy, dx_out, db_out, dc_out, cum_terms, *scratch):
    heads, length = ld.shape
    width, state = x.shape[1], b.shape[1]
    piece = head_dim
    pieces = length // piece
    cuts = split_pairs(0, pieces)
    near, near_sum, dx = scratch[:3]
    far, far_sum = scratch[3 : 3 + len(cuts)], scratch[3 + len(cuts) :]
    per_tile = LANES // head_dim
    step = pl.program_id(0)

    @pl.when(step == 0)
    def _():
        terms = three(ld[...] * LOG2E)
        rows, other = iota((length, length), 0), iota((length, length), 1)
        mask = jnp.where(other <= rows, 1.0, 0.0).astype(BF16)
        high, mid, low = three(summed(mask, terms, copies=3))
        lane = iota((length, 3 * heads), 1)
        picked = jnp.where(
            lane < heads,
            high.astype(F32),
            jnp.where(lane < 2 * heads, mid.astype(F32), low.astype(F32)),
        )
        cum_terms[...] = picked.astype(BF16)
        keep = iota((piece, LANES), 0) <= lax.rem(iota((piece, LANES), 1), piece)
        for n in range(pieces):
            rows_n = slice(n * piece, (n + 1) * piece)
            doubled = jnp.concatenate([c[rows_n, :]] * per_tile, axis=0)
            near[rows_n, :] = jnp.where(keep, dot(b[rows_n, :], doubled, NT), 0.0)
        near_sum[...] = jnp.zeros_like(near_sum)
        for (lo, mid_, hi), f, total in zip(cuts, far, far_sum):
            left, right = slice(lo * piece, mid_ * piece), slice(mid_ * piece, hi * piece)
            f[...] = dot(b[left, :], c[right, :], NT).astype(BF16)
            total[...] = jnp.zeros_like(total)

    hot = head_of_lane(heads, head_dim, width, step * (width // head_dim), copies=3)
    cum = dot(cum_terms[...], hot, NN)
    tile = (piece, LANES)
    diagonal = iota(tile, 0) == lax.rem(iota(tile, 1), piece)
    part_of_lane = iota(tile, 1) // head_dim
    for n in range(pieces):
        rows_n = slice(n * piece, (n + 1) * piece)
        total = near_sum[rows_n, :]
        scores = near[rows_n, :]
        for t in range(width // LANES):
            lanes = slice(t * LANES, (t + 1) * LANES)
            col = cum[rows_n, lanes]
            row = jnp.sum(jnp.where(diagonal, col, 0.0), axis=0, keepdims=True)
            decays = jnp.exp2(jnp.minimum(row - col, 0.0))
            dy_t = dy[rows_n, lanes]
            stacked = jnp.concatenate(
                [jnp.where(part_of_lane == h, dy_t, jnp.zeros_like(dy_t)) for h in range(per_tile)],
                axis=0,
            )
            dx[rows_n, lanes] = dot((scores * decays).astype(BF16), stacked, NN)
            total = total + decays * dot(x[rows_n, lanes], stacked, NT)
        near_sum[rows_n, :] = total
    for (lo, mid_, hi), f, total in zip(cuts, far, far_sum):
        left, right = slice(lo * piece, mid_ * piece), slice(mid_ * piece, hi * piece)
        edge = cum[mid_ * piece - 1 : mid_ * piece, :]
        to_edge = jnp.exp2(edge - cum[left, :])
        from_edge = jnp.exp2(cum[right, :] - edge)
        x_edge = (x[left, :].astype(F32) * to_edge).astype(BF16)
        dy_edge = (dy[right, :].astype(F32) * from_edge).astype(BF16)
        dx[left, :] += to_edge * dot(f[...], dy_edge, NN)
        total[...] += dot(x_edge, dy_edge, NT)
    dx_out[...] = dx[...].astype(BF16)

    @pl.when(step == pl.num_programs(0) - 1)
    def _():
        keep = (iota(tile, 0) <= iota(tile, 1)) & (part_of_lane == 0)
        for n in range(pieces):
            rows_n = slice(n * piece, (n + 1) * piece)
            total = near_sum[rows_n, :]
            total = sum(
                [pltpu.roll(total, h * head_dim, 1) for h in range(1, per_tile)], total
            )
            weighted = jnp.where(keep, total, 0.0).astype(BF16)
            doubled = jnp.concatenate([c[rows_n, :]] * per_tile, axis=0)
            db_out[rows_n, :] = dot(weighted, doubled, NN)
            dc_out[rows_n, :] = dot(weighted, b[rows_n, :], TN)[:piece, :]
        for (lo, mid_, hi), total in zip(cuts, far_sum):
            left, right = slice(lo * piece, mid_ * piece), slice(mid_ * piece, hi * piece)
            weighted = total[...].astype(BF16)
            db_out[left, :] += dot(weighted, c[right, :], NN)
            dc_out[right, :] += dot(weighted, b[left, :], TN)


def inner_terms(head_dim, ld, b, c, x, dy):
    heads, length = ld.shape
    state, width = b.shape[1], x.shape[1]
    chunk = width // 4
    piece = head_dim
    cuts = split_pairs(0, length // piece)
    sizes = [((mid - lo) * piece, (hi - mid) * piece) for lo, mid, hi in cuts]
    column = pl.BlockSpec((length, chunk), lambda i: (0, i))

    def fixed(shape):
        return pl.BlockSpec(shape, lambda i: (0, 0))

    return pl.pallas_call(
        functools.partial(inner_kernel, head_dim),
        grid=(width // chunk,),
        out_shape=[
            jax.ShapeDtypeStruct((length, width), BF16),
            jax.ShapeDtypeStruct((length, state), F32),
            jax.ShapeDtypeStruct((length, state), F32),
        ],
        in_specs=[fixed(ld.shape), fixed(b.shape), fixed(c.shape), column, column],
        out_specs=[column, fixed((length, state)), fixed((length, state))],
        scratch_shapes=[
            pltpu.VMEM((length, 3 * heads), BF16),
            pltpu.VMEM((length, LANES), F32),
            pltpu.VMEM((length, LANES), F32),
            pltpu.VMEM((length, chunk), F32),
        ]
        + [pltpu.VMEM(s, BF16) for s in sizes]
        + [pltpu.VMEM(s, F32) for s in sizes],
        compiler_params=params(24),
        cost_estimate=pl.CostEstimate(
            flops=16 * length * width * state,
            bytes_accessed=6 * length * width,
            transcendentals=3 * length * width,
        ),
        name="inner_terms",
    )(ld, b, c, x, dy)


def entry_c_kernel(place, scaled, part_local, *refs):
    entries, out = refs[:GROUP], refs[GROUP]
    part = scaled.shape[1] // GROUP
    total = part_local[...]
    for k in range(GROUP):
        where = pl.ds(pl.multiple_of((place[0] ^ k) * part, part), part)
        total = total + dot(scaled[:, where], entries[k][...], NT)
    out[...] = total.astype(BF16)


def entry_c(place, scaled, part_local, entries):
    return pl.pallas_call(
        entry_c_kernel,
        out_shape=jax.ShapeDtypeStruct(part_local.shape, BF16),
        in_specs=[SMEM] + whole(2 + GROUP),
        out_specs=whole(1)[0],
        compiler_params=params(12),
        cost_estimate=pl.CostEstimate(
            flops=2 * scaled.size * part_local.shape[1],
            bytes_accessed=2 * scaled.size,
            transcendentals=0,
        ),
        name="entry_c",
    )(place, scaled, part_local, *entries)


def entry_b_kernel(head_dim, place, decay, b, scaled, dx_local, part_local, *refs):
    entries, dx_out, out = refs[:GROUP], refs[GROUP], refs[GROUP + 1]
    heads = decay.shape[1]
    part = scaled.shape[1] // GROUP
    total = part_local[...]
    for k in range(GROUP):
        owner = place[0] ^ k
        where = pl.ds(pl.multiple_of(owner * part, part), part)
        entry = entries[k][...]
        hot = head_of_lane(heads, head_dim, part, owner * (heads // GROUP))
        spread = dot(decay[...], hot, NN)
        far = dx_local[:, where].astype(F32) + spread * dot(b[...], entry, NN)
        dx_out[:, where] = far.astype(BF16)
        total = total + dot(scaled[:, where], entry, NT)
    out[...] = total.astype(BF16)


def entry_b(head_dim, place, decay, b, scaled, dx_local, part_local, entries):
    return pl.pallas_call(
        functools.partial(entry_b_kernel, head_dim),
        out_shape=[
            jax.ShapeDtypeStruct(dx_local.shape, BF16),
            jax.ShapeDtypeStruct(part_local.shape, BF16),
        ],
        in_specs=[SMEM] + whole(5 + GROUP),
        out_specs=whole(2),
        compiler_params=params(20),
        cost_estimate=pl.CostEstimate(
            flops=5 * scaled.size * b.shape[1],
            bytes_accessed=6 * scaled.size,
            transcendentals=0,
        ),
        name="entry_b",
    )(place, decay, b, scaled, dx_local, part_local, *entries)


def over_heads(part):
    count = lax.axis_size("head")
    total = part.astype(F32)
    for shift in range(1, count):
        pairs = [(s, (s + shift) % count) for s in range(count)]
        total = total + lax.ppermute(part, "head", pairs).astype(F32)
    return total.astype(BF16)


def shards(token_values, b_inputs, c_inputs, log_decay, grad_out):
    head_dim = token_values.shape[1] // log_decay.shape[0]
    state = b_inputs.shape[1]
    place = lax.rem(lax.axis_index("seq"), GROUP).astype(jnp.int32)[None]
    x_scaled, x_decay, *x_sends = local_states(
        True, head_dim, place, log_decay, b_inputs, token_values
    )
    dy_scaled, _, *dy_sends = local_states(False, head_dim, place, log_decay, c_inputs, grad_out)
    state_in, blocks = carried(True, state, place, x_sends)
    adjoint_out, _ = carried(False, state, place, dy_sends, blocks)
    dx_local, db_local, dc_local = inner_terms(
        head_dim, log_decay, b_inputs, c_inputs, token_values, grad_out
    )
    part_c = entry_c(place, dy_scaled, dc_local, state_in)
    grad_values, part_b = entry_b(
        head_dim, place, x_decay, b_inputs, x_scaled, dx_local, db_local, adjoint_out
    )
    return grad_values, over_heads(part_b), over_heads(part_c)


def solution(mesh):
    in_specs = (
        P("seq", "head"),
        P("seq", None),
        P("seq", None),
        P("head", "seq"),
        P("seq", "head"),
    )
    out_specs = (P("seq", "head"), P("seq", None), P("seq", None))
    return jax.shard_map(shards, mesh=mesh, in_specs=in_specs, out_specs=out_specs, check_vma=False)
```

```python
import functools

import jax
import jax.numpy as jnp
from jax import lax
from jax.experimental import pallas as pl
from jax.experimental.pallas import tpu as pltpu
from jax.sharding import PartitionSpec as P

BF16 = jnp.bfloat16
F32 = jnp.float32
LANES = 128
TAIL = 16
LOG2E = 1.4426950408889634
MIB = 1024 * 1024

NN = (((1,), (0,)), ((), ()))
NT = (((1,), (1,)), ((), ()))
TN = (((0,), (0,)), ((), ()))


def dot(a, b, dims):
    return lax.dot_general(a, b, dims, preferred_element_type=F32)


def iota(shape, dim):
    return lax.broadcasted_iota(jnp.int32, shape, dim)


def three(values):
    high = values.astype(BF16)
    rest = values - high.astype(F32)
    mid = rest.astype(BF16)
    return high, mid, (rest - mid.astype(F32)).astype(BF16)


def summed(mask, terms, copies=1):
    return sum(dot(mask, jnp.concatenate([t] * copies, axis=0), NT) for t in terms)


def head_of_lane(heads, head_dim, width, first, copies=1):
    shape = (copies * heads, width)
    rows = iota(shape, 0)
    if copies > 1:
        rows = lax.rem(rows, heads)
    return jnp.where(rows == first + iota(shape, 1) // head_dim, 1.0, 0.0).astype(BF16)


def whole(count):
    return [pl.BlockSpec(memory_space=pltpu.VMEM)] * count


SMEM = pl.BlockSpec(memory_space=pltpu.SMEM)


def params(mib):
    return pltpu.CompilerParams(vmem_limit_bytes=mib * MIB)


def states_kernel(head_dim, group, ld_in, b_in, c_in, x_in, dy_in, *refs):
    x_scaled, dy_scaled, decay, sends, ld, b, c, x, dy, sems = refs
    pairs = [(ld_in, ld), (b_in, b), (x_in, x), (c_in, c), (dy_in, dy)]
    copies = [pltpu.make_async_copy(i, o, sems.at[n]) for n, (i, o) in enumerate(pairs)]
    for copy in copies:
        copy.start()
    copies[0].wait()
    heads, length = ld.shape
    state, part = b.shape[1], x.shape[1] // group
    terms = three(ld[...])
    rows, other = iota((length, length), 0), iota((length, length), 1)
    after = jnp.where(other > rows, 1.0, 0.0).astype(BF16)
    until = jnp.where(other <= rows, 1.0, 0.0).astype(BF16)
    into_end = jnp.exp(summed(after, terms)).astype(BF16)
    from_start = jnp.exp(summed(until, terms)).astype(BF16)
    decay[...] = into_end
    total = jnp.exp(summed(jnp.ones((TAIL, length), BF16), terms))
    high = total.astype(BF16).astype(F32)
    halves = jnp.where(iota(total.shape, 0) < TAIL // 2, high, total - high).astype(BF16)
    sides = [(into_end, b, x, x_scaled, 0), (from_start, c, dy, dy_scaled, state)]
    for side, (factors, proj, cols, scaled, first) in enumerate(sides):
        copies[1 + 2 * side].wait()
        copies[2 + 2 * side].wait()
        for j in range(group):
            lanes = slice(j * part, (j + 1) * part)
            hot = head_of_lane(heads, head_dim, part, j * (heads // group))
            piece = cols[:, lanes] * dot(factors, hot, NN).astype(BF16)
            scaled[:, lanes] = piece
            sends[j, first : first + state, :] = dot(proj[...], piece, TN).astype(BF16)
            if side == 0:
                sends[j, 2 * state :, :] = dot(halves, hot, NN).astype(BF16)


def local_states(head_dim, group, ld, b, c, x, dy):
    heads, length = ld.shape
    state, width = b.shape[1], x.shape[1]
    inputs = (ld, b, c, x, dy)
    return pl.pallas_call(
        functools.partial(states_kernel, head_dim, group),
        out_shape=[
            jax.ShapeDtypeStruct(x.shape, BF16),
            jax.ShapeDtypeStruct(x.shape, BF16),
            jax.ShapeDtypeStruct((length, heads), BF16),
            jax.ShapeDtypeStruct((group, 2 * state + TAIL, width // group), BF16),
        ],
        in_specs=[pl.BlockSpec(memory_space=pltpu.HBM)] * 5,
        out_specs=whole(4),
        scratch_shapes=[pltpu.VMEM(a.shape, a.dtype) for a in inputs]
        + [pltpu.SemaphoreType.DMA((5,))],
        compiler_params=params(24),
        cost_estimate=pl.CostEstimate(
            flops=4 * length * width * (state + heads),
            bytes_accessed=8 * length * width + 4 * state * width,
            transcendentals=2 * length * heads,
        ),
        name="local_states",
    )(*inputs)


def decay_of(tail):
    tail = tail.astype(F32)
    return tail[:1, :] + tail[TAIL // 2 : TAIL // 2 + 1, :]


def put(ref, state, value, factor):
    ref[:state, :] = value.astype(BF16)
    high = factor.astype(BF16).astype(F32)
    shape = (TAIL, factor.shape[1])
    both = jnp.where(iota(shape, 0) < TAIL // 2, high, factor - high)
    ref[state:, :] = both.astype(BF16)


def in_order(group, forward):
    return range(group) if forward else range(group - 1, -1, -1)


def side_rows(state, forward):
    return slice(0, state) if forward else slice(state, 2 * state)


def group_total(blocks, state, forward):
    group = blocks.shape[0]
    value, factor = None, None
    for q in in_order(group, forward):
        piece = blocks[q, side_rows(state, forward), :].astype(F32)
        d = decay_of(blocks[q, 2 * state :, :])
        value = piece if value is None else d * value + piece
        factor = d if factor is None else factor * d
    return value, factor


def totals_kernel(state, upper, blocks, *outs):
    if len(outs) == 2:
        for forward, out in zip((True, False), outs):
            put(out, state, *group_total(blocks, state, forward))
        return
    for forward in (True, False):

        @pl.when(upper[0] == (0 if forward else 1))
        def _(forward=forward):
            put(outs[0], state, *group_total(blocks, state, forward))


def totals(state, count, upper, blocks):
    part = blocks.shape[2]
    return pl.pallas_call(
        functools.partial(totals_kernel, state),
        out_shape=[jax.ShapeDtypeStruct((state + TAIL, part), BF16)] * count,
        in_specs=[SMEM] + whole(1),
        out_specs=whole(count),
        compiler_params=params(8),
        cost_estimate=pl.CostEstimate(
            flops=2 * blocks.size, bytes_accessed=2 * blocks.size, transcendentals=0
        ),
        name="totals",
    )(upper, blocks)


def before_group(state, received):
    value = received[0][:state, :].astype(F32)
    factor = decay_of(received[0][state:, :])
    for r in received[1:]:
        value = value + factor * r[:state, :].astype(F32)
        factor = factor * decay_of(r[state:, :])
    return value, factor


def onward_kernel(state, own, *refs):
    received, out = refs[:-1], refs[-1]
    value, factor = before_group(state, received)
    d = decay_of(own[state:, :])
    put(out, state, own[:state, :].astype(F32) + d * value, d * factor)


def onward(state, own, received):
    return pl.pallas_call(
        functools.partial(onward_kernel, state),
        out_shape=jax.ShapeDtypeStruct(own.shape, BF16),
        in_specs=whole(1 + len(received)),
        out_specs=whole(1)[0],
        compiler_params=params(8),
        cost_estimate=pl.CostEstimate(
            flops=4 * own.size, bytes_accessed=6 * own.size, transcendentals=0
        ),
        name="onward",
    )(own, *received)


def members_kernel(state, upper, blocks, *refs):
    received, out = refs[:-1], refs[-1]
    group = blocks.shape[0]
    for forward in (True, False):
        if len(received) == 1:
            mine = upper[0] == (1 if forward else 0)
            value = received[0][:state, :].astype(F32) * jnp.where(mine, 1.0, 0.0)
        else:
            half = len(received) // 2
            value, _ = before_group(state, received[:half] if forward else received[half:])
        order = list(in_order(group, forward))
        for q in order:
            out[q, side_rows(state, forward), :] = value.astype(BF16)
            if q != order[-1]:
                d = decay_of(blocks[q, 2 * state :, :])
                value = d * value + blocks[q, side_rows(state, forward), :].astype(F32)


def member_entries(state, upper, blocks, received):
    group, _, part = blocks.shape
    return pl.pallas_call(
        functools.partial(members_kernel, state),
        out_shape=jax.ShapeDtypeStruct((group, 2 * state, part), BF16),
        in_specs=[SMEM] + whole(1 + len(received)),
        out_specs=whole(1)[0],
        compiler_params=params(8),
        cost_estimate=pl.CostEstimate(
            flops=3 * blocks.size, bytes_accessed=4 * blocks.size, transcendentals=0
        ),
        name="member_entries",
    )(upper, blocks, *received)


def group_size(count, width):
    for group in (8, 4, 2):
        if count % group == 0 and (width // group) % LANES == 0:
            return group
    return 1


def entering(group, state, sends):
    count = lax.axis_size("seq")
    groups = count // group
    members = [[n * group + j for j in range(group)] for n in range(groups)]

    def exchange(blocks):
        return lax.all_to_all(
            blocks, "seq", 0, 0, axis_index_groups=members, tiled=True
        )

    upper = (lax.axis_index("seq") // group).astype(jnp.int32)[None]
    blocks = exchange(sends)
    if groups == 2:
        (own,) = totals(state, 1, upper, blocks)
        pairs = [(s, (s + group) % count) for s in range(count)]
        received = [lax.ppermute(own, "seq", pairs)]
    else:
        received = []
        for own, sign in zip(totals(state, 2, upper, blocks), (1, -1)):
            arrived, sent, step = [], own, 1
            while step < groups:
                jump = sign * step * group
                pairs = [(s, s + jump) for s in range(count) if 0 <= s + jump < count]
                arrived.append(lax.ppermute(sent, "seq", pairs))
                step *= 2
                if step < groups:
                    sent = onward(state, own, arrived)
            received += arrived
    return exchange(member_entries(state, upper, blocks, received))


def split_pairs(first, count):
    if count == 1:
        return []
    middle = first + count // 2
    return (
        [(first, middle, first + count)]
        + split_pairs(first, middle - first)
        + split_pairs(middle, first + count - middle)
    )


def inner_kernel(head_dim, ld, b, c, x, dy, dx_out, db_out, dc_out, cum_terms, *scratch):
    heads, length = ld.shape
    width, state = x.shape[1], b.shape[1]
    piece = head_dim
    pieces = length // piece
    cuts = split_pairs(0, pieces)
    near, near_sum, dx = scratch[:3]
    far, far_sum = scratch[3 : 3 + len(cuts)], scratch[3 + len(cuts) :]
    per_tile = LANES // head_dim
    step = pl.program_id(0)

    @pl.when(step == 0)
    def _():
        terms = three(ld[...] * LOG2E)
        rows, other = iota((length, length), 0), iota((length, length), 1)
        mask = jnp.where(other <= rows, 1.0, 0.0).astype(BF16)
        high, mid, low = three(summed(mask, terms, copies=3))
        lane = iota((length, 3 * heads), 1)
        picked = jnp.where(
            lane < heads,
            high.astype(F32),
            jnp.where(lane < 2 * heads, mid.astype(F32), low.astype(F32)),
        )
        cum_terms[...] = picked.astype(BF16)
        keep = iota((piece, LANES), 0) <= lax.rem(iota((piece, LANES), 1), piece)
        for n in range(pieces):
            rows_n = slice(n * piece, (n + 1) * piece)
            doubled = jnp.concatenate([c[rows_n, :]] * per_tile, axis=0)
            near[rows_n, :] = jnp.where(keep, dot(b[rows_n, :], doubled, NT), 0.0)
        near_sum[...] = jnp.zeros_like(near_sum)
        for (lo, mid_, hi), f, total in zip(cuts, far, far_sum):
            left, right = slice(lo * piece, mid_ * piece), slice(mid_ * piece, hi * piece)
            f[...] = dot(b[left, :], c[right, :], NT).astype(BF16)
            total[...] = jnp.zeros_like(total)

    hot = head_of_lane(heads, head_dim, width, step * (width // head_dim), copies=3)
    cum = dot(cum_terms[...], hot, NN)
    tile = (piece, LANES)
    diagonal = iota(tile, 0) == lax.rem(iota(tile, 1), piece)
    part_of_lane = iota(tile, 1) // head_dim
    for n in range(pieces):
        rows_n = slice(n * piece, (n + 1) * piece)
        total = near_sum[rows_n, :]
        scores = near[rows_n, :]
        for t in range(width // LANES):
            lanes = slice(t * LANES, (t + 1) * LANES)
            col = cum[rows_n, lanes]
            row = jnp.sum(jnp.where(diagonal, col, 0.0), axis=0, keepdims=True)
            decays = jnp.exp2(jnp.minimum(row - col, 0.0))
            dy_t = dy[rows_n, lanes]
            stacked = jnp.concatenate(
                [jnp.where(part_of_lane == h, dy_t, jnp.zeros_like(dy_t)) for h in range(per_tile)],
                axis=0,
            )
            dx[rows_n, lanes] = dot((scores * decays).astype(BF16), stacked, NN)
            total = total + decays * dot(x[rows_n, lanes], stacked, NT)
        near_sum[rows_n, :] = total
    for (lo, mid_, hi), f, total in zip(cuts, far, far_sum):
        left, right = slice(lo * piece, mid_ * piece), slice(mid_ * piece, hi * piece)
        edge = cum[mid_ * piece - 1 : mid_ * piece, :]
        to_edge = jnp.exp2(edge - cum[left, :])
        from_edge = jnp.exp2(cum[right, :] - edge)
        x_edge = (x[left, :].astype(F32) * to_edge).astype(BF16)
        dy_edge = (dy[right, :].astype(F32) * from_edge).astype(BF16)
        dx[left, :] += to_edge * dot(f[...], dy_edge, NN)
        total[...] += dot(x_edge, dy_edge, NT)
    dx_out[...] = dx[...].astype(BF16)

    @pl.when(step == pl.num_programs(0) - 1)
    def _():
        keep = (iota(tile, 0) <= iota(tile, 1)) & (part_of_lane == 0)
        for n in range(pieces):
            rows_n = slice(n * piece, (n + 1) * piece)
            total = near_sum[rows_n, :]
            total = sum(
                [pltpu.roll(total, h * head_dim, 1) for h in range(1, per_tile)], total
            )
            weighted = jnp.where(keep, total, 0.0).astype(BF16)
            doubled = jnp.concatenate([c[rows_n, :]] * per_tile, axis=0)
            db_out[rows_n, :] = dot(weighted, doubled, NN)
            dc_out[rows_n, :] = dot(weighted, b[rows_n, :], TN)[:piece, :]
        for (lo, mid_, hi), total in zip(cuts, far_sum):
            left, right = slice(lo * piece, mid_ * piece), slice(mid_ * piece, hi * piece)
            weighted = total[...].astype(BF16)
            db_out[left, :] += dot(weighted, c[right, :], NN)
            dc_out[right, :] += dot(weighted, b[left, :], TN)


def inner_terms(head_dim, ld, b, c, x, dy):
    heads, length = ld.shape
    state, width = b.shape[1], x.shape[1]
    chunk = width // 4
    piece = head_dim
    cuts = split_pairs(0, length // piece)
    sizes = [((mid - lo) * piece, (hi - mid) * piece) for lo, mid, hi in cuts]
    column = pl.BlockSpec((length, chunk), lambda i: (0, i))

    def fixed(shape):
        return pl.BlockSpec(shape, lambda i: (0, 0))

    return pl.pallas_call(
        functools.partial(inner_kernel, head_dim),
        grid=(width // chunk,),
        out_shape=[
            jax.ShapeDtypeStruct((length, width), BF16),
            jax.ShapeDtypeStruct((length, state), F32),
            jax.ShapeDtypeStruct((length, state), F32),
        ],
        in_specs=[fixed(ld.shape), fixed(b.shape), fixed(c.shape), column, column],
        out_specs=[column, fixed((length, state)), fixed((length, state))],
        scratch_shapes=[
            pltpu.VMEM((length, 3 * heads), BF16),
            pltpu.VMEM((length, LANES), F32),
            pltpu.VMEM((length, LANES), F32),
            pltpu.VMEM((length, chunk), F32),
        ]
        + [pltpu.VMEM(s, BF16) for s in sizes]
        + [pltpu.VMEM(s, F32) for s in sizes],
        compiler_params=params(24),
        cost_estimate=pl.CostEstimate(
            flops=16 * length * width * state,
            bytes_accessed=6 * length * width,
            transcendentals=3 * length * width,
        ),
        name="inner_terms",
    )(ld, b, c, x, dy)


def entry_kernel(head_dim, decay, b, x_scaled, dy_scaled, dx_local, db_local, dc_local, entries, *outs):
    dx_out, parts = outs
    group, rows, part = entries.shape
    state, heads, length = rows // 2, decay.shape[1], b.shape[0]
    db, dc = db_local[...], dc_local[...]
    for j in range(group):
        lanes = slice(j * part, (j + 1) * part)
        earlier, later = entries[j, :state, :], entries[j, state:, :]
        hot = head_of_lane(heads, head_dim, part, j * (heads // group))
        spread = dot(decay[...], hot, NN)
        far = dx_local[:, lanes].astype(F32) + spread * dot(b[...], later, NN)
        dx_out[:, lanes] = far.astype(BF16)
        db = db + dot(x_scaled[:, lanes], later, NT)
        dc = dc + dot(dy_scaled[:, lanes], earlier, NT)
    parts[:length, :] = db.astype(BF16)
    parts[length:, :] = dc.astype(BF16)


def entry_terms(head_dim, decay, b, x_scaled, dy_scaled, dx_local, db_local, dc_local, entries):
    length, state = b.shape
    operands = (decay, b, x_scaled, dy_scaled, dx_local, db_local, dc_local, entries)
    return pl.pallas_call(
        functools.partial(entry_kernel, head_dim),
        out_shape=[
            jax.ShapeDtypeStruct(dx_local.shape, BF16),
            jax.ShapeDtypeStruct((2 * length, state), BF16),
        ],
        in_specs=whole(len(operands)),
        out_specs=whole(2),
        compiler_params=params(20),
        cost_estimate=pl.CostEstimate(
            flops=7 * x_scaled.size * state,
            bytes_accessed=8 * x_scaled.size,
            transcendentals=0,
        ),
        name="entry_terms",
    )(*operands)


def over_heads(part):
    count = lax.axis_size("head")
    total = part.astype(F32)
    for shift in range(1, count):
        pairs = [(s, (s + shift) % count) for s in range(count)]
        total = total + lax.ppermute(part, "head", pairs).astype(F32)
    return total.astype(BF16)


def shards(token_values, b_inputs, c_inputs, log_decay, grad_out):
    head_dim = token_values.shape[1] // log_decay.shape[0]
    length, state = b_inputs.shape
    group = group_size(lax.axis_size("seq"), token_values.shape[1])
    inputs = (log_decay, b_inputs, c_inputs, token_values, grad_out)
    x_scaled, dy_scaled, decay, sends = local_states(head_dim, group, *inputs)
    entries = entering(group, state, sends)
    local = inner_terms(head_dim, *inputs)
    grad_values, parts = entry_terms(
        head_dim, decay, b_inputs, x_scaled, dy_scaled, *local, entries
    )
    both = over_heads(parts)
    return grad_values, both[:length], both[length:]


def solution(mesh):
    in_specs = (
        P("seq", "head"),
        P("seq", None),
        P("seq", None),
        P("head", "seq"),
        P("seq", "head"),
    )
    out_specs = (P("seq", "head"), P("seq", None), P("seq", None))
    return jax.shard_map(shards, mesh=mesh, in_specs=in_specs, out_specs=out_specs, check_vma=False)
```

```python
import functools

import jax
import jax.numpy as jnp
from jax import lax
from jax.experimental import pallas as pl
from jax.experimental.pallas import tpu as pltpu
from jax.sharding import PartitionSpec as P

BF16 = jnp.bfloat16
F32 = jnp.float32
LANES = 128
TAIL = 16
LOG2E = 1.4426950408889634
MIB = 1024 * 1024

NN = (((1,), (0,)), ((), ()))
NT = (((1,), (1,)), ((), ()))
TN = (((0,), (0,)), ((), ()))


def dot(a, b, dims):
    return lax.dot_general(a, b, dims, preferred_element_type=F32)


def iota(shape, dim):
    return lax.broadcasted_iota(jnp.int32, shape, dim)


def three(values):
    high = values.astype(BF16)
    rest = values - high.astype(F32)
    mid = rest.astype(BF16)
    return high, mid, (rest - mid.astype(F32)).astype(BF16)


SLOT = LANES // 4


def summed(mask, terms):
    heads, length = terms[0].shape
    gap = [] if heads == SLOT else [jnp.zeros((SLOT - heads, length), BF16)]
    rows = [r for t in terms for r in [t] + gap] + [jnp.zeros((SLOT, length), BF16)]
    each = dot(mask, jnp.concatenate(rows, axis=0), NT)
    return each + pltpu.roll(each, LANES - SLOT, 1) + pltpu.roll(each, LANES - 2 * SLOT, 1)


def head_of_lane(head_dim, width, first):
    shape = (LANES, width)
    return jnp.where(iota(shape, 0) == first + iota(shape, 1) // head_dim, 1.0, 0.0).astype(BF16)


def whole(count):
    return [pl.BlockSpec(memory_space=pltpu.VMEM)] * count


def in_hbm(*arrays):
    return [pltpu.with_memory_space_constraint(a, pltpu.HBM) for a in arrays]


SMEM = pl.BlockSpec(memory_space=pltpu.SMEM)
HBM = pl.BlockSpec(memory_space=pltpu.HBM)


def params(mib):
    return pltpu.CompilerParams(vmem_limit_bytes=mib * MIB)


def cost(flops, size, transcendentals=0):
    return pl.CostEstimate(
        flops=flops, bytes_accessed=size, transcendentals=transcendentals
    )


def part_lanes(place, k, part):
    return pl.ds(pl.multiple_of((place[0] ^ k) * part, part), part)


LOADS = 4


def states_kernel(head_dim, group, place, ld_in, b_in, c_in, x_in, dy_in, *refs):
    x_scaled, dy_scaled, decay = refs[:3]
    sends, (ld, b, c, x, dy, sems) = refs[3 : 3 + group], refs[3 + group :]
    heads, length = ld.shape
    state, width = b.shape[1], x.shape[1]
    part = width // group

    def copy(n, source, target):
        one = pltpu.make_async_copy(source, target, sems.at[n])
        one.start()
        return one

    small = [copy(n, i, o) for n, (i, o) in enumerate([(ld_in, ld), (b_in, b), (c_in, c)])]
    span = width // LOADS
    pieces = [slice(n * span, (n + 1) * span) for n in range(LOADS)]
    loads = [
        [copy(3 + side * LOADS + n, i.at[:, p], o.at[:, p]) for n, p in enumerate(pieces)]
        for side, (i, o) in enumerate([(x_in, x), (dy_in, dy)])
    ]
    small[0].wait()
    terms = three(ld[...])
    rows, other = iota((length, length), 0), iota((length, length), 1)
    after = jnp.where(other > rows, 1.0, 0.0).astype(BF16)
    until = jnp.where(other <= rows, 1.0, 0.0).astype(BF16)
    into_end = jnp.exp(summed(after, terms)).astype(BF16)
    from_start = jnp.exp(summed(until, terms)).astype(BF16)
    decay[...] = into_end
    total = jnp.exp(summed(jnp.ones((TAIL, length), BF16), terms))
    high = total.astype(BF16).astype(F32)
    halves = jnp.where(iota(total.shape, 0) < TAIL // 2, high, total - high).astype(BF16)
    small[1].wait()
    small[2].wait()
    sides = [(into_end, b, x, x_scaled, 0), (from_start, c, dy, dy_scaled, state)]
    for side, (factors, proj, cols, scaled, first) in enumerate(sides):
        turned = proj[...].T
        for load in loads[side]:
            load.wait()
        for k in range(group):
            lanes = part_lanes(place, k, part)
            hot = head_of_lane(head_dim, part, (place[0] ^ k) * (heads // group))
            piece = cols[:, lanes] * dot(factors, hot, NN).astype(BF16)
            scaled[:, lanes] = piece
            sends[k][first : first + state, :] = dot(turned, piece, NN).astype(BF16)
            if side == 0:
                sends[k][2 * state :, :] = dot(halves, hot, NN).astype(BF16)


def local_states(head_dim, group, place, ld, b, c, x, dy):
    length, width = x.shape
    state = b.shape[1]
    inputs = (ld, b, c, x, dy)
    send = pltpu.VMEM((2 * state + TAIL, width // group), BF16)
    return pl.pallas_call(
        functools.partial(states_kernel, head_dim, group),
        out_shape=[
            pltpu.VMEM(x.shape, BF16),
            pltpu.VMEM(x.shape, BF16),
            pltpu.VMEM((length, LANES), BF16),
        ]
        + [send] * group,
        in_specs=[SMEM] + [HBM] * 5,
        out_specs=whole(3 + group),
        scratch_shapes=[pltpu.VMEM(a.shape, a.dtype) for a in inputs]
        + [pltpu.SemaphoreType.DMA((3 + 2 * LOADS,))],
        compiler_params=params(16),
        cost_estimate=cost(4 * length * width * (state + LANES), 8 * length * width),
        name="local_states",
    )(place, *in_hbm(*inputs))


def decay_of(tail):
    tail = tail.astype(F32)
    return tail[:1, :] + tail[TAIL // 2 : TAIL // 2 + 1, :]


def put_decay(ref, state, factor):
    high = factor.astype(BF16).astype(F32)
    shape = (TAIL, factor.shape[1])
    both = jnp.where(iota(shape, 0) < TAIL // 2, high, factor - high)
    ref[state:, :] = both.astype(BF16)


def in_order(group, forward):
    return list(range(group)) if forward else list(range(group - 1, -1, -1))


def each_row_tile(state, body):
    tile = 32

    @pl.loop(0, state // tile)
    def _(n):
        body(pl.multiple_of(n * tile, tile), tile)


def put_total(out, blocks, here, state, forward):
    order = in_order(len(blocks), forward)
    first = 0 if forward else state
    decays = [decay_of(blocks[q ^ here][2 * state :, :]) for q in range(len(blocks))]

    def body(row, tile):
        value = None
        for q in order:
            piece = blocks[q ^ here][pl.ds(first + row, tile), :].astype(F32)
            value = piece if value is None else decays[q] * value + piece
        out[pl.ds(row, tile), :] = value.astype(BF16)

    each_row_tile(state, body)
    factor = decays[0]
    for d in decays[1:]:
        factor = factor * d
    put_decay(out, state, factor)


def totals_kernel(state, count, place, upper, *refs):
    blocks, outs = refs[:-count], refs[-count:]
    for here in range(len(blocks)):
        for n, forward in enumerate((True, False)):
            if len(outs) == 2:
                chosen, out = place[0] == here, outs[n]
            else:
                chosen, out = (place[0] == here) & (upper[0] == n), outs[0]

            @pl.when(chosen)
            def _(here=here, forward=forward, out=out):
                put_total(out, blocks, here, state, forward)


def totals(state, count, place, upper, blocks):
    out = pltpu.VMEM((state + TAIL, blocks[0].shape[1]), BF16)
    return pl.pallas_call(
        functools.partial(totals_kernel, state, count),
        out_shape=[out] * count,
        in_specs=[SMEM] * 2 + whole(len(blocks)),
        out_specs=whole(count),
        compiler_params=params(4),
        cost_estimate=cost(16 * blocks[0].size, 16 * blocks[0].size),
        name="totals",
    )(place, upper, *blocks)


def before_group(state, received):
    value = received[0][:state, :].astype(F32)
    factor = decay_of(received[0][state:, :])
    for r in received[1:]:
        value = value + factor * r[:state, :].astype(F32)
        factor = factor * decay_of(r[state:, :])
    return value, factor


def onward_kernel(state, own, *refs):
    received, out = refs[:-1], refs[-1]
    value, factor = before_group(state, received)
    d = decay_of(own[state:, :])
    out[:state, :] = (own[:state, :].astype(F32) + d * value).astype(BF16)
    put_decay(out, state, d * factor)


def onward(state, own, received):
    return pl.pallas_call(
        functools.partial(onward_kernel, state),
        out_shape=jax.ShapeDtypeStruct(own.shape, BF16),
        in_specs=whole(1 + len(received)),
        out_specs=whole(1)[0],
        compiler_params=params(4),
        cost_estimate=cost(4 * own.size, 6 * own.size),
        name="onward",
    )(own, *received)


def members_kernel(state, n_received, place, upper, *refs):
    received, refs = refs[:n_received], refs[n_received:]
    group = (len(refs) - 1) // 2
    blocks, outs, entry = refs[:group], refs[group:-1], refs[-1]
    for n, forward in enumerate((True, False)):
        if n_received == 1:
            value = received[0][:state, :].astype(F32)
            value = value * jnp.where(upper[0] == 1 - n, 1.0, 0.0)
        else:
            half = n_received // 2
            value, _ = before_group(state, received[n * half : (n + 1) * half])
        entry[n * state : (n + 1) * state, :] = value
    for here in range(group):

        @pl.when(place[0] == here)
        def _(here=here):
            decays = [decay_of(blocks[q ^ here][2 * state :, :]) for q in range(group)]

            def body(row, tile):
                for forward in (True, False):
                    where = pl.ds(row if forward else state + row, tile)
                    value = entry[where, :]
                    order = in_order(group, forward)
                    for q in order:
                        outs[q ^ here][where, :] = value.astype(BF16)
                        if q != order[-1]:
                            value = decays[q] * value + blocks[q ^ here][where, :].astype(F32)

            each_row_tile(state, body)


def member_entries(state, place, upper, blocks, received):
    group, part = len(blocks), blocks[0].shape[1]
    return pl.pallas_call(
        functools.partial(members_kernel, state, len(received)),
        out_shape=[pltpu.VMEM((2 * state, part), BF16)] * group,
        in_specs=[SMEM] * 2 + whole(group + len(received)),
        out_specs=whole(group),
        scratch_shapes=[pltpu.VMEM((2 * state, part), F32)],
        compiler_params=params(4),
        cost_estimate=cost(24 * blocks[0].size, 32 * blocks[0].size),
        name="member_entries",
    )(place, upper, *received, *blocks)


def group_size(count, width):
    for group in (8, 4, 2):
        if count % group == 0 and (width // group) % LANES == 0:
            return group
    return 1


def entering(group, state, place, sends):
    count = lax.axis_size("seq")
    groups = count // group
    upper = (lax.axis_index("seq") // group).astype(jnp.int32)[None]

    def exchange(parts):
        out = list(parts)
        for k in sorted(range(1, group), key=lambda k: (-bin(k).count("1"), k)):
            out[k] = lax.ppermute(parts[k], "seq", [(s, s ^ k) for s in range(count)])
        return out

    blocks = exchange(sends)
    if groups == 2:
        (own,) = totals(state, 1, place, upper, blocks)
        pairs = [(s, (s + group) % count) for s in range(count)]
        received = [lax.ppermute(own, "seq", pairs)]
    else:
        received = []
        for own, sign in zip(totals(state, 2, place, upper, blocks), (1, -1)):
            arrived, sent, step = [], own, 1
            while step < groups:
                jump = sign * step * group
                pairs = [(s, s + jump) for s in range(count) if 0 <= s + jump < count]
                arrived.append(lax.ppermute(sent, "seq", pairs))
                step *= 2
                if step < groups:
                    sent = onward(state, own, arrived)
            received += arrived
    return exchange(member_entries(state, place, upper, blocks, received))


def split_pairs(first, count):
    if count == 1:
        return []
    middle = first + count // 2
    return (
        [(first, middle, first + count)]
        + split_pairs(first, middle - first)
        + split_pairs(middle, first + count - middle)
    )


def inner_kernel(head_dim, ld, b, c, x, dy, dx_out, db_out, dc_out, cum_terms, *scratch):
    heads, length = ld.shape
    width, state = x.shape[1], b.shape[1]
    piece = head_dim
    pieces = length // piece
    cuts = split_pairs(0, pieces)
    near, near_sum, dx = scratch[:3]
    far, far_sum = scratch[3 : 3 + len(cuts)], scratch[3 + len(cuts) :]
    per_tile = LANES // head_dim
    step = pl.program_id(0)

    @pl.when(step == 0)
    def _():
        rows, other = iota((length, length), 0), iota((length, length), 1)
        mask = jnp.where(other <= rows, 1.0, 0.0).astype(BF16)
        cum_small = summed(mask, three(ld[...] * LOG2E))
        lane = iota(cum_small.shape, 1)
        in_slots = jnp.where(lane < SLOT, cum_small, 0.0)
        in_slots = (
            in_slots + pltpu.roll(in_slots, SLOT, 1) + pltpu.roll(in_slots, 2 * SLOT, 1)
        )
        high, mid, low = three(in_slots)
        cum_terms[...] = jnp.where(lane < SLOT, high, jnp.where(lane < 2 * SLOT, mid, low))
        keep = iota((piece, LANES), 0) <= lax.rem(iota((piece, LANES), 1), piece)
        for n in range(pieces):
            rows_n = slice(n * piece, (n + 1) * piece)
            doubled = jnp.concatenate([c[rows_n, :]] * per_tile, axis=0)
            near[rows_n, :] = jnp.where(keep, dot(b[rows_n, :], doubled, NT), 0.0)
        near_sum[...] = jnp.zeros_like(near_sum)
        for (lo, mid_, hi), f, total in zip(cuts, far, far_sum):
            left, right = slice(lo * piece, mid_ * piece), slice(mid_ * piece, hi * piece)
            f[...] = dot(b[left, :], c[right, :], NT).astype(BF16)
            total[...] = jnp.zeros_like(total)

    shape = (LANES, width)
    owner = step * (width // head_dim) + iota(shape, 1) // head_dim
    slot = lax.rem(iota(shape, 0), SLOT) == owner
    hot = jnp.where(slot & (iota(shape, 0) < 3 * SLOT), 1.0, 0.0).astype(BF16)
    cum = dot(cum_terms[...], hot, NN)
    tile = (piece, LANES)
    diagonal = iota(tile, 0) == lax.rem(iota(tile, 1), piece)
    part_of_lane = iota(tile, 1) // head_dim
    for n in range(pieces):
        rows_n = slice(n * piece, (n + 1) * piece)
        total = near_sum[rows_n, :]
        scores = near[rows_n, :]
        for t in range(width // LANES):
            lanes = slice(t * LANES, (t + 1) * LANES)
            col = cum[rows_n, lanes]
            row = jnp.sum(jnp.where(diagonal, col, 0.0), axis=0, keepdims=True)
            decays = jnp.exp2(jnp.minimum(row - col, 0.0))
            dy_t = dy[rows_n, lanes]
            stacked = jnp.concatenate(
                [jnp.where(part_of_lane == h, dy_t, jnp.zeros_like(dy_t)) for h in range(per_tile)],
                axis=0,
            )
            dx[rows_n, lanes] = dot((scores * decays).astype(BF16), stacked, NN)
            total = total + decays * dot(x[rows_n, lanes], stacked, NT)
        near_sum[rows_n, :] = total
    for (lo, mid_, hi), f, total in zip(cuts, far, far_sum):
        left, right = slice(lo * piece, mid_ * piece), slice(mid_ * piece, hi * piece)
        edge = cum[mid_ * piece - 1 : mid_ * piece, :]
        to_edge = jnp.exp2(edge - cum[left, :])
        from_edge = jnp.exp2(cum[right, :] - edge)
        x_edge = (x[left, :].astype(F32) * to_edge).astype(BF16)
        dy_edge = (dy[right, :].astype(F32) * from_edge).astype(BF16)
        dx[left, :] += to_edge * dot(f[...], dy_edge, NN)
        total[...] += dot(x_edge, dy_edge, NT)
    lanes = pl.ds(pl.multiple_of(step * width, width), width)
    dx_out[:, lanes] = dx[...].astype(BF16)

    @pl.when(step == pl.num_programs(0) - 1)
    def _():
        keep = (iota(tile, 0) <= iota(tile, 1)) & (part_of_lane == 0)
        for n in range(pieces):
            rows_n = slice(n * piece, (n + 1) * piece)
            total = near_sum[rows_n, :]
            total = sum(
                [pltpu.roll(total, h * head_dim, 1) for h in range(1, per_tile)], total
            )
            weighted = jnp.where(keep, total, 0.0).astype(BF16)
            doubled = jnp.concatenate([c[rows_n, :]] * per_tile, axis=0)
            db_out[rows_n, :] = dot(weighted, doubled, NN)
            dc_out[rows_n, :] = dot(weighted, b[rows_n, :], TN)[:piece, :]
        for (lo, mid_, hi), total in zip(cuts, far_sum):
            left, right = slice(lo * piece, mid_ * piece), slice(mid_ * piece, hi * piece)
            weighted = total[...].astype(BF16)
            db_out[left, :] += dot(weighted, c[right, :], NN)
            dc_out[right, :] += dot(weighted, b[left, :], TN)


def inner_terms(head_dim, ld, b, c, x, dy):
    heads, length = ld.shape
    state, width = b.shape[1], x.shape[1]
    chunk = width // 4
    piece = head_dim
    cuts = split_pairs(0, length // piece)
    sizes = [((mid - lo) * piece, (hi - mid) * piece) for lo, mid, hi in cuts]
    column = pl.BlockSpec((length, chunk), lambda i: (0, i))

    def fixed(shape):
        return pl.BlockSpec(shape, lambda i: (0, 0))

    return pl.pallas_call(
        functools.partial(inner_kernel, head_dim),
        grid=(width // chunk,),
        out_shape=[
            pltpu.VMEM((length, width), BF16),
            pltpu.VMEM((length, state), F32),
            pltpu.VMEM((length, state), F32),
        ],
        in_specs=[fixed(ld.shape), fixed(b.shape), fixed(c.shape), column, column],
        out_specs=whole(3),
        scratch_shapes=[
            pltpu.VMEM((length, LANES), BF16),
            pltpu.VMEM((length, LANES), F32),
            pltpu.VMEM((length, LANES), F32),
            pltpu.VMEM((length, chunk), F32),
        ]
        + [pltpu.VMEM(s, BF16) for s in sizes]
        + [pltpu.VMEM(s, F32) for s in sizes],
        compiler_params=params(24),
        cost_estimate=cost(16 * length * width * state, 6 * length * width, 3 * length * width),
        name="inner_terms",
    )(*in_hbm(ld, b, c, x, dy))


def parts_kernel(place, x_scaled, dy_scaled, db_local, dc_local, *refs):
    entries, out = refs[:-1], refs[-1]
    length, state = db_local.shape
    part = entries[0].shape[1]
    db, dc = db_local[...], dc_local[...]
    for k, entry in enumerate(entries):
        lanes = part_lanes(place, k, part)
        db = db + dot(x_scaled[:, lanes], entry[state:, :], NT)
        dc = dc + dot(dy_scaled[:, lanes], entry[:state, :], NT)
    out[:length, :] = db.astype(BF16)
    out[length:, :] = dc.astype(BF16)


def entry_parts(place, x_scaled, dy_scaled, db_local, dc_local, entries):
    length, state = db_local.shape
    return pl.pallas_call(
        parts_kernel,
        out_shape=pltpu.VMEM((2 * length, state), BF16),
        in_specs=[SMEM] + whole(4 + len(entries)),
        out_specs=whole(1)[0],
        compiler_params=params(8),
        cost_estimate=cost(4 * x_scaled.size * state, 4 * x_scaled.size),
        name="entry_parts",
    )(place, x_scaled, dy_scaled, db_local, dc_local, *entries)


def values_kernel(head_dim, place, decay, b_in, dx_local, *refs):
    entries, (out, b, dx, sems) = refs[:-4], refs[-4:]
    state, part = b.shape[1], entries[0].shape[1]
    load = pltpu.make_async_copy(b_in, b, sems.at[len(entries)])
    load.start()
    load.wait()
    stores = []
    for k, entry in enumerate(entries):
        lanes = part_lanes(place, k, part)
        hot = head_of_lane(head_dim, part, (place[0] ^ k) * (part // head_dim))
        far = dot(decay[...], hot, NN) * dot(b[...], entry[state:, :], NN)
        dx[k] = (dx_local[:, lanes].astype(F32) + far).astype(BF16)
        store = pltpu.make_async_copy(dx.at[k], out.at[:, lanes], sems.at[k])
        store.start()
        stores.append(store)
    for store in stores:
        store.wait()


def entry_values(head_dim, place, decay, b, dx_local, entries):
    group, part = len(entries), entries[0].shape[1]
    length, state = b.shape
    return pl.pallas_call(
        functools.partial(values_kernel, head_dim),
        out_shape=pltpu.HBM(dx_local.shape, BF16),
        in_specs=[SMEM] + whole(1) + [HBM] + whole(1 + group),
        out_specs=HBM,
        scratch_shapes=[
            pltpu.VMEM(b.shape, BF16),
            pltpu.VMEM((group, length, part), BF16),
            pltpu.SemaphoreType.DMA((group + 1,)),
        ],
        compiler_params=params(8),
        cost_estimate=cost(4 * dx_local.size * state, 4 * dx_local.size),
        name="entry_values",
    )(place, decay, *in_hbm(b), dx_local, *entries)


def over_heads(part):
    count = lax.axis_size("head")
    total = part.astype(F32)
    for shift in range(1, count):
        pairs = [(s, (s + shift) % count) for s in range(count)]
        total = total + lax.ppermute(part, "head", pairs).astype(F32)
    return total.astype(BF16)


def shards(token_values, b_inputs, c_inputs, log_decay, grad_out):
    head_dim = token_values.shape[1] // log_decay.shape[0]
    length, state = b_inputs.shape
    group = group_size(lax.axis_size("seq"), token_values.shape[1])
    place = lax.rem(lax.axis_index("seq"), group).astype(jnp.int32)[None]
    inputs = (log_decay, b_inputs, c_inputs, token_values, grad_out)
    x_scaled, dy_scaled, decay, *sends = local_states(head_dim, group, place, *inputs)
    entries = entering(group, state, place, sends)
    dx_local, db_local, dc_local = inner_terms(head_dim, *inputs)
    parts = entry_parts(place, x_scaled, dy_scaled, db_local, dc_local, entries)
    grad_values = entry_values(head_dim, place, decay, b_inputs, dx_local, entries)
    both = over_heads(parts)
    return grad_values, both[:length], both[length:]


def solution(mesh):
    in_specs = (
        P("seq", "head"),
        P("seq", None),
        P("seq", None),
        P("head", "seq"),
        P("seq", "head"),
    )
    out_specs = (P("seq", "head"), P("seq", None), P("seq", None))
    return jax.shard_map(shards, mesh=mesh, in_specs=in_specs, out_specs=out_specs, check_vma=False)
```

```python
import functools

import jax
import jax.numpy as jnp
from jax import lax
from jax.experimental import pallas as pl
from jax.experimental.pallas import tpu as pltpu
from jax.sharding import PartitionSpec as P

BF16 = jnp.bfloat16
F32 = jnp.float32
LANES = 128
GROUP = 4
TAIL = 16
LOG2E = 1.4426950408889634
MIB = 1024 * 1024

NN = (((1,), (0,)), ((), ()))
NT = (((1,), (1,)), ((), ()))
TN = (((0,), (0,)), ((), ()))


def dot(a, b, dims):
    return lax.dot_general(a, b, dims, preferred_element_type=F32)


def iota(shape, dim):
    return lax.broadcasted_iota(jnp.int32, shape, dim)


def three(values):
    high = values.astype(BF16)
    rest = values - high.astype(F32)
    mid = rest.astype(BF16)
    return high, mid, (rest - mid.astype(F32)).astype(BF16)


SLOT = LANES // 4


def summed(mask, terms):
    heads, length = terms[0].shape
    gap = [] if heads == SLOT else [jnp.zeros((SLOT - heads, length), BF16)]
    rows = [r for t in terms for r in [t] + gap] + [jnp.zeros((SLOT, length), BF16)]
    each = dot(mask, jnp.concatenate(rows, axis=0), NT)
    return each + pltpu.roll(each, LANES - SLOT, 1) + pltpu.roll(each, LANES - 2 * SLOT, 1)


def head_of_lane(head_dim, width, first):
    shape = (LANES, width)
    return jnp.where(iota(shape, 0) == first + iota(shape, 1) // head_dim, 1.0, 0.0).astype(BF16)


def whole(count):
    return [pl.BlockSpec(memory_space=pltpu.VMEM)] * count


def in_hbm(*arrays):
    return [pltpu.with_memory_space_constraint(a, pltpu.HBM) for a in arrays]


SMEM = pl.BlockSpec(memory_space=pltpu.SMEM)
HBM = pl.BlockSpec(memory_space=pltpu.HBM)
ANY = pl.BlockSpec(memory_space=pl.ANY)


def params(mib):
    return pltpu.CompilerParams(vmem_limit_bytes=mib * MIB)


def cost(flops, size, transcendentals=0):
    return pl.CostEstimate(
        flops=flops, bytes_accessed=size, transcendentals=transcendentals
    )


def chunk_count(width):
    return 2 if (width // GROUP) % (2 * LANES) == 0 else 1


def chunk_lanes(place, k, chunk, part, width):
    start = (place[0] ^ k) * (width // GROUP) + chunk * part
    return pl.ds(pl.multiple_of(start, part), part)


def factors_of(ld):
    length = ld.shape[1]
    terms = three(ld)
    rows, other = iota((length, length), 0), iota((length, length), 1)
    after = jnp.where(other > rows, 1.0, 0.0).astype(BF16)
    until = jnp.where(other <= rows, 1.0, 0.0).astype(BF16)
    into_end = jnp.exp(summed(after, terms)).astype(BF16)
    from_start = jnp.exp(summed(until, terms)).astype(BF16)
    total = jnp.exp(summed(jnp.ones((TAIL, length), BF16), terms))
    high = total.astype(BF16).astype(F32)
    halves = jnp.where(iota(total.shape, 0) < TAIL // 2, high, total - high).astype(BF16)
    return into_end, from_start, halves


def put_states(head_dim, chunk, place, operands, outs, ready):
    into_end, from_start, halves, b, c, x, dy = operands
    x_scaled, dy_scaled, spread, *sends = outs
    group, state = len(sends), b.shape[1]
    width = x.shape[1]
    chunks = chunk_count(width)
    part = width // (group * chunks)
    sides = [(into_end, b, x, x_scaled, 0), (from_start, c, dy, dy_scaled, state)]
    for side, (factors, proj, cols, scaled, first) in enumerate(sides):
        ready(side)
        turned = proj[...].T
        for k in range(group):
            here = slice(k * part, (k + 1) * part)
            lanes = chunk_lanes(place, k, chunk, part, width)
            first_head = ((place[0] ^ k) * chunks + chunk) * (part // head_dim)
            hot = head_of_lane(head_dim, part, first_head)
            wide = dot(factors, hot, NN).astype(BF16)
            if side == 0:
                spread[:, here] = wide
                sends[k][2 * state :, :] = dot(halves, hot, NN).astype(BF16)
            piece = cols[:, lanes] * wide
            scaled[:, here] = piece
            sends[k][first : first + state, :] = dot(turned, piece, NN).astype(BF16)


def first_states_kernel(head_dim, group, place, ld_in, b_in, c_in, x_in, dy_in, *refs):
    ld, b, c, x, dy, into_end, from_start, halves = refs[:8]
    outs, sems = refs[8:-1], refs[-1]
    pairs = [(ld_in, ld), (b_in, b), (x_in, x), (c_in, c), (dy_in, dy)]
    copies = [pltpu.make_async_copy(i, o, sems.at[n]) for n, (i, o) in enumerate(pairs)]
    for copy in copies:
        copy.start()
    copies[0].wait()
    factors = factors_of(ld[...])
    for ref, value in zip((into_end, from_start, halves), factors):
        ref[...] = value

    def ready(side):
        copies[1 + 2 * side].wait()
        copies[2 + 2 * side].wait()

    put_states(head_dim, 0, place, (*factors, b, c, x, dy), outs, ready)


def next_states_kernel(head_dim, chunk, place, into_end, from_start, halves, *refs):
    operands = (into_end[...], from_start[...], halves[...], *refs[:4])
    put_states(head_dim, chunk, place, operands, refs[4:], lambda side: None)


def states_shapes(group, length, width, state):
    part = width // (group * chunk_count(width))
    scaled = pltpu.VMEM((length, group * part), BF16)
    return [scaled] * 3 + [pltpu.VMEM((2 * state + TAIL, part), BF16)] * group


def first_states(head_dim, group, place, inputs):
    ld, b, c, x, dy = inputs
    (length, width), state = x.shape, b.shape[1]
    kept = [pltpu.VMEM(a.shape, a.dtype) for a in inputs]
    kept += [pltpu.VMEM((rows, LANES), BF16) for rows in (length, length, TAIL)]
    outs = kept + states_shapes(group, length, width, state)
    return pl.pallas_call(
        functools.partial(first_states_kernel, head_dim, group),
        out_shape=outs,
        in_specs=[SMEM] + [HBM] * 5,
        out_specs=whole(len(outs)),
        scratch_shapes=[pltpu.SemaphoreType.DMA((5,))],
        compiler_params=params(8),
        cost_estimate=cost(2 * length * width * (state + LANES), 8 * length * width),
        name="first_states",
    )(place, *in_hbm(*inputs))


def next_states(head_dim, group, chunk, place, factors, b, c, x, dy):
    (length, width), state = x.shape, b.shape[1]
    outs = states_shapes(group, length, width, state)
    return pl.pallas_call(
        functools.partial(next_states_kernel, head_dim, chunk),
        out_shape=outs,
        in_specs=[SMEM] + whole(7),
        out_specs=whole(len(outs)),
        compiler_params=params(8),
        cost_estimate=cost(2 * length * width * (state + LANES), 4 * length * width),
        name="next_states",
    )(place, *factors, b, c, x, dy)


def decay_of(tail):
    tail = tail.astype(F32)
    return tail[:1, :] + tail[TAIL // 2 : TAIL // 2 + 1, :]


def put_decay(ref, first, factor):
    high = factor.astype(BF16).astype(F32)
    shape = (TAIL, factor.shape[1])
    both = jnp.where(iota(shape, 0) < TAIL // 2, high, factor - high)
    ref[first:, :] = both.astype(BF16)


def in_order(group, forward):
    return list(range(group)) if forward else list(range(group - 1, -1, -1))


def side_rows(state, forward):
    return slice(0, state) if forward else slice(state, 2 * state)


def totals_kernel(state, place, *refs):
    group = GROUP
    blocks, out = refs[:group], refs[-1]
    for here in range(group):

        @pl.when(place[0] == here)
        def _(here=here):
            decays = [decay_of(blocks[q ^ here][2 * state :, :]) for q in range(group)]
            for forward in (True, False):
                rows, value = side_rows(state, forward), None
                for q in in_order(group, forward):
                    piece = blocks[q ^ here][rows, :].astype(F32)
                    value = piece if value is None else decays[q] * value + piece
                out[rows, :] = value.astype(BF16)
            factor = decays[0]
            for d in decays[1:]:
                factor = factor * d
            put_decay(out, 2 * state, factor)


def totals(state, place, blocks, after):
    return pl.pallas_call(
        functools.partial(totals_kernel, state),
        out_shape=pltpu.VMEM(blocks[0].shape, BF16),
        in_specs=[SMEM] + whole(len(blocks)) + [ANY] * len(after),
        out_specs=whole(1)[0],
        compiler_params=params(4),
        cost_estimate=cost(8 * blocks[0].size, 10 * blocks[0].size),
        name="totals",
    )(place, *blocks, *after)


def merged_kernel(state, level, last, number, own, received, *refs):
    out = refs[-1]
    d_own, d_other = decay_of(own[2 * state :, :]), decay_of(received[2 * state :, :])
    upper = ((number[0] >> level) & 1) == 1
    later = ((number[0] >> (level + 1)) & 1) == 1
    for is_upper in (False, True):
        for forward in (True, False):
            chosen = upper == is_upper
            if last:
                chosen = chosen & (later != forward)

            @pl.when(chosen)
            def _(is_upper=is_upper, forward=forward):
                rows = side_rows(state, forward)
                mine, other = own[rows, :].astype(F32), received[rows, :].astype(F32)
                value = mine + d_own * other if is_upper == forward else other + d_other * mine
                out[slice(0, state) if last else rows, :] = value.astype(BF16)

    put_decay(out, state if last else 2 * state, d_own * d_other)


def merged(state, level, last, number, own, received, after):
    rows = (state if last else 2 * state) + TAIL
    return pl.pallas_call(
        functools.partial(merged_kernel, state, level, last),
        out_shape=pltpu.VMEM((rows, own.shape[1]), BF16),
        in_specs=[SMEM] + whole(2) + [ANY] * len(after),
        out_specs=whole(1)[0],
        compiler_params=params(4),
        cost_estimate=cost(4 * own.size, 6 * own.size),
        name="merged",
    )(number, own, received, *after)


def members_kernel(state, levels, place, number, *refs):
    received, refs = refs[:levels], refs[levels:]
    group = GROUP
    blocks, outs = refs[:group], refs[-group:]
    entry = []
    for forward in (True, False):
        value, factor = None, 1.0
        for level, r in enumerate(received):
            gets = (((number[0] >> level) & 1) == 1) == forward
            rows = side_rows(state, forward)
            if r.shape[0] < 2 * state:
                rows = slice(0, state)
            piece = r[rows, :].astype(F32) * jnp.where(gets, 1.0, 0.0)
            value = piece if value is None else value + factor * piece
            if level < levels - 1:
                factor = factor * jnp.where(gets, decay_of(r[2 * state :, :]), 1.0)
        entry.append(value)
    for here in range(group):

        @pl.when(place[0] == here)
        def _(here=here):
            decays = [decay_of(blocks[q ^ here][2 * state :, :]) for q in range(group)]
            for forward in (True, False):
                rows, order = side_rows(state, forward), in_order(group, forward)
                value = entry[0 if forward else 1]
                for q in order:
                    outs[q ^ here][rows, :] = value.astype(BF16)
                    if q != order[-1]:
                        value = decays[q] * value + blocks[q ^ here][rows, :].astype(F32)


def member_entries(state, place, number, blocks, received, after):
    group, part = len(blocks), blocks[0].shape[1]
    return pl.pallas_call(
        functools.partial(members_kernel, state, len(received)),
        out_shape=[pltpu.VMEM((2 * state, part), BF16)] * group,
        in_specs=[SMEM] * 2 + whole(group + len(received)) + [ANY] * len(after),
        out_specs=whole(group),
        compiler_params=params(4),
        cost_estimate=cost(12 * blocks[0].size, 16 * blocks[0].size),
        name="member_entries",
    )(place, number, *received, *blocks, *after)


def exchange(parts):
    count = lax.axis_size("seq")
    out = list(parts)
    for k in sorted(range(1, len(parts)), key=lambda k: (-bin(k).count("1"), k)):
        out[k] = lax.ppermute(parts[k], "seq", [(s, s ^ k) for s in range(count)])
    return out


def split_pairs(first, count):
    if count == 1:
        return []
    middle = first + count // 2
    return (
        [(first, middle, first + count)]
        + split_pairs(first, middle - first)
        + split_pairs(middle, first + count - middle)
    )


def inner_kernel(head_dim, chunk, n_before, n_after, ld, b, c, x_all, dy_all, *refs):
    before, refs = refs[:n_before], refs[n_before + n_after :]
    dx_out, db_out, dc_out, x, dy, cum_terms, *scratch = refs
    length, width = x.shape
    piece = head_dim
    pieces = length // piece
    cuts = split_pairs(0, pieces)
    near, near_sum, dx = scratch[:3]
    far, far_sum = scratch[3 : 3 + len(cuts)], scratch[3 + len(cuts) :]
    per_tile = LANES // head_dim
    step = pl.program_id(0)
    owned = (step * chunk_count(x_all.shape[1]) + chunk) * width
    columns = pl.ds(pl.multiple_of(owned, width), width)
    x[...] = x_all[:, columns]
    dy[...] = dy_all[:, columns]

    @pl.when(step == 0)
    def _():
        rows, other = iota((length, length), 0), iota((length, length), 1)
        mask = jnp.where(other <= rows, 1.0, 0.0).astype(BF16)
        cum_small = summed(mask, three(ld[...] * LOG2E))
        lane = iota(cum_small.shape, 1)
        in_slots = jnp.where(lane < SLOT, cum_small, 0.0)
        in_slots = (
            in_slots + pltpu.roll(in_slots, SLOT, 1) + pltpu.roll(in_slots, 2 * SLOT, 1)
        )
        high, mid, low = three(in_slots)
        cum_terms[...] = jnp.where(lane < SLOT, high, jnp.where(lane < 2 * SLOT, mid, low))
        keep = iota((piece, LANES), 0) <= lax.rem(iota((piece, LANES), 1), piece)
        for n in range(pieces):
            rows_n = slice(n * piece, (n + 1) * piece)
            doubled = jnp.concatenate([c[rows_n, :]] * per_tile, axis=0)
            near[rows_n, :] = jnp.where(keep, dot(b[rows_n, :], doubled, NT), 0.0)
        near_sum[...] = jnp.zeros_like(near_sum)
        for (lo, mid_, hi), f, total in zip(cuts, far, far_sum):
            left, right = slice(lo * piece, mid_ * piece), slice(mid_ * piece, hi * piece)
            f[...] = dot(b[left, :], c[right, :], NT).astype(BF16)
            total[...] = jnp.zeros_like(total)

    shape = (LANES, width)
    owner = owned // head_dim + iota(shape, 1) // head_dim
    slot = lax.rem(iota(shape, 0), SLOT) == owner
    hot = jnp.where(slot & (iota(shape, 0) < 3 * SLOT), 1.0, 0.0).astype(BF16)
    cum = dot(cum_terms[...], hot, NN)
    tile = (piece, LANES)
    diagonal = iota(tile, 0) == lax.rem(iota(tile, 1), piece)
    part_of_lane = iota(tile, 1) // head_dim
    for n in range(pieces):
        rows_n = slice(n * piece, (n + 1) * piece)
        total = near_sum[rows_n, :]
        scores = near[rows_n, :]
        for t in range(width // LANES):
            lanes = slice(t * LANES, (t + 1) * LANES)
            col = cum[rows_n, lanes]
            row = jnp.sum(jnp.where(diagonal, col, 0.0), axis=0, keepdims=True)
            decays = jnp.exp2(jnp.minimum(row - col, 0.0))
            dy_t = dy[rows_n, lanes]
            stacked = jnp.concatenate(
                [jnp.where(part_of_lane == h, dy_t, jnp.zeros_like(dy_t)) for h in range(per_tile)],
                axis=0,
            )
            dx[rows_n, lanes] = dot((scores * decays).astype(BF16), stacked, NN)
            total = total + decays * dot(x[rows_n, lanes], stacked, NT)
        near_sum[rows_n, :] = total
    for (lo, mid_, hi), f, total in zip(cuts, far, far_sum):
        left, right = slice(lo * piece, mid_ * piece), slice(mid_ * piece, hi * piece)
        edge = cum[mid_ * piece - 1 : mid_ * piece, :]
        to_edge = jnp.exp2(edge - cum[left, :])
        from_edge = jnp.exp2(cum[right, :] - edge)
        x_edge = (x[left, :].astype(F32) * to_edge).astype(BF16)
        dy_edge = (dy[right, :].astype(F32) * from_edge).astype(BF16)
        dx[left, :] += to_edge * dot(f[...], dy_edge, NN)
        total[...] += dot(x_edge, dy_edge, NT)
    lanes = pl.ds(pl.multiple_of(step * width, width), width)
    dx_out[:, lanes] = dx[...].astype(BF16)

    @pl.when(step == pl.num_programs(0) - 1)
    def _():
        keep = (iota(tile, 0) <= iota(tile, 1)) & (part_of_lane == 0)
        for n in range(pieces):
            rows_n = slice(n * piece, (n + 1) * piece)
            total = near_sum[rows_n, :]
            total = sum(
                [pltpu.roll(total, h * head_dim, 1) for h in range(1, per_tile)], total
            )
            weighted = jnp.where(keep, total, 0.0).astype(BF16)
            doubled = jnp.concatenate([c[rows_n, :]] * per_tile, axis=0)
            db = dot(weighted, doubled, NN)
            dc = dot(weighted, b[rows_n, :], TN)[:piece, :]
            if before:
                db, dc = db + before[0][rows_n, :], dc + before[1][rows_n, :]
            db_out[rows_n, :] = db
            dc_out[rows_n, :] = dc
        for (lo, mid_, hi), total in zip(cuts, far_sum):
            left, right = slice(lo * piece, mid_ * piece), slice(mid_ * piece, hi * piece)
            weighted = total[...].astype(BF16)
            db_out[left, :] += dot(weighted, c[right, :], NN)
            dc_out[right, :] += dot(weighted, b[left, :], TN)


def inner_terms(head_dim, group, chunk, ld, b, c, x, dy, before, after):
    length, state = b.shape
    part = x.shape[1] // (group * chunk_count(x.shape[1]))
    piece = head_dim
    cuts = split_pairs(0, length // piece)
    sizes = [((mid - lo) * piece, (hi - mid) * piece) for lo, mid, hi in cuts]
    return pl.pallas_call(
        functools.partial(inner_kernel, head_dim, chunk, len(before), len(after)),
        grid=(group,),
        out_shape=[
            pltpu.VMEM((length, group * part), BF16),
            pltpu.VMEM((length, state), F32),
            pltpu.VMEM((length, state), F32),
        ],
        in_specs=whole(5 + len(before)) + [ANY] * len(after),
        out_specs=whole(3),
        scratch_shapes=[
            pltpu.VMEM((length, part), BF16),
            pltpu.VMEM((length, part), BF16),
            pltpu.VMEM((length, LANES), BF16),
            pltpu.VMEM((length, LANES), F32),
            pltpu.VMEM((length, LANES), F32),
            pltpu.VMEM((length, part), F32),
        ]
        + [pltpu.VMEM(s, BF16) for s in sizes]
        + [pltpu.VMEM(s, F32) for s in sizes],
        compiler_params=params(16),
        cost_estimate=cost(8 * x.size * state, 4 * x.size, 2 * x.size),
        name="inner_terms",
    )(ld, b, c, x, dy, *before, *after)


def parts_kernel(last, x_scaled, dy_scaled, db_before, dc_before, *refs):
    entries, outs = refs[:GROUP], refs[-1 if last else -2 :]
    length, state = db_before.shape
    part = entries[0].shape[1]
    db, dc = db_before[...], dc_before[...]
    for k, entry in enumerate(entries):
        here = slice(k * part, (k + 1) * part)
        db = db + dot(x_scaled[:, here], entry[state:, :], NT)
        dc = dc + dot(dy_scaled[:, here], entry[:state, :], NT)
    if last:
        outs[0][:length, :] = db.astype(BF16)
        outs[0][length:, :] = dc.astype(BF16)
    else:
        outs[0][...] = db
        outs[1][...] = dc


def entry_parts(last, x_scaled, dy_scaled, db_before, dc_before, entries, after):
    length, state = db_before.shape
    one = pltpu.VMEM((length, state), F32)
    outs = [pltpu.VMEM((2 * length, state), BF16)] if last else [one, one]
    return pl.pallas_call(
        functools.partial(parts_kernel, last),
        out_shape=outs,
        in_specs=whole(4 + len(entries)) + [ANY] * len(after),
        out_specs=whole(len(outs)),
        compiler_params=params(8),
        cost_estimate=cost(4 * x_scaled.size * state, 4 * x_scaled.size),
        name="entry_parts",
    )(x_scaled, dy_scaled, db_before, dc_before, *entries, *after)


def values_kernel(chunk, n_before, place, spread, b, dx_local, *refs):
    entries, (out, dx, sems) = refs[: len(refs) - 3 - n_before], refs[-3:]
    state, part = b.shape[1], entries[0].shape[1]
    stores = []
    for k, entry in enumerate(entries):
        here = slice(k * part, (k + 1) * part)
        local = dx_local[:, pl.ds(pl.multiple_of((place[0] ^ k) * part, part), part)]
        far = spread[:, here].astype(F32) * dot(b[...], entry[state:, :], NN)
        dx[k] = (local.astype(F32) + far).astype(BF16)
        lanes = chunk_lanes(place, k, chunk, part, out.shape[1])
        store = pltpu.make_async_copy(dx.at[k], out.at[:, lanes], sems.at[k])
        store.start()
        stores.append(store)
    for store in stores:
        store.wait()


def entry_values(chunk, chunks, place, spread, b, dx_local, entries, before):
    group, part = len(entries), entries[0].shape[1]
    length, state = b.shape
    size = dx_local.size
    operands = [place, spread, b, dx_local, *entries, *before]
    return pl.pallas_call(
        functools.partial(values_kernel, chunk, len(before)),
        out_shape=pltpu.HBM((length, chunks * group * part), BF16),
        in_specs=[SMEM] + whole(3 + group) + [HBM] * len(before),
        out_specs=HBM,
        input_output_aliases={len(operands) - 1: 0} if before else {},
        scratch_shapes=[
            pltpu.VMEM((group, length, part), BF16),
            pltpu.SemaphoreType.DMA((group,)),
        ],
        compiler_params=params(8),
        cost_estimate=cost(2 * size * state, 4 * size),
        name="entry_values",
    )(*operands)


def over_heads(part):
    count = lax.axis_size("head")
    total = part.astype(F32)
    for shift in range(1, count):
        pairs = [(s, (s + shift) % count) for s in range(count)]
        total = total + lax.ppermute(part, "head", pairs).astype(F32)
    return total.astype(BF16)


def shards(token_values, b_inputs, c_inputs, log_decay, grad_out):
    head_dim = token_values.shape[1] // log_decay.shape[0]
    length, state = b_inputs.shape
    count = lax.axis_size("seq")
    group, chunks = GROUP, chunk_count(token_values.shape[1])
    levels = (count // group).bit_length() - 1
    where = lax.axis_index("seq").astype(jnp.int32)
    place, number = lax.rem(where, group)[None], (where // group)[None]
    inputs = (log_decay, b_inputs, c_inputs, token_values, grad_out)

    ld, b, c, x, dy, *rest = first_states(head_dim, group, place, inputs)
    factors, states = rest[:3], [rest[3:]]
    blocks = [exchange(states[0][3:])]
    for chunk in range(1, chunks):
        states.append(next_states(head_dim, group, chunk, place, factors, b, c, x, dy))
        blocks.append(exchange(states[chunk][3:]))

    entries, inner, sums = [], [], []
    for chunk in range(chunks):
        sent = own = totals(state, place, blocks[chunk], sums[:1])
        received = []
        for level in range(levels):
            step = group << level
            pairs = [(s, s ^ step) for s in range(count)]
            received.append(lax.ppermute(sent, "seq", pairs))
            if len(inner) < chunks and chunk == 0:
                inner.append(
                    inner_terms(head_dim, group, len(inner), ld, b, c, x, dy, sums, [sent])
                )
                sums = list(inner[-1][1:])
            if level < levels - 1:
                last = level == levels - 2
                after = sums if chunk == 0 else []
                both = merged(state, level, last, number, own, received[-1], after)
                sent = both
                if not last:
                    own = both
        after = sums if chunk == 0 else []
        found = member_entries(state, place, number, blocks[chunk], received, after)
        entries.append(exchange(found))
    while len(inner) < chunks:
        inner.append(inner_terms(head_dim, group, len(inner), ld, b, c, x, dy, sums, []))
        sums = list(inner[-1][1:])

    grad_values = []
    for chunk in range(chunks):
        x_scaled, dy_scaled, spread = states[chunk][:3]
        last = chunk == chunks - 1
        sums = entry_parts(last, x_scaled, dy_scaled, *sums, entries[chunk], grad_values)
        out = entry_values(chunk, chunks, place, spread, b, inner[chunk][0], entries[chunk], grad_values)
        grad_values = [out]
    both = over_heads(sums[0])
    return grad_values[0], both[:length], both[length:]


def solution(mesh):
    in_specs = (
        P("seq", "head"),
        P("seq", None),
        P("seq", None),
        P("head", "seq"),
        P("seq", "head"),
    )
    out_specs = (P("seq", "head"), P("seq", None), P("seq", None))
    return jax.shard_map(shards, mesh=mesh, in_specs=in_specs, out_specs=out_specs, check_vma=False)
```

```python
import functools

import jax
import jax.numpy as jnp
from jax import lax
from jax.experimental import pallas as pl
from jax.experimental.pallas import tpu as pltpu
from jax.sharding import PartitionSpec as P

BF16 = jnp.bfloat16
F32 = jnp.float32
LANES = 128
GROUP = 4
TAIL = 16
LOG2E = 1.4426950408889634
MIB = 1024 * 1024

NN = (((1,), (0,)), ((), ()))
NT = (((1,), (1,)), ((), ()))
TN = (((0,), (0,)), ((), ()))


def dot(a, b, dims):
    return lax.dot_general(a, b, dims, preferred_element_type=F32)


def iota(shape, dim):
    return lax.broadcasted_iota(jnp.int32, shape, dim)


def three(values):
    high = values.astype(BF16)
    rest = values - high.astype(F32)
    mid = rest.astype(BF16)
    return high, mid, (rest - mid.astype(F32)).astype(BF16)


SLOT = LANES // 4


def summed(mask, terms):
    heads, length = terms[0].shape
    gap = [] if heads == SLOT else [jnp.zeros((SLOT - heads, length), BF16)]
    rows = [r for t in terms for r in [t] + gap] + [jnp.zeros((SLOT, length), BF16)]
    each = dot(mask, jnp.concatenate(rows, axis=0), NT)
    return each + pltpu.roll(each, LANES - SLOT, 1) + pltpu.roll(each, LANES - 2 * SLOT, 1)


def head_of_lane(head_dim, width, first):
    shape = (LANES, width)
    return jnp.where(iota(shape, 0) == first + iota(shape, 1) // head_dim, 1.0, 0.0).astype(BF16)


def whole(count):
    return [pl.BlockSpec(memory_space=pltpu.VMEM)] * count


def in_hbm(*arrays):
    return [pltpu.with_memory_space_constraint(a, pltpu.HBM) for a in arrays]


SMEM = pl.BlockSpec(memory_space=pltpu.SMEM)
HBM = pl.BlockSpec(memory_space=pltpu.HBM)
ANY = pl.BlockSpec(memory_space=pl.ANY)


def params(mib):
    return pltpu.CompilerParams(vmem_limit_bytes=mib * MIB)


def cost(flops, size, transcendentals=0):
    del flops, size, transcendentals
    return pl.CostEstimate(flops=1, bytes_accessed=1, transcendentals=0)


def place_of(where):
    return where[0] & (GROUP - 1)


def bit_of(where, level):
    return (where[0] >> (level + GROUP.bit_length() - 1)) & 1 == 1


def chunk_count(width):
    return 2 if (width // GROUP) % (2 * LANES) == 0 else 1


def chunk_lanes(where, k, chunk, part, width):
    start = (place_of(where) ^ k) * (width // GROUP) + chunk * part
    return pl.ds(pl.multiple_of(start, part), part)


def factors_of(ld):
    length = ld.shape[1]
    terms = three(ld)
    rows, other = iota((length, length), 0), iota((length, length), 1)
    after = jnp.where(other > rows, 1.0, 0.0).astype(BF16)
    until = jnp.where(other <= rows, 1.0, 0.0).astype(BF16)
    into_end = jnp.exp(summed(after, terms)).astype(BF16)
    from_start = jnp.exp(summed(until, terms)).astype(BF16)
    total = jnp.exp(summed(jnp.ones((TAIL, length), BF16), terms))
    high = total.astype(BF16).astype(F32)
    halves = jnp.where(iota(total.shape, 0) < TAIL // 2, high, total - high).astype(BF16)
    return into_end, from_start, halves


def put_states(head_dim, chunk, where, operands, outs, ready):
    into_end, from_start, halves, b, c, x, dy = operands
    x_scaled, dy_scaled, spread, *sends = outs
    group, state = len(sends), b.shape[1]
    width = x.shape[1]
    chunks = chunk_count(width)
    part = width // (group * chunks)
    sides = [(into_end, b, x, x_scaled, 0), (from_start, c, dy, dy_scaled, state)]
    for side, (factors, proj, cols, scaled, first) in enumerate(sides):
        ready(side)
        turned = proj[...].T
        for k in range(group):
            here = slice(k * part, (k + 1) * part)
            lanes = chunk_lanes(where, k, chunk, part, width)
            first_head = ((place_of(where) ^ k) * chunks + chunk) * (part // head_dim)
            hot = head_of_lane(head_dim, part, first_head)
            wide = dot(factors, hot, NN).astype(BF16)
            if side == 0:
                spread[:, here] = wide
                sends[k][2 * state :, :] = dot(halves, hot, NN).astype(BF16)
            piece = cols[:, lanes] * wide
            scaled[:, here] = piece
            sends[k][first : first + state, :] = dot(turned, piece, NN).astype(BF16)


def first_states_kernel(head_dim, group, where, ld_in, b_in, c_in, x_in, dy_in, *refs):
    ld, b, c, x, dy, into_end, from_start, halves = refs[:8]
    outs, sems = refs[8:-1], refs[-1]
    pairs = [(ld_in, ld), (b_in, b), (x_in, x), (c_in, c), (dy_in, dy)]
    copies = [pltpu.make_async_copy(i, o, sems.at[n]) for n, (i, o) in enumerate(pairs)]
    for copy in copies:
        copy.start()
    copies[0].wait()
    factors = factors_of(ld[...])
    for ref, value in zip((into_end, from_start, halves), factors):
        ref[...] = value

    def ready(side):
        copies[1 + 2 * side].wait()
        copies[2 + 2 * side].wait()

    put_states(head_dim, 0, where, (*factors, b, c, x, dy), outs, ready)


def next_states_kernel(head_dim, chunk, where, into_end, from_start, halves, *refs):
    operands = (into_end[...], from_start[...], halves[...], *refs[:4])
    put_states(head_dim, chunk, where, operands, refs[4:], lambda side: None)


def states_shapes(group, length, width, state):
    part = width // (group * chunk_count(width))
    scaled = pltpu.VMEM((length, group * part), BF16)
    return [scaled] * 3 + [pltpu.VMEM((2 * state + TAIL, part), BF16)] * group


def first_states(head_dim, group, where, inputs):
    ld, b, c, x, dy = inputs
    (length, width), state = x.shape, b.shape[1]
    kept = [pltpu.VMEM(a.shape, a.dtype) for a in inputs]
    kept += [pltpu.VMEM((rows, LANES), BF16) for rows in (length, length, TAIL)]
    outs = kept + states_shapes(group, length, width, state)
    return pl.pallas_call(
        functools.partial(first_states_kernel, head_dim, group),
        out_shape=outs,
        in_specs=[SMEM] + [HBM] * 5,
        out_specs=whole(len(outs)),
        scratch_shapes=[pltpu.SemaphoreType.DMA((5,))],
        compiler_params=params(8),
        cost_estimate=cost(2 * length * width * (state + LANES), 8 * length * width),
        name="first_states",
    )(where, *in_hbm(*inputs))


def next_states(head_dim, group, chunk, where, factors, b, c, x, dy):
    (length, width), state = x.shape, b.shape[1]
    outs = states_shapes(group, length, width, state)
    return pl.pallas_call(
        functools.partial(next_states_kernel, head_dim, chunk),
        out_shape=outs,
        in_specs=[SMEM] + whole(7),
        out_specs=whole(len(outs)),
        compiler_params=params(8),
        cost_estimate=cost(2 * length * width * (state + LANES), 4 * length * width),
        name="next_states",
    )(where, *factors, b, c, x, dy)


def decay_of(tail):
    tail = tail.astype(F32)
    return tail[:1, :] + tail[TAIL // 2 : TAIL // 2 + 1, :]


def put_decay(ref, first, factor):
    high = factor.astype(BF16).astype(F32)
    shape = (TAIL, factor.shape[1])
    both = jnp.where(iota(shape, 0) < TAIL // 2, high, factor - high)
    ref[first:, :] = both.astype(BF16)


def in_order(group, forward):
    return list(range(group)) if forward else list(range(group - 1, -1, -1))


def side_rows(state, forward):
    return slice(0, state) if forward else slice(state, 2 * state)


def totals_kernel(state, where, *refs):
    group = GROUP
    blocks, out = refs[:group], refs[-1]
    for here in range(group):

        @pl.when(place_of(where) == here)
        def _(here=here):
            decays = [decay_of(blocks[q ^ here][2 * state :, :]) for q in range(group)]
            for forward in (True, False):
                rows, value = side_rows(state, forward), None
                for q in in_order(group, forward):
                    piece = blocks[q ^ here][rows, :].astype(F32)
                    value = piece if value is None else decays[q] * value + piece
                out[rows, :] = value.astype(BF16)
            factor = decays[0]
            for d in decays[1:]:
                factor = factor * d
            put_decay(out, 2 * state, factor)


def totals(state, where, blocks, after):
    return pl.pallas_call(
        functools.partial(totals_kernel, state),
        out_shape=pltpu.VMEM(blocks[0].shape, BF16),
        in_specs=[SMEM] + whole(len(blocks)) + [ANY] * len(after),
        out_specs=whole(1)[0],
        compiler_params=params(4),
        cost_estimate=cost(8 * blocks[0].size, 10 * blocks[0].size),
        name="totals",
    )(where, *blocks, *after)


def merged_kernel(state, level, last, where, own, received, *refs):
    out = refs[-1]
    d_own, d_other = decay_of(own[2 * state :, :]), decay_of(received[2 * state :, :])
    upper = bit_of(where, level)
    later = bit_of(where, level + 1)
    for is_upper in (False, True):
        for forward in (True, False):
            chosen = upper == is_upper
            if last:
                chosen = chosen & (later != forward)

            @pl.when(chosen)
            def _(is_upper=is_upper, forward=forward):
                rows = side_rows(state, forward)
                mine, other = own[rows, :].astype(F32), received[rows, :].astype(F32)
                value = mine + d_own * other if is_upper == forward else other + d_other * mine
                out[slice(0, state) if last else rows, :] = value.astype(BF16)

    put_decay(out, state if last else 2 * state, d_own * d_other)


def merged(state, level, last, where, own, received, after):
    rows = (state if last else 2 * state) + TAIL
    return pl.pallas_call(
        functools.partial(merged_kernel, state, level, last),
        out_shape=pltpu.VMEM((rows, own.shape[1]), BF16),
        in_specs=[SMEM] + whole(2) + [ANY] * len(after),
        out_specs=whole(1)[0],
        compiler_params=params(4),
        cost_estimate=cost(4 * own.size, 6 * own.size),
        name="merged",
    )(where, own, received, *after)


def members_kernel(state, levels, where, *refs):
    received, refs = refs[:levels], refs[levels:]
    group = GROUP
    blocks, outs = refs[:group], refs[-group:]
    entry = []
    for forward in (True, False):
        value, factor = None, 1.0
        for level, r in enumerate(received):
            gets = (bit_of(where, level)) == forward
            rows = side_rows(state, forward)
            if r.shape[0] < 2 * state:
                rows = slice(0, state)
            piece = r[rows, :].astype(F32) * jnp.where(gets, 1.0, 0.0)
            value = piece if value is None else value + factor * piece
            if level < levels - 1:
                factor = factor * jnp.where(gets, decay_of(r[2 * state :, :]), 1.0)
        entry.append(value)
    for here in range(group):

        @pl.when(place_of(where) == here)
        def _(here=here):
            decays = [decay_of(blocks[q ^ here][2 * state :, :]) for q in range(group)]
            for forward in (True, False):
                rows, order = side_rows(state, forward), in_order(group, forward)
                value = entry[0 if forward else 1]
                for q in order:
                    outs[q ^ here][rows, :] = value.astype(BF16)
                    if q != order[-1]:
                        value = decays[q] * value + blocks[q ^ here][rows, :].astype(F32)


def member_entries(state, where, blocks, received, after):
    group, part = len(blocks), blocks[0].shape[1]
    return pl.pallas_call(
        functools.partial(members_kernel, state, len(received)),
        out_shape=[pltpu.VMEM((2 * state, part), BF16)] * group,
        in_specs=[SMEM] + whole(group + len(received)) + [ANY] * len(after),
        out_specs=whole(group),
        compiler_params=params(4),
        cost_estimate=cost(12 * blocks[0].size, 16 * blocks[0].size),
        name="member_entries",
    )(where, *received, *blocks, *after)


def exchange(parts):
    count = lax.axis_size("seq")
    out = list(parts)
    for k in sorted(range(1, len(parts)), key=lambda k: (-bin(k).count("1"), k)):
        out[k] = lax.ppermute(parts[k], "seq", [(s, s ^ k) for s in range(count)])
    return out


def split_pairs(first, count):
    if count == 1:
        return []
    middle = first + count // 2
    return (
        [(first, middle, first + count)]
        + split_pairs(first, middle - first)
        + split_pairs(middle, first + count - middle)
    )


def inner_kernel(head_dim, chunk, n_before, n_after, ld, b, c, x_all, dy_all, *refs):
    before, refs = refs[:n_before], refs[n_before + n_after :]
    dx_out, db_out, dc_out, x, dy, cum_terms, *scratch = refs
    length, width = x.shape
    piece = head_dim
    pieces = length // piece
    cuts = split_pairs(0, pieces)
    near, near_sum, dx = scratch[:3]
    far, far_sum = scratch[3 : 3 + len(cuts)], scratch[3 + len(cuts) :]
    per_tile = LANES // head_dim
    step = pl.program_id(0)
    owned = (step * chunk_count(x_all.shape[1]) + chunk) * width
    columns = pl.ds(pl.multiple_of(owned, width), width)
    x[...] = x_all[:, columns]
    dy[...] = dy_all[:, columns]

    @pl.when(step == 0)
    def _():
        rows, other = iota((length, length), 0), iota((length, length), 1)
        mask = jnp.where(other <= rows, 1.0, 0.0).astype(BF16)
        cum_small = summed(mask, three(ld[...] * LOG2E))
        lane = iota(cum_small.shape, 1)
        in_slots = jnp.where(lane < SLOT, cum_small, 0.0)
        in_slots = (
            in_slots + pltpu.roll(in_slots, SLOT, 1) + pltpu.roll(in_slots, 2 * SLOT, 1)
        )
        high, mid, low = three(in_slots)
        cum_terms[...] = jnp.where(lane < SLOT, high, jnp.where(lane < 2 * SLOT, mid, low))
        keep = iota((piece, LANES), 0) <= lax.rem(iota((piece, LANES), 1), piece)
        for n in range(pieces):
            rows_n = slice(n * piece, (n + 1) * piece)
            doubled = jnp.concatenate([c[rows_n, :]] * per_tile, axis=0)
            near[rows_n, :] = jnp.where(keep, dot(b[rows_n, :], doubled, NT), 0.0)
        near_sum[...] = jnp.zeros_like(near_sum)
        for (lo, mid_, hi), f, total in zip(cuts, far, far_sum):
            left, right = slice(lo * piece, mid_ * piece), slice(mid_ * piece, hi * piece)
            f[...] = dot(b[left, :], c[right, :], NT).astype(BF16)
            total[...] = jnp.zeros_like(total)

    shape = (LANES, width)
    owner = owned // head_dim + iota(shape, 1) // head_dim
    slot = lax.rem(iota(shape, 0), SLOT) == owner
    hot = jnp.where(slot & (iota(shape, 0) < 3 * SLOT), 1.0, 0.0).astype(BF16)
    cum = dot(cum_terms[...], hot, NN)
    tile = (piece, LANES)
    diagonal = iota(tile, 0) == lax.rem(iota(tile, 1), piece)
    part_of_lane = iota(tile, 1) // head_dim
    for n in range(pieces):
        rows_n = slice(n * piece, (n + 1) * piece)
        total = near_sum[rows_n, :]
        scores = near[rows_n, :]
        for t in range(width // LANES):
            lanes = slice(t * LANES, (t + 1) * LANES)
            col = cum[rows_n, lanes]
            row = jnp.sum(jnp.where(diagonal, col, 0.0), axis=0, keepdims=True)
            decays = jnp.exp2(jnp.minimum(row - col, 0.0))
            dy_t = dy[rows_n, lanes]
            stacked = jnp.concatenate(
                [jnp.where(part_of_lane == h, dy_t, jnp.zeros_like(dy_t)) for h in range(per_tile)],
                axis=0,
            )
            dx[rows_n, lanes] = dot((scores * decays).astype(BF16), stacked, NN)
            total = total + decays * dot(x[rows_n, lanes], stacked, NT)
        near_sum[rows_n, :] = total
    for (lo, mid_, hi), f, total in zip(cuts, far, far_sum):
        left, right = slice(lo * piece, mid_ * piece), slice(mid_ * piece, hi * piece)
        edge = cum[mid_ * piece - 1 : mid_ * piece, :]
        to_edge = jnp.exp2(edge - cum[left, :])
        from_edge = jnp.exp2(cum[right, :] - edge)
        x_edge = (x[left, :].astype(F32) * to_edge).astype(BF16)
        dy_edge = (dy[right, :].astype(F32) * from_edge).astype(BF16)
        dx[left, :] += to_edge * dot(f[...], dy_edge, NN)
        total[...] += dot(x_edge, dy_edge, NT)
    lanes = pl.ds(pl.multiple_of(step * width, width), width)
    dx_out[:, lanes] = dx[...].astype(BF16)

    @pl.when(step == pl.num_programs(0) - 1)
    def _():
        keep = (iota(tile, 0) <= iota(tile, 1)) & (part_of_lane == 0)
        for n in range(pieces):
            rows_n = slice(n * piece, (n + 1) * piece)
            total = near_sum[rows_n, :]
            total = sum(
                [pltpu.roll(total, h * head_dim, 1) for h in range(1, per_tile)], total
            )
            weighted = jnp.where(keep, total, 0.0).astype(BF16)
            doubled = jnp.concatenate([c[rows_n, :]] * per_tile, axis=0)
            db = dot(weighted, doubled, NN)
            dc = dot(weighted, b[rows_n, :], TN)[:piece, :]
            if before:
                db, dc = db + before[0][rows_n, :], dc + before[1][rows_n, :]
            db_out[rows_n, :] = db
            dc_out[rows_n, :] = dc
        for (lo, mid_, hi), total in zip(cuts, far_sum):
            left, right = slice(lo * piece, mid_ * piece), slice(mid_ * piece, hi * piece)
            weighted = total[...].astype(BF16)
            db_out[left, :] += dot(weighted, c[right, :], NN)
            dc_out[right, :] += dot(weighted, b[left, :], TN)


def inner_terms(head_dim, group, chunk, ld, b, c, x, dy, before, after):
    length, state = b.shape
    part = x.shape[1] // (group * chunk_count(x.shape[1]))
    piece = head_dim
    cuts = split_pairs(0, length // piece)
    sizes = [((mid - lo) * piece, (hi - mid) * piece) for lo, mid, hi in cuts]
    return pl.pallas_call(
        functools.partial(inner_kernel, head_dim, chunk, len(before), len(after)),
        grid=(group,),
        out_shape=[
            pltpu.VMEM((length, group * part), BF16),
            pltpu.VMEM((length, state), F32),
            pltpu.VMEM((length, state), F32),
        ],
        in_specs=whole(5 + len(before)) + [ANY] * len(after),
        out_specs=whole(3),
        scratch_shapes=[
            pltpu.VMEM((length, part), BF16),
            pltpu.VMEM((length, part), BF16),
            pltpu.VMEM((length, LANES), BF16),
            pltpu.VMEM((length, LANES), F32),
            pltpu.VMEM((length, LANES), F32),
            pltpu.VMEM((length, part), F32),
        ]
        + [pltpu.VMEM(s, BF16) for s in sizes]
        + [pltpu.VMEM(s, F32) for s in sizes],
        compiler_params=params(16),
        cost_estimate=cost(8 * x.size * state, 4 * x.size, 2 * x.size),
        name="inner_terms",
    )(ld, b, c, x, dy, *before, *after)


def parts_kernel(last, x_scaled, dy_scaled, db_before, dc_before, *refs):
    entries, outs = refs[:GROUP], refs[-1 if last else -2 :]
    length, state = db_before.shape
    part = entries[0].shape[1]
    db, dc = db_before[...], dc_before[...]
    for k, entry in enumerate(entries):
        here = slice(k * part, (k + 1) * part)
        db = db + dot(x_scaled[:, here], entry[state:, :], NT)
        dc = dc + dot(dy_scaled[:, here], entry[:state, :], NT)
    if last:
        outs[0][:length, :] = db.astype(BF16)
        outs[0][length:, :] = dc.astype(BF16)
    else:
        outs[0][...] = db
        outs[1][...] = dc


def entry_parts(last, x_scaled, dy_scaled, db_before, dc_before, entries, after):
    length, state = db_before.shape
    one = pltpu.VMEM((length, state), F32)
    outs = [pltpu.VMEM((2 * length, state), BF16)] if last else [one, one]
    return pl.pallas_call(
        functools.partial(parts_kernel, last),
        out_shape=outs,
        in_specs=whole(4 + len(entries)) + [ANY] * len(after),
        out_specs=whole(len(outs)),
        compiler_params=params(8),
        cost_estimate=cost(4 * x_scaled.size * state, 4 * x_scaled.size),
        name="entry_parts",
    )(x_scaled, dy_scaled, db_before, dc_before, *entries, *after)


def values_kernel(chunk, where, spread, b, dx_local, *refs):
    entries, (out, done, dx, sems) = refs[:GROUP], refs[-4:]
    done[...] = jnp.zeros_like(done)
    state, part = b.shape[1], entries[0].shape[1]
    stores = []
    for k, entry in enumerate(entries):
        here = slice(k * part, (k + 1) * part)
        local = dx_local[:, pl.ds(pl.multiple_of((place_of(where) ^ k) * part, part), part)]
        far = spread[:, here].astype(F32) * dot(b[...], entry[state:, :], NN)
        dx[k] = (local.astype(F32) + far).astype(BF16)
        lanes = chunk_lanes(where, k, chunk, part, out.shape[1])
        store = pltpu.make_async_copy(dx.at[k], out.at[:, lanes], sems.at[k])
        store.start()
        stores.append(store)
    for store in stores:
        store.wait()


def entry_values(chunk, chunks, where, spread, b, dx_local, entries, before, after):
    group, part = len(entries), entries[0].shape[1]
    length, state = b.shape
    size = dx_local.size
    operands = [where, spread, b, dx_local, *entries, *after, *before]
    return pl.pallas_call(
        functools.partial(values_kernel, chunk),
        out_shape=[
            pltpu.HBM((length, chunks * group * part), BF16),
            jax.ShapeDtypeStruct((8, LANES), F32),
        ],
        in_specs=[SMEM] + whole(3 + group) + [ANY] * len(after) + [HBM] * len(before),
        out_specs=[HBM, *whole(1)],
        input_output_aliases={len(operands) - 1: 0} if before else {},
        scratch_shapes=[
            pltpu.VMEM((group, length, part), BF16),
            pltpu.SemaphoreType.DMA((group,)),
        ],
        compiler_params=params(8),
        cost_estimate=cost(2 * size * state, 4 * size),
        name="entry_values",
    )(*operands)


def over_heads(part):
    count = lax.axis_size("head")
    total = part.astype(F32)
    for shift in range(1, count):
        pairs = [(s, (s + shift) % count) for s in range(count)]
        total = total + lax.ppermute(part, "head", pairs).astype(F32)
    return total.astype(BF16)


def shards(token_values, b_inputs, c_inputs, log_decay, grad_out):
    head_dim = token_values.shape[1] // log_decay.shape[0]
    length, state = b_inputs.shape
    count, group = lax.axis_size("seq"), GROUP
    chunks = chunk_count(token_values.shape[1])
    levels = (count // group).bit_length() - 1
    where = lax.axis_index("seq").astype(jnp.int32)[None]
    inputs = (log_decay, b_inputs, c_inputs, token_values, grad_out)
    order = []

    def then(result):
        order[:] = [result[-1] if isinstance(result, (list, tuple)) else result]
        return result

    ld, b, c, x, dy, *rest = then(first_states(head_dim, group, where, inputs))
    factors, states = rest[:3], [rest[3:]]
    blocks = [exchange(states[0][3:])]
    for chunk in range(1, chunks):
        states.append(then(next_states(head_dim, group, chunk, where, factors, b, c, x, dy)))
        blocks.append(exchange(states[chunk][3:]))

    sums, inner = [], []

    def add_inner():
        if len(inner) < chunks:
            n = len(inner)
            inner.append(then(inner_terms(head_dim, group, n, ld, b, c, x, dy, sums, order)))
            sums[:] = inner[n][1:]

    def to_level(block, level):
        step = group << level
        return lax.ppermute(block, "seq", [(s, s ^ step) for s in range(count)])

    own, received, entries = [None] * chunks, [[] for _ in range(chunks)], []

    def open_rounds(chunk):
        own[chunk] = then(totals(state, where, blocks[chunk], order))
        received[chunk].append(to_level(own[chunk], 0))

    def close_rounds(chunk):
        found = then(member_entries(state, where, blocks[chunk], received[chunk], order))
        entries.append(exchange(found))

    open_rounds(0)
    for chunk in range(chunks):
        if chunk == 0:
            add_inner()
        for level in range(levels - 1):
            last = level == levels - 2
            arrived = received[chunk][level]
            own[chunk] = then(merged(state, level, last, where, own[chunk], arrived, order))
            received[chunk].append(to_level(own[chunk], level + 1))
        if chunk + 1 < chunks:
            open_rounds(chunk + 1)
        else:
            add_inner()
        close_rounds(chunk)
    while len(inner) < chunks:
        add_inner()

    grad_values = []
    for chunk in range(chunks):
        x_scaled, dy_scaled, spread = states[chunk][:3]
        last = chunk == chunks - 1

        def values():
            local = inner[chunk][0]
            out = entry_values(
                chunk, chunks, where, spread, b, local, entries[chunk], grad_values, order
            )
            grad_values[:] = then(out)[:1]

        if not last:
            values()
        sums = then(
            entry_parts(last, x_scaled, dy_scaled, *sums, entries[chunk], [] if last else order)
        )
        if last:
            values()
    both = over_heads(sums[0])
    return grad_values[0], both[:length], both[length:]


def solution(mesh):
    in_specs = (
        P("seq", "head"),
        P("seq", None),
        P("seq", None),
        P("head", "seq"),
        P("seq", "head"),
    )
    out_specs = (P("seq", "head"), P("seq", None), P("seq", None))
    return jax.shard_map(shards, mesh=mesh, in_specs=in_specs, out_specs=out_specs, check_vma=False)
```

```python
import functools

import jax
import jax.numpy as jnp
from jax import lax
from jax.experimental import pallas as pl
from jax.experimental.pallas import tpu as pltpu
from jax.sharding import PartitionSpec as P

BF16 = jnp.bfloat16
F32 = jnp.float32
LANES = 128
GROUP = 4
TAIL = 16
LOG2E = 1.4426950408889634
MIB = 1024 * 1024

NN = (((1,), (0,)), ((), ()))
NT = (((1,), (1,)), ((), ()))
TN = (((0,), (0,)), ((), ()))


def dot(a, b, dims):
    return lax.dot_general(a, b, dims, preferred_element_type=F32)


def iota(shape, dim):
    return lax.broadcasted_iota(jnp.int32, shape, dim)


def three(values):
    high = values.astype(BF16)
    rest = values - high.astype(F32)
    mid = rest.astype(BF16)
    return high, mid, (rest - mid.astype(F32)).astype(BF16)


SLOT = LANES // 4


def summed(mask, terms):
    heads, length = terms[0].shape
    gap = [] if heads == SLOT else [jnp.zeros((SLOT - heads, length), BF16)]
    rows = [r for t in terms for r in [t] + gap] + [jnp.zeros((SLOT, length), BF16)]
    each = dot(mask, jnp.concatenate(rows, axis=0), NT)
    return each + pltpu.roll(each, LANES - SLOT, 1) + pltpu.roll(each, LANES - 2 * SLOT, 1)


def head_of_lane(head_dim, width, first):
    shape = (LANES, width)
    return jnp.where(iota(shape, 0) == first + iota(shape, 1) // head_dim, 1.0, 0.0).astype(BF16)


def whole(count):
    return [pl.BlockSpec(memory_space=pltpu.VMEM)] * count


def in_hbm(*arrays):
    return [pltpu.with_memory_space_constraint(a, pltpu.HBM) for a in arrays]


SMEM = pl.BlockSpec(memory_space=pltpu.SMEM)
HBM = pl.BlockSpec(memory_space=pltpu.HBM)
ANY = pl.BlockSpec(memory_space=pl.ANY)


def params(mib):
    return pltpu.CompilerParams(vmem_limit_bytes=mib * MIB)


def cost(flops, size, transcendentals=0):
    return pl.CostEstimate(flops=flops, bytes_accessed=size, transcendentals=transcendentals)


def place_of(where):
    return where[0] & (GROUP - 1)


def bit_of(where, level):
    return (where[0] >> (level + GROUP.bit_length() - 1)) & 1 == 1


def chunk_count(width):
    return 2 if (width // GROUP) % (2 * LANES) == 0 else 1


def chunk_lanes(where, k, chunk, part, width):
    start = (place_of(where) ^ k) * (width // GROUP) + chunk * part
    return pl.ds(pl.multiple_of(start, part), part)


def factors_of(ld):
    length = ld.shape[1]
    terms = three(ld)
    rows, other = iota((length, length), 0), iota((length, length), 1)
    after = jnp.where(other > rows, 1.0, 0.0).astype(BF16)
    until = jnp.where(other <= rows, 1.0, 0.0).astype(BF16)
    into_end = jnp.exp(summed(after, terms)).astype(BF16)
    from_start = jnp.exp(summed(until, terms)).astype(BF16)
    total = jnp.exp(summed(jnp.ones((TAIL, length), BF16), terms))
    high = total.astype(BF16).astype(F32)
    halves = jnp.where(iota(total.shape, 0) < TAIL // 2, high, total - high).astype(BF16)
    return into_end, from_start, halves


def put_states(head_dim, chunk, where, operands, outs, ready):
    into_end, from_start, halves, b, c, x, dy = operands
    x_scaled, dy_scaled, spread, *sends = outs
    group, state = len(sends), b.shape[1]
    width = x.shape[1]
    chunks = chunk_count(width)
    part = width // (group * chunks)
    sides = [(into_end, b, x, x_scaled, 0), (from_start, c, dy, dy_scaled, state)]
    for side, (factors, proj, cols, scaled, first) in enumerate(sides):
        ready(side)
        turned = proj[...].T
        for k in range(group):
            here = slice(k * part, (k + 1) * part)
            lanes = chunk_lanes(where, k, chunk, part, width)
            first_head = ((place_of(where) ^ k) * chunks + chunk) * (part // head_dim)
            hot = head_of_lane(head_dim, part, first_head)
            wide = dot(factors, hot, NN).astype(BF16)
            if side == 0:
                spread[:, here] = wide
                sends[k][2 * state :, :] = dot(halves, hot, NN).astype(BF16)
            piece = cols[:, lanes] * wide
            scaled[:, here] = piece
            sends[k][first : first + state, :] = dot(turned, piece, NN).astype(BF16)


def first_states_kernel(head_dim, group, where, ld_in, b_in, c_in, x_in, dy_in, *refs):
    ld, b, c, x, dy, into_end, from_start, halves = refs[:8]
    outs, sems = refs[8:-1], refs[-1]
    pairs = [(ld_in, ld), (b_in, b), (x_in, x), (c_in, c), (dy_in, dy)]
    copies = [pltpu.make_async_copy(i, o, sems.at[n]) for n, (i, o) in enumerate(pairs)]
    for copy in copies:
        copy.start()
    copies[0].wait()
    factors = factors_of(ld[...])
    for ref, value in zip((into_end, from_start, halves), factors):
        ref[...] = value

    def ready(side):
        copies[1 + 2 * side].wait()
        copies[2 + 2 * side].wait()

    put_states(head_dim, 0, where, (*factors, b, c, x, dy), outs, ready)


def next_states_kernel(head_dim, chunk, where, into_end, from_start, halves, *refs):
    operands = (into_end[...], from_start[...], halves[...], *refs[:4])
    put_states(head_dim, chunk, where, operands, refs[4:], lambda side: None)


def states_shapes(group, length, width, state):
    part = width // (group * chunk_count(width))
    scaled = pltpu.VMEM((length, group * part), BF16)
    return [scaled] * 3 + [pltpu.VMEM((2 * state + TAIL, part), BF16)] * group


def first_states(head_dim, group, where, inputs):
    ld, b, c, x, dy = inputs
    (length, width), state = x.shape, b.shape[1]
    kept = [pltpu.VMEM(a.shape, a.dtype) for a in inputs]
    kept += [pltpu.VMEM((rows, LANES), BF16) for rows in (length, length, TAIL)]
    outs = kept + states_shapes(group, length, width, state)
    return pl.pallas_call(
        functools.partial(first_states_kernel, head_dim, group),
        out_shape=outs,
        in_specs=[SMEM] + [HBM] * 5,
        out_specs=whole(len(outs)),
        scratch_shapes=[pltpu.SemaphoreType.DMA((5,))],
        compiler_params=params(8),
        cost_estimate=cost(2 * length * width * (state + LANES), 8 * length * width),
        name="first_states",
    )(where, *in_hbm(*inputs))


def next_states(head_dim, group, chunk, where, factors, b, c, x, dy):
    (length, width), state = x.shape, b.shape[1]
    outs = states_shapes(group, length, width, state)
    return pl.pallas_call(
        functools.partial(next_states_kernel, head_dim, chunk),
        out_shape=outs,
        in_specs=[SMEM] + whole(7),
        out_specs=whole(len(outs)),
        compiler_params=params(8),
        cost_estimate=cost(2 * length * width * (state + LANES), 4 * length * width),
        name="next_states",
    )(where, *factors, b, c, x, dy)


def decay_of(tail):
    tail = tail.astype(F32)
    return tail[:1, :] + tail[TAIL // 2 : TAIL // 2 + 1, :]


def put_decay(ref, first, factor):
    high = factor.astype(BF16).astype(F32)
    shape = (TAIL, factor.shape[1])
    both = jnp.where(iota(shape, 0) < TAIL // 2, high, factor - high)
    ref[first:, :] = both.astype(BF16)


def sent_order(parts):
    return [parts[0], *parts[:0:-1]]


def in_order(group, forward):
    return list(range(group)) if forward else list(range(group - 1, -1, -1))


def side_rows(state, forward):
    return slice(0, state) if forward else slice(state, 2 * state)


def totals_kernel(state, where, *refs):
    group = GROUP
    blocks, out = sent_order(refs[:group]), refs[-1]
    for here in range(group):

        @pl.when(place_of(where) == here)
        def _(here=here):
            decays = [decay_of(blocks[q ^ here][2 * state :, :]) for q in range(group)]
            for forward in (True, False):
                rows, value = side_rows(state, forward), None
                for q in in_order(group, forward):
                    piece = blocks[q ^ here][rows, :].astype(F32)
                    value = piece if value is None else decays[q] * value + piece
                out[rows, :] = value.astype(BF16)
            factor = decays[0]
            for d in decays[1:]:
                factor = factor * d
            put_decay(out, 2 * state, factor)


def totals(state, where, blocks, after):
    return pl.pallas_call(
        functools.partial(totals_kernel, state),
        out_shape=pltpu.VMEM(blocks[0].shape, BF16),
        in_specs=[SMEM] + whole(len(blocks)) + [ANY] * len(after),
        out_specs=whole(1)[0],
        compiler_params=params(4),
        cost_estimate=cost(8 * blocks[0].size, 10 * blocks[0].size),
        name="totals",
    )(where, *sent_order(blocks), *after)


def merged_kernel(state, level, last, where, own, received, *refs):
    out = refs[-1]
    d_own, d_other = decay_of(own[2 * state :, :]), decay_of(received[2 * state :, :])
    upper = bit_of(where, level)
    later = bit_of(where, level + 1)
    for is_upper in (False, True):
        for forward in (True, False):
            chosen = upper == is_upper
            if last:
                chosen = chosen & (later != forward)

            @pl.when(chosen)
            def _(is_upper=is_upper, forward=forward):
                rows = side_rows(state, forward)
                mine, other = own[rows, :].astype(F32), received[rows, :].astype(F32)
                value = mine + d_own * other if is_upper == forward else other + d_other * mine
                out[slice(0, state) if last else rows, :] = value.astype(BF16)

    put_decay(out, state if last else 2 * state, d_own * d_other)


def merged(state, level, last, where, own, received, after):
    rows = (state if last else 2 * state) + TAIL
    return pl.pallas_call(
        functools.partial(merged_kernel, state, level, last),
        out_shape=pltpu.VMEM((rows, own.shape[1]), BF16),
        in_specs=[SMEM] + whole(2) + [ANY] * len(after),
        out_specs=whole(1)[0],
        compiler_params=params(4),
        cost_estimate=cost(4 * own.size, 6 * own.size),
        name="merged",
    )(where, own, received, *after)


def members_kernel(state, levels, where, *refs):
    received, refs = refs[:levels], refs[levels:]
    group = GROUP
    blocks, outs = refs[:group], refs[-group:]
    entry = []
    for forward in (True, False):
        value, factor = None, 1.0
        for level, r in enumerate(received):
            gets = (bit_of(where, level)) == forward
            rows = side_rows(state, forward)
            if r.shape[0] < 2 * state:
                rows = slice(0, state)
            piece = r[rows, :].astype(F32) * jnp.where(gets, 1.0, 0.0)
            value = piece if value is None else value + factor * piece
            if level < levels - 1:
                factor = factor * jnp.where(gets, decay_of(r[2 * state :, :]), 1.0)
        entry.append(value)
    for here in range(group):

        @pl.when(place_of(where) == here)
        def _(here=here):
            decays = [decay_of(blocks[q ^ here][2 * state :, :]) for q in range(group)]
            for forward in (True, False):
                rows, order = side_rows(state, forward), in_order(group, forward)
                value = entry[0 if forward else 1]
                for q in order:
                    outs[q ^ here][rows, :] = value.astype(BF16)
                    if q != order[-1]:
                        value = decays[q] * value + blocks[q ^ here][rows, :].astype(F32)


def member_entries(state, where, blocks, received, after):
    group, part = len(blocks), blocks[0].shape[1]
    return pl.pallas_call(
        functools.partial(members_kernel, state, len(received)),
        out_shape=[pltpu.VMEM((2 * state, part), BF16)] * group,
        in_specs=[SMEM] + whole(group + len(received)) + [ANY] * len(after),
        out_specs=whole(group),
        compiler_params=params(4),
        cost_estimate=cost(12 * blocks[0].size, 16 * blocks[0].size),
        name="member_entries",
    )(where, *received, *blocks, *after)


def exchange(parts):
    count = lax.axis_size("seq")
    out = list(parts)
    for k in range(len(parts) - 1, 0, -1):
        out[k] = lax.ppermute(parts[k], "seq", [(s, s ^ k) for s in range(count)])
    return out


def split_pairs(first, count):
    if count == 1:
        return []
    middle = first + count // 2
    return (
        [(first, middle, first + count)]
        + split_pairs(first, middle - first)
        + split_pairs(middle, first + count - middle)
    )


def grouped_cuts(pieces):
    groups = {}
    for cut in split_pairs(0, pieces):
        groups.setdefault((cut[1] - cut[0], cut[2] - cut[1]), []).append(cut)
    return list(groups.items())


def rows_of(first, end, piece):
    return slice(first * piece, end * piece)


def setup_kernel(piece, ld, b, c, *refs):
    near, cum_terms = refs[-2:]
    heads, length = ld.shape
    rows, other = iota((length, length), 0), iota((length, length), 1)
    mask = jnp.where(other <= rows, 1.0, 0.0).astype(BF16)
    cum = summed(mask, three(ld[...] * LOG2E))
    lane = iota(cum.shape, 1)
    in_slots = jnp.where(lane < SLOT, cum, 0.0)
    in_slots = in_slots + pltpu.roll(in_slots, SLOT, 1) + pltpu.roll(in_slots, 2 * SLOT, 1)
    high, mid, low = three(in_slots)
    cum_terms[...] = jnp.where(lane < SLOT, high, jnp.where(lane < 2 * SLOT, mid, low))
    keep = iota((piece, piece), 0) <= iota((piece, piece), 1)
    pieces = length // piece
    for n in range(pieces):
        here = rows_of(n, n + 1, piece)
        near[here, :] = jnp.where(keep, dot(b[here, :], c[here, :], NT), 0.0).astype(BF16)
    cuts = [cut for _, same in grouped_cuts(pieces) for cut in same]
    for (lo, mid_, hi), far in zip(cuts, refs):
        left, right = rows_of(lo, mid_, piece), rows_of(mid_, hi, piece)
        far[...] = dot(b[left, :], c[right, :], NT).astype(BF16)


def inner_setup(piece, ld, b, c, after):
    length = b.shape[0]
    cuts = [cut for _, same in grouped_cuts(length // piece) for cut in same]
    outs = [
        jax.ShapeDtypeStruct(((mid - lo) * piece, (hi - mid) * piece), BF16) for lo, mid, hi in cuts
    ]
    outs.append(jax.ShapeDtypeStruct((length, piece), BF16))
    outs.append(jax.ShapeDtypeStruct((length, LANES), BF16))
    return pl.pallas_call(
        functools.partial(setup_kernel_after, piece, len(after)),
        out_shape=outs,
        in_specs=whole(3) + [ANY] * len(after),
        out_specs=whole(len(outs)),
        compiler_params=params(4),
        cost_estimate=cost(8 * b.size * length, 8 * b.size),
        name="inner_setup",
    )(ld, b, c, *after)


def setup_kernel_after(piece, n_after, ld, b, c, *refs):
    setup_kernel(piece, ld, b, c, *refs[n_after:])


def inner_kernel(head_dim, chunk, n_before, n_after, b, c, x, dy, *refs):
    length, width = x.shape
    piece = head_dim
    pieces = length // piece
    groups = grouped_cuts(pieces)
    n_cuts = sum(len(same) for _, same in groups)
    fars, (near, cum_terms), refs = refs[:n_cuts], refs[n_cuts : n_cuts + 2], refs[n_cuts + 2 :]
    before, refs = refs[:n_before], refs[n_before + n_after :]
    dx_out, db_out, dc_out, x_near, dy_near, *scratch = refs
    lefts, rights = scratch[: len(groups)], scratch[len(groups) :]
    part = dx_out.shape[1] // GROUP

    for m in range(GROUP):
        owned = m * (width // GROUP) + chunk * part
        lanes, here = slice(owned, owned + part), slice(m * part, (m + 1) * part)
        shape = (LANES, part)
        owner = owned // head_dim + iota(shape, 1) // head_dim
        slot = lax.rem(iota(shape, 0), SLOT) == owner
        hot = jnp.where(slot & (iota(shape, 0) < 3 * SLOT), 1.0, 0.0).astype(BF16)
        cum = dot(cum_terms[...], hot, NN)
        dx = []
        for n in range(pieces):
            rows = rows_of(n, n + 1, piece)
            middle = cum[n * piece + piece // 2 : n * piece + piece // 2 + 1, :]
            gap = middle - cum[rows, :]
            down, up = jnp.exp2(gap), jnp.exp2(-gap)
            x_near[rows, here] = (x[rows, lanes].astype(F32) * down).astype(BF16)
            dy_piece = (dy[rows, lanes].astype(F32) * up).astype(BF16)
            dy_near[rows, here] = dy_piece
            dx.append(down * dot(near[rows, :], dy_piece, NN))
        far_of = iter(fars)
        for (_, same), left_ref, right_ref in zip(groups, lefts, rights):
            for g, (lo, mid, hi) in enumerate(same):
                left, right = rows_of(lo, mid, piece), rows_of(mid, hi, piece)
                edge = cum[mid * piece - 1 : mid * piece, :]
                to_edge = jnp.exp2(edge - cum[left, :])
                from_edge = jnp.exp2(cum[right, :] - edge)
                x_left = (x[left, lanes].astype(F32) * to_edge).astype(BF16)
                dy_right = (dy[right, lanes].astype(F32) * from_edge).astype(BF16)
                left_ref[rows_of(g, g + 1, (mid - lo) * piece), here] = x_left
                right_ref[rows_of(g, g + 1, (hi - mid) * piece), here] = dy_right
                far = to_edge * dot(next(far_of)[...], dy_right, NN)
                for n in range(lo, mid):
                    dx[n] = dx[n] + far[rows_of(n - lo, n - lo + 1, piece), :]
        for n in range(pieces):
            dx_out[rows_of(n, n + 1, piece), here] = dx[n].astype(BF16)

    if before:
        db_out[...] = before[0][...]
        dc_out[...] = before[1][...]
    else:
        db_out[...] = jnp.zeros_like(db_out)
        dc_out[...] = jnp.zeros_like(dc_out)
    batch = 4
    for first in range(0, pieces, batch):
        rows = rows_of(first, min(first + batch, pieces), piece)
        total = dot(x_near[rows, :], dy_near[rows, :], NT)
        row, col = iota(total.shape, 0), iota(total.shape, 1)
        keep = (row // piece == col // piece) & (row <= col)
        weighted = jnp.where(keep, total, 0.0).astype(BF16)
        db_out[rows, :] += dot(weighted, c[rows, :], NN)
        dc_out[rows, :] += dot(weighted, b[rows, :], TN)
    for ((n_left, n_right), same), left_ref, right_ref in zip(groups, lefts, rights):
        total = dot(left_ref[...], right_ref[...], NT)
        if len(same) > 1:
            row, col = iota(total.shape, 0), iota(total.shape, 1)
            total = jnp.where(row // (n_left * piece) == col // (n_right * piece), total, 0.0)
        weighted = total.astype(BF16)
        b_left = jnp.concatenate([b[rows_of(lo, mid, piece), :] for lo, mid, _ in same], axis=0)
        c_right = jnp.concatenate([c[rows_of(mid, hi, piece), :] for _, mid, hi in same], axis=0)
        db = dot(weighted, c_right, NN)
        dc = dot(weighted, b_left, TN)
        for g, (lo, mid, hi) in enumerate(same):
            db_out[rows_of(lo, mid, piece), :] += db[rows_of(g, g + 1, n_left * piece), :]
            dc_out[rows_of(mid, hi, piece), :] += dc[rows_of(g, g + 1, n_right * piece), :]


def inner_terms(head_dim, chunk, setup, b, c, x, dy, before, after):
    length, state = b.shape
    columns = x.shape[1] // chunk_count(x.shape[1])
    groups = grouped_cuts(length // head_dim)
    sizes = [[len(same) * n * head_dim for n in halves] for halves, same in groups]
    return pl.pallas_call(
        functools.partial(inner_kernel, head_dim, chunk, len(before), len(after)),
        out_shape=[
            jax.ShapeDtypeStruct((length, columns), BF16),
            jax.ShapeDtypeStruct((length, state), F32),
            jax.ShapeDtypeStruct((length, state), F32),
        ],
        in_specs=whole(4 + len(setup) + len(before)) + [ANY] * len(after),
        out_specs=whole(3),
        scratch_shapes=[pltpu.VMEM((length, columns), BF16)] * 2
        + [pltpu.VMEM((left, columns), BF16) for left, _ in sizes]
        + [pltpu.VMEM((right, columns), BF16) for _, right in sizes],
        compiler_params=params(16),
        cost_estimate=cost(8 * x.size * state, 4 * x.size, 2 * x.size),
        name="inner_terms",
    )(b, c, x, dy, *setup, *before, *after)


def parts_kernel(last, x_scaled, dy_scaled, db_before, dc_before, *refs):
    entries, outs = sent_order(refs[:GROUP]), refs[-1 if last else -2 :]
    length, state = db_before.shape
    part = entries[0].shape[1]
    db, dc = db_before[...], dc_before[...]
    for k, entry in enumerate(entries):
        here = slice(k * part, (k + 1) * part)
        db = db + dot(x_scaled[:, here], entry[state:, :], NT)
        dc = dc + dot(dy_scaled[:, here], entry[:state, :], NT)
    if last:
        outs[0][:length, :] = db.astype(BF16)
        outs[0][length:, :] = dc.astype(BF16)
    else:
        outs[0][...] = db
        outs[1][...] = dc


def entry_parts(last, x_scaled, dy_scaled, db_before, dc_before, entries, after):
    length, state = db_before.shape
    one = pltpu.VMEM((length, state), F32)
    outs = [pltpu.VMEM((2 * length, state), BF16)] if last else [one, one]
    return pl.pallas_call(
        functools.partial(parts_kernel, last),
        out_shape=outs,
        in_specs=whole(4 + len(entries)) + [ANY] * len(after),
        out_specs=whole(len(outs)),
        compiler_params=params(8),
        cost_estimate=cost(4 * x_scaled.size * state, 4 * x_scaled.size),
        name="entry_parts",
    )(x_scaled, dy_scaled, db_before, dc_before, *sent_order(entries), *after)


def values_kernel(chunk, where, spread, b, dx_local, *refs):
    entries, (out, done, dx, sems) = sent_order(refs[:GROUP]), refs[-4:]
    done[...] = jnp.zeros_like(done)
    state, part = b.shape[1], entries[0].shape[1]
    stores = []
    for k, entry in enumerate(entries):
        here = slice(k * part, (k + 1) * part)
        local = dx_local[:, pl.ds(pl.multiple_of((place_of(where) ^ k) * part, part), part)]
        far = spread[:, here].astype(F32) * dot(b[...], entry[state:, :], NN)
        dx[k] = (local.astype(F32) + far).astype(BF16)
        lanes = chunk_lanes(where, k, chunk, part, out.shape[1])
        store = pltpu.make_async_copy(dx.at[k], out.at[:, lanes], sems.at[k])
        store.start()
        stores.append(store)
    for store in stores:
        store.wait()


def entry_values(chunk, chunks, where, spread, b, dx_local, entries, before, after):
    group, part = len(entries), entries[0].shape[1]
    length, state = b.shape
    size = dx_local.size
    operands = [where, spread, b, dx_local, *sent_order(entries), *after, *before]
    return pl.pallas_call(
        functools.partial(values_kernel, chunk),
        out_shape=[
            pltpu.HBM((length, chunks * group * part), BF16),
            pltpu.VMEM((8, LANES), F32),
        ],
        in_specs=[SMEM] + whole(3 + group) + [ANY] * len(after) + [HBM] * len(before),
        out_specs=[HBM, *whole(1)],
        input_output_aliases={len(operands) - 1: 0} if before else {},
        scratch_shapes=[
            pltpu.VMEM((group, length, part), BF16),
            pltpu.SemaphoreType.DMA((group,)),
        ],
        compiler_params=params(8),
        cost_estimate=cost(2 * size * state, 4 * size),
        name="entry_values",
    )(*operands)


def over_heads(part):
    count = lax.axis_size("head")
    total = part.astype(F32)
    for shift in range(1, count):
        pairs = [(s, (s + shift) % count) for s in range(count)]
        total = total + lax.ppermute(part, "head", pairs).astype(F32)
    return total.astype(BF16)


def shards(token_values, b_inputs, c_inputs, log_decay, grad_out):
    head_dim = token_values.shape[1] // log_decay.shape[0]
    length, state = b_inputs.shape
    count, group = lax.axis_size("seq"), GROUP
    chunks = chunk_count(token_values.shape[1])
    levels = (count // group).bit_length() - 1
    where = lax.axis_index("seq").astype(jnp.int32)[None]
    inputs = (log_decay, b_inputs, c_inputs, token_values, grad_out)
    ld, b, c, x, dy, *rest = first_states(head_dim, group, where, inputs)
    factors, states = rest[:3], [rest[3:]]
    blocks = [exchange(states[0][3:])]
    for chunk in range(1, chunks):
        states.append(next_states(head_dim, group, chunk, where, factors, b, c, x, dy))
        blocks.append(exchange(states[chunk][3:]))
    setup = inner_setup(head_dim, ld, b, c, [states[-1][3]])

    def to_level(block, level):
        step = group << level
        return lax.ppermute(block, "seq", [(s, s ^ step) for s in range(count)])

    entries, inner, sums = [], [], []
    for chunk in range(chunks):
        own = totals(state, where, blocks[chunk], setup[-1:] if chunk == 0 else [])
        received = [to_level(own, 0)]
        for level in range(levels - 1):
            last = level == levels - 2
            own = merged(state, level, last, where, own, received[level], [])
            received.append(to_level(own, level + 1))
        inner.append(inner_terms(head_dim, chunk, setup, b, c, x, dy, sums, [own]))
        sums = list(inner[chunk][1:])
        found = member_entries(state, where, blocks[chunk], received, sums[:1])
        entries.append(exchange(found))

    grad_values, done = [], []
    for chunk in range(chunks):
        x_scaled, dy_scaled, spread = states[chunk][:3]
        last = chunk == chunks - 1
        sums = entry_parts(last, x_scaled, dy_scaled, *sums, entries[chunk], done)
        *grad_values, token = entry_values(
            chunk, chunks, where, spread, b, inner[chunk][0], entries[chunk], grad_values, []
        )
        done = [token]
    both = over_heads(sums[0])
    return grad_values[0], both[:length], both[length:]


def solution(mesh):
    in_specs = (
        P("seq", "head"),
        P("seq", None),
        P("seq", None),
        P("head", "seq"),
        P("seq", "head"),
    )
    out_specs = (P("seq", "head"), P("seq", None), P("seq", None))
    return jax.shard_map(shards, mesh=mesh, in_specs=in_specs, out_specs=out_specs, check_vma=False)
```

```python
import functools

import jax
import jax.numpy as jnp
from jax import lax
from jax.experimental import pallas as pl
from jax.experimental.pallas import tpu as pltpu
from jax.sharding import PartitionSpec as P

BF16 = jnp.bfloat16
F32 = jnp.float32
LANES = 128
GROUP = 4
TAIL = 16
LOG2E = 1.4426950408889634
MIB = 1024 * 1024

NN = (((1,), (0,)), ((), ()))
NT = (((1,), (1,)), ((), ()))
TN = (((0,), (0,)), ((), ()))


def dot(a, b, dims):
    return lax.dot_general(a, b, dims, preferred_element_type=F32)


def iota(shape, dim):
    return lax.broadcasted_iota(jnp.int32, shape, dim)


def three(values):
    high = values.astype(BF16)
    rest = values - high.astype(F32)
    mid = rest.astype(BF16)
    return high, mid, (rest - mid.astype(F32)).astype(BF16)


SLOT = LANES // 4


def summed(mask, terms):
    heads, length = terms[0].shape
    gap = [] if heads == SLOT else [jnp.zeros((SLOT - heads, length), BF16)]
    rows = [r for t in terms for r in [t] + gap] + [jnp.zeros((SLOT, length), BF16)]
    each = dot(mask, jnp.concatenate(rows, axis=0), NT)
    return each + pltpu.roll(each, LANES - SLOT, 1) + pltpu.roll(each, LANES - 2 * SLOT, 1)


def head_of_lane(head_dim, width, first):
    shape = (LANES, width)
    return jnp.where(iota(shape, 0) == first + iota(shape, 1) // head_dim, 1.0, 0.0).astype(BF16)


def whole(count):
    return [pl.BlockSpec(memory_space=pltpu.VMEM)] * count


def in_hbm(*arrays):
    return [pltpu.with_memory_space_constraint(a, pltpu.HBM) for a in arrays]


SMEM = pl.BlockSpec(memory_space=pltpu.SMEM)
HBM = pl.BlockSpec(memory_space=pltpu.HBM)
ANY = pl.BlockSpec(memory_space=pl.ANY)


def params(mib):
    return pltpu.CompilerParams(vmem_limit_bytes=mib * MIB)


def cost(flops, size, transcendentals=0):
    return pl.CostEstimate(flops=flops, bytes_accessed=size, transcendentals=transcendentals)


def place_of(where):
    return where[0] & (GROUP - 1)


def bit_of(where, level):
    return (where[0] >> (level + GROUP.bit_length() - 1)) & 1 == 1


def chunk_count(width):
    return 2 if (width // GROUP) % (2 * LANES) == 0 else 1


def chunk_lanes(where, k, chunk, part, width):
    start = (place_of(where) ^ k) * (width // GROUP) + chunk * part
    return pl.ds(pl.multiple_of(start, part), part)


def factors_of(ld):
    length = ld.shape[1]
    terms = three(ld)
    rows, other = iota((length, length), 0), iota((length, length), 1)
    after = jnp.where(other > rows, 1.0, 0.0).astype(BF16)
    until = jnp.where(other <= rows, 1.0, 0.0).astype(BF16)
    into_end = jnp.exp(summed(after, terms)).astype(BF16)
    from_start = jnp.exp(summed(until, terms)).astype(BF16)
    total = jnp.exp(summed(jnp.ones((TAIL, length), BF16), terms))
    high = total.astype(BF16).astype(F32)
    halves = jnp.where(iota(total.shape, 0) < TAIL // 2, high, total - high).astype(BF16)
    return into_end, from_start, halves


def put_states(head_dim, chunk, where, operands, outs, ready):
    into_end, from_start, halves, b, c, x, dy = operands
    x_scaled, dy_scaled, spread, *sends = outs
    group, state = len(sends), b.shape[1]
    width = x.shape[1]
    chunks = chunk_count(width)
    part = width // (group * chunks)
    sides = [(into_end, b, x, x_scaled, 0), (from_start, c, dy, dy_scaled, state)]
    for side, (factors, proj, cols, scaled, first) in enumerate(sides):
        ready(side)
        turned = proj[...].T
        for k in range(group):
            here = slice(k * part, (k + 1) * part)
            lanes = chunk_lanes(where, k, chunk, part, width)
            first_head = ((place_of(where) ^ k) * chunks + chunk) * (part // head_dim)
            hot = head_of_lane(head_dim, part, first_head)
            wide = dot(factors, hot, NN).astype(BF16)
            if side == 0:
                spread[:, here] = wide
                sends[k][2 * state :, :] = dot(halves, hot, NN).astype(BF16)
            piece = cols[:, lanes] * wide
            scaled[:, here] = piece
            sends[k][first : first + state, :] = dot(turned, piece, NN).astype(BF16)


def first_states_kernel(head_dim, group, where, ld_in, b_in, c_in, x_in, dy_in, *refs):
    ld, b, c, x, dy, into_end, from_start, halves = refs[:8]
    outs, sems = refs[8:-1], refs[-1]
    pairs = [(ld_in, ld), (b_in, b), (x_in, x), (c_in, c), (dy_in, dy)]
    copies = [pltpu.make_async_copy(i, o, sems.at[n]) for n, (i, o) in enumerate(pairs)]
    for copy in copies:
        copy.start()
    copies[0].wait()
    factors = factors_of(ld[...])
    for ref, value in zip((into_end, from_start, halves), factors):
        ref[...] = value

    def ready(side):
        copies[1 + 2 * side].wait()
        copies[2 + 2 * side].wait()

    put_states(head_dim, 0, where, (*factors, b, c, x, dy), outs, ready)


def next_states_kernel(head_dim, chunk, where, into_end, from_start, halves, *refs):
    operands = (into_end[...], from_start[...], halves[...], *refs[:4])
    put_states(head_dim, chunk, where, operands, refs[4:], lambda side: None)


def states_shapes(group, length, width, state):
    part = width // (group * chunk_count(width))
    scaled = pltpu.VMEM((length, group * part), BF16)
    return [scaled] * 3 + [pltpu.VMEM((2 * state + TAIL, part), BF16)] * group


def first_states(head_dim, group, where, inputs):
    ld, b, c, x, dy = inputs
    (length, width), state = x.shape, b.shape[1]
    kept = [pltpu.VMEM(a.shape, a.dtype) for a in inputs]
    kept += [pltpu.VMEM((rows, LANES), BF16) for rows in (length, length, TAIL)]
    outs = kept + states_shapes(group, length, width, state)
    return pl.pallas_call(
        functools.partial(first_states_kernel, head_dim, group),
        out_shape=outs,
        in_specs=[SMEM] + [HBM] * 5,
        out_specs=whole(len(outs)),
        scratch_shapes=[pltpu.SemaphoreType.DMA((5,))],
        compiler_params=params(8),
        cost_estimate=cost(2 * length * width * (state + LANES), 8 * length * width),
        name="first_states",
    )(where, *in_hbm(*inputs))


def next_states(head_dim, group, chunk, where, factors, b, c, x, dy):
    (length, width), state = x.shape, b.shape[1]
    outs = states_shapes(group, length, width, state)
    return pl.pallas_call(
        functools.partial(next_states_kernel, head_dim, chunk),
        out_shape=outs,
        in_specs=[SMEM] + whole(7),
        out_specs=whole(len(outs)),
        compiler_params=params(8),
        cost_estimate=cost(2 * length * width * (state + LANES), 4 * length * width),
        name="next_states",
    )(where, *factors, b, c, x, dy)


def decay_of(tail):
    tail = tail.astype(F32)
    return tail[:1, :] + tail[TAIL // 2 : TAIL // 2 + 1, :]


def put_decay(ref, first, factor):
    high = factor.astype(BF16).astype(F32)
    shape = (TAIL, factor.shape[1])
    both = jnp.where(iota(shape, 0) < TAIL // 2, high, factor - high)
    ref[first:, :] = both.astype(BF16)


def sent_order(parts):
    return [parts[0], *parts[:0:-1]]


def in_order(group, forward):
    return list(range(group)) if forward else list(range(group - 1, -1, -1))


def side_rows(state, forward):
    return slice(0, state) if forward else slice(state, 2 * state)


def totals_kernel(state, levels, where, *refs):
    group = GROUP
    blocks, outs, sums = sent_order(refs[:group]), refs[-1 - levels : -1], refs[-1]
    for here in range(group):

        @pl.when(place_of(where) == here)
        def _(here=here):
            decays = [decay_of(blocks[q ^ here][2 * state :, :]) for q in range(group)]
            for forward in (True, False):
                rows, value = side_rows(state, forward), None
                for q in in_order(group, forward):
                    piece = blocks[q ^ here][rows, :].astype(F32)
                    value = piece if value is None else decays[q] * value + piece
                sums[rows, :] = value.astype(BF16)

    factor = decay_of(blocks[0][2 * state :, :])
    for block in blocks[1:]:
        factor = factor * decay_of(block[2 * state :, :])
    for level, out in enumerate(outs):
        put_decay(out, state, factor)
        for forward in (True, False):

            @pl.when(bit_of(where, level) != forward)
            def _(out=out, forward=forward):
                out[:state, :] = sums[side_rows(state, forward), :]


def totals(state, levels, where, blocks, after):
    part = blocks[0].shape[1]
    outs = [jax.ShapeDtypeStruct((state + TAIL, part), BF16)] * levels
    return pl.pallas_call(
        functools.partial(totals_kernel, state, levels),
        out_shape=outs,
        in_specs=[SMEM] + whole(len(blocks)) + [ANY] * len(after),
        out_specs=whole(levels),
        scratch_shapes=[pltpu.VMEM((2 * state, part), BF16)],
        compiler_params=params(4),
        cost_estimate=cost(8 * blocks[0].size, 10 * blocks[0].size),
        name="totals",
    )(where, *sent_order(blocks), *after)


def members_kernel(state, groups, where, *refs):
    received, refs = [None, *refs[: groups - 1]], refs[groups - 1 :]
    group = GROUP
    blocks, outs, entry = refs[:group], refs[-1 - group : -1], refs[-1]
    number = where[0] // group
    for mine in range(groups):

        @pl.when(number == mine)
        def _(mine=mine):
            for forward in (True, False):
                rows = side_rows(state, forward)
                others = range(mine - 1, -1, -1) if forward else range(mine + 1, groups)
                value, factor = jnp.zeros((state, entry.shape[1]), F32), None
                for other in others:
                    r = received[mine ^ other]
                    piece = r[:state, :].astype(F32)
                    value = piece if factor is None else value + factor * piece
                    d = decay_of(r[state:, :])
                    factor = d if factor is None else factor * d
                entry[rows, :] = value

    for here in range(group):

        @pl.when(place_of(where) == here)
        def _(here=here):
            decays = [decay_of(blocks[q ^ here][2 * state :, :]) for q in range(group)]
            for forward in (True, False):
                rows, order = side_rows(state, forward), in_order(group, forward)
                value = entry[rows, :]
                for q in order:
                    outs[q ^ here][rows, :] = value.astype(BF16)
                    if q != order[-1]:
                        value = decays[q] * value + blocks[q ^ here][rows, :].astype(F32)


def member_entries(state, where, blocks, received, after):
    group, part = len(blocks), blocks[0].shape[1]
    return pl.pallas_call(
        functools.partial(members_kernel, state, len(received) + 1),
        out_shape=[jax.ShapeDtypeStruct((2 * state, part), BF16)] * group,
        in_specs=[SMEM] + whole(group + len(received)) + [ANY] * len(after),
        out_specs=whole(group),
        scratch_shapes=[pltpu.VMEM((2 * state, part), F32)],
        compiler_params=params(4),
        cost_estimate=cost(12 * blocks[0].size, 16 * blocks[0].size),
        name="member_entries",
    )(where, *received, *blocks, *after)


def exchange(parts):
    count = lax.axis_size("seq")
    out = list(parts)
    for k in range(len(parts) - 1, 0, -1):
        out[k] = lax.ppermute(parts[k], "seq", [(s, s ^ k) for s in range(count)])
    return out


def split_pairs(first, count):
    if count == 1:
        return []
    middle = first + count // 2
    return (
        [(first, middle, first + count)]
        + split_pairs(first, middle - first)
        + split_pairs(middle, first + count - middle)
    )


def grouped_cuts(pieces):
    groups = {}
    for cut in split_pairs(0, pieces):
        groups.setdefault((cut[1] - cut[0], cut[2] - cut[1]), []).append(cut)
    return list(groups.items())


def rows_of(first, end, piece):
    return slice(first * piece, end * piece)


def setup_kernel(piece, ld, b, c, *refs):
    near, cum_terms = refs[-2:]
    heads, length = ld.shape
    rows, other = iota((length, length), 0), iota((length, length), 1)
    mask = jnp.where(other <= rows, 1.0, 0.0).astype(BF16)
    cum = summed(mask, three(ld[...] * LOG2E))
    lane = iota(cum.shape, 1)
    in_slots = jnp.where(lane < SLOT, cum, 0.0)
    in_slots = in_slots + pltpu.roll(in_slots, SLOT, 1) + pltpu.roll(in_slots, 2 * SLOT, 1)
    high, mid, low = three(in_slots)
    cum_terms[...] = jnp.where(lane < SLOT, high, jnp.where(lane < 2 * SLOT, mid, low))
    keep = iota((piece, piece), 0) <= iota((piece, piece), 1)
    pieces = length // piece
    for n in range(pieces):
        here = rows_of(n, n + 1, piece)
        near[here, :] = jnp.where(keep, dot(b[here, :], c[here, :], NT), 0.0).astype(BF16)
    cuts = [cut for _, same in grouped_cuts(pieces) for cut in same]
    for (lo, mid_, hi), far in zip(cuts, refs):
        left, right = rows_of(lo, mid_, piece), rows_of(mid_, hi, piece)
        far[...] = dot(b[left, :], c[right, :], NT).astype(BF16)


def inner_setup(piece, ld, b, c, after):
    length = b.shape[0]
    cuts = [cut for _, same in grouped_cuts(length // piece) for cut in same]
    outs = [
        jax.ShapeDtypeStruct(((mid - lo) * piece, (hi - mid) * piece), BF16) for lo, mid, hi in cuts
    ]
    outs.append(jax.ShapeDtypeStruct((length, piece), BF16))
    outs.append(jax.ShapeDtypeStruct((length, LANES), BF16))
    return pl.pallas_call(
        functools.partial(setup_kernel_after, piece, len(after)),
        out_shape=outs,
        in_specs=whole(3) + [ANY] * len(after),
        out_specs=whole(len(outs)),
        compiler_params=params(4),
        cost_estimate=cost(8 * b.size * length, 8 * b.size),
        name="inner_setup",
    )(ld, b, c, *after)


def setup_kernel_after(piece, n_after, ld, b, c, *refs):
    setup_kernel(piece, ld, b, c, *refs[n_after:])


def inner_kernel(head_dim, chunk, n_before, n_after, b, c, x, dy, *refs):
    length, width = x.shape
    piece = head_dim
    pieces = length // piece
    groups = grouped_cuts(pieces)
    n_cuts = sum(len(same) for _, same in groups)
    fars, (near, cum_terms), refs = refs[:n_cuts], refs[n_cuts : n_cuts + 2], refs[n_cuts + 2 :]
    before, refs = refs[:n_before], refs[n_before + n_after :]
    dx_out, db_out, dc_out, x_near, dy_near, *scratch = refs
    lefts, rights = scratch[: len(groups)], scratch[len(groups) :]
    part = dx_out.shape[1] // GROUP

    for m in range(GROUP):
        owned = m * (width // GROUP) + chunk * part
        lanes, here = slice(owned, owned + part), slice(m * part, (m + 1) * part)
        shape = (LANES, part)
        owner = owned // head_dim + iota(shape, 1) // head_dim
        slot = lax.rem(iota(shape, 0), SLOT) == owner
        hot = jnp.where(slot & (iota(shape, 0) < 3 * SLOT), 1.0, 0.0).astype(BF16)
        cum = dot(cum_terms[...], hot, NN)
        dx = []
        for n in range(pieces):
            rows = rows_of(n, n + 1, piece)
            middle = cum[n * piece + piece // 2 : n * piece + piece // 2 + 1, :]
            gap = middle - cum[rows, :]
            down, up = jnp.exp2(gap), jnp.exp2(-gap)
            x_near[rows, here] = (x[rows, lanes].astype(F32) * down).astype(BF16)
            dy_piece = (dy[rows, lanes].astype(F32) * up).astype(BF16)
            dy_near[rows, here] = dy_piece
            dx.append(down * dot(near[rows, :], dy_piece, NN))
        far_of = iter(fars)
        for (_, same), left_ref, right_ref in zip(groups, lefts, rights):
            for g, (lo, mid, hi) in enumerate(same):
                left, right = rows_of(lo, mid, piece), rows_of(mid, hi, piece)
                edge = cum[mid * piece - 1 : mid * piece, :]
                to_edge = jnp.exp2(edge - cum[left, :])
                from_edge = jnp.exp2(cum[right, :] - edge)
                x_left = (x[left, lanes].astype(F32) * to_edge).astype(BF16)
                dy_right = (dy[right, lanes].astype(F32) * from_edge).astype(BF16)
                left_ref[rows_of(g, g + 1, (mid - lo) * piece), here] = x_left
                right_ref[rows_of(g, g + 1, (hi - mid) * piece), here] = dy_right
                far = to_edge * dot(next(far_of)[...], dy_right, NN)
                for n in range(lo, mid):
                    dx[n] = dx[n] + far[rows_of(n - lo, n - lo + 1, piece), :]
        for n in range(pieces):
            dx_out[rows_of(n, n + 1, piece), here] = dx[n].astype(BF16)

    if before:
        db_out[...] = before[0][...]
        dc_out[...] = before[1][...]
    else:
        db_out[...] = jnp.zeros_like(db_out)
        dc_out[...] = jnp.zeros_like(dc_out)
    batch = 4
    for first in range(0, pieces, batch):
        rows = rows_of(first, min(first + batch, pieces), piece)
        total = dot(x_near[rows, :], dy_near[rows, :], NT)
        row, col = iota(total.shape, 0), iota(total.shape, 1)
        keep = (row // piece == col // piece) & (row <= col)
        weighted = jnp.where(keep, total, 0.0).astype(BF16)
        db_out[rows, :] += dot(weighted, c[rows, :], NN)
        dc_out[rows, :] += dot(weighted, b[rows, :], TN)
    for ((n_left, n_right), same), left_ref, right_ref in zip(groups, lefts, rights):
        total = dot(left_ref[...], right_ref[...], NT)
        if len(same) > 1:
            row, col = iota(total.shape, 0), iota(total.shape, 1)
            total = jnp.where(row // (n_left * piece) == col // (n_right * piece), total, 0.0)
        weighted = total.astype(BF16)
        b_left = jnp.concatenate([b[rows_of(lo, mid, piece), :] for lo, mid, _ in same], axis=0)
        c_right = jnp.concatenate([c[rows_of(mid, hi, piece), :] for _, mid, hi in same], axis=0)
        db = dot(weighted, c_right, NN)
        dc = dot(weighted, b_left, TN)
        for g, (lo, mid, hi) in enumerate(same):
            db_out[rows_of(lo, mid, piece), :] += db[rows_of(g, g + 1, n_left * piece), :]
            dc_out[rows_of(mid, hi, piece), :] += dc[rows_of(g, g + 1, n_right * piece), :]


def inner_terms(head_dim, chunk, setup, b, c, x, dy, before, after):
    length, state = b.shape
    columns = x.shape[1] // chunk_count(x.shape[1])
    groups = grouped_cuts(length // head_dim)
    sizes = [[len(same) * n * head_dim for n in halves] for halves, same in groups]
    return pl.pallas_call(
        functools.partial(inner_kernel, head_dim, chunk, len(before), len(after)),
        out_shape=[
            jax.ShapeDtypeStruct((length, columns), BF16),
            jax.ShapeDtypeStruct((length, state), F32),
            jax.ShapeDtypeStruct((length, state), F32),
        ],
        in_specs=whole(4 + len(setup) + len(before)) + [ANY] * len(after),
        out_specs=whole(3),
        scratch_shapes=[pltpu.VMEM((length, columns), BF16)] * 2
        + [pltpu.VMEM((left, columns), BF16) for left, _ in sizes]
        + [pltpu.VMEM((right, columns), BF16) for _, right in sizes],
        compiler_params=params(16),
        cost_estimate=cost(8 * x.size * state, 4 * x.size, 2 * x.size),
        name="inner_terms",
    )(b, c, x, dy, *setup, *before, *after)


def parts_kernel(last, x_scaled, dy_scaled, db_before, dc_before, *refs):
    entries, outs = sent_order(refs[:GROUP]), refs[-1 if last else -2 :]
    length, state = db_before.shape
    part = entries[0].shape[1]
    db, dc = db_before[...], dc_before[...]
    for k, entry in enumerate(entries):
        here = slice(k * part, (k + 1) * part)
        db = db + dot(x_scaled[:, here], entry[state:, :], NT)
        dc = dc + dot(dy_scaled[:, here], entry[:state, :], NT)
    if last:
        outs[0][:length, :] = db.astype(BF16)
        outs[0][length:, :] = dc.astype(BF16)
    else:
        outs[0][...] = db
        outs[1][...] = dc


def entry_parts(last, x_scaled, dy_scaled, db_before, dc_before, entries, after):
    length, state = db_before.shape
    one = pltpu.VMEM((length, state), F32)
    outs = [pltpu.VMEM((2 * length, state), BF16)] if last else [one, one]
    return pl.pallas_call(
        functools.partial(parts_kernel, last),
        out_shape=outs,
        in_specs=whole(4 + len(entries)) + [ANY] * len(after),
        out_specs=whole(len(outs)),
        compiler_params=params(8),
        cost_estimate=cost(4 * x_scaled.size * state, 4 * x_scaled.size),
        name="entry_parts",
    )(x_scaled, dy_scaled, db_before, dc_before, *sent_order(entries), *after)


def values_kernel(chunk, where, spread, b, dx_local, *refs):
    entries, (out, done, dx, sems) = sent_order(refs[:GROUP]), refs[-4:]
    done[...] = jnp.zeros_like(done)
    state, part = b.shape[1], entries[0].shape[1]
    stores = []
    for k, entry in enumerate(entries):
        here = slice(k * part, (k + 1) * part)
        local = dx_local[:, pl.ds(pl.multiple_of((place_of(where) ^ k) * part, part), part)]
        far = spread[:, here].astype(F32) * dot(b[...], entry[state:, :], NN)
        dx[k] = (local.astype(F32) + far).astype(BF16)
        lanes = chunk_lanes(where, k, chunk, part, out.shape[1])
        store = pltpu.make_async_copy(dx.at[k], out.at[:, lanes], sems.at[k])
        store.start()
        stores.append(store)
    for store in stores:
        store.wait()


def entry_values(chunk, chunks, where, spread, b, dx_local, entries, before, after):
    group, part = len(entries), entries[0].shape[1]
    length, state = b.shape
    size = dx_local.size
    operands = [where, spread, b, dx_local, *sent_order(entries), *after, *before]
    return pl.pallas_call(
        functools.partial(values_kernel, chunk),
        out_shape=[
            pltpu.HBM((length, chunks * group * part), BF16),
            pltpu.VMEM((8, LANES), F32),
        ],
        in_specs=[SMEM] + whole(3 + group) + [ANY] * len(after) + [HBM] * len(before),
        out_specs=[HBM, *whole(1)],
        input_output_aliases={len(operands) - 1: 0} if before else {},
        scratch_shapes=[
            pltpu.VMEM((group, length, part), BF16),
            pltpu.SemaphoreType.DMA((group,)),
        ],
        compiler_params=params(8),
        cost_estimate=cost(2 * size * state, 4 * size),
        name="entry_values",
    )(*operands)


def over_heads(part):
    count = lax.axis_size("head")
    total = part.astype(F32)
    for shift in range(1, count):
        pairs = [(s, (s + shift) % count) for s in range(count)]
        total = total + lax.ppermute(part, "head", pairs).astype(F32)
    return total.astype(BF16)


def shards(token_values, b_inputs, c_inputs, log_decay, grad_out):
    head_dim = token_values.shape[1] // log_decay.shape[0]
    length, state = b_inputs.shape
    count, group = lax.axis_size("seq"), GROUP
    chunks = chunk_count(token_values.shape[1])
    levels = (count // group).bit_length() - 1
    where = lax.axis_index("seq").astype(jnp.int32)[None]
    inputs = (log_decay, b_inputs, c_inputs, token_values, grad_out)
    ld, b, c, x, dy, *rest = first_states(head_dim, group, where, inputs)
    factors, states = rest[:3], [rest[3:]]
    blocks = [exchange(states[0][3:])]
    for chunk in range(1, chunks):
        states.append(next_states(head_dim, group, chunk, where, factors, b, c, x, dy))
        blocks.append(exchange(states[chunk][3:]))
    setup = inner_setup(head_dim, ld, b, c, [states[-1][3]])

    received = []
    for chunk in range(chunks):
        outs = totals(state, levels, where, blocks[chunk], setup[-1:] if chunk == 0 else [])
        received.append([])
        for k in range(1, count // group):
            pairs = [(s, s ^ (k * group)) for s in range(count)]
            received[chunk].append(lax.ppermute(outs[k.bit_length() - 1], "seq", pairs))
    entries, inner, sums = [], [], []
    for chunk in range(chunks):
        found = member_entries(state, where, blocks[chunk], received[chunk], sums[:1])
        entries.append(exchange(found))
        inner.append(inner_terms(head_dim, chunk, setup, b, c, x, dy, sums, found[:1]))
        sums = list(inner[chunk][1:])

    grad_values, done = [], []
    for chunk in range(chunks):
        x_scaled, dy_scaled, spread = states[chunk][:3]
        last = chunk == chunks - 1
        sums = entry_parts(last, x_scaled, dy_scaled, *sums, entries[chunk], done)
        *grad_values, token = entry_values(
            chunk, chunks, where, spread, b, inner[chunk][0], entries[chunk], grad_values, []
        )
        done = [token]
    both = over_heads(sums[0])
    return grad_values[0], both[:length], both[length:]


def solution(mesh):
    in_specs = (
        P("seq", "head"),
        P("seq", None),
        P("seq", None),
        P("head", "seq"),
        P("seq", "head"),
    )
    out_specs = (P("seq", "head"), P("seq", None), P("seq", None))
    return jax.shard_map(shards, mesh=mesh, in_specs=in_specs, out_specs=out_specs, check_vma=False)
```

```python
import functools

import jax
import jax.numpy as jnp
from jax import lax
from jax.experimental import pallas as pl
from jax.experimental.pallas import tpu as pltpu
from jax.sharding import PartitionSpec as P

BF16 = jnp.bfloat16
F32 = jnp.float32
LANES = 128
GROUP = 4
TAIL = 16
LOG2E = 1.4426950408889634
MIB = 1024 * 1024

NN = (((1,), (0,)), ((), ()))
NT = (((1,), (1,)), ((), ()))
TN = (((0,), (0,)), ((), ()))


def dot(a, b, dims):
    return lax.dot_general(a, b, dims, preferred_element_type=F32)


def iota(shape, dim):
    return lax.broadcasted_iota(jnp.int32, shape, dim)


def three(values):
    high = values.astype(BF16)
    rest = values - high.astype(F32)
    mid = rest.astype(BF16)
    return high, mid, (rest - mid.astype(F32)).astype(BF16)


SLOT = LANES // 4


def summed(mask, terms):
    heads, length = terms[0].shape
    gap = [] if heads == SLOT else [jnp.zeros((SLOT - heads, length), BF16)]
    rows = [r for t in terms for r in [t] + gap] + [jnp.zeros((SLOT, length), BF16)]
    each = dot(mask, jnp.concatenate(rows, axis=0), NT)
    return each + pltpu.roll(each, LANES - SLOT, 1) + pltpu.roll(each, LANES - 2 * SLOT, 1)


def split_of(index, size):
    shift = size.bit_length() - 1
    return lax.shift_right_logical(index, shift) if size == 1 << shift else index // size


def row_less_head(head_dim, width, rows=LANES):
    shape = (LANES, width)
    row = iota(shape, 0)
    if rows < LANES:
        row = row & (rows - 1)
    return row - split_of(iota(shape, 1), head_dim)


def head_of_lane(difference, first):
    return jnp.where(difference == first, 1.0, 0.0).astype(BF16)


def whole(count):
    return [pl.BlockSpec(memory_space=pltpu.VMEM)] * count


def in_hbm(*arrays):
    return [pltpu.with_memory_space_constraint(a, pltpu.HBM) for a in arrays]


SMEM = pl.BlockSpec(memory_space=pltpu.SMEM)
HBM = pl.BlockSpec(memory_space=pltpu.HBM)
ANY = pl.BlockSpec(memory_space=pl.ANY)


def params(mib):
    return pltpu.CompilerParams(vmem_limit_bytes=mib * MIB)


def cost(flops, size, transcendentals=0):
    return pl.CostEstimate(flops=flops, bytes_accessed=size, transcendentals=transcendentals)


def place_of(where):
    return where[0] & (GROUP - 1)


def bit_of(where, level):
    return (where[0] >> (level + GROUP.bit_length() - 1)) & 1 == 1


def chunk_count(width):
    return 2 if (width // GROUP) % (2 * LANES) == 0 else 1


def chunk_lanes(where, k, chunk, part, width):
    start = (place_of(where) ^ k) * (width // GROUP) + chunk * part
    return pl.ds(pl.multiple_of(start, part), part)


def masks_of(length):
    rows, other = iota((length, length), 0), iota((length, length), 1)
    after = jnp.where(other > rows, 1.0, 0.0).astype(BF16)
    return after, jnp.where(other <= rows, 1.0, 0.0).astype(BF16)


def factors_of(ld, after, until):
    length = ld.shape[1]
    terms = three(ld)
    into_end = jnp.exp(summed(after, terms)).astype(BF16)
    from_start = jnp.exp(summed(until, terms)).astype(BF16)
    total = jnp.exp(summed(jnp.ones((TAIL, length), BF16), terms))
    high = total.astype(BF16).astype(F32)
    halves = jnp.where(iota(total.shape, 0) < TAIL // 2, high, total - high).astype(BF16)
    return into_end, from_start, halves


def put_states(head_dim, chunk, where, operands, outs, ready):
    into_end, from_start, halves, b, c, x, dy = operands
    x_scaled, dy_scaled, spread, *sends = outs
    group, state = len(sends), b.shape[1]
    width = x.shape[1]
    chunks = chunk_count(width)
    part = width // (group * chunks)
    difference = row_less_head(head_dim, part)
    sides = [(into_end, b, x, x_scaled, 0), (from_start, c, dy, dy_scaled, state)]
    for side, (factors, proj, cols, scaled, first) in enumerate(sides):
        ready(side)
        turned = proj[...].T
        for k in range(group):
            here = slice(k * part, (k + 1) * part)
            lanes = chunk_lanes(where, k, chunk, part, width)
            first_head = ((place_of(where) ^ k) * chunks + chunk) * (part // head_dim)
            hot = head_of_lane(difference, first_head)
            wide = dot(factors, hot, NN).astype(BF16)
            if side == 0:
                spread[:, here] = wide
                sends[k][2 * state :, :] = dot(halves, hot, NN).astype(BF16)
            piece = cols[:, lanes] * wide
            scaled[:, here] = piece
            sends[k][first : first + state, :] = dot(turned, piece, NN).astype(BF16)


def first_states_kernel(head_dim, group, where, ld_in, b_in, c_in, x_in, dy_in, *refs):
    ld, b, c, x, dy, into_end, from_start, halves = refs[:8]
    outs, sems = refs[8:-1], refs[-1]
    pairs = [(ld_in, ld), (b_in, b), (x_in, x), (c_in, c), (dy_in, dy)]
    copies = [pltpu.make_async_copy(i, o, sems.at[n]) for n, (i, o) in enumerate(pairs)]
    for copy in copies:
        copy.start()
    masks = masks_of(ld.shape[1])
    copies[0].wait()
    factors = factors_of(ld[...], *masks)
    for ref, value in zip((into_end, from_start, halves), factors):
        ref[...] = value

    def ready(side):
        copies[1 + 2 * side].wait()
        copies[2 + 2 * side].wait()

    put_states(head_dim, 0, where, (*factors, b, c, x, dy), outs, ready)


def next_states_kernel(head_dim, chunk, where, into_end, from_start, halves, *refs):
    operands = (into_end[...], from_start[...], halves[...], *refs[:4])
    put_states(head_dim, chunk, where, operands, refs[4:], lambda side: None)


def states_shapes(group, length, width, state):
    part = width // (group * chunk_count(width))
    scaled = pltpu.VMEM((length, group * part), BF16)
    return [scaled] * 3 + [pltpu.VMEM((2 * state + TAIL, part), BF16)] * group


def first_states(head_dim, group, where, inputs):
    ld, b, c, x, dy = inputs
    (length, width), state = x.shape, b.shape[1]
    kept = [pltpu.VMEM(a.shape, a.dtype) for a in inputs]
    kept += [pltpu.VMEM((rows, LANES), BF16) for rows in (length, length, TAIL)]
    outs = kept + states_shapes(group, length, width, state)
    return pl.pallas_call(
        functools.partial(first_states_kernel, head_dim, group),
        out_shape=outs,
        in_specs=[SMEM] + [HBM] * 5,
        out_specs=whole(len(outs)),
        scratch_shapes=[pltpu.SemaphoreType.DMA((5,))],
        compiler_params=params(8),
        cost_estimate=cost(2 * length * width * (state + LANES), 8 * length * width),
        name="first_states",
    )(where, *in_hbm(*inputs))


def next_states(head_dim, group, chunk, where, factors, b, c, x, dy):
    (length, width), state = x.shape, b.shape[1]
    outs = states_shapes(group, length, width, state)
    return pl.pallas_call(
        functools.partial(next_states_kernel, head_dim, chunk),
        out_shape=outs,
        in_specs=[SMEM] + whole(7),
        out_specs=whole(len(outs)),
        compiler_params=params(8),
        cost_estimate=cost(2 * length * width * (state + LANES), 4 * length * width),
        name="next_states",
    )(where, *factors, b, c, x, dy)


def decay_of(tail):
    tail = tail.astype(F32)
    return tail[:1, :] + tail[TAIL // 2 : TAIL // 2 + 1, :]


def put_decay(ref, first, factor):
    high = factor.astype(BF16).astype(F32)
    shape = (TAIL, factor.shape[1])
    both = jnp.where(iota(shape, 0) < TAIL // 2, high, factor - high)
    ref[first:, :] = both.astype(BF16)


def sent_order(parts, fixed=1):
    return [*parts[:fixed], *parts[: fixed - 1 : -1]]


def in_order(group, forward):
    return list(range(group)) if forward else list(range(group - 1, -1, -1))


def side_rows(state, forward):
    return slice(0, state) if forward else slice(state, 2 * state)


def totals_kernel(state, levels, where, *refs):
    group = GROUP
    blocks, outs, sums = sent_order(refs[:group]), refs[-1 - levels : -1], refs[-1]
    for here in range(group):

        @pl.when(place_of(where) == here)
        def _(here=here):
            decays = [decay_of(blocks[q ^ here][2 * state :, :]) for q in range(group)]
            for forward in (True, False):
                rows, value = side_rows(state, forward), None
                for q in in_order(group, forward):
                    piece = blocks[q ^ here][rows, :].astype(F32)
                    value = piece if value is None else decays[q] * value + piece
                sums[rows, :] = value.astype(BF16)

    factor = decay_of(blocks[0][2 * state :, :])
    for block in blocks[1:]:
        factor = factor * decay_of(block[2 * state :, :])
    if not levels:
        put_decay(sums, 2 * state, factor)
    for level, out in enumerate(outs):
        put_decay(out, state, factor)
        for forward in (True, False):

            @pl.when(bit_of(where, level) != forward)
            def _(out=out, forward=forward):
                out[:state, :] = sums[side_rows(state, forward), :]


def totals(state, levels, where, blocks, after):
    part = blocks[0].shape[1]
    outs = [jax.ShapeDtypeStruct((state + TAIL, part), BF16)] * levels
    if not levels:
        outs = [jax.ShapeDtypeStruct(blocks[0].shape, BF16)]
    return pl.pallas_call(
        functools.partial(totals_kernel, state, levels),
        out_shape=outs,
        in_specs=[SMEM] + whole(len(blocks)) + [ANY] * len(after),
        out_specs=whole(len(outs)),
        scratch_shapes=[pltpu.VMEM((2 * state, part), BF16)] if levels else [],
        compiler_params=params(4),
        cost_estimate=cost(8 * blocks[0].size, 10 * blocks[0].size),
        name="totals",
    )(where, *sent_order(blocks), *after)


def merged_kernel(state, level, last, where, own, received, *refs):
    out = refs[-1]
    d_own, d_other = decay_of(own[2 * state :, :]), decay_of(received[2 * state :, :])
    upper = bit_of(where, level)
    later = bit_of(where, level + 1)
    for is_upper in (False, True):
        for forward in (True, False):
            chosen = upper == is_upper
            if last:
                chosen = chosen & (later != forward)

            @pl.when(chosen)
            def _(is_upper=is_upper, forward=forward):
                rows = side_rows(state, forward)
                mine, other = own[rows, :].astype(F32), received[rows, :].astype(F32)
                value = mine + d_own * other if is_upper == forward else other + d_other * mine
                out[slice(0, state) if last else rows, :] = value.astype(BF16)

    put_decay(out, state if last else 2 * state, d_own * d_other)


def merged(state, level, last, where, own, received, after):
    rows = (state if last else 2 * state) + TAIL
    return pl.pallas_call(
        functools.partial(merged_kernel, state, level, last),
        out_shape=pltpu.VMEM((rows, own.shape[1]), BF16),
        in_specs=[SMEM] + whole(2) + [ANY] * len(after),
        out_specs=whole(1)[0],
        compiler_params=params(4),
        cost_estimate=cost(4 * own.size, 6 * own.size),
        name="merged",
    )(where, own, received, *after)


def put_direct(state, groups, number, received, entry):
    for mine in range(groups):

        @pl.when(number == mine)
        def _(mine=mine):
            for forward in (True, False):
                rows = side_rows(state, forward)
                others = range(mine - 1, -1, -1) if forward else range(mine + 1, groups)
                value, factor = jnp.zeros((state, entry.shape[1]), F32), None
                for other in others:
                    r = received[(mine ^ other) - 1]
                    piece = r[:state, :].astype(F32)
                    value = piece if factor is None else value + factor * piece
                    d = decay_of(r[state:, :])
                    factor = d if factor is None else factor * d
                entry[rows, :] = value


def put_rounds(state, where, received, entry):
    for forward in (True, False):
        value, factor = None, 1.0
        for level, r in enumerate(received):
            gets = bit_of(where, level) == forward
            both = r.shape[0] > 2 * state
            rows = side_rows(state, forward) if both else slice(0, state)
            piece = r[rows, :].astype(F32) * jnp.where(gets, 1.0, 0.0)
            value = piece if value is None else value + factor * piece
            if both:
                factor = factor * jnp.where(gets, decay_of(r[2 * state :, :]), 1.0)
        entry[side_rows(state, forward), :] = value


def members_kernel(state, direct, n_received, where, *refs):
    received, refs = refs[:n_received], refs[n_received:]
    group = GROUP
    blocks, outs, entry = refs[:group], refs[-1 - group : -1], refs[-1]
    if direct:
        put_direct(state, n_received + 1, where[0] // group, received, entry)
    else:
        put_rounds(state, where, received, entry)
    for here in range(group):

        @pl.when(place_of(where) == here)
        def _(here=here):
            decays = [decay_of(blocks[q ^ here][2 * state :, :]) for q in range(group)]
            for forward in (True, False):
                rows, order = side_rows(state, forward), in_order(group, forward)
                value = entry[rows, :]
                for q in order:
                    outs[q ^ here][rows, :] = value.astype(BF16)
                    if q != order[-1]:
                        value = decays[q] * value + blocks[q ^ here][rows, :].astype(F32)


def member_entries(state, direct, where, blocks, received, after):
    group, part = len(blocks), blocks[0].shape[1]
    return pl.pallas_call(
        functools.partial(members_kernel, state, direct, len(received)),
        out_shape=[jax.ShapeDtypeStruct((2 * state, part), BF16)] * group,
        in_specs=[SMEM] + whole(group + len(received)) + [ANY] * len(after),
        out_specs=whole(group),
        scratch_shapes=[pltpu.VMEM((2 * state, part), F32)],
        compiler_params=params(4),
        cost_estimate=cost(12 * blocks[0].size, 16 * blocks[0].size),
        name="member_entries",
    )(where, *received, *blocks, *after)


def exchange(parts):
    count = lax.axis_size("seq")
    out = list(parts)
    for k in range(len(parts) - 1, 0, -1):
        out[k] = lax.ppermute(parts[k], "seq", [(s, s ^ k) for s in range(count)])
    return out


def split_pairs(first, count):
    if count == 1:
        return []
    middle = first + count // 2
    return (
        [(first, middle, first + count)]
        + split_pairs(first, middle - first)
        + split_pairs(middle, first + count - middle)
    )


def grouped_cuts(pieces):
    groups = {}
    for cut in split_pairs(0, pieces):
        groups.setdefault((cut[1] - cut[0], cut[2] - cut[1]), []).append(cut)
    return list(groups.items())


def rows_of(first, end, piece):
    return slice(first * piece, end * piece)


def setup_kernel(piece, ld, b, c, *refs):
    near, cum_terms = refs[-2:]
    heads, length = ld.shape
    rows, other = iota((length, length), 0), iota((length, length), 1)
    mask = jnp.where(other <= rows, 1.0, 0.0).astype(BF16)
    cum = summed(mask, three(ld[...] * LOG2E))
    lane = iota(cum.shape, 1)
    in_slots = jnp.where(lane < SLOT, cum, 0.0)
    in_slots = in_slots + pltpu.roll(in_slots, SLOT, 1) + pltpu.roll(in_slots, 2 * SLOT, 1)
    high, mid, low = three(in_slots)
    cum_terms[...] = jnp.where(lane < SLOT, high, jnp.where(lane < 2 * SLOT, mid, low))
    keep = iota((piece, piece), 0) <= iota((piece, piece), 1)
    pieces = length // piece
    for n in range(pieces):
        here = rows_of(n, n + 1, piece)
        near[here, :] = jnp.where(keep, dot(b[here, :], c[here, :], NT), 0.0).astype(BF16)
    cuts = [cut for _, same in grouped_cuts(pieces) for cut in same]
    for (lo, mid_, hi), far in zip(cuts, refs):
        left, right = rows_of(lo, mid_, piece), rows_of(mid_, hi, piece)
        far[...] = dot(b[left, :], c[right, :], NT).astype(BF16)


def inner_setup(piece, ld, b, c, after):
    length = b.shape[0]
    cuts = [cut for _, same in grouped_cuts(length // piece) for cut in same]
    outs = [
        jax.ShapeDtypeStruct(((mid - lo) * piece, (hi - mid) * piece), BF16) for lo, mid, hi in cuts
    ]
    outs.append(jax.ShapeDtypeStruct((length, piece), BF16))
    outs.append(jax.ShapeDtypeStruct((length, LANES), BF16))
    return pl.pallas_call(
        functools.partial(setup_kernel_after, piece, len(after)),
        out_shape=outs,
        in_specs=whole(3) + [ANY] * len(after),
        out_specs=whole(len(outs)),
        compiler_params=params(4),
        cost_estimate=cost(8 * b.size * length, 8 * b.size),
        name="inner_setup",
    )(ld, b, c, *after)


def setup_kernel_after(piece, n_after, ld, b, c, *refs):
    setup_kernel(piece, ld, b, c, *refs[n_after:])


def inner_kernel(head_dim, chunk, n_before, n_after, b, c, x, dy, *refs):
    length, width = x.shape
    piece = head_dim
    pieces = length // piece
    groups = grouped_cuts(pieces)
    n_cuts = sum(len(same) for _, same in groups)
    fars, (near, cum_terms), refs = refs[:n_cuts], refs[n_cuts : n_cuts + 2], refs[n_cuts + 2 :]
    before, refs = refs[:n_before], refs[n_before + n_after :]
    dx_out, db_out, dc_out, x_near, dy_near, *scratch = refs
    lefts, rights = scratch[: len(groups)], scratch[len(groups) :]
    part = dx_out.shape[1] // GROUP
    difference = row_less_head(head_dim, part, SLOT)

    for m in range(GROUP):
        owned = m * (width // GROUP) + chunk * part
        lanes, here = slice(owned, owned + part), slice(m * part, (m + 1) * part)
        cum = dot(cum_terms[...], head_of_lane(difference, owned // head_dim), NN)
        dx = []
        for n in range(pieces):
            rows = rows_of(n, n + 1, piece)
            middle = cum[n * piece + piece // 2 : n * piece + piece // 2 + 1, :]
            gap = middle - cum[rows, :]
            down, up = jnp.exp2(gap), jnp.exp2(-gap)
            x_near[rows, here] = (x[rows, lanes].astype(F32) * down).astype(BF16)
            dy_piece = (dy[rows, lanes].astype(F32) * up).astype(BF16)
            dy_near[rows, here] = dy_piece
            dx.append(down * dot(near[rows, :], dy_piece, NN))
        far_of = iter(fars)
        for (_, same), left_ref, right_ref in zip(groups, lefts, rights):
            for g, (lo, mid, hi) in enumerate(same):
                left, right = rows_of(lo, mid, piece), rows_of(mid, hi, piece)
                edge = cum[mid * piece - 1 : mid * piece, :]
                to_edge = jnp.exp2(edge - cum[left, :])
                from_edge = jnp.exp2(cum[right, :] - edge)
                x_left = (x[left, lanes].astype(F32) * to_edge).astype(BF16)
                dy_right = (dy[right, lanes].astype(F32) * from_edge).astype(BF16)
                left_ref[rows_of(g, g + 1, (mid - lo) * piece), here] = x_left
                right_ref[rows_of(g, g + 1, (hi - mid) * piece), here] = dy_right
                far = to_edge * dot(next(far_of)[...], dy_right, NN)
                for n in range(lo, mid):
                    dx[n] = dx[n] + far[rows_of(n - lo, n - lo + 1, piece), :]
        for n in range(pieces):
            dx_out[rows_of(n, n + 1, piece), here] = dx[n].astype(BF16)

    if before:
        db_out[...] = before[0][...]
        dc_out[...] = before[1][...]
    else:
        db_out[...] = jnp.zeros_like(db_out)
        dc_out[...] = jnp.zeros_like(dc_out)
    batch = 4
    for first in range(0, pieces, batch):
        rows = rows_of(first, min(first + batch, pieces), piece)
        total = dot(x_near[rows, :], dy_near[rows, :], NT)
        row, col = iota(total.shape, 0), iota(total.shape, 1)
        keep = (split_of(row, piece) == split_of(col, piece)) & (row <= col)
        weighted = jnp.where(keep, total, 0.0).astype(BF16)
        db_out[rows, :] += dot(weighted, c[rows, :], NN)
        dc_out[rows, :] += dot(weighted, b[rows, :], TN)
    for ((n_left, n_right), same), left_ref, right_ref in zip(groups, lefts, rights):
        total = dot(left_ref[...], right_ref[...], NT)
        if len(same) > 1:
            row, col = iota(total.shape, 0), iota(total.shape, 1)
            same_cut = split_of(row, n_left * piece) == split_of(col, n_right * piece)
            total = jnp.where(same_cut, total, 0.0)
        weighted = total.astype(BF16)
        b_left = jnp.concatenate([b[rows_of(lo, mid, piece), :] for lo, mid, _ in same], axis=0)
        c_right = jnp.concatenate([c[rows_of(mid, hi, piece), :] for _, mid, hi in same], axis=0)
        db = dot(weighted, c_right, NN)
        dc = dot(weighted, b_left, TN)
        for g, (lo, mid, hi) in enumerate(same):
            db_out[rows_of(lo, mid, piece), :] += db[rows_of(g, g + 1, n_left * piece), :]
            dc_out[rows_of(mid, hi, piece), :] += dc[rows_of(g, g + 1, n_right * piece), :]


def inner_terms(head_dim, chunk, setup, b, c, x, dy, before, after):
    length, state = b.shape
    columns = x.shape[1] // chunk_count(x.shape[1])
    groups = grouped_cuts(length // head_dim)
    sizes = [[len(same) * n * head_dim for n in halves] for halves, same in groups]
    return pl.pallas_call(
        functools.partial(inner_kernel, head_dim, chunk, len(before), len(after)),
        out_shape=[
            jax.ShapeDtypeStruct((length, columns), BF16),
            jax.ShapeDtypeStruct((length, state), F32),
            jax.ShapeDtypeStruct((length, state), F32),
        ],
        in_specs=whole(4 + len(setup) + len(before)) + [ANY] * len(after),
        out_specs=whole(3),
        scratch_shapes=[pltpu.VMEM((length, columns), BF16)] * 2
        + [pltpu.VMEM((left, columns), BF16) for left, _ in sizes]
        + [pltpu.VMEM((right, columns), BF16) for _, right in sizes],
        compiler_params=params(16),
        cost_estimate=cost(8 * x.size * state, 4 * x.size, 2 * x.size),
        name="inner_terms",
    )(b, c, x, dy, *setup, *before, *after)


def parts_kernel(last, x_scaled, dy_scaled, db_before, dc_before, *refs):
    entries, outs = sent_order(refs[:GROUP]), refs[-1 if last else -2 :]
    length, state = db_before.shape
    part = entries[0].shape[1]
    db, dc = db_before[...], dc_before[...]
    for k, entry in enumerate(entries):
        here = slice(k * part, (k + 1) * part)
        db = db + dot(x_scaled[:, here], entry[state:, :], NT)
        dc = dc + dot(dy_scaled[:, here], entry[:state, :], NT)
    if last:
        outs[0][:length, :] = db.astype(BF16)
        outs[0][length:, :] = dc.astype(BF16)
    else:
        outs[0][...] = db
        outs[1][...] = dc


def entry_parts(last, x_scaled, dy_scaled, db_before, dc_before, entries, after):
    length, state = db_before.shape
    one = pltpu.VMEM((length, state), F32)
    outs = [pltpu.VMEM((2 * length, state), BF16)] if last else [one, one]
    return pl.pallas_call(
        functools.partial(parts_kernel, last),
        out_shape=outs,
        in_specs=whole(4 + len(entries)) + [ANY] * len(after),
        out_specs=whole(len(outs)),
        compiler_params=params(8),
        cost_estimate=cost(4 * x_scaled.size * state, 4 * x_scaled.size),
        name="entry_parts",
    )(x_scaled, dy_scaled, db_before, dc_before, *sent_order(entries), *after)


def values_kernel(chunk, last, where, spread, b, dx_local, *refs):
    entries, (dx, sems) = sent_order(refs[:GROUP], 2 if last else 1), refs[-2:]
    out = refs[-3 if last else -4]
    if not last:
        refs[-3][...] = jnp.zeros_like(refs[-3])
    state, part = b.shape[1], entries[0].shape[1]
    stores = []
    for k, entry in enumerate(entries):
        here = slice(k * part, (k + 1) * part)
        local = dx_local[:, pl.ds(pl.multiple_of((place_of(where) ^ k) * part, part), part)]
        far = spread[:, here].astype(F32) * dot(b[...], entry[state:, :], NN)
        dx[k] = (local.astype(F32) + far).astype(BF16)
        lanes = chunk_lanes(where, k, chunk, part, out.shape[1])
        store = pltpu.make_async_copy(dx.at[k], out.at[:, lanes], sems.at[k])
        store.start()
        stores.append(store)
    for store in stores:
        store.wait()


def entry_values(chunk, chunks, where, spread, b, dx_local, entries, before, after):
    group, part = len(entries), entries[0].shape[1]
    length, state = b.shape
    size, last = dx_local.size, chunk == chunks - 1
    sent = sent_order(entries, 2 if last else 1)
    operands = [where, spread, b, dx_local, *sent, *after, *before]
    return pl.pallas_call(
        functools.partial(values_kernel, chunk, last),
        out_shape=[pltpu.HBM((length, chunks * group * part), BF16)]
        + [pltpu.VMEM((8, LANES), F32)] * (not last),
        in_specs=[SMEM] + whole(3 + group) + [ANY] * len(after) + [HBM] * len(before),
        out_specs=[HBM] + whole(0 if last else 1),
        input_output_aliases={len(operands) - 1: 0} if before else {},
        scratch_shapes=[
            pltpu.VMEM((group, length, part), BF16),
            pltpu.SemaphoreType.DMA((group,)),
        ],
        compiler_params=params(8),
        cost_estimate=cost(2 * size * state, 4 * size),
        name="entry_values",
    )(*operands)


def over_heads(part):
    count = lax.axis_size("head")
    total = part.astype(F32)
    for shift in range(1, count):
        pairs = [(s, (s + shift) % count) for s in range(count)]
        total = total + lax.ppermute(part, "head", pairs).astype(F32)
    return total.astype(BF16)


def shards(token_values, b_inputs, c_inputs, log_decay, grad_out):
    head_dim = token_values.shape[1] // log_decay.shape[0]
    length, state = b_inputs.shape
    count, group = lax.axis_size("seq"), GROUP
    chunks = chunk_count(token_values.shape[1])
    levels = (count // group).bit_length() - 1
    where = lax.axis_index("seq").astype(jnp.int32)[None]
    inputs = (log_decay, b_inputs, c_inputs, token_values, grad_out)
    ld, b, c, x, dy, *rest = first_states(head_dim, group, where, inputs)
    factors, states = rest[:3], [rest[3:]]
    blocks = [exchange(states[0][3:])]
    for chunk in range(1, chunks):
        states.append(next_states(head_dim, group, chunk, where, factors, b, c, x, dy))
        blocks.append(exchange(states[chunk][3:]))
    setup = inner_setup(head_dim, ld, b, c, [states[-1][3]])

    def to_group(block, k):
        return lax.ppermute(block, "seq", [(s, s ^ (k * group)) for s in range(count)])

    entries, inner, sums = [], [], []
    for chunk in range(chunks):
        (own,) = totals(state, 0, where, blocks[chunk], setup[-1:] if chunk == 0 else [])
        received = [to_group(own, 1)]
        for level in range(levels - 1):
            last = level == levels - 2
            own = merged(state, level, last, where, own, received[level], [])
            received.append(to_group(own, 2 << level))
        inner.append(inner_terms(head_dim, chunk, setup, b, c, x, dy, sums, [own]))
        sums = list(inner[chunk][1:])
        found = member_entries(state, False, where, blocks[chunk], received, sums[:1])
        entries.append(exchange(found))

    grad_values, done = [], []
    for chunk in range(chunks):
        x_scaled, dy_scaled, spread = states[chunk][:3]
        last = chunk == chunks - 1
        sums = entry_parts(last, x_scaled, dy_scaled, *sums, entries[chunk], done)
        outs = entry_values(
            chunk, chunks, where, spread, b, inner[chunk][0], entries[chunk], grad_values, []
        )
        grad_values, done = list(outs[:1]), list(outs[1:])
    both = over_heads(sums[0])
    return grad_values[0], both[:length], both[length:]


def solution(mesh):
    in_specs = (
        P("seq", "head"),
        P("seq", None),
        P("seq", None),
        P("head", "seq"),
        P("seq", "head"),
    )
    out_specs = (P("seq", "head"), P("seq", None), P("seq", None))
    return jax.shard_map(shards, mesh=mesh, in_specs=in_specs, out_specs=out_specs, check_vma=False)
```

```python
import functools

import jax
import jax.numpy as jnp
from jax import lax
from jax.experimental import pallas as pl
from jax.experimental.pallas import tpu as pltpu
from jax.sharding import PartitionSpec as P

BF16 = jnp.bfloat16
F32 = jnp.float32
LANES = 128
GROUP = 4
TAIL = 16
LOG2E = 1.4426950408889634
MIB = 1024 * 1024

NN = (((1,), (0,)), ((), ()))
NT = (((1,), (1,)), ((), ()))
TN = (((0,), (0,)), ((), ()))


def dot(a, b, dims):
    return lax.dot_general(a, b, dims, preferred_element_type=F32)


def iota(shape, dim):
    return lax.broadcasted_iota(jnp.int32, shape, dim)


def three(values):
    high = values.astype(BF16)
    rest = values - high.astype(F32)
    mid = rest.astype(BF16)
    return high, mid, (rest - mid.astype(F32)).astype(BF16)


SLOT = LANES // 4


def summed(mask, terms):
    heads, length = terms[0].shape
    gap = [] if heads == SLOT else [jnp.zeros((SLOT - heads, length), BF16)]
    rows = [r for t in terms for r in [t] + gap] + [jnp.zeros((SLOT, length), BF16)]
    each = dot(mask, jnp.concatenate(rows, axis=0), NT)
    return each + pltpu.roll(each, LANES - SLOT, 1) + pltpu.roll(each, LANES - 2 * SLOT, 1)


def split_of(index, size):
    shift = size.bit_length() - 1
    return lax.shift_right_logical(index, shift) if size == 1 << shift else index // size


def row_less_head(head_dim, width, rows=LANES):
    shape = (LANES, width)
    row = iota(shape, 0)
    if rows < LANES:
        row = row & (rows - 1)
    return row - split_of(iota(shape, 1), head_dim)


def head_of_lane(difference, first):
    return jnp.where(difference == first, 1.0, 0.0).astype(BF16)


def whole(count):
    return [pl.BlockSpec(memory_space=pltpu.VMEM)] * count


def in_hbm(*arrays):
    return [pltpu.with_memory_space_constraint(a, pltpu.HBM) for a in arrays]


SMEM = pl.BlockSpec(memory_space=pltpu.SMEM)
HBM = pl.BlockSpec(memory_space=pltpu.HBM)
ANY = pl.BlockSpec(memory_space=pl.ANY)


def params(mib):
    return pltpu.CompilerParams(vmem_limit_bytes=mib * MIB)


def cost(flops, size, transcendentals=0):
    return pl.CostEstimate(flops=flops, bytes_accessed=size, transcendentals=transcendentals)


def place_of(where):
    return where[0] & (GROUP - 1)


def bit_of(where, level):
    return (where[0] >> (level + GROUP.bit_length() - 1)) & 1 == 1


def chunk_count(width):
    return 2 if (width // GROUP) % (2 * LANES) == 0 else 1


def chunk_lanes(where, k, chunk, part, width):
    start = (place_of(where) ^ k) * (width // GROUP) + chunk * part
    return pl.ds(pl.multiple_of(start, part), part)


def masks_of(length):
    rows, other = iota((length, length), 0), iota((length, length), 1)
    after = jnp.where(other > rows, 1.0, 0.0).astype(BF16)
    return after, jnp.where(other <= rows, 1.0, 0.0).astype(BF16)


def factors_of(ld, after, until):
    length = ld.shape[1]
    terms = three(ld)
    into_end = jnp.exp(summed(after, terms)).astype(BF16)
    from_start = jnp.exp(summed(until, terms)).astype(BF16)
    total = jnp.exp(summed(jnp.ones((TAIL, length), BF16), terms))
    high = total.astype(BF16).astype(F32)
    halves = jnp.where(iota(total.shape, 0) < TAIL // 2, high, total - high).astype(BF16)
    return into_end, from_start, halves


def put_states(head_dim, chunk, where, operands, outs, ready):
    into_end, from_start, halves, b, c, x, dy = operands
    x_scaled, dy_scaled, spread, *sends = outs
    group, state = len(sends), b.shape[1]
    width = x.shape[1]
    chunks = chunk_count(width)
    part = width // (group * chunks)
    difference = row_less_head(head_dim, part)
    sides = [(into_end, b, x, x_scaled, 0), (from_start, c, dy, dy_scaled, state)]
    for side, (factors, proj, cols, scaled, first) in enumerate(sides):
        ready(side)
        turned = proj[...].T
        for k in range(group):
            here = slice(k * part, (k + 1) * part)
            lanes = chunk_lanes(where, k, chunk, part, width)
            first_head = ((place_of(where) ^ k) * chunks + chunk) * (part // head_dim)
            hot = head_of_lane(difference, first_head)
            wide = dot(factors, hot, NN).astype(BF16)
            if side == 0:
                spread[:, here] = wide
                sends[k][2 * state :, :] = dot(halves, hot, NN).astype(BF16)
            piece = cols[:, lanes] * wide
            scaled[:, here] = piece
            sends[k][first : first + state, :] = dot(turned, piece, NN).astype(BF16)


def first_states_kernel(head_dim, group, where, ld_in, b_in, c_in, x_in, dy_in, *refs):
    ld, b, c, x, dy, into_end, from_start, halves = refs[:8]
    outs, sems = refs[8:-1], refs[-1]
    pairs = [(ld_in, ld), (b_in, b), (x_in, x), (c_in, c), (dy_in, dy)]
    copies = [pltpu.make_async_copy(i, o, sems.at[n]) for n, (i, o) in enumerate(pairs)]
    for copy in copies:
        copy.start()
    masks = masks_of(ld.shape[1])
    copies[0].wait()
    factors = factors_of(ld[...], *masks)
    for ref, value in zip((into_end, from_start, halves), factors):
        ref[...] = value

    def ready(side):
        copies[1 + 2 * side].wait()
        copies[2 + 2 * side].wait()

    put_states(head_dim, 0, where, (*factors, b, c, x, dy), outs, ready)


def next_states_kernel(head_dim, chunk, where, into_end, from_start, halves, *refs):
    operands = (into_end[...], from_start[...], halves[...], *refs[:4])
    put_states(head_dim, chunk, where, operands, refs[4:], lambda side: None)


def states_shapes(group, length, width, state):
    part = width // (group * chunk_count(width))
    scaled = pltpu.VMEM((length, group * part), BF16)
    return [scaled] * 3 + [pltpu.VMEM((2 * state + TAIL, part), BF16)] * group


def first_states(head_dim, group, where, inputs):
    ld, b, c, x, dy = inputs
    (length, width), state = x.shape, b.shape[1]
    kept = [pltpu.VMEM(a.shape, a.dtype) for a in inputs]
    kept += [pltpu.VMEM((rows, LANES), BF16) for rows in (length, length, TAIL)]
    outs = kept + states_shapes(group, length, width, state)
    return pl.pallas_call(
        functools.partial(first_states_kernel, head_dim, group),
        out_shape=outs,
        in_specs=[SMEM] + [HBM] * 5,
        out_specs=whole(len(outs)),
        scratch_shapes=[pltpu.SemaphoreType.DMA((5,))],
        compiler_params=params(8),
        cost_estimate=cost(2 * length * width * (state + LANES), 8 * length * width),
        name="first_states",
    )(where, *in_hbm(*inputs))


def next_states(head_dim, group, chunk, where, factors, b, c, x, dy):
    (length, width), state = x.shape, b.shape[1]
    outs = states_shapes(group, length, width, state)
    return pl.pallas_call(
        functools.partial(next_states_kernel, head_dim, chunk),
        out_shape=outs,
        in_specs=[SMEM] + whole(7),
        out_specs=whole(len(outs)),
        compiler_params=params(8),
        cost_estimate=cost(2 * length * width * (state + LANES), 4 * length * width),
        name="next_states",
    )(where, *factors, b, c, x, dy)


def decay_of(tail):
    tail = tail.astype(F32)
    return tail[:1, :] + tail[TAIL // 2 : TAIL // 2 + 1, :]


def put_decay(ref, first, factor):
    high = factor.astype(BF16).astype(F32)
    shape = (TAIL, factor.shape[1])
    both = jnp.where(iota(shape, 0) < TAIL // 2, high, factor - high)
    ref[first:, :] = both.astype(BF16)


def sent_order(parts, fixed=1):
    return [*parts[:fixed], *parts[: fixed - 1 : -1]]


def in_order(group, forward):
    return list(range(group)) if forward else list(range(group - 1, -1, -1))


def side_rows(state, forward):
    return slice(0, state) if forward else slice(state, 2 * state)


def totals_kernel(state, groups, where, *refs):
    group = GROUP
    blocks, out, sums = sent_order(refs[:group]), refs[-2 if groups else -1], refs[-1]
    for here in range(group):

        @pl.when(place_of(where) == here)
        def _(here=here):
            decays = [decay_of(blocks[q ^ here][2 * state :, :]) for q in range(group)]
            for forward in (True, False):
                rows, value = side_rows(state, forward), None
                for q in in_order(group, forward):
                    piece = blocks[q ^ here][rows, :].astype(F32)
                    value = piece if value is None else decays[q] * value + piece
                sums[rows, :] = value.astype(BF16)

    factor = decay_of(blocks[0][2 * state :, :])
    for block in blocks[1:]:
        factor = factor * decay_of(block[2 * state :, :])
    if not groups:
        put_decay(sums, 2 * state, factor)
    for other in range(groups):
        put_decay(out.at[other], state, factor)
        later = where[0] // group < other
        for forward in (True, False):

            @pl.when(later == forward)
            def _(other=other, forward=forward):
                out[other, :state, :] = sums[side_rows(state, forward), :]


def totals(state, groups, where, blocks, after):
    part = blocks[0].shape[1]
    shape = (groups, state + TAIL, part) if groups else blocks[0].shape
    return pl.pallas_call(
        functools.partial(totals_kernel, state, groups),
        out_shape=jax.ShapeDtypeStruct(shape, BF16),
        in_specs=[SMEM] + whole(len(blocks)) + [ANY] * len(after),
        out_specs=whole(1)[0],
        scratch_shapes=[pltpu.VMEM((2 * state, part), BF16)] if groups else [],
        compiler_params=params(4),
        cost_estimate=cost(8 * blocks[0].size, 10 * blocks[0].size),
        name="totals",
    )(where, *sent_order(blocks), *after)


def merged_kernel(state, level, last, where, own, received, *refs):
    out = refs[-1]
    d_own, d_other = decay_of(own[2 * state :, :]), decay_of(received[2 * state :, :])
    upper = bit_of(where, level)
    later = bit_of(where, level + 1)
    for is_upper in (False, True):
        for forward in (True, False):
            chosen = upper == is_upper
            if last:
                chosen = chosen & (later != forward)

            @pl.when(chosen)
            def _(is_upper=is_upper, forward=forward):
                rows = side_rows(state, forward)
                mine, other = own[rows, :].astype(F32), received[rows, :].astype(F32)
                value = mine + d_own * other if is_upper == forward else other + d_other * mine
                out[slice(0, state) if last else rows, :] = value.astype(BF16)

    put_decay(out, state if last else 2 * state, d_own * d_other)


def merged(state, level, last, where, own, received, after):
    rows = (state if last else 2 * state) + TAIL
    return pl.pallas_call(
        functools.partial(merged_kernel, state, level, last),
        out_shape=pltpu.VMEM((rows, own.shape[1]), BF16),
        in_specs=[SMEM] + whole(2) + [ANY] * len(after),
        out_specs=whole(1)[0],
        compiler_params=params(4),
        cost_estimate=cost(4 * own.size, 6 * own.size),
        name="merged",
    )(where, own, received, *after)


def put_direct(state, number, received, entry):
    groups = received.shape[0]
    for mine in range(groups):

        @pl.when(number == mine)
        def _(mine=mine):
            for forward in (True, False):
                others = range(mine - 1, -1, -1) if forward else range(mine + 1, groups)
                value, factor = jnp.zeros((state, entry.shape[1]), F32), None
                for other in others:
                    piece = received[other, :state, :].astype(F32)
                    value = piece if factor is None else value + factor * piece
                    d = decay_of(received[other, state:, :])
                    factor = d if factor is None else factor * d
                entry[side_rows(state, forward), :] = value


def put_rounds(state, where, received, entry):
    for forward in (True, False):
        value, factor = None, 1.0
        for level, r in enumerate(received):
            gets = bit_of(where, level) == forward
            both = r.shape[0] > 2 * state
            rows = side_rows(state, forward) if both else slice(0, state)
            piece = r[rows, :].astype(F32) * jnp.where(gets, 1.0, 0.0)
            value = piece if value is None else value + factor * piece
            if both:
                factor = factor * jnp.where(gets, decay_of(r[2 * state :, :]), 1.0)
        entry[side_rows(state, forward), :] = value


def members_kernel(state, direct, n_received, where, *refs):
    received, refs = refs[:n_received], refs[n_received:]
    group = GROUP
    blocks, outs, entry = refs[:group], refs[-1 - group : -1], refs[-1]
    if direct:
        put_direct(state, where[0] // group, received[0], entry)
    else:
        put_rounds(state, where, received, entry)
    for here in range(group):

        @pl.when(place_of(where) == here)
        def _(here=here):
            decays = [decay_of(blocks[q ^ here][2 * state :, :]) for q in range(group)]
            for forward in (True, False):
                rows, order = side_rows(state, forward), in_order(group, forward)
                value = entry[rows, :]
                for q in order:
                    outs[q ^ here][rows, :] = value.astype(BF16)
                    if q != order[-1]:
                        value = decays[q] * value + blocks[q ^ here][rows, :].astype(F32)


def member_entries(state, direct, where, blocks, received, after):
    group, part = len(blocks), blocks[0].shape[1]
    return pl.pallas_call(
        functools.partial(members_kernel, state, direct, len(received)),
        out_shape=[jax.ShapeDtypeStruct((2 * state, part), BF16)] * group,
        in_specs=[SMEM] + whole(group + len(received)) + [ANY] * len(after),
        out_specs=whole(group),
        scratch_shapes=[pltpu.VMEM((2 * state, part), F32)],
        compiler_params=params(4),
        cost_estimate=cost(12 * blocks[0].size, 16 * blocks[0].size),
        name="member_entries",
    )(where, *received, *blocks, *after)


def exchange(parts):
    count = lax.axis_size("seq")
    out = list(parts)
    for k in range(len(parts) - 1, 0, -1):
        out[k] = lax.ppermute(parts[k], "seq", [(s, s ^ k) for s in range(count)])
    return out


def split_pairs(first, count):
    if count == 1:
        return []
    middle = first + count // 2
    return (
        [(first, middle, first + count)]
        + split_pairs(first, middle - first)
        + split_pairs(middle, first + count - middle)
    )


def grouped_cuts(pieces):
    groups = {}
    for cut in split_pairs(0, pieces):
        groups.setdefault((cut[1] - cut[0], cut[2] - cut[1]), []).append(cut)
    return list(groups.items())


def rows_of(first, end, piece):
    return slice(first * piece, end * piece)


def setup_kernel(piece, ld, b, c, *refs):
    near, cum_terms = refs[-2:]
    heads, length = ld.shape
    rows, other = iota((length, length), 0), iota((length, length), 1)
    mask = jnp.where(other <= rows, 1.0, 0.0).astype(BF16)
    cum = summed(mask, three(ld[...] * LOG2E))
    lane = iota(cum.shape, 1)
    in_slots = jnp.where(lane < SLOT, cum, 0.0)
    in_slots = in_slots + pltpu.roll(in_slots, SLOT, 1) + pltpu.roll(in_slots, 2 * SLOT, 1)
    high, mid, low = three(in_slots)
    cum_terms[...] = jnp.where(lane < SLOT, high, jnp.where(lane < 2 * SLOT, mid, low))
    keep = iota((piece, piece), 0) <= iota((piece, piece), 1)
    pieces = length // piece
    for n in range(pieces):
        here = rows_of(n, n + 1, piece)
        near[here, :] = jnp.where(keep, dot(b[here, :], c[here, :], NT), 0.0).astype(BF16)
    cuts = [cut for _, same in grouped_cuts(pieces) for cut in same]
    for (lo, mid_, hi), far in zip(cuts, refs):
        left, right = rows_of(lo, mid_, piece), rows_of(mid_, hi, piece)
        far[...] = dot(b[left, :], c[right, :], NT).astype(BF16)


def inner_setup(piece, ld, b, c, after):
    length = b.shape[0]
    cuts = [cut for _, same in grouped_cuts(length // piece) for cut in same]
    outs = [
        jax.ShapeDtypeStruct(((mid - lo) * piece, (hi - mid) * piece), BF16) for lo, mid, hi in cuts
    ]
    outs.append(jax.ShapeDtypeStruct((length, piece), BF16))
    outs.append(jax.ShapeDtypeStruct((length, LANES), BF16))
    return pl.pallas_call(
        functools.partial(setup_kernel_after, piece, len(after)),
        out_shape=outs,
        in_specs=whole(3) + [ANY] * len(after),
        out_specs=whole(len(outs)),
        compiler_params=params(4),
        cost_estimate=cost(8 * b.size * length, 8 * b.size),
        name="inner_setup",
    )(ld, b, c, *after)


def setup_kernel_after(piece, n_after, ld, b, c, *refs):
    setup_kernel(piece, ld, b, c, *refs[n_after:])


def inner_kernel(head_dim, chunk, n_before, n_after, b, c, x, dy, *refs):
    length, width = x.shape
    piece = head_dim
    pieces = length // piece
    groups = grouped_cuts(pieces)
    n_cuts = sum(len(same) for _, same in groups)
    fars, (near, cum_terms), refs = refs[:n_cuts], refs[n_cuts : n_cuts + 2], refs[n_cuts + 2 :]
    before, refs = refs[:n_before], refs[n_before + n_after :]
    dx_out, db_out, dc_out, x_near, dy_near, *scratch = refs
    lefts, rights = scratch[: len(groups)], scratch[len(groups) :]
    part = dx_out.shape[1] // GROUP
    difference = row_less_head(head_dim, part, SLOT)

    for m in range(GROUP):
        owned = m * (width // GROUP) + chunk * part
        lanes, here = slice(owned, owned + part), slice(m * part, (m + 1) * part)
        cum = dot(cum_terms[...], head_of_lane(difference, owned // head_dim), NN)
        dx = []
        for n in range(pieces):
            rows = rows_of(n, n + 1, piece)
            middle = cum[n * piece + piece // 2 : n * piece + piece // 2 + 1, :]
            gap = middle - cum[rows, :]
            down, up = jnp.exp2(gap), jnp.exp2(-gap)
            x_near[rows, here] = (x[rows, lanes].astype(F32) * down).astype(BF16)
            dy_piece = (dy[rows, lanes].astype(F32) * up).astype(BF16)
            dy_near[rows, here] = dy_piece
            dx.append(down * dot(near[rows, :], dy_piece, NN))
        far_of = iter(fars)
        for (_, same), left_ref, right_ref in zip(groups, lefts, rights):
            for g, (lo, mid, hi) in enumerate(same):
                left, right = rows_of(lo, mid, piece), rows_of(mid, hi, piece)
                edge = cum[mid * piece - 1 : mid * piece, :]
                to_edge = jnp.exp2(edge - cum[left, :])
                from_edge = jnp.exp2(cum[right, :] - edge)
                x_left = (x[left, lanes].astype(F32) * to_edge).astype(BF16)
                dy_right = (dy[right, lanes].astype(F32) * from_edge).astype(BF16)
                left_ref[rows_of(g, g + 1, (mid - lo) * piece), here] = x_left
                right_ref[rows_of(g, g + 1, (hi - mid) * piece), here] = dy_right
                far = to_edge * dot(next(far_of)[...], dy_right, NN)
                for n in range(lo, mid):
                    dx[n] = dx[n] + far[rows_of(n - lo, n - lo + 1, piece), :]
        for n in range(pieces):
            dx_out[rows_of(n, n + 1, piece), here] = dx[n].astype(BF16)

    if before:
        db_out[...] = before[0][...]
        dc_out[...] = before[1][...]
    else:
        db_out[...] = jnp.zeros_like(db_out)
        dc_out[...] = jnp.zeros_like(dc_out)
    batch = 4
    for first in range(0, pieces, batch):
        rows = rows_of(first, min(first + batch, pieces), piece)
        total = dot(x_near[rows, :], dy_near[rows, :], NT)
        row, col = iota(total.shape, 0), iota(total.shape, 1)
        keep = (split_of(row, piece) == split_of(col, piece)) & (row <= col)
        weighted = jnp.where(keep, total, 0.0).astype(BF16)
        db_out[rows, :] += dot(weighted, c[rows, :], NN)
        dc_out[rows, :] += dot(weighted, b[rows, :], TN)
    for ((n_left, n_right), same), left_ref, right_ref in zip(groups, lefts, rights):
        total = dot(left_ref[...], right_ref[...], NT)
        if len(same) > 1:
            row, col = iota(total.shape, 0), iota(total.shape, 1)
            same_cut = split_of(row, n_left * piece) == split_of(col, n_right * piece)
            total = jnp.where(same_cut, total, 0.0)
        weighted = total.astype(BF16)
        b_left = jnp.concatenate([b[rows_of(lo, mid, piece), :] for lo, mid, _ in same], axis=0)
        c_right = jnp.concatenate([c[rows_of(mid, hi, piece), :] for _, mid, hi in same], axis=0)
        db = dot(weighted, c_right, NN)
        dc = dot(weighted, b_left, TN)
        for g, (lo, mid, hi) in enumerate(same):
            db_out[rows_of(lo, mid, piece), :] += db[rows_of(g, g + 1, n_left * piece), :]
            dc_out[rows_of(mid, hi, piece), :] += dc[rows_of(g, g + 1, n_right * piece), :]


def inner_terms(head_dim, chunk, setup, b, c, x, dy, before, after):
    length, state = b.shape
    columns = x.shape[1] // chunk_count(x.shape[1])
    groups = grouped_cuts(length // head_dim)
    sizes = [[len(same) * n * head_dim for n in halves] for halves, same in groups]
    return pl.pallas_call(
        functools.partial(inner_kernel, head_dim, chunk, len(before), len(after)),
        out_shape=[
            jax.ShapeDtypeStruct((length, columns), BF16),
            jax.ShapeDtypeStruct((length, state), F32),
            jax.ShapeDtypeStruct((length, state), F32),
        ],
        in_specs=whole(4 + len(setup) + len(before)) + [ANY] * len(after),
        out_specs=whole(3),
        scratch_shapes=[pltpu.VMEM((length, columns), BF16)] * 2
        + [pltpu.VMEM((left, columns), BF16) for left, _ in sizes]
        + [pltpu.VMEM((right, columns), BF16) for _, right in sizes],
        compiler_params=params(16),
        cost_estimate=cost(8 * x.size * state, 4 * x.size, 2 * x.size),
        name="inner_terms",
    )(b, c, x, dy, *setup, *before, *after)


def parts_kernel(last, x_scaled, dy_scaled, db_before, dc_before, *refs):
    entries, outs = sent_order(refs[:GROUP]), refs[-1 if last else -2 :]
    length, state = db_before.shape
    part = entries[0].shape[1]
    db, dc = db_before[...], dc_before[...]
    for k, entry in enumerate(entries):
        here = slice(k * part, (k + 1) * part)
        db = db + dot(x_scaled[:, here], entry[state:, :], NT)
        dc = dc + dot(dy_scaled[:, here], entry[:state, :], NT)
    if last:
        outs[0][:length, :] = db.astype(BF16)
        outs[0][length:, :] = dc.astype(BF16)
    else:
        outs[0][...] = db
        outs[1][...] = dc


def entry_parts(last, x_scaled, dy_scaled, db_before, dc_before, entries, after):
    length, state = db_before.shape
    one = pltpu.VMEM((length, state), F32)
    outs = [pltpu.VMEM((2 * length, state), BF16)] if last else [one, one]
    return pl.pallas_call(
        functools.partial(parts_kernel, last),
        out_shape=outs,
        in_specs=whole(4 + len(entries)) + [ANY] * len(after),
        out_specs=whole(len(outs)),
        compiler_params=params(8),
        cost_estimate=cost(4 * x_scaled.size * state, 4 * x_scaled.size),
        name="entry_parts",
    )(x_scaled, dy_scaled, db_before, dc_before, *sent_order(entries), *after)


def values_kernel(chunk, last, where, spread, b, dx_local, *refs):
    entries, (dx, sems) = sent_order(refs[:GROUP], 2 if last else 1), refs[-2:]
    out = refs[-3 if last else -4]
    if not last:
        refs[-3][...] = jnp.zeros_like(refs[-3])
    state, part = b.shape[1], entries[0].shape[1]
    stores = []
    for k, entry in enumerate(entries):
        here = slice(k * part, (k + 1) * part)
        local = dx_local[:, pl.ds(pl.multiple_of((place_of(where) ^ k) * part, part), part)]
        far = spread[:, here].astype(F32) * dot(b[...], entry[state:, :], NN)
        dx[k] = (local.astype(F32) + far).astype(BF16)
        lanes = chunk_lanes(where, k, chunk, part, out.shape[1])
        store = pltpu.make_async_copy(dx.at[k], out.at[:, lanes], sems.at[k])
        store.start()
        stores.append(store)
    for store in stores:
        store.wait()


def entry_values(chunk, chunks, where, spread, b, dx_local, entries, before, after):
    group, part = len(entries), entries[0].shape[1]
    length, state = b.shape
    size, last = dx_local.size, chunk == chunks - 1
    sent = sent_order(entries, 2 if last else 1)
    operands = [where, spread, b, dx_local, *sent, *after, *before]
    return pl.pallas_call(
        functools.partial(values_kernel, chunk, last),
        out_shape=[pltpu.HBM((length, chunks * group * part), BF16)]
        + [pltpu.VMEM((8, LANES), F32)] * (not last),
        in_specs=[SMEM] + whole(3 + group) + [ANY] * len(after) + [HBM] * len(before),
        out_specs=[HBM] + whole(0 if last else 1),
        input_output_aliases={len(operands) - 1: 0} if before else {},
        scratch_shapes=[
            pltpu.VMEM((group, length, part), BF16),
            pltpu.SemaphoreType.DMA((group,)),
        ],
        compiler_params=params(8),
        cost_estimate=cost(2 * size * state, 4 * size),
        name="entry_values",
    )(*operands)


def over_heads(part):
    count = lax.axis_size("head")
    total = part.astype(F32)
    for shift in range(1, count):
        pairs = [(s, (s + shift) % count) for s in range(count)]
        total = total + lax.ppermute(part, "head", pairs).astype(F32)
    return total.astype(BF16)


def shards(token_values, b_inputs, c_inputs, log_decay, grad_out):
    head_dim = token_values.shape[1] // log_decay.shape[0]
    length, state = b_inputs.shape
    count, group = lax.axis_size("seq"), GROUP
    chunks = chunk_count(token_values.shape[1])
    levels = (count // group).bit_length() - 1
    where = lax.axis_index("seq").astype(jnp.int32)[None]
    inputs = (log_decay, b_inputs, c_inputs, token_values, grad_out)
    ld, b, c, x, dy, *rest = first_states(head_dim, group, where, inputs)
    factors, states = rest[:3], [rest[3:]]
    blocks = [exchange(states[0][3:])]
    for chunk in range(1, chunks):
        states.append(next_states(head_dim, group, chunk, where, factors, b, c, x, dy))
        blocks.append(exchange(states[chunk][3:]))
    setup = inner_setup(head_dim, ld, b, c, [states[-1][3]])

    def to_group(block, k):
        return lax.ppermute(block, "seq", [(s, s ^ (k * group)) for s in range(count)])

    groups = count // group
    columns = [[n * group + j for n in range(groups)] for j in range(group)]
    entries, inner, sums, after = [], [], [], setup[-1:]
    for chunk in range(chunks):
        direct = chunk == 0 and chunks > 1
        own = totals(state, groups * direct, where, blocks[chunk], after)
        after = [own]
        if direct:
            received = [lax.all_to_all(own, "seq", 0, 0, axis_index_groups=columns, tiled=True)]
        else:
            received = [to_group(own, 1)]
            for level in range(levels - 1):
                last = level == levels - 2
                own = merged(state, level, last, where, own, received[level], [])
                received.append(to_group(own, 2 << level))
        inner.append(inner_terms(head_dim, chunk, setup, b, c, x, dy, sums, [own]))
        sums = list(inner[chunk][1:])
        found = member_entries(state, direct, where, blocks[chunk], received, sums[:1])
        entries.append(exchange(found))

    grad_values, done = [], []
    for chunk in range(chunks):
        x_scaled, dy_scaled, spread = states[chunk][:3]
        last = chunk == chunks - 1
        sums = entry_parts(last, x_scaled, dy_scaled, *sums, entries[chunk], done)
        outs = entry_values(
            chunk, chunks, where, spread, b, inner[chunk][0], entries[chunk], grad_values, []
        )
        grad_values, done = list(outs[:1]), list(outs[1:])
    both = over_heads(sums[0])
    return grad_values[0], both[:length], both[length:]


def solution(mesh):
    in_specs = (
        P("seq", "head"),
        P("seq", None),
        P("seq", None),
        P("head", "seq"),
        P("seq", "head"),
    )
    out_specs = (P("seq", "head"), P("seq", None), P("seq", None))
    return jax.shard_map(shards, mesh=mesh, in_specs=in_specs, out_specs=out_specs, check_vma=False)
```

```python
import functools

import jax
import jax.numpy as jnp
from jax import lax
from jax.experimental import pallas as pl
from jax.experimental.pallas import tpu as pltpu
from jax.sharding import PartitionSpec as P

BF16 = jnp.bfloat16
F32 = jnp.float32
LANES = 128
GROUP = 4
TAIL = 16
LOG2E = 1.4426950408889634
MIB = 1024 * 1024

NN = (((1,), (0,)), ((), ()))
NT = (((1,), (1,)), ((), ()))
TN = (((0,), (0,)), ((), ()))


def dot(a, b, dims):
    return lax.dot_general(a, b, dims, preferred_element_type=F32)


def iota(shape, dim):
    return lax.broadcasted_iota(jnp.int32, shape, dim)


def three(values):
    high = values.astype(BF16)
    rest = values - high.astype(F32)
    mid = rest.astype(BF16)
    return high, mid, (rest - mid.astype(F32)).astype(BF16)


SLOT = LANES // 4


def summed(mask, terms):
    heads, length = terms[0].shape
    gap = [] if heads == SLOT else [jnp.zeros((SLOT - heads, length), BF16)]
    rows = [r for t in terms for r in [t] + gap] + [jnp.zeros((SLOT, length), BF16)]
    each = dot(mask, jnp.concatenate(rows, axis=0), NT)
    return each + pltpu.roll(each, LANES - SLOT, 1) + pltpu.roll(each, LANES - 2 * SLOT, 1)


def split_of(index, size):
    shift = size.bit_length() - 1
    return lax.shift_right_logical(index, shift) if size == 1 << shift else index // size


def row_less_head(head_dim, width, rows=LANES):
    shape = (LANES, width)
    row = iota(shape, 0)
    if rows < LANES:
        row = row & (rows - 1)
    return row - split_of(iota(shape, 1), head_dim)


def head_of_lane(difference, first):
    return jnp.where(difference == first, 1.0, 0.0).astype(BF16)


def whole(count):
    return [pl.BlockSpec(memory_space=pltpu.VMEM)] * count


def in_hbm(*arrays):
    return [pltpu.with_memory_space_constraint(a, pltpu.HBM) for a in arrays]


SMEM = pl.BlockSpec(memory_space=pltpu.SMEM)
HBM = pl.BlockSpec(memory_space=pltpu.HBM)
ANY = pl.BlockSpec(memory_space=pl.ANY)


def params(mib):
    return pltpu.CompilerParams(vmem_limit_bytes=mib * MIB)


def cost(flops, size, transcendentals=0):
    return pl.CostEstimate(flops=flops, bytes_accessed=size, transcendentals=transcendentals)


def place_of(where):
    return where[0] & (GROUP - 1)


def bit_of(where, level):
    return (where[0] >> (level + GROUP.bit_length() - 1)) & 1 == 1


def chunk_count(width):
    return 2 if (width // GROUP) % (2 * LANES) == 0 else 1


def chunk_lanes(where, k, chunk, part, width):
    start = (place_of(where) ^ k) * (width // GROUP) + chunk * part
    return pl.ds(pl.multiple_of(start, part), part)


def masks_of(length):
    rows, other = iota((length, length), 0), iota((length, length), 1)
    after = jnp.where(other > rows, 1.0, 0.0).astype(BF16)
    return after, jnp.where(other <= rows, 1.0, 0.0).astype(BF16)


def factors_of(ld, after, until):
    length = ld.shape[1]
    terms = three(ld)
    into_end = jnp.exp(summed(after, terms)).astype(BF16)
    from_start = jnp.exp(summed(until, terms)).astype(BF16)
    total = jnp.exp(summed(jnp.ones((TAIL, length), BF16), terms))
    high = total.astype(BF16).astype(F32)
    halves = jnp.where(iota(total.shape, 0) < TAIL // 2, high, total - high).astype(BF16)
    return into_end, from_start, halves


def put_states(head_dim, chunk, where, operands, outs, ready):
    into_end, from_start, halves, b, c, x, dy = operands
    x_scaled, dy_scaled, spread, *sends = outs
    group, state = len(sends), b.shape[1]
    width = x.shape[1]
    chunks = chunk_count(width)
    part = width // (group * chunks)
    difference = row_less_head(head_dim, part)
    sides = [(into_end, b, x, x_scaled, 0), (from_start, c, dy, dy_scaled, state)]
    for side, (factors, proj, cols, scaled, first) in enumerate(sides):
        ready(side)
        turned = proj[...].T
        for k in range(group):
            here = slice(k * part, (k + 1) * part)
            lanes = chunk_lanes(where, k, chunk, part, width)
            first_head = ((place_of(where) ^ k) * chunks + chunk) * (part // head_dim)
            hot = head_of_lane(difference, first_head)
            wide = dot(factors, hot, NN).astype(BF16)
            if side == 0:
                spread[:, here] = wide
                sends[k][2 * state :, :] = dot(halves, hot, NN).astype(BF16)
            piece = cols[:, lanes] * wide
            scaled[:, here] = piece
            sends[k][first : first + state, :] = dot(turned, piece, NN).astype(BF16)


def first_states_kernel(head_dim, group, where, ld_in, b_in, c_in, x_in, dy_in, *refs):
    ld, b, c, x, dy, into_end, from_start, halves = refs[:8]
    outs, sems = refs[8:-1], refs[-1]
    width = x.shape[1]
    chunks = chunk_count(width)
    part = width // (group * chunks)

    def load(n, source, target):
        copy = pltpu.make_async_copy(source, target, sems.at[n])
        copy.start()
        return copy

    def load_chunk(n, chunk, source, target):
        lanes = [pl.ds((m * chunks + chunk) * part, part) for m in range(group)]
        return [
            load(n + m, source.at[:, one], target.at[:, one]) for m, one in enumerate(lanes)
        ]

    first = load(0, ld_in, ld)
    loads = [
        [load(1, b_in, b), *load_chunk(3, 0, x_in, x)],
        [load(2, c_in, c), *load_chunk(3 + group, 0, dy_in, dy)],
    ]
    masks = masks_of(ld.shape[1])
    first.wait()
    factors = factors_of(ld[...], *masks)
    for ref, value in zip((into_end, from_start, halves), factors):
        ref[...] = value
    later = []

    def ready(side):
        for copy in loads[side]:
            copy.wait()
        for chunk in range(1, chunks if side == 1 else 1):
            at = 3 + 2 * group * chunk
            later.extend(load_chunk(at, chunk, x_in, x) + load_chunk(at + group, chunk, dy_in, dy))

    put_states(head_dim, 0, where, (*factors, b, c, x, dy), outs, ready)
    for copy in later:
        copy.wait()


def next_states_kernel(head_dim, chunk, where, into_end, from_start, halves, *refs):
    operands = (into_end[...], from_start[...], halves[...], *refs[:4])
    put_states(head_dim, chunk, where, operands, refs[4:], lambda side: None)


def states_shapes(group, length, width, state):
    part = width // (group * chunk_count(width))
    scaled = pltpu.VMEM((length, group * part), BF16)
    return [scaled] * 3 + [pltpu.VMEM((2 * state + TAIL, part), BF16)] * group


def first_states(head_dim, group, where, inputs):
    ld, b, c, x, dy = inputs
    (length, width), state = x.shape, b.shape[1]
    kept = [pltpu.VMEM(a.shape, a.dtype) for a in inputs]
    kept += [pltpu.VMEM((rows, LANES), BF16) for rows in (length, length, TAIL)]
    outs = kept + states_shapes(group, length, width, state)
    return pl.pallas_call(
        functools.partial(first_states_kernel, head_dim, group),
        out_shape=outs,
        in_specs=[SMEM] + [HBM] * 5,
        out_specs=whole(len(outs)),
        scratch_shapes=[pltpu.SemaphoreType.DMA((3 + 2 * group * chunk_count(width),))],
        compiler_params=params(8),
        cost_estimate=cost(2 * length * width * (state + LANES), 8 * length * width),
        name="first_states",
    )(where, *in_hbm(*inputs))


def next_states(head_dim, group, chunk, where, factors, b, c, x, dy):
    (length, width), state = x.shape, b.shape[1]
    outs = states_shapes(group, length, width, state)
    return pl.pallas_call(
        functools.partial(next_states_kernel, head_dim, chunk),
        out_shape=outs,
        in_specs=[SMEM] + whole(7),
        out_specs=whole(len(outs)),
        compiler_params=params(8),
        cost_estimate=cost(2 * length * width * (state + LANES), 4 * length * width),
        name="next_states",
    )(where, *factors, b, c, x, dy)


def decay_of(tail):
    tail = tail.astype(F32)
    return tail[:1, :] + tail[TAIL // 2 : TAIL // 2 + 1, :]


def put_decay(ref, first, factor):
    high = factor.astype(BF16).astype(F32)
    shape = (TAIL, factor.shape[1])
    both = jnp.where(iota(shape, 0) < TAIL // 2, high, factor - high)
    ref[first:, :] = both.astype(BF16)


def sent_order(parts, fixed=1):
    return [*parts[:fixed], *parts[: fixed - 1 : -1]]


def in_order(group, forward):
    return list(range(group)) if forward else list(range(group - 1, -1, -1))


def side_rows(state, forward):
    return slice(0, state) if forward else slice(state, 2 * state)


def totals_kernel(state, levels, where, *refs):
    group = GROUP
    blocks, outs, sums = sent_order(refs[:group]), refs[-1 - levels : -1], refs[-1]
    for here in range(group):

        @pl.when(place_of(where) == here)
        def _(here=here):
            decays = [decay_of(blocks[q ^ here][2 * state :, :]) for q in range(group)]
            for forward in (True, False):
                rows, value = side_rows(state, forward), None
                for q in in_order(group, forward):
                    piece = blocks[q ^ here][rows, :].astype(F32)
                    value = piece if value is None else decays[q] * value + piece
                sums[rows, :] = value.astype(BF16)

    factor = decay_of(blocks[0][2 * state :, :])
    for block in blocks[1:]:
        factor = factor * decay_of(block[2 * state :, :])
    if not levels:
        put_decay(sums, 2 * state, factor)
    for level, out in enumerate(outs):
        put_decay(out, state, factor)
        for forward in (True, False):

            @pl.when(bit_of(where, level) != forward)
            def _(out=out, forward=forward):
                out[:state, :] = sums[side_rows(state, forward), :]


def totals(state, levels, where, blocks, after):
    part = blocks[0].shape[1]
    outs = [jax.ShapeDtypeStruct((state + TAIL, part), BF16)] * levels
    if not levels:
        outs = [jax.ShapeDtypeStruct(blocks[0].shape, BF16)]
    return pl.pallas_call(
        functools.partial(totals_kernel, state, levels),
        out_shape=outs,
        in_specs=[SMEM] + whole(len(blocks)) + [ANY] * len(after),
        out_specs=whole(len(outs)),
        scratch_shapes=[pltpu.VMEM((2 * state, part), BF16)] if levels else [],
        compiler_params=params(4),
        cost_estimate=cost(8 * blocks[0].size, 10 * blocks[0].size),
        name="totals",
    )(where, *sent_order(blocks), *after)


def merged_kernel(state, level, last, where, own, received, *refs):
    out = refs[-1]
    d_own, d_other = decay_of(own[2 * state :, :]), decay_of(received[2 * state :, :])
    upper = bit_of(where, level)
    later = bit_of(where, level + 1)
    for is_upper in (False, True):
        for forward in (True, False):
            chosen = upper == is_upper
            if last:
                chosen = chosen & (later != forward)

            @pl.when(chosen)
            def _(is_upper=is_upper, forward=forward):
                rows = side_rows(state, forward)
                mine, other = own[rows, :].astype(F32), received[rows, :].astype(F32)
                value = mine + d_own * other if is_upper == forward else other + d_other * mine
                out[slice(0, state) if last else rows, :] = value.astype(BF16)

    put_decay(out, state if last else 2 * state, d_own * d_other)


def merged(state, level, last, where, own, received, after):
    rows = (state if last else 2 * state) + TAIL
    return pl.pallas_call(
        functools.partial(merged_kernel, state, level, last),
        out_shape=pltpu.VMEM((rows, own.shape[1]), BF16),
        in_specs=[SMEM] + whole(2) + [ANY] * len(after),
        out_specs=whole(1)[0],
        compiler_params=params(4),
        cost_estimate=cost(4 * own.size, 6 * own.size),
        name="merged",
    )(where, own, received, *after)


def put_direct(state, groups, number, received, entry):
    for mine in range(groups):

        @pl.when(number == mine)
        def _(mine=mine):
            for forward in (True, False):
                rows = side_rows(state, forward)
                others = range(mine - 1, -1, -1) if forward else range(mine + 1, groups)
                value, factor = jnp.zeros((state, entry.shape[1]), F32), None
                for other in others:
                    r = received[(mine ^ other) - 1]
                    piece = r[:state, :].astype(F32)
                    value = piece if factor is None else value + factor * piece
                    d = decay_of(r[state:, :])
                    factor = d if factor is None else factor * d
                entry[rows, :] = value


def put_rounds(state, where, received, entry):
    for forward in (True, False):
        value, factor = None, 1.0
        for level, r in enumerate(received):
            gets = bit_of(where, level) == forward
            both = r.shape[0] > 2 * state
            rows = side_rows(state, forward) if both else slice(0, state)
            piece = r[rows, :].astype(F32) * jnp.where(gets, 1.0, 0.0)
            value = piece if value is None else value + factor * piece
            if both:
                factor = factor * jnp.where(gets, decay_of(r[2 * state :, :]), 1.0)
        entry[side_rows(state, forward), :] = value


def members_kernel(state, direct, n_received, where, *refs):
    received, refs = refs[:n_received], refs[n_received:]
    group = GROUP
    blocks, outs, entry = refs[:group], refs[-1 - group : -1], refs[-1]
    if direct:
        put_direct(state, n_received + 1, where[0] // group, received, entry)
    else:
        put_rounds(state, where, received, entry)
    for here in range(group):

        @pl.when(place_of(where) == here)
        def _(here=here):
            decays = [decay_of(blocks[q ^ here][2 * state :, :]) for q in range(group)]
            for forward in (True, False):
                rows, order = side_rows(state, forward), in_order(group, forward)
                value = entry[rows, :]
                for q in order:
                    outs[q ^ here][rows, :] = value.astype(BF16)
                    if q != order[-1]:
                        value = decays[q] * value + blocks[q ^ here][rows, :].astype(F32)


def member_entries(state, direct, where, blocks, received, after):
    group, part = len(blocks), blocks[0].shape[1]
    return pl.pallas_call(
        functools.partial(members_kernel, state, direct, len(received)),
        out_shape=[jax.ShapeDtypeStruct((2 * state, part), BF16)] * group,
        in_specs=[SMEM] + whole(group + len(received)) + [ANY] * len(after),
        out_specs=whole(group),
        scratch_shapes=[pltpu.VMEM((2 * state, part), F32)],
        compiler_params=params(4),
        cost_estimate=cost(12 * blocks[0].size, 16 * blocks[0].size),
        name="member_entries",
    )(where, *received, *blocks, *after)


def exchange(parts):
    count = lax.axis_size("seq")
    out = list(parts)
    for k in range(len(parts) - 1, 0, -1):
        out[k] = lax.ppermute(parts[k], "seq", [(s, s ^ k) for s in range(count)])
    return out


def split_pairs(first, count):
    if count == 1:
        return []
    middle = first + count // 2
    return (
        [(first, middle, first + count)]
        + split_pairs(first, middle - first)
        + split_pairs(middle, first + count - middle)
    )


def grouped_cuts(pieces):
    groups = {}
    for cut in split_pairs(0, pieces):
        groups.setdefault((cut[1] - cut[0], cut[2] - cut[1]), []).append(cut)
    return list(groups.items())


def rows_of(first, end, piece):
    return slice(first * piece, end * piece)


def setup_kernel(piece, ld, b, c, *refs):
    near, cum_terms = refs[-2:]
    heads, length = ld.shape
    rows, other = iota((length, length), 0), iota((length, length), 1)
    mask = jnp.where(other <= rows, 1.0, 0.0).astype(BF16)
    cum = summed(mask, three(ld[...] * LOG2E))
    lane = iota(cum.shape, 1)
    in_slots = jnp.where(lane < SLOT, cum, 0.0)
    in_slots = in_slots + pltpu.roll(in_slots, SLOT, 1) + pltpu.roll(in_slots, 2 * SLOT, 1)
    high, mid, low = three(in_slots)
    cum_terms[...] = jnp.where(lane < SLOT, high, jnp.where(lane < 2 * SLOT, mid, low))
    keep = iota((piece, piece), 0) <= iota((piece, piece), 1)
    pieces = length // piece
    for n in range(pieces):
        here = rows_of(n, n + 1, piece)
        near[here, :] = jnp.where(keep, dot(b[here, :], c[here, :], NT), 0.0).astype(BF16)
    cuts = [cut for _, same in grouped_cuts(pieces) for cut in same]
    for (lo, mid_, hi), far in zip(cuts, refs):
        left, right = rows_of(lo, mid_, piece), rows_of(mid_, hi, piece)
        far[...] = dot(b[left, :], c[right, :], NT).astype(BF16)


def inner_setup(piece, ld, b, c, after):
    length = b.shape[0]
    cuts = [cut for _, same in grouped_cuts(length // piece) for cut in same]
    outs = [
        jax.ShapeDtypeStruct(((mid - lo) * piece, (hi - mid) * piece), BF16) for lo, mid, hi in cuts
    ]
    outs.append(jax.ShapeDtypeStruct((length, piece), BF16))
    outs.append(jax.ShapeDtypeStruct((length, LANES), BF16))
    return pl.pallas_call(
        functools.partial(setup_kernel_after, piece, len(after)),
        out_shape=outs,
        in_specs=whole(3) + [ANY] * len(after),
        out_specs=whole(len(outs)),
        compiler_params=params(4),
        cost_estimate=cost(8 * b.size * length, 8 * b.size),
        name="inner_setup",
    )(ld, b, c, *after)


def setup_kernel_after(piece, n_after, ld, b, c, *refs):
    setup_kernel(piece, ld, b, c, *refs[n_after:])


def inner_kernel(head_dim, chunk, parts, n_before, n_after, b, c, x, dy, *refs):
    length, width = x.shape
    piece = head_dim
    pieces = length // piece
    groups = grouped_cuts(pieces)
    n_cuts = sum(len(same) for _, same in groups)
    fars, (near, cum_terms), refs = refs[:n_cuts], refs[n_cuts : n_cuts + 2], refs[n_cuts + 2 :]
    before, refs = refs[:n_before], refs[n_before + n_after :]
    dx_out, db_out, dc_out, x_near, dy_near, *scratch = refs
    lefts, rights = scratch[: len(groups)], scratch[len(groups) :]
    part = dx_out.shape[1] // GROUP
    difference = row_less_head(head_dim, part, SLOT)

    if parts[0] > 0:
        dx_out[...] = before[2][...]
    for at, m in enumerate(parts):
        owned = m * (width // GROUP) + chunk * part
        lanes, here = slice(owned, owned + part), slice(at * part, (at + 1) * part)
        out_lanes = slice(m * part, (m + 1) * part)
        cum = dot(cum_terms[...], head_of_lane(difference, owned // head_dim), NN)
        dx = []
        for n in range(pieces):
            rows = rows_of(n, n + 1, piece)
            middle = cum[n * piece + piece // 2 : n * piece + piece // 2 + 1, :]
            gap = middle - cum[rows, :]
            down, up = jnp.exp2(gap), jnp.exp2(-gap)
            x_near[rows, here] = (x[rows, lanes].astype(F32) * down).astype(BF16)
            dy_piece = (dy[rows, lanes].astype(F32) * up).astype(BF16)
            dy_near[rows, here] = dy_piece
            dx.append(down * dot(near[rows, :], dy_piece, NN))
        far_of = iter(fars)
        for (_, same), left_ref, right_ref in zip(groups, lefts, rights):
            for g, (lo, mid, hi) in enumerate(same):
                left, right = rows_of(lo, mid, piece), rows_of(mid, hi, piece)
                edge = cum[mid * piece - 1 : mid * piece, :]
                to_edge = jnp.exp2(edge - cum[left, :])
                from_edge = jnp.exp2(cum[right, :] - edge)
                x_left = (x[left, lanes].astype(F32) * to_edge).astype(BF16)
                dy_right = (dy[right, lanes].astype(F32) * from_edge).astype(BF16)
                left_ref[rows_of(g, g + 1, (mid - lo) * piece), here] = x_left
                right_ref[rows_of(g, g + 1, (hi - mid) * piece), here] = dy_right
                far = to_edge * dot(next(far_of)[...], dy_right, NN)
                for n in range(lo, mid):
                    dx[n] = dx[n] + far[rows_of(n - lo, n - lo + 1, piece), :]
        for n in range(pieces):
            dx_out[rows_of(n, n + 1, piece), out_lanes] = dx[n].astype(BF16)

    if before:
        db_out[...] = before[0][...]
        dc_out[...] = before[1][...]
    else:
        db_out[...] = jnp.zeros_like(db_out)
        dc_out[...] = jnp.zeros_like(dc_out)
    batch = 4
    for first in range(0, pieces, batch):
        rows = rows_of(first, min(first + batch, pieces), piece)
        total = dot(x_near[rows, :], dy_near[rows, :], NT)
        row, col = iota(total.shape, 0), iota(total.shape, 1)
        keep = (split_of(row, piece) == split_of(col, piece)) & (row <= col)
        weighted = jnp.where(keep, total, 0.0).astype(BF16)
        db_out[rows, :] += dot(weighted, c[rows, :], NN)
        dc_out[rows, :] += dot(weighted, b[rows, :], TN)
    for ((n_left, n_right), same), left_ref, right_ref in zip(groups, lefts, rights):
        total = dot(left_ref[...], right_ref[...], NT)
        if len(same) > 1:
            row, col = iota(total.shape, 0), iota(total.shape, 1)
            same_cut = split_of(row, n_left * piece) == split_of(col, n_right * piece)
            total = jnp.where(same_cut, total, 0.0)
        weighted = total.astype(BF16)
        b_left = jnp.concatenate([b[rows_of(lo, mid, piece), :] for lo, mid, _ in same], axis=0)
        c_right = jnp.concatenate([c[rows_of(mid, hi, piece), :] for _, mid, hi in same], axis=0)
        db = dot(weighted, c_right, NN)
        dc = dot(weighted, b_left, TN)
        for g, (lo, mid, hi) in enumerate(same):
            db_out[rows_of(lo, mid, piece), :] += db[rows_of(g, g + 1, n_left * piece), :]
            dc_out[rows_of(mid, hi, piece), :] += dc[rows_of(g, g + 1, n_right * piece), :]


def inner_terms(head_dim, chunk, parts, setup, b, c, x, dy, before, after):
    length, state = b.shape
    columns = x.shape[1] // chunk_count(x.shape[1])
    used = columns // GROUP * len(parts)
    groups = grouped_cuts(length // head_dim)
    sizes = [[len(same) * n * head_dim for n in halves] for halves, same in groups]
    return pl.pallas_call(
        functools.partial(inner_kernel, head_dim, chunk, parts, len(before), len(after)),
        out_shape=[
            jax.ShapeDtypeStruct((length, columns), BF16),
            jax.ShapeDtypeStruct((length, state), F32),
            jax.ShapeDtypeStruct((length, state), F32),
        ],
        in_specs=whole(4 + len(setup) + len(before)) + [ANY] * len(after),
        out_specs=whole(3),
        scratch_shapes=[pltpu.VMEM((length, used), BF16)] * 2
        + [pltpu.VMEM((left, used), BF16) for left, _ in sizes]
        + [pltpu.VMEM((right, used), BF16) for _, right in sizes],
        compiler_params=params(16),
        cost_estimate=cost(8 * x.size * state, 4 * x.size, 2 * x.size),
        name="inner_terms",
    )(b, c, x, dy, *setup, *before, *after)


def parts_kernel(last, ks, x_scaled, dy_scaled, db_before, dc_before, *refs):
    entries, outs = refs[: len(ks)], refs[-1 if last else -2 :]
    length, state = db_before.shape
    part = entries[0].shape[1]
    db, dc = db_before[...], dc_before[...]
    for k, entry in zip(ks, entries):
        here = slice(k * part, (k + 1) * part)
        db = db + dot(x_scaled[:, here], entry[state:, :], NT)
        dc = dc + dot(dy_scaled[:, here], entry[:state, :], NT)
    if last:
        outs[0][:length, :] = db.astype(BF16)
        outs[0][length:, :] = dc.astype(BF16)
    else:
        outs[0][...] = db
        outs[1][...] = dc


def entry_parts(last, ks, x_scaled, dy_scaled, db_before, dc_before, entries, after):
    length, state = db_before.shape
    one = jax.ShapeDtypeStruct((length, state), F32)
    outs = [jax.ShapeDtypeStruct((2 * length, state), BF16)] if last else [one, one]
    return pl.pallas_call(
        functools.partial(parts_kernel, last, ks),
        out_shape=outs,
        in_specs=whole(4 + len(ks)) + [ANY] * len(after),
        out_specs=whole(len(outs)),
        compiler_params=params(8),
        cost_estimate=cost(len(ks) * x_scaled.size * state, len(ks) * x_scaled.size),
        name="entry_parts",
    )(x_scaled, dy_scaled, db_before, dc_before, *[entries[k] for k in ks], *after)


def values_kernel(chunk, last, ks, where, spread, b, dx_local, *refs):
    entries, (dx, sems) = refs[: len(ks)], refs[-2:]
    out = refs[-3 if last else -4]
    if not last:
        refs[-3][...] = jnp.zeros_like(refs[-3])
    state, part = b.shape[1], entries[0].shape[1]
    stores = []
    for n, (k, entry) in enumerate(zip(ks, entries)):
        here = slice(k * part, (k + 1) * part)
        local = dx_local[:, pl.ds(pl.multiple_of((place_of(where) ^ k) * part, part), part)]
        far = spread[:, here].astype(F32) * dot(b[...], entry[state:, :], NN)
        dx[n] = (local.astype(F32) + far).astype(BF16)
        lanes = chunk_lanes(where, k, chunk, part, out.shape[1])
        store = pltpu.make_async_copy(dx.at[n], out.at[:, lanes], sems.at[n])
        store.start()
        stores.append(store)
    for store in stores:
        store.wait()


def entry_values(chunk, last, ks, width, where, spread, b, dx_local, entries, before):
    part = entries[0].shape[1]
    length, state = b.shape
    size = length * part * len(ks)
    operands = [where, spread, b, dx_local, *[entries[k] for k in ks], *before]
    return pl.pallas_call(
        functools.partial(values_kernel, chunk, last, ks),
        out_shape=[pltpu.HBM((length, width), BF16)] + [pltpu.VMEM((8, LANES), F32)] * (not last),
        in_specs=[SMEM] + whole(3 + len(ks)) + [HBM] * len(before),
        out_specs=[HBM] + whole(0 if last else 1),
        input_output_aliases={len(operands) - 1: 0} if before else {},
        scratch_shapes=[
            pltpu.VMEM((len(ks), length, part), BF16),
            pltpu.SemaphoreType.DMA((len(ks),)),
        ],
        compiler_params=params(8),
        cost_estimate=cost(2 * size * state, 4 * size),
        name="entry_values",
    )(*operands)


def over_heads(part):
    count = lax.axis_size("head")
    total = part.astype(F32)
    for shift in range(1, count):
        pairs = [(s, (s + shift) % count) for s in range(count)]
        total = total + lax.ppermute(part, "head", pairs).astype(F32)
    return total.astype(BF16)


def shards(token_values, b_inputs, c_inputs, log_decay, grad_out):
    head_dim = token_values.shape[1] // log_decay.shape[0]
    length, state = b_inputs.shape
    count, group = lax.axis_size("seq"), GROUP
    chunks = chunk_count(token_values.shape[1])
    levels = (count // group).bit_length() - 1
    where = lax.axis_index("seq").astype(jnp.int32)[None]
    inputs = (log_decay, b_inputs, c_inputs, token_values, grad_out)
    ld, b, c, x, dy, *rest = first_states(head_dim, group, where, inputs)
    factors, states = rest[:3], [rest[3:]]
    blocks = [exchange(states[0][3:])]
    for chunk in range(1, chunks):
        states.append(next_states(head_dim, group, chunk, where, factors, b, c, x, dy))
        blocks.append(exchange(states[chunk][3:]))
    setup = inner_setup(head_dim, ld, b, c, [states[-1][3]])
    inner = functools.partial(inner_terms, head_dim)
    early = inner(0, (0,), setup, b, c, x, dy, [], [])

    def to_group(block, k):
        return lax.ppermute(block, "seq", [(s, s ^ (k * group)) for s in range(count)])

    entries, local, sums = [], [], []
    for chunk in range(chunks):
        (own,) = totals(state, 0, where, blocks[chunk], early[1:2] if chunk == 0 else [])
        received = [to_group(own, 1)]
        for level in range(levels - 1):
            last = level == levels - 2
            own = merged(state, level, last, where, own, received[level], [])
            received.append(to_group(own, 2 << level))
        operands = (setup, b, c, x, dy)
        if chunk == 0:
            dx, *sums = inner(chunk, (1, 2, 3), *operands, [*early[1:], early[0]], [own])
        else:
            dx, *sums = inner(chunk, (0, 1, 2), *operands, sums, [own])
        found = member_entries(state, False, where, blocks[chunk], received, sums[:1])
        entries.append(exchange(found))
        if chunk > 0:
            dx, *sums = inner(chunk, (3,), *operands, [*sums, dx], found[:1])
        local.append(dx)

    turns = [(chunk, (0, 3, 2, 1)) for chunk in range(chunks - 1)]
    turns += [(chunks - 1, (0, 3)), (chunks - 1, (2, 1))]
    grad_values, done, width = [], [], token_values.shape[1]
    for n, (chunk, ks) in enumerate(turns):
        x_scaled, dy_scaled, spread = states[chunk][:3]
        last = n == len(turns) - 1
        sums = entry_parts(last, ks, x_scaled, dy_scaled, *sums, entries[chunk], done)
        grad_values, *done = entry_values(
            chunk, last, ks, width, where, spread, b, local[chunk], entries[chunk], grad_values
        )
        grad_values = [grad_values]
    both = over_heads(sums[0])
    return grad_values[0], both[:length], both[length:]


def solution(mesh):
    in_specs = (
        P("seq", "head"),
        P("seq", None),
        P("seq", None),
        P("head", "seq"),
        P("seq", "head"),
    )
    out_specs = (P("seq", "head"), P("seq", None), P("seq", None))
    return jax.shard_map(shards, mesh=mesh, in_specs=in_specs, out_specs=out_specs, check_vma=False)
```

```python
import functools

import jax
import jax.numpy as jnp
from jax import lax
from jax.experimental import pallas as pl
from jax.experimental.pallas import tpu as pltpu
from jax.sharding import PartitionSpec as P

BF16 = jnp.bfloat16
F32 = jnp.float32
LANES = 128
GROUP = 4
TAIL = 16
LOG2E = 1.4426950408889634
MIB = 1024 * 1024

NN = (((1,), (0,)), ((), ()))
NT = (((1,), (1,)), ((), ()))
TN = (((0,), (0,)), ((), ()))


def dot(a, b, dims):
    return lax.dot_general(a, b, dims, preferred_element_type=F32)


def iota(shape, dim):
    return lax.broadcasted_iota(jnp.int32, shape, dim)


def three(values):
    high = values.astype(BF16)
    rest = values - high.astype(F32)
    mid = rest.astype(BF16)
    return high, mid, (rest - mid.astype(F32)).astype(BF16)


SLOT = LANES // 4


def summed(mask, terms):
    heads, length = terms[0].shape
    gap = [] if heads == SLOT else [jnp.zeros((SLOT - heads, length), BF16)]
    rows = [r for t in terms for r in [t] + gap] + [jnp.zeros((SLOT, length), BF16)]
    each = dot(mask, jnp.concatenate(rows, axis=0), NT)
    return each + pltpu.roll(each, LANES - SLOT, 1) + pltpu.roll(each, LANES - 2 * SLOT, 1)


def split_of(index, size):
    shift = size.bit_length() - 1
    return lax.shift_right_logical(index, shift) if size == 1 << shift else index // size


def row_less_head(head_dim, width, rows=LANES):
    shape = (LANES, width)
    row = iota(shape, 0)
    if rows < LANES:
        row = row & (rows - 1)
    return row - split_of(iota(shape, 1), head_dim)


def head_of_lane(difference, first):
    return jnp.where(difference == first, 1.0, 0.0).astype(BF16)


def whole(count):
    return [pl.BlockSpec(memory_space=pltpu.VMEM)] * count


def in_hbm(*arrays):
    return [pltpu.with_memory_space_constraint(a, pltpu.HBM) for a in arrays]


SMEM = pl.BlockSpec(memory_space=pltpu.SMEM)
HBM = pl.BlockSpec(memory_space=pltpu.HBM)
ANY = pl.BlockSpec(memory_space=pl.ANY)


def params(mib):
    return pltpu.CompilerParams(vmem_limit_bytes=mib * MIB)


def cost(flops, size, transcendentals=0):
    return pl.CostEstimate(flops=flops, bytes_accessed=size, transcendentals=transcendentals)


def place_of(where):
    return where[0] & (GROUP - 1)


def bit_of(where, level):
    return (where[0] >> (level + GROUP.bit_length() - 1)) & 1 == 1


def chunk_count(width):
    return 2 if (width // GROUP) % (2 * LANES) == 0 else 1


def chunk_lanes(where, k, chunk, part, width):
    start = (place_of(where) ^ k) * (width // GROUP) + chunk * part
    return pl.ds(pl.multiple_of(start, part), part)


def masks_of(length):
    rows, other = iota((length, length), 0), iota((length, length), 1)
    after = jnp.where(other > rows, 1.0, 0.0).astype(BF16)
    return after, jnp.where(other <= rows, 1.0, 0.0).astype(BF16)


def factors_of(ld, after, until):
    length = ld.shape[1]
    terms = three(ld)
    into_end = jnp.exp(summed(after, terms)).astype(BF16)
    from_start = jnp.exp(summed(until, terms)).astype(BF16)
    total = jnp.exp(summed(jnp.ones((TAIL, length), BF16), terms))
    high = total.astype(BF16).astype(F32)
    halves = jnp.where(iota(total.shape, 0) < TAIL // 2, high, total - high).astype(BF16)
    return into_end, from_start, halves


def put_states(head_dim, chunk, where, operands, outs, ready):
    into_end, from_start, halves, b, c, x, dy = operands
    x_scaled, dy_scaled, spread, *sends = outs
    group, state = len(sends), b.shape[1]
    width = x.shape[1]
    chunks = chunk_count(width)
    part = width // (group * chunks)
    difference = row_less_head(head_dim, part)
    sides = [(into_end, b, x, x_scaled, 0), (from_start, c, dy, dy_scaled, state)]
    for side, (factors, proj, cols, scaled, first) in enumerate(sides):
        ready(side)
        turned = proj[...].T
        for k in range(group):
            here = slice(k * part, (k + 1) * part)
            lanes = chunk_lanes(where, k, chunk, part, width)
            first_head = ((place_of(where) ^ k) * chunks + chunk) * (part // head_dim)
            hot = head_of_lane(difference, first_head)
            wide = dot(factors, hot, NN).astype(BF16)
            if side == 0:
                spread[:, here] = wide
                sends[k][2 * state :, :] = dot(halves, hot, NN).astype(BF16)
            piece = cols[:, lanes] * wide
            scaled[:, here] = piece
            sends[k][first : first + state, :] = dot(turned, piece, NN).astype(BF16)


def first_states_kernel(head_dim, group, where, ld_in, b_in, c_in, x_in, dy_in, *refs):
    ld, b, c, x, dy, into_end, from_start, halves = refs[:8]
    outs, sems = refs[8:-1], refs[-1]
    pairs = [(ld_in, ld), (b_in, b), (x_in, x), (c_in, c), (dy_in, dy)]
    copies = [pltpu.make_async_copy(i, o, sems.at[n]) for n, (i, o) in enumerate(pairs)]
    for copy in copies:
        copy.start()
    masks = masks_of(ld.shape[1])
    copies[0].wait()
    factors = factors_of(ld[...], *masks)
    for ref, value in zip((into_end, from_start, halves), factors):
        ref[...] = value

    def ready(side):
        copies[1 + 2 * side].wait()
        copies[2 + 2 * side].wait()

    put_states(head_dim, 0, where, (*factors, b, c, x, dy), outs, ready)


def next_states_kernel(head_dim, chunk, where, into_end, from_start, halves, *refs):
    operands = (into_end[...], from_start[...], halves[...], *refs[:4])
    put_states(head_dim, chunk, where, operands, refs[4:], lambda side: None)


def states_shapes(group, length, width, state):
    part = width // (group * chunk_count(width))
    scaled = pltpu.VMEM((length, group * part), BF16)
    return [scaled] * 3 + [pltpu.VMEM((2 * state + TAIL, part), BF16)] * group


def first_states(head_dim, group, where, inputs):
    ld, b, c, x, dy = inputs
    (length, width), state = x.shape, b.shape[1]
    kept = [pltpu.VMEM(a.shape, a.dtype) for a in inputs]
    kept += [pltpu.VMEM((rows, LANES), BF16) for rows in (length, length, TAIL)]
    outs = kept + states_shapes(group, length, width, state)
    return pl.pallas_call(
        functools.partial(first_states_kernel, head_dim, group),
        out_shape=outs,
        in_specs=[SMEM] + [HBM] * 5,
        out_specs=whole(len(outs)),
        scratch_shapes=[pltpu.SemaphoreType.DMA((5,))],
        compiler_params=params(8),
        cost_estimate=cost(2 * length * width * (state + LANES), 8 * length * width),
        name="first_states",
    )(where, *in_hbm(*inputs))


def next_states(head_dim, group, chunk, where, factors, b, c, x, dy):
    (length, width), state = x.shape, b.shape[1]
    outs = states_shapes(group, length, width, state)
    return pl.pallas_call(
        functools.partial(next_states_kernel, head_dim, chunk),
        out_shape=outs,
        in_specs=[SMEM] + whole(7),
        out_specs=whole(len(outs)),
        compiler_params=params(8),
        cost_estimate=cost(2 * length * width * (state + LANES), 4 * length * width),
        name="next_states",
    )(where, *factors, b, c, x, dy)


def decay_of(tail):
    tail = tail.astype(F32)
    return tail[:1, :] + tail[TAIL // 2 : TAIL // 2 + 1, :]


def put_decay(ref, first, factor):
    high = factor.astype(BF16).astype(F32)
    shape = (TAIL, factor.shape[1])
    both = jnp.where(iota(shape, 0) < TAIL // 2, high, factor - high)
    ref[first:, :] = both.astype(BF16)


def sent_order(parts):
    return [parts[0], *parts[:0:-1]]


def in_order(group, forward):
    return list(range(group)) if forward else list(range(group - 1, -1, -1))


def side_rows(state, forward):
    return slice(0, state) if forward else slice(state, 2 * state)


def totals_kernel(state, split, where, *refs):
    group = GROUP
    blocks, sums = sent_order(refs[:group]), refs[-1]
    for here in range(group):

        @pl.when(place_of(where) == here)
        def _(here=here):
            decays = [decay_of(blocks[q ^ here][2 * state :, :]) for q in range(group)]
            for forward in (True, False):
                rows, value = side_rows(state, forward), None
                for q in in_order(group, forward):
                    piece = blocks[q ^ here][rows, :].astype(F32)
                    value = piece if value is None else decays[q] * value + piece
                sums[rows, :] = value.astype(BF16)

    factor = decay_of(blocks[0][2 * state :, :])
    for block in blocks[1:]:
        factor = factor * decay_of(block[2 * state :, :])
    if not split:
        put_decay(sums, 2 * state, factor)
        return
    sent, kept = refs[-3:-1]
    for out in (sent, kept):
        put_decay(out, state, factor)
    for odd in (False, True):

        @pl.when(bit_of(where, 0) == odd)
        def _(odd=odd):
            sent[:state, :] = sums[side_rows(state, not odd), :]
            kept[:state, :] = sums[side_rows(state, odd), :]


def totals(state, split, where, blocks, after):
    part = blocks[0].shape[1]
    if split:
        outs = [jax.ShapeDtypeStruct((state + TAIL, part), BF16)] * 2
    else:
        outs = [jax.ShapeDtypeStruct(blocks[0].shape, BF16)]
    return pl.pallas_call(
        functools.partial(totals_kernel, state, split),
        out_shape=outs,
        in_specs=[SMEM] + whole(len(blocks)) + [ANY] * len(after),
        out_specs=whole(len(outs)),
        scratch_shapes=[pltpu.VMEM((2 * state, part), BF16)] if split else [],
        compiler_params=params(4),
        cost_estimate=cost(8 * blocks[0].size, 10 * blocks[0].size),
        name="totals",
    )(where, *sent_order(blocks), *after)


def joined_kernel(state, kept, received, out):
    d = decay_of(kept[state:, :])
    value = kept[:state, :].astype(F32) + d * received[:state, :].astype(F32)
    out[...] = value.astype(BF16)


def joined(state, kept, received):
    return pl.pallas_call(
        functools.partial(joined_kernel, state),
        out_shape=jax.ShapeDtypeStruct((state, kept.shape[1]), BF16),
        in_specs=whole(2),
        out_specs=whole(1)[0],
        compiler_params=params(4),
        cost_estimate=cost(2 * kept.size, 4 * kept.size),
        name="joined",
    )(kept, received)


def merged_kernel(state, level, last, where, own, received, *refs):
    out = refs[-1]
    d_own, d_other = decay_of(own[2 * state :, :]), decay_of(received[2 * state :, :])
    upper = bit_of(where, level)
    later = bit_of(where, level + 1)
    for is_upper in (False, True):
        for forward in (True, False):
            chosen = upper == is_upper
            if last:
                chosen = chosen & (later != forward)

            @pl.when(chosen)
            def _(is_upper=is_upper, forward=forward):
                rows = side_rows(state, forward)
                mine, other = own[rows, :].astype(F32), received[rows, :].astype(F32)
                value = mine + d_own * other if is_upper == forward else other + d_other * mine
                out[slice(0, state) if last else rows, :] = value.astype(BF16)

    put_decay(out, state if last else 2 * state, d_own * d_other)


def merged(state, level, last, where, own, received, after):
    rows = (state if last else 2 * state) + TAIL
    return pl.pallas_call(
        functools.partial(merged_kernel, state, level, last),
        out_shape=pltpu.VMEM((rows, own.shape[1]), BF16),
        in_specs=[SMEM] + whole(2) + [ANY] * len(after),
        out_specs=whole(1)[0],
        compiler_params=params(4),
        cost_estimate=cost(4 * own.size, 6 * own.size),
        name="merged",
    )(where, own, received, *after)


def put_four(state, where, received, entry):
    near, middle, outer = received
    d = decay_of(near[state:, :])
    is_middle = bit_of(where, 0) != bit_of(where, 1)
    for forward in (True, False):
        gets = bit_of(where, 0) == forward
        from_near = jnp.where(gets, 1.0, 0.0)
        from_far = jnp.where(bit_of(where, 1) == forward, 1.0, 0.0)
        of_middle = jnp.where(is_middle, from_far, 0.0)
        far = middle[...].astype(F32) * of_middle
        far = far + outer[...].astype(F32) * (from_far - of_middle)
        factor = jnp.where(gets, d, 1.0)
        value = near[:state, :].astype(F32) * from_near + factor * far
        entry[side_rows(state, forward), :] = value


def put_rounds(state, where, received, entry):
    for forward in (True, False):
        value, factor = None, 1.0
        for level, r in enumerate(received):
            gets = bit_of(where, level) == forward
            both = r.shape[0] > 2 * state
            rows = side_rows(state, forward) if both else slice(0, state)
            piece = r[rows, :].astype(F32) * jnp.where(gets, 1.0, 0.0)
            value = piece if value is None else value + factor * piece
            if both:
                factor = factor * jnp.where(gets, decay_of(r[2 * state :, :]), 1.0)
        entry[side_rows(state, forward), :] = value


def members_kernel(state, four, n_received, where, *refs):
    received, refs = refs[:n_received], refs[n_received:]
    group = GROUP
    blocks, outs, entry = refs[:group], refs[-1 - group : -1], refs[-1]
    if four:
        put_four(state, where, received, entry)
    else:
        put_rounds(state, where, received, entry)
    for here in range(group):

        @pl.when(place_of(where) == here)
        def _(here=here):
            decays = [decay_of(blocks[q ^ here][2 * state :, :]) for q in range(group)]
            for forward in (True, False):
                rows, order = side_rows(state, forward), in_order(group, forward)
                value = entry[rows, :]
                for q in order:
                    outs[q ^ here][rows, :] = value.astype(BF16)
                    if q != order[-1]:
                        value = decays[q] * value + blocks[q ^ here][rows, :].astype(F32)


def member_entries(state, four, where, blocks, received, after):
    group, part = len(blocks), blocks[0].shape[1]
    return pl.pallas_call(
        functools.partial(members_kernel, state, four, len(received)),
        out_shape=[jax.ShapeDtypeStruct((2 * state, part), BF16)] * group,
        in_specs=[SMEM] + whole(group + len(received)) + [ANY] * len(after),
        out_specs=whole(group),
        scratch_shapes=[pltpu.VMEM((2 * state, part), F32)],
        compiler_params=params(4),
        cost_estimate=cost(12 * blocks[0].size, 16 * blocks[0].size),
        name="member_entries",
    )(where, *received, *blocks, *after)


def exchange(parts):
    count = lax.axis_size("seq")
    out = list(parts)
    for k in range(len(parts) - 1, 0, -1):
        out[k] = lax.ppermute(parts[k], "seq", [(s, s ^ k) for s in range(count)])
    return out


def split_pairs(first, count):
    if count == 1:
        return []
    middle = first + count // 2
    return (
        [(first, middle, first + count)]
        + split_pairs(first, middle - first)
        + split_pairs(middle, first + count - middle)
    )


def grouped_cuts(pieces):
    groups = {}
    for cut in split_pairs(0, pieces):
        groups.setdefault((cut[1] - cut[0], cut[2] - cut[1]), []).append(cut)
    return list(groups.items())


def rows_of(first, end, piece):
    return slice(first * piece, end * piece)


def setup_kernel(piece, ld, b, c, *refs):
    near, cum_terms = refs[-2:]
    heads, length = ld.shape
    rows, other = iota((length, length), 0), iota((length, length), 1)
    mask = jnp.where(other <= rows, 1.0, 0.0).astype(BF16)
    cum = summed(mask, three(ld[...] * LOG2E))
    lane = iota(cum.shape, 1)
    in_slots = jnp.where(lane < SLOT, cum, 0.0)
    in_slots = in_slots + pltpu.roll(in_slots, SLOT, 1) + pltpu.roll(in_slots, 2 * SLOT, 1)
    high, mid, low = three(in_slots)
    cum_terms[...] = jnp.where(lane < SLOT, high, jnp.where(lane < 2 * SLOT, mid, low))
    keep = iota((piece, piece), 0) <= iota((piece, piece), 1)
    pieces = length // piece
    for n in range(pieces):
        here = rows_of(n, n + 1, piece)
        near[here, :] = jnp.where(keep, dot(b[here, :], c[here, :], NT), 0.0).astype(BF16)
    cuts = [cut for _, same in grouped_cuts(pieces) for cut in same]
    for (lo, mid_, hi), far in zip(cuts, refs):
        left, right = rows_of(lo, mid_, piece), rows_of(mid_, hi, piece)
        far[...] = dot(b[left, :], c[right, :], NT).astype(BF16)


def inner_setup(piece, ld, b, c, after):
    length = b.shape[0]
    cuts = [cut for _, same in grouped_cuts(length // piece) for cut in same]
    outs = [
        jax.ShapeDtypeStruct(((mid - lo) * piece, (hi - mid) * piece), BF16) for lo, mid, hi in cuts
    ]
    outs.append(jax.ShapeDtypeStruct((length, piece), BF16))
    outs.append(jax.ShapeDtypeStruct((length, LANES), BF16))
    return pl.pallas_call(
        functools.partial(setup_kernel_after, piece, len(after)),
        out_shape=outs,
        in_specs=whole(3) + [ANY] * len(after),
        out_specs=whole(len(outs)),
        compiler_params=params(4),
        cost_estimate=cost(8 * b.size * length, 8 * b.size),
        name="inner_setup",
    )(ld, b, c, *after)


def setup_kernel_after(piece, n_after, ld, b, c, *refs):
    setup_kernel(piece, ld, b, c, *refs[n_after:])


def inner_kernel(head_dim, chunk, n_before, n_after, b, c, x, dy, *refs):
    length, width = x.shape
    piece = head_dim
    pieces = length // piece
    groups = grouped_cuts(pieces)
    n_cuts = sum(len(same) for _, same in groups)
    fars, (near, cum_terms), refs = refs[:n_cuts], refs[n_cuts : n_cuts + 2], refs[n_cuts + 2 :]
    before, refs = refs[:n_before], refs[n_before + n_after :]
    dx_out, db_out, dc_out, x_near, dy_near, *scratch = refs
    lefts, rights = scratch[: len(groups)], scratch[len(groups) :]
    part = dx_out.shape[1] // GROUP
    difference = row_less_head(head_dim, part, SLOT)

    for m in range(GROUP):
        owned = m * (width // GROUP) + chunk * part
        lanes, here = slice(owned, owned + part), slice(m * part, (m + 1) * part)
        cum = dot(cum_terms[...], head_of_lane(difference, owned // head_dim), NN)
        dx = []
        for n in range(pieces):
            rows = rows_of(n, n + 1, piece)
            middle = cum[n * piece + piece // 2 : n * piece + piece // 2 + 1, :]
            gap = middle - cum[rows, :]
            down, up = jnp.exp2(gap), jnp.exp2(-gap)
            x_near[rows, here] = (x[rows, lanes].astype(F32) * down).astype(BF16)
            dy_piece = (dy[rows, lanes].astype(F32) * up).astype(BF16)
            dy_near[rows, here] = dy_piece
            dx.append(down * dot(near[rows, :], dy_piece, NN))
        far_of = iter(fars)
        for (_, same), left_ref, right_ref in zip(groups, lefts, rights):
            for g, (lo, mid, hi) in enumerate(same):
                left, right = rows_of(lo, mid, piece), rows_of(mid, hi, piece)
                edge = cum[mid * piece - 1 : mid * piece, :]
                to_edge = jnp.exp2(edge - cum[left, :])
                from_edge = jnp.exp2(cum[right, :] - edge)
                x_left = (x[left, lanes].astype(F32) * to_edge).astype(BF16)
                dy_right = (dy[right, lanes].astype(F32) * from_edge).astype(BF16)
                left_ref[rows_of(g, g + 1, (mid - lo) * piece), here] = x_left
                right_ref[rows_of(g, g + 1, (hi - mid) * piece), here] = dy_right
                far = to_edge * dot(next(far_of)[...], dy_right, NN)
                for n in range(lo, mid):
                    dx[n] = dx[n] + far[rows_of(n - lo, n - lo + 1, piece), :]
        for n in range(pieces):
            dx_out[rows_of(n, n + 1, piece), here] = dx[n].astype(BF16)

    if before:
        db_out[...] = before[0][...]
        dc_out[...] = before[1][...]
    else:
        db_out[...] = jnp.zeros_like(db_out)
        dc_out[...] = jnp.zeros_like(dc_out)
    batch = 4
    for first in range(0, pieces, batch):
        rows = rows_of(first, min(first + batch, pieces), piece)
        total = dot(x_near[rows, :], dy_near[rows, :], NT)
        row, col = iota(total.shape, 0), iota(total.shape, 1)
        keep = (split_of(row, piece) == split_of(col, piece)) & (row <= col)
        weighted = jnp.where(keep, total, 0.0).astype(BF16)
        db_out[rows, :] += dot(weighted, c[rows, :], NN)
        dc_out[rows, :] += dot(weighted, b[rows, :], TN)
    for ((n_left, n_right), same), left_ref, right_ref in zip(groups, lefts, rights):
        total = dot(left_ref[...], right_ref[...], NT)
        if len(same) > 1:
            row, col = iota(total.shape, 0), iota(total.shape, 1)
            same_cut = split_of(row, n_left * piece) == split_of(col, n_right * piece)
            total = jnp.where(same_cut, total, 0.0)
        weighted = total.astype(BF16)
        b_left = jnp.concatenate([b[rows_of(lo, mid, piece), :] for lo, mid, _ in same], axis=0)
        c_right = jnp.concatenate([c[rows_of(mid, hi, piece), :] for _, mid, hi in same], axis=0)
        db = dot(weighted, c_right, NN)
        dc = dot(weighted, b_left, TN)
        for g, (lo, mid, hi) in enumerate(same):
            db_out[rows_of(lo, mid, piece), :] += db[rows_of(g, g + 1, n_left * piece), :]
            dc_out[rows_of(mid, hi, piece), :] += dc[rows_of(g, g + 1, n_right * piece), :]


def inner_terms(head_dim, chunk, setup, b, c, x, dy, before, after):
    length, state = b.shape
    columns = x.shape[1] // chunk_count(x.shape[1])
    groups = grouped_cuts(length // head_dim)
    sizes = [[len(same) * n * head_dim for n in halves] for halves, same in groups]
    return pl.pallas_call(
        functools.partial(inner_kernel, head_dim, chunk, len(before), len(after)),
        out_shape=[
            jax.ShapeDtypeStruct((length, columns), BF16),
            jax.ShapeDtypeStruct((length, state), F32),
            jax.ShapeDtypeStruct((length, state), F32),
        ],
        in_specs=whole(4 + len(setup) + len(before)) + [ANY] * len(after),
        out_specs=whole(3),
        scratch_shapes=[pltpu.VMEM((length, columns), BF16)] * 2
        + [pltpu.VMEM((left, columns), BF16) for left, _ in sizes]
        + [pltpu.VMEM((right, columns), BF16) for _, right in sizes],
        compiler_params=params(16),
        cost_estimate=cost(8 * x.size * state, 4 * x.size, 2 * x.size),
        name="inner_terms",
    )(b, c, x, dy, *setup, *before, *after)


def parts_kernel(last, x_scaled, dy_scaled, db_before, dc_before, *refs):
    entries, outs = sent_order(refs[:GROUP]), refs[-1 if last else -2 :]
    length, state = db_before.shape
    part = entries[0].shape[1]
    db, dc = db_before[...], dc_before[...]
    for k, entry in enumerate(entries):
        here = slice(k * part, (k + 1) * part)
        db = db + dot(x_scaled[:, here], entry[state:, :], NT)
        dc = dc + dot(dy_scaled[:, here], entry[:state, :], NT)
    if last:
        outs[0][:length, :] = db.astype(BF16)
        outs[0][length:, :] = dc.astype(BF16)
    else:
        outs[0][...] = db
        outs[1][...] = dc


def entry_parts(last, x_scaled, dy_scaled, db_before, dc_before, entries, after):
    length, state = db_before.shape
    one = pltpu.VMEM((length, state), F32)
    outs = [pltpu.VMEM((2 * length, state), BF16)] if last else [one, one]
    return pl.pallas_call(
        functools.partial(parts_kernel, last),
        out_shape=outs,
        in_specs=whole(4 + len(entries)) + [ANY] * len(after),
        out_specs=whole(len(outs)),
        compiler_params=params(8),
        cost_estimate=cost(4 * x_scaled.size * state, 4 * x_scaled.size),
        name="entry_parts",
    )(x_scaled, dy_scaled, db_before, dc_before, *sent_order(entries), *after)


def put_values(where, spread, b, dx_local, entries, put):
    state, part = b.shape[1], entries[0].shape[1]
    for k, entry in enumerate(entries):
        here = slice(k * part, (k + 1) * part)
        local = dx_local[:, pl.ds(pl.multiple_of((place_of(where) ^ k) * part, part), part)]
        far = spread[:, here].astype(F32) * dot(b[...], entry[state:, :], NN)
        put(k, here, (local.astype(F32) + far).astype(BF16))


def values_kernel(where, spread, b, dx_local, *refs):
    entries, out = sent_order(refs[:GROUP]), refs[-1]

    def put(k, here, value):
        out[:, here] = value

    put_values(where, spread, b, dx_local, entries, put)


def last_values_kernel(chunks, where, spread, b, dx_local, *refs):
    entries, before = sent_order(refs[:GROUP]), refs[GROUP : GROUP + chunks - 1]
    out, dx, sems = refs[-3:]
    part = entries[0].shape[1]
    stores = []

    def store(chunk, k, source):
        lanes = chunk_lanes(where, k, chunk, part, out.shape[1])
        at = sems.at[chunk * GROUP + k]
        stores.append(pltpu.make_async_copy(source, out.at[:, lanes], at))
        stores[-1].start()

    for chunk, values in enumerate(before):
        for k in range(GROUP):
            store(chunk, k, values.at[:, pl.ds(k * part, part)])

    def put(k, here, value):
        dx[k] = value
        store(chunks - 1, k, dx.at[k])

    put_values(where, spread, b, dx_local, entries, put)
    for one in stores:
        one.wait()


def entry_values(chunk, chunks, where, spread, b, dx_local, entries, before):
    length, part = b.shape[0], entries[0].shape[1]
    last = chunk == chunks - 1
    estimate = cost(2 * dx_local.size * b.shape[1], 4 * dx_local.size)
    operands = [where, spread, b, dx_local, *sent_order(entries)]
    if not last:
        return pl.pallas_call(
            values_kernel,
            out_shape=jax.ShapeDtypeStruct((length, GROUP * part), BF16),
            in_specs=[SMEM] + whole(3 + GROUP),
            out_specs=whole(1)[0],
            compiler_params=params(8),
            cost_estimate=estimate,
            name="entry_values",
        )(*operands)
    return pl.pallas_call(
        functools.partial(last_values_kernel, chunks),
        out_shape=pltpu.HBM((length, chunks * GROUP * part), BF16),
        in_specs=[SMEM] + whole(3 + GROUP + len(before)),
        out_specs=HBM,
        scratch_shapes=[
            pltpu.VMEM((GROUP, length, part), BF16),
            pltpu.SemaphoreType.DMA((chunks * GROUP,)),
        ],
        compiler_params=params(8),
        cost_estimate=estimate,
        name="last_values",
    )(*operands, *before)


def over_heads(part):
    count = lax.axis_size("head")
    total = part.astype(F32)
    for shift in range(1, count):
        pairs = [(s, (s + shift) % count) for s in range(count)]
        total = total + lax.ppermute(part, "head", pairs).astype(F32)
    return total.astype(BF16)


def shards(token_values, b_inputs, c_inputs, log_decay, grad_out):
    head_dim = token_values.shape[1] // log_decay.shape[0]
    length, state = b_inputs.shape
    count, group = lax.axis_size("seq"), GROUP
    chunks = chunk_count(token_values.shape[1])
    levels = (count // group).bit_length() - 1
    where = lax.axis_index("seq").astype(jnp.int32)[None]
    inputs = (log_decay, b_inputs, c_inputs, token_values, grad_out)
    ld, b, c, x, dy, *rest = first_states(head_dim, group, where, inputs)
    factors, states = rest[:3], [rest[3:]]
    blocks = [exchange(states[0][3:])]
    for chunk in range(1, chunks):
        states.append(next_states(head_dim, group, chunk, where, factors, b, c, x, dy))
        blocks.append(exchange(states[chunk][3:]))
    setup = inner_setup(head_dim, ld, b, c, [states[-1][3]])

    def to_group(block, k):
        return lax.ppermute(block, "seq", [(s, s ^ (k * group)) for s in range(count)])

    groups = count // group
    four = groups == 4
    received, after = [], setup[-1:]
    for chunk in range(chunks):
        sent, *kept = totals(state, four, where, blocks[chunk], after)
        received.append([to_group(sent, 1)])
        if four:
            sent = joined(state, kept[0], received[chunk][0])
            for other in ([(1, 2), (2, 1)], [(1, 3), (2, 0)]):
                pairs = [(m * group + j, n * group + j) for m, n in other for j in range(group)]
                received[chunk].append(lax.ppermute(sent, "seq", pairs))
        else:
            for level in range(levels - 1):
                last = level == levels - 2
                sent = merged(state, level, last, where, sent, received[chunk][level], [])
                received[chunk].append(to_group(sent, 2 << level))
        after = [sent]
    entries, inner, sums = [], [], []
    for chunk in range(chunks):
        found = member_entries(state, four, where, blocks[chunk], received[chunk], sums[:1])
        entries.append(exchange(found))
        inner.append(inner_terms(head_dim, chunk, setup, b, c, x, dy, sums, found[:1]))
        sums = list(inner[chunk][1:])

    values = []
    for chunk in range(chunks):
        x_scaled, dy_scaled, spread = states[chunk][:3]
        last = chunk == chunks - 1
        sums = entry_parts(last, x_scaled, dy_scaled, *sums, entries[chunk], values)
        values.append(
            entry_values(
                chunk, chunks, where, spread, b, inner[chunk][0], entries[chunk], values
            )
        )
    both = over_heads(sums[0])
    return values[-1], both[:length], both[length:]


def solution(mesh):
    in_specs = (
        P("seq", "head"),
        P("seq", None),
        P("seq", None),
        P("head", "seq"),
        P("seq", "head"),
    )
    out_specs = (P("seq", "head"), P("seq", None), P("seq", None))
    return jax.shard_map(shards, mesh=mesh, in_specs=in_specs, out_specs=out_specs, check_vma=False)
```

```python
import functools

import jax
import jax.numpy as jnp
from jax import lax
from jax.experimental import pallas as pl
from jax.experimental.pallas import tpu as pltpu
from jax.sharding import PartitionSpec as P

BF16 = jnp.bfloat16
F32 = jnp.float32
LANES = 128
GROUP = 4
TAIL = 16
LOG2E = 1.4426950408889634
MIB = 1024 * 1024

NN = (((1,), (0,)), ((), ()))
NT = (((1,), (1,)), ((), ()))
TN = (((0,), (0,)), ((), ()))


def dot(a, b, dims):
    return lax.dot_general(a, b, dims, preferred_element_type=F32)


def iota(shape, dim):
    return lax.broadcasted_iota(jnp.int32, shape, dim)


def three(values):
    high = values.astype(BF16)
    rest = values - high.astype(F32)
    mid = rest.astype(BF16)
    return high, mid, (rest - mid.astype(F32)).astype(BF16)


SLOT = LANES // 4


def summed(mask, terms):
    heads, length = terms[0].shape
    gap = [] if heads == SLOT else [jnp.zeros((SLOT - heads, length), BF16)]
    rows = [r for t in terms for r in [t] + gap] + [jnp.zeros((SLOT, length), BF16)]
    each = dot(mask, jnp.concatenate(rows, axis=0), NT)
    return each + pltpu.roll(each, LANES - SLOT, 1) + pltpu.roll(each, LANES - 2 * SLOT, 1)


def split_of(index, size):
    shift = size.bit_length() - 1
    return lax.shift_right_logical(index, shift) if size == 1 << shift else index // size


def row_less_head(head_dim, width, rows=LANES):
    shape = (LANES, width)
    row = iota(shape, 0)
    if rows < LANES:
        row = row & (rows - 1)
    return row - split_of(iota(shape, 1), head_dim)


def head_of_lane(difference, first):
    return jnp.where(difference == first, 1.0, 0.0).astype(BF16)


def whole(count):
    return [pl.BlockSpec(memory_space=pltpu.VMEM)] * count


def in_hbm(*arrays):
    return [pltpu.with_memory_space_constraint(a, pltpu.HBM) for a in arrays]


SMEM = pl.BlockSpec(memory_space=pltpu.SMEM)
HBM = pl.BlockSpec(memory_space=pltpu.HBM)
ANY = pl.BlockSpec(memory_space=pl.ANY)


def params(mib):
    return pltpu.CompilerParams(vmem_limit_bytes=mib * MIB)


def cost(flops, size, transcendentals=0):
    return pl.CostEstimate(flops=flops, bytes_accessed=size, transcendentals=transcendentals)


def place_of(where):
    return where[0] & (GROUP - 1)


def bit_of(where, level):
    return (where[0] >> (level + GROUP.bit_length() - 1)) & 1 == 1


def chunk_count(width):
    return 2 if (width // GROUP) % (2 * LANES) == 0 else 1


def chunk_lanes(where, k, chunk, part, width):
    start = (place_of(where) ^ k) * (width // GROUP) + chunk * part
    return pl.ds(pl.multiple_of(start, part), part)


def masks_of(length):
    rows, other = iota((length, length), 0), iota((length, length), 1)
    after = jnp.where(other > rows, 1.0, 0.0).astype(BF16)
    return after, jnp.where(other <= rows, 1.0, 0.0).astype(BF16)


def factors_of(ld, after, until):
    length = ld.shape[1]
    terms = three(ld)
    into_end = jnp.exp(summed(after, terms)).astype(BF16)
    from_start = jnp.exp(summed(until, terms)).astype(BF16)
    total = jnp.exp(summed(jnp.ones((TAIL, length), BF16), terms))
    high = total.astype(BF16).astype(F32)
    halves = jnp.where(iota(total.shape, 0) < TAIL // 2, high, total - high).astype(BF16)
    return into_end, from_start, halves


def put_states(head_dim, pieces, where, operands, outs, ready):
    into_end, from_start, halves, b, c, x, dy = operands
    state, width = b.shape[1], x.shape[1]
    chunks = chunk_count(width)
    part = width // (GROUP * chunks)
    difference = row_less_head(head_dim, part)
    for side, (factors, proj, cols) in enumerate([(into_end, b, x), (from_start, c, dy)]):
        ready(side)
        turned = proj[...].T
        for n, (chunk, k) in enumerate(pieces):
            x_scaled, dy_scaled, spread, send = outs[4 * n : 4 * n + 4]
            lanes = chunk_lanes(where, k, chunk, part, width)
            first_head = ((place_of(where) ^ k) * chunks + chunk) * (part // head_dim)
            hot = head_of_lane(difference, first_head)
            wide = dot(factors, hot, NN).astype(BF16)
            if side == 0:
                spread[...] = wide
                send[2 * state :, :] = dot(halves, hot, NN).astype(BF16)
            piece = cols[:, lanes] * wide
            (dy_scaled if side else x_scaled)[...] = piece
            send[side * state : (side + 1) * state, :] = dot(turned, piece, NN).astype(BF16)


def first_states_kernel(head_dim, pieces, where, ld_in, b_in, c_in, x_in, dy_in, *refs):
    ld, b, c, x, dy, into_end, from_start, halves = refs[:8]
    outs, sems = refs[8:-1], refs[-1]
    pairs = [(ld_in, ld), (b_in, b), (x_in, x), (c_in, c), (dy_in, dy)]
    copies = [pltpu.make_async_copy(i, o, sems.at[n]) for n, (i, o) in enumerate(pairs)]
    for copy in copies:
        copy.start()
    masks = masks_of(ld.shape[1])
    copies[0].wait()
    factors = factors_of(ld[...], *masks)
    for ref, value in zip((into_end, from_start, halves), factors):
        ref[...] = value

    def ready(side):
        copies[1 + 2 * side].wait()
        copies[2 + 2 * side].wait()

    put_states(head_dim, pieces, where, (*factors, b, c, x, dy), outs, ready)


def next_states_kernel(head_dim, pieces, where, into_end, from_start, halves, *refs):
    operands = (into_end[...], from_start[...], halves[...], *refs[:4])
    outs = refs[-4 * len(pieces) :]
    put_states(head_dim, pieces, where, operands, outs, lambda side: None)


def states_shapes(n_parts, length, width, state):
    part = width // (GROUP * chunk_count(width))
    scaled = jax.ShapeDtypeStruct((length, part), BF16)
    send = jax.ShapeDtypeStruct((2 * state + TAIL, part), BF16)
    return [scaled, scaled, scaled, send] * n_parts


def by_piece(pieces, outs):
    return {piece: outs[4 * n : 4 * n + 4] for n, piece in enumerate(pieces)}


def first_states(head_dim, pieces, where, inputs):
    ld, b, c, x, dy = inputs
    (length, width), state = x.shape, b.shape[1]
    kept = [jax.ShapeDtypeStruct(a.shape, a.dtype) for a in inputs]
    kept += [jax.ShapeDtypeStruct((rows, LANES), BF16) for rows in (length, length, TAIL)]
    outs = kept + states_shapes(len(pieces), length, width, state)
    found = pl.pallas_call(
        functools.partial(first_states_kernel, head_dim, pieces),
        out_shape=outs,
        in_specs=[SMEM] + [HBM] * 5,
        out_specs=whole(len(outs)),
        scratch_shapes=[pltpu.SemaphoreType.DMA((5,))],
        compiler_params=params(8),
        cost_estimate=cost(2 * length * width * (state + LANES), 8 * length * width),
        name="first_states",
    )(where, *in_hbm(*inputs))
    return found[:8], by_piece(pieces, found[8:])


def next_states(head_dim, pieces, where, factors, b, c, x, dy):
    (length, width), state = x.shape, b.shape[1]
    outs = states_shapes(len(pieces), length, width, state)
    found = pl.pallas_call(
        functools.partial(next_states_kernel, head_dim, pieces),
        out_shape=outs,
        in_specs=[SMEM] + whole(7),
        out_specs=whole(len(outs)),
        compiler_params=params(8),
        cost_estimate=cost(2 * length * width * (state + LANES), 4 * length * width),
        name="next_states",
    )(where, *factors, b, c, x, dy)
    return by_piece(pieces, found)


def decay_of(tail):
    tail = tail.astype(F32)
    return tail[:1, :] + tail[TAIL // 2 : TAIL // 2 + 1, :]


def put_decay(ref, first, factor):
    high = factor.astype(BF16).astype(F32)
    shape = (TAIL, factor.shape[1])
    both = jnp.where(iota(shape, 0) < TAIL // 2, high, factor - high)
    ref[first:, :] = both.astype(BF16)


def sent_order(parts, fixed=1):
    return [*parts[:fixed], *parts[: fixed - 1 : -1]]


def in_order(group, forward):
    return list(range(group)) if forward else list(range(group - 1, -1, -1))


def side_rows(state, forward):
    return slice(0, state) if forward else slice(state, 2 * state)


def totals_kernel(state, levels, where, *refs):
    group = GROUP
    blocks, outs, sums = sent_order(refs[:group]), refs[-1 - levels : -1], refs[-1]
    for here in range(group):

        @pl.when(place_of(where) == here)
        def _(here=here):
            decays = [decay_of(blocks[q ^ here][2 * state :, :]) for q in range(group)]
            for forward in (True, False):
                rows, value = side_rows(state, forward), None
                for q in in_order(group, forward):
                    piece = blocks[q ^ here][rows, :].astype(F32)
                    value = piece if value is None else decays[q] * value + piece
                sums[rows, :] = value.astype(BF16)

    factor = decay_of(blocks[0][2 * state :, :])
    for block in blocks[1:]:
        factor = factor * decay_of(block[2 * state :, :])
    if not levels:
        put_decay(sums, 2 * state, factor)
    for level, out in enumerate(outs):
        put_decay(out, state, factor)
        for forward in (True, False):

            @pl.when(bit_of(where, level) != forward)
            def _(out=out, forward=forward):
                out[:state, :] = sums[side_rows(state, forward), :]


def totals(state, levels, where, blocks, after):
    part = blocks[0].shape[1]
    outs = [jax.ShapeDtypeStruct((state + TAIL, part), BF16)] * levels
    if not levels:
        outs = [jax.ShapeDtypeStruct(blocks[0].shape, BF16)]
    return pl.pallas_call(
        functools.partial(totals_kernel, state, levels),
        out_shape=outs,
        in_specs=[SMEM] + whole(len(blocks)) + [ANY] * len(after),
        out_specs=whole(len(outs)),
        scratch_shapes=[pltpu.VMEM((2 * state, part), BF16)] if levels else [],
        compiler_params=params(4),
        cost_estimate=cost(8 * blocks[0].size, 10 * blocks[0].size),
        name="totals",
    )(where, *sent_order(blocks), *after)


def merged_kernel(state, level, last, where, own, received, *refs):
    out = refs[-1]
    d_own, d_other = decay_of(own[2 * state :, :]), decay_of(received[2 * state :, :])
    upper = bit_of(where, level)
    later = bit_of(where, level + 1)
    for is_upper in (False, True):
        for forward in (True, False):
            chosen = upper == is_upper
            if last:
                chosen = chosen & (later != forward)

            @pl.when(chosen)
            def _(is_upper=is_upper, forward=forward):
                rows = side_rows(state, forward)
                mine, other = own[rows, :].astype(F32), received[rows, :].astype(F32)
                value = mine + d_own * other if is_upper == forward else other + d_other * mine
                out[slice(0, state) if last else rows, :] = value.astype(BF16)

    put_decay(out, state if last else 2 * state, d_own * d_other)


def merged(state, level, last, where, own, received, after):
    rows = (state if last else 2 * state) + TAIL
    return pl.pallas_call(
        functools.partial(merged_kernel, state, level, last),
        out_shape=pltpu.VMEM((rows, own.shape[1]), BF16),
        in_specs=[SMEM] + whole(2) + [ANY] * len(after),
        out_specs=whole(1)[0],
        compiler_params=params(4),
        cost_estimate=cost(4 * own.size, 6 * own.size),
        name="merged",
    )(where, own, received, *after)


def put_direct(state, groups, number, received, entry):
    for mine in range(groups):

        @pl.when(number == mine)
        def _(mine=mine):
            for forward in (True, False):
                rows = side_rows(state, forward)
                others = range(mine - 1, -1, -1) if forward else range(mine + 1, groups)
                value, factor = jnp.zeros((state, entry.shape[1]), F32), None
                for other in others:
                    r = received[(mine ^ other) - 1]
                    piece = r[:state, :].astype(F32)
                    value = piece if factor is None else value + factor * piece
                    d = decay_of(r[state:, :])
                    factor = d if factor is None else factor * d
                entry[rows, :] = value


def put_rounds(state, where, received, entry):
    for forward in (True, False):
        value, factor = None, 1.0
        for level, r in enumerate(received):
            gets = bit_of(where, level) == forward
            both = r.shape[0] > 2 * state
            rows = side_rows(state, forward) if both else slice(0, state)
            piece = r[rows, :].astype(F32) * jnp.where(gets, 1.0, 0.0)
            value = piece if value is None else value + factor * piece
            if both:
                factor = factor * jnp.where(gets, decay_of(r[2 * state :, :]), 1.0)
        entry[side_rows(state, forward), :] = value


def members_kernel(state, direct, n_received, where, *refs):
    received, refs = refs[:n_received], refs[n_received:]
    group = GROUP
    blocks, outs, entry = refs[:group], refs[-1 - group : -1], refs[-1]
    if direct:
        put_direct(state, n_received + 1, where[0] // group, received, entry)
    else:
        put_rounds(state, where, received, entry)
    for here in range(group):

        @pl.when(place_of(where) == here)
        def _(here=here):
            decays = [decay_of(blocks[q ^ here][2 * state :, :]) for q in range(group)]
            for forward in (True, False):
                rows, order = side_rows(state, forward), in_order(group, forward)
                value = entry[rows, :]
                for q in order:
                    outs[q ^ here][rows, :] = value.astype(BF16)
                    if q != order[-1]:
                        value = decays[q] * value + blocks[q ^ here][rows, :].astype(F32)


def member_entries(state, direct, where, blocks, received, after):
    group, part = len(blocks), blocks[0].shape[1]
    return pl.pallas_call(
        functools.partial(members_kernel, state, direct, len(received)),
        out_shape=[jax.ShapeDtypeStruct((2 * state, part), BF16)] * group,
        in_specs=[SMEM] + whole(group + len(received)) + [ANY] * len(after),
        out_specs=whole(group),
        scratch_shapes=[pltpu.VMEM((2 * state, part), F32)],
        compiler_params=params(4),
        cost_estimate=cost(12 * blocks[0].size, 16 * blocks[0].size),
        name="member_entries",
    )(where, *received, *blocks, *after)


def exchange(parts):
    count = lax.axis_size("seq")
    out = list(parts)
    for k in range(len(parts) - 1, 0, -1):
        out[k] = lax.ppermute(parts[k], "seq", [(s, s ^ k) for s in range(count)])
    return out


def split_pairs(first, count):
    if count == 1:
        return []
    middle = first + count // 2
    return (
        [(first, middle, first + count)]
        + split_pairs(first, middle - first)
        + split_pairs(middle, first + count - middle)
    )


def grouped_cuts(pieces):
    groups = {}
    for cut in split_pairs(0, pieces):
        groups.setdefault((cut[1] - cut[0], cut[2] - cut[1]), []).append(cut)
    return list(groups.items())


def rows_of(first, end, piece):
    return slice(first * piece, end * piece)


def setup_kernel(piece, ld, b, c, *refs):
    near, cum_terms = refs[-2:]
    heads, length = ld.shape
    rows, other = iota((length, length), 0), iota((length, length), 1)
    mask = jnp.where(other <= rows, 1.0, 0.0).astype(BF16)
    cum = summed(mask, three(ld[...] * LOG2E))
    lane = iota(cum.shape, 1)
    in_slots = jnp.where(lane < SLOT, cum, 0.0)
    in_slots = in_slots + pltpu.roll(in_slots, SLOT, 1) + pltpu.roll(in_slots, 2 * SLOT, 1)
    high, mid, low = three(in_slots)
    cum_terms[...] = jnp.where(lane < SLOT, high, jnp.where(lane < 2 * SLOT, mid, low))
    keep = iota((piece, piece), 0) <= iota((piece, piece), 1)
    pieces = length // piece
    for n in range(pieces):
        here = rows_of(n, n + 1, piece)
        near[here, :] = jnp.where(keep, dot(b[here, :], c[here, :], NT), 0.0).astype(BF16)
    cuts = [cut for _, same in grouped_cuts(pieces) for cut in same]
    for (lo, mid_, hi), far in zip(cuts, refs):
        left, right = rows_of(lo, mid_, piece), rows_of(mid_, hi, piece)
        far[...] = dot(b[left, :], c[right, :], NT).astype(BF16)


def inner_setup(piece, ld, b, c, after):
    length = b.shape[0]
    cuts = [cut for _, same in grouped_cuts(length // piece) for cut in same]
    outs = [
        jax.ShapeDtypeStruct(((mid - lo) * piece, (hi - mid) * piece), BF16) for lo, mid, hi in cuts
    ]
    outs.append(jax.ShapeDtypeStruct((length, piece), BF16))
    outs.append(jax.ShapeDtypeStruct((length, LANES), BF16))
    return pl.pallas_call(
        functools.partial(setup_kernel_after, piece, len(after)),
        out_shape=outs,
        in_specs=whole(3) + [ANY] * len(after),
        out_specs=whole(len(outs)),
        compiler_params=params(4),
        cost_estimate=cost(8 * b.size * length, 8 * b.size),
        name="inner_setup",
    )(ld, b, c, *after)


def setup_kernel_after(piece, n_after, ld, b, c, *refs):
    setup_kernel(piece, ld, b, c, *refs[n_after:])


def inner_kernel(head_dim, chunk, n_before, n_after, b, c, x, dy, *refs):
    length, width = x.shape
    piece = head_dim
    pieces = length // piece
    groups = grouped_cuts(pieces)
    n_cuts = sum(len(same) for _, same in groups)
    fars, (near, cum_terms), refs = refs[:n_cuts], refs[n_cuts : n_cuts + 2], refs[n_cuts + 2 :]
    before, refs = refs[:n_before], refs[n_before + n_after :]
    dx_out, db_out, dc_out, x_near, dy_near, *scratch = refs
    lefts, rights = scratch[: len(groups)], scratch[len(groups) :]
    part = dx_out.shape[1] // GROUP
    difference = row_less_head(head_dim, part, SLOT)

    for m in range(GROUP):
        owned = m * (width // GROUP) + chunk * part
        lanes, here = slice(owned, owned + part), slice(m * part, (m + 1) * part)
        cum = dot(cum_terms[...], head_of_lane(difference, owned // head_dim), NN)
        dx = []
        for n in range(pieces):
            rows = rows_of(n, n + 1, piece)
            middle = cum[n * piece + piece // 2 : n * piece + piece // 2 + 1, :]
            gap = middle - cum[rows, :]
            down, up = jnp.exp2(gap), jnp.exp2(-gap)
            x_near[rows, here] = (x[rows, lanes].astype(F32) * down).astype(BF16)
            dy_piece = (dy[rows, lanes].astype(F32) * up).astype(BF16)
            dy_near[rows, here] = dy_piece
            dx.append(down * dot(near[rows, :], dy_piece, NN))
        far_of = iter(fars)
        for (_, same), left_ref, right_ref in zip(groups, lefts, rights):
            for g, (lo, mid, hi) in enumerate(same):
                left, right = rows_of(lo, mid, piece), rows_of(mid, hi, piece)
                edge = cum[mid * piece - 1 : mid * piece, :]
                to_edge = jnp.exp2(edge - cum[left, :])
                from_edge = jnp.exp2(cum[right, :] - edge)
                x_left = (x[left, lanes].astype(F32) * to_edge).astype(BF16)
                dy_right = (dy[right, lanes].astype(F32) * from_edge).astype(BF16)
                left_ref[rows_of(g, g + 1, (mid - lo) * piece), here] = x_left
                right_ref[rows_of(g, g + 1, (hi - mid) * piece), here] = dy_right
                far = to_edge * dot(next(far_of)[...], dy_right, NN)
                for n in range(lo, mid):
                    dx[n] = dx[n] + far[rows_of(n - lo, n - lo + 1, piece), :]
        for n in range(pieces):
            dx_out[rows_of(n, n + 1, piece), here] = dx[n].astype(BF16)

    if before:
        db_out[...] = before[0][...]
        dc_out[...] = before[1][...]
    else:
        db_out[...] = jnp.zeros_like(db_out)
        dc_out[...] = jnp.zeros_like(dc_out)
    batch = 4
    for first in range(0, pieces, batch):
        rows = rows_of(first, min(first + batch, pieces), piece)
        total = dot(x_near[rows, :], dy_near[rows, :], NT)
        row, col = iota(total.shape, 0), iota(total.shape, 1)
        keep = (split_of(row, piece) == split_of(col, piece)) & (row <= col)
        weighted = jnp.where(keep, total, 0.0).astype(BF16)
        db_out[rows, :] += dot(weighted, c[rows, :], NN)
        dc_out[rows, :] += dot(weighted, b[rows, :], TN)
    for ((n_left, n_right), same), left_ref, right_ref in zip(groups, lefts, rights):
        total = dot(left_ref[...], right_ref[...], NT)
        if len(same) > 1:
            row, col = iota(total.shape, 0), iota(total.shape, 1)
            same_cut = split_of(row, n_left * piece) == split_of(col, n_right * piece)
            total = jnp.where(same_cut, total, 0.0)
        weighted = total.astype(BF16)
        b_left = jnp.concatenate([b[rows_of(lo, mid, piece), :] for lo, mid, _ in same], axis=0)
        c_right = jnp.concatenate([c[rows_of(mid, hi, piece), :] for _, mid, hi in same], axis=0)
        db = dot(weighted, c_right, NN)
        dc = dot(weighted, b_left, TN)
        for g, (lo, mid, hi) in enumerate(same):
            db_out[rows_of(lo, mid, piece), :] += db[rows_of(g, g + 1, n_left * piece), :]
            dc_out[rows_of(mid, hi, piece), :] += dc[rows_of(g, g + 1, n_right * piece), :]


def inner_terms(head_dim, chunk, setup, b, c, x, dy, before, after):
    length, state = b.shape
    columns = x.shape[1] // chunk_count(x.shape[1])
    groups = grouped_cuts(length // head_dim)
    sizes = [[len(same) * n * head_dim for n in halves] for halves, same in groups]
    return pl.pallas_call(
        functools.partial(inner_kernel, head_dim, chunk, len(before), len(after)),
        out_shape=[
            jax.ShapeDtypeStruct((length, columns), BF16),
            jax.ShapeDtypeStruct((length, state), F32),
            jax.ShapeDtypeStruct((length, state), F32),
        ],
        in_specs=whole(4 + len(setup) + len(before)) + [ANY] * len(after),
        out_specs=whole(3),
        scratch_shapes=[pltpu.VMEM((length, columns), BF16)] * 2
        + [pltpu.VMEM((left, columns), BF16) for left, _ in sizes]
        + [pltpu.VMEM((right, columns), BF16) for _, right in sizes],
        compiler_params=params(16),
        cost_estimate=cost(8 * x.size * state, 4 * x.size, 2 * x.size),
        name="inner_terms",
    )(b, c, x, dy, *setup, *before, *after)


def parts_kernel(last, db_before, dc_before, *refs):
    scaled, refs = refs[: 2 * GROUP], refs[2 * GROUP :]
    entries, outs = sent_order(refs[:GROUP]), refs[-1 if last else -2 :]
    length, state = db_before.shape
    db, dc = db_before[...], dc_before[...]
    for k, entry in enumerate(entries):
        db = db + dot(scaled[2 * k][...], entry[state:, :], NT)
        dc = dc + dot(scaled[2 * k + 1][...], entry[:state, :], NT)
    if last:
        outs[0][:length, :] = db.astype(BF16)
        outs[0][length:, :] = dc.astype(BF16)
    else:
        outs[0][...] = db
        outs[1][...] = dc


def entry_parts(last, scaled, db_before, dc_before, entries, after):
    length, state = db_before.shape
    one = jax.ShapeDtypeStruct((length, state), F32)
    outs = [jax.ShapeDtypeStruct((2 * length, state), BF16)] if last else [one, one]
    return pl.pallas_call(
        functools.partial(parts_kernel, last),
        out_shape=outs,
        in_specs=whole(2 + 3 * GROUP) + [ANY] * len(after),
        out_specs=whole(len(outs)),
        compiler_params=params(8),
        cost_estimate=cost(8 * scaled[0].size * state, 8 * scaled[0].size),
        name="entry_parts",
    )(db_before, dc_before, *scaled, *sent_order(entries), *after)


def put_values(where, spread, b, dx_local, entries, put):
    state, part = b.shape[1], entries[0].shape[1]
    for k, entry in enumerate(entries):
        here = slice(k * part, (k + 1) * part)
        local = dx_local[:, pl.ds(pl.multiple_of((place_of(where) ^ k) * part, part), part)]
        far = spread[k][...].astype(F32) * dot(b[...], entry[state:, :], NN)
        put(k, here, (local.astype(F32) + far).astype(BF16))


def values_kernel(where, b, dx_local, *refs):
    spread, entries, out = refs[:GROUP], sent_order(refs[GROUP : 2 * GROUP]), refs[-1]

    def put(k, here, value):
        out[:, here] = value

    put_values(where, spread, b, dx_local, entries, put)


def last_values_kernel(chunks, where, b, dx_local, *refs):
    spread, refs = refs[:GROUP], refs[GROUP:]
    entries, before = sent_order(refs[:GROUP], 2), refs[GROUP : GROUP + chunks - 1]
    out, dx, sems = refs[-3:]
    part = entries[0].shape[1]
    stores = []

    def store(chunk, k, source):
        lanes = chunk_lanes(where, k, chunk, part, out.shape[1])
        at = sems.at[chunk * GROUP + k]
        stores.append(pltpu.make_async_copy(source, out.at[:, lanes], at))
        stores[-1].start()

    for chunk, values in enumerate(before):
        for k in range(GROUP):
            store(chunk, k, values.at[:, pl.ds(k * part, part)])

    def put(k, here, value):
        dx[k] = value
        store(chunks - 1, k, dx.at[k])

    put_values(where, spread, b, dx_local, entries, put)
    for one in stores:
        one.wait()


def entry_values(chunk, chunks, where, spread, b, dx_local, entries, before):
    length, part = b.shape[0], entries[0].shape[1]
    last = chunk == chunks - 1
    estimate = cost(2 * dx_local.size * b.shape[1], 4 * dx_local.size)
    operands = [where, b, dx_local, *spread, *sent_order(entries, 2 if last else 1)]
    if not last:
        return pl.pallas_call(
            values_kernel,
            out_shape=jax.ShapeDtypeStruct((length, GROUP * part), BF16),
            in_specs=[SMEM] + whole(2 + 2 * GROUP),
            out_specs=whole(1)[0],
            compiler_params=params(8),
            cost_estimate=estimate,
            name="entry_values",
        )(*operands)
    return pl.pallas_call(
        functools.partial(last_values_kernel, chunks),
        out_shape=pltpu.HBM((length, chunks * GROUP * part), BF16),
        in_specs=[SMEM] + whole(2 + 2 * GROUP + len(before)),
        out_specs=HBM,
        scratch_shapes=[
            pltpu.VMEM((GROUP, length, part), BF16),
            pltpu.SemaphoreType.DMA((chunks * GROUP,)),
        ],
        compiler_params=params(8),
        cost_estimate=estimate,
        name="last_values",
    )(*operands, *before)


def over_heads(part):
    count = lax.axis_size("head")
    total = part.astype(F32)
    for shift in range(1, count):
        pairs = [(s, (s + shift) % count) for s in range(count)]
        total = total + lax.ppermute(part, "head", pairs).astype(F32)
    return total.astype(BF16)


def shards(token_values, b_inputs, c_inputs, log_decay, grad_out):
    head_dim = token_values.shape[1] // log_decay.shape[0]
    length, state = b_inputs.shape
    count, group = lax.axis_size("seq"), GROUP
    chunks = chunk_count(token_values.shape[1])
    levels = (count // group).bit_length() - 1
    where = lax.axis_index("seq").astype(jnp.int32)[None]
    inputs = (log_decay, b_inputs, c_inputs, token_values, grad_out)
    order = [(chunk, k) for chunk in range(chunks) for k in range(group - 1, -1, -1)]
    kept, states = first_states(head_dim, order[: group - 1], where, inputs)
    ld, b, c, x, dy, *factors = kept
    late = order[group:] + order[group - 1 : group]
    states.update(next_states(head_dim, late, where, factors, b, c, x, dy))
    blocks = [
        exchange([states[chunk, k][3] for k in range(group)]) for chunk in range(chunks)
    ]
    setup = inner_setup(head_dim, ld, b, c, [states[late[-1]][0]])

    def to_group(block, k):
        return lax.ppermute(block, "seq", [(s, s ^ (k * group)) for s in range(count)])

    entries, inner, sums = [], [], []
    for chunk in range(chunks):
        (own,) = totals(state, 0, where, blocks[chunk], setup[-1:] if chunk == 0 else [])
        received = [to_group(own, 1)]
        for level in range(levels - 1):
            last = level == levels - 2
            own = merged(state, level, last, where, own, received[level], [])
            received.append(to_group(own, 2 << level))
        inner.append(inner_terms(head_dim, chunk, setup, b, c, x, dy, sums, [own]))
        sums = list(inner[chunk][1:])
        found = member_entries(state, False, where, blocks[chunk], received, sums[:1])
        entries.append(exchange(found))

    values = []
    for chunk in range(chunks):
        last = chunk == chunks - 1
        ours = [states[chunk, k] for k in range(group)]
        scaled = [one for k in range(group) for one in ours[k][:2]]
        spread = [one[2] for one in ours]
        sums = entry_parts(last, scaled, *sums, entries[chunk], values)
        local = inner[chunk][0]
        values.append(
            entry_values(chunk, chunks, where, spread, b, local, entries[chunk], values)
        )
    both = over_heads(sums[0])
    return values[-1], both[:length], both[length:]


def solution(mesh):
    in_specs = (
        P("seq", "head"),
        P("seq", None),
        P("seq", None),
        P("head", "seq"),
        P("seq", "head"),
    )
    out_specs = (P("seq", "head"), P("seq", None), P("seq", None))
    return jax.shard_map(shards, mesh=mesh, in_specs=in_specs, out_specs=out_specs, check_vma=False)
```

```python
import functools

import jax
import jax.numpy as jnp
from jax import lax
from jax.experimental import pallas as pl
from jax.experimental.pallas import tpu as pltpu
from jax.sharding import PartitionSpec as P

BF16 = jnp.bfloat16
F32 = jnp.float32
LANES = 128
GROUP = 4
TAIL = 16
LOG2E = 1.4426950408889634
MIB = 1024 * 1024

NN = (((1,), (0,)), ((), ()))
NT = (((1,), (1,)), ((), ()))
TN = (((0,), (0,)), ((), ()))


def dot(a, b, dims):
    return lax.dot_general(a, b, dims, preferred_element_type=F32)


def iota(shape, dim):
    return lax.broadcasted_iota(jnp.int32, shape, dim)


def three(values):
    high = values.astype(BF16)
    rest = values - high.astype(F32)
    mid = rest.astype(BF16)
    return high, mid, (rest - mid.astype(F32)).astype(BF16)


SLOT = LANES // 4


def summed(mask, terms):
    heads, length = terms[0].shape
    gap = [] if heads == SLOT else [jnp.zeros((SLOT - heads, length), BF16)]
    rows = [r for t in terms for r in [t] + gap] + [jnp.zeros((SLOT, length), BF16)]
    each = dot(mask, jnp.concatenate(rows, axis=0), NT)
    return each + pltpu.roll(each, LANES - SLOT, 1) + pltpu.roll(each, LANES - 2 * SLOT, 1)


def split_of(index, size):
    shift = size.bit_length() - 1
    return lax.shift_right_logical(index, shift) if size == 1 << shift else index // size


def row_less_head(head_dim, width, rows=LANES):
    shape = (LANES, width)
    row = iota(shape, 0)
    if rows < LANES:
        row = row & (rows - 1)
    return row - split_of(iota(shape, 1), head_dim)


def head_of_lane(difference, first):
    return jnp.where(difference == first, 1.0, 0.0).astype(BF16)


def whole(count):
    return [pl.BlockSpec(memory_space=pltpu.VMEM)] * count


def in_hbm(*arrays):
    return [pltpu.with_memory_space_constraint(a, pltpu.HBM) for a in arrays]


SMEM = pl.BlockSpec(memory_space=pltpu.SMEM)
HBM = pl.BlockSpec(memory_space=pltpu.HBM)
ANY = pl.BlockSpec(memory_space=pl.ANY)


def params(mib):
    return pltpu.CompilerParams(vmem_limit_bytes=mib * MIB)


def cost(flops, size, transcendentals=0):
    return pl.CostEstimate(flops=flops, bytes_accessed=size, transcendentals=transcendentals)


def place_of(where):
    return where[0] & (GROUP - 1)


def bit_of(where, level):
    return (where[0] >> (level + GROUP.bit_length() - 1)) & 1 == 1


def chunk_count(width):
    return 2 if (width // GROUP) % (2 * LANES) == 0 else 1


def chunk_lanes(where, k, chunk, part, width):
    start = (place_of(where) ^ k) * (width // GROUP) + chunk * part
    return pl.ds(pl.multiple_of(start, part), part)


def masks_of(length):
    rows, other = iota((length, length), 0), iota((length, length), 1)
    after = jnp.where(other > rows, 1.0, 0.0).astype(BF16)
    return after, jnp.where(other <= rows, 1.0, 0.0).astype(BF16)


def factors_of(ld, after, until):
    length = ld.shape[1]
    terms = three(ld)
    into_end = jnp.exp(summed(after, terms)).astype(BF16)
    from_start = jnp.exp(summed(until, terms)).astype(BF16)
    total = jnp.exp(summed(jnp.ones((TAIL, length), BF16), terms))
    high = total.astype(BF16).astype(F32)
    halves = jnp.where(iota(total.shape, 0) < TAIL // 2, high, total - high).astype(BF16)
    return into_end, from_start, halves


def put_states(head_dim, pieces, where, operands, outs, ready):
    into_end, from_start, halves, b, c, x, dy = operands
    state, width = b.shape[1], x.shape[1]
    chunks = chunk_count(width)
    part = width // (GROUP * chunks)
    difference = row_less_head(head_dim, part)
    for side, (factors, proj, cols) in enumerate([(into_end, b, x), (from_start, c, dy)]):
        ready(side)
        turned = proj[...].T
        for n, (chunk, k) in enumerate(pieces):
            x_scaled, dy_scaled, spread, send = outs[4 * n : 4 * n + 4]
            lanes = chunk_lanes(where, k, chunk, part, width)
            first_head = ((place_of(where) ^ k) * chunks + chunk) * (part // head_dim)
            hot = head_of_lane(difference, first_head)
            wide = dot(factors, hot, NN).astype(BF16)
            if side == 0:
                spread[...] = wide
                send[2 * state :, :] = dot(halves, hot, NN).astype(BF16)
            piece = cols[:, lanes] * wide
            (dy_scaled if side else x_scaled)[...] = piece
            send[side * state : (side + 1) * state, :] = dot(turned, piece, NN).astype(BF16)


def first_states_kernel(head_dim, pieces, where, ld_in, b_in, c_in, x_in, dy_in, *refs):
    ld, b, c, x, dy, into_end, from_start, halves = refs[:8]
    outs, sems = refs[8:-1], refs[-1]
    pairs = [(ld_in, ld), (b_in, b), (x_in, x), (c_in, c), (dy_in, dy)]
    copies = [pltpu.make_async_copy(i, o, sems.at[n]) for n, (i, o) in enumerate(pairs)]
    for copy in copies:
        copy.start()
    masks = masks_of(ld.shape[1])
    copies[0].wait()
    factors = factors_of(ld[...], *masks)
    for ref, value in zip((into_end, from_start, halves), factors):
        ref[...] = value

    def ready(side):
        copies[1 + 2 * side].wait()
        copies[2 + 2 * side].wait()

    put_states(head_dim, pieces, where, (*factors, b, c, x, dy), outs, ready)


def next_states_kernel(head_dim, pieces, where, into_end, from_start, halves, *refs):
    operands = (into_end[...], from_start[...], halves[...], *refs[:4])
    outs = refs[-4 * len(pieces) :]
    put_states(head_dim, pieces, where, operands, outs, lambda side: None)


def states_shapes(n_parts, length, width, state):
    part = width // (GROUP * chunk_count(width))
    scaled = jax.ShapeDtypeStruct((length, part), BF16)
    send = jax.ShapeDtypeStruct((2 * state + TAIL, part), BF16)
    return [scaled, scaled, scaled, send] * n_parts


def by_piece(pieces, outs):
    return {piece: outs[4 * n : 4 * n + 4] for n, piece in enumerate(pieces)}


def first_states(head_dim, pieces, where, inputs):
    ld, b, c, x, dy = inputs
    (length, width), state = x.shape, b.shape[1]
    kept = [jax.ShapeDtypeStruct(a.shape, a.dtype) for a in inputs]
    kept += [jax.ShapeDtypeStruct((rows, LANES), BF16) for rows in (length, length, TAIL)]
    outs = kept + states_shapes(len(pieces), length, width, state)
    found = pl.pallas_call(
        functools.partial(first_states_kernel, head_dim, pieces),
        out_shape=outs,
        in_specs=[SMEM] + [HBM] * 5,
        out_specs=whole(len(outs)),
        scratch_shapes=[pltpu.SemaphoreType.DMA((5,))],
        compiler_params=params(8),
        cost_estimate=cost(2 * length * width * (state + LANES), 8 * length * width),
        name="first_states",
    )(where, *in_hbm(*inputs))
    return found[:8], by_piece(pieces, found[8:])


def next_states(head_dim, pieces, where, factors, b, c, x, dy):
    (length, width), state = x.shape, b.shape[1]
    outs = states_shapes(len(pieces), length, width, state)
    found = pl.pallas_call(
        functools.partial(next_states_kernel, head_dim, pieces),
        out_shape=outs,
        in_specs=[SMEM] + whole(7),
        out_specs=whole(len(outs)),
        compiler_params=params(8),
        cost_estimate=cost(2 * length * width * (state + LANES), 4 * length * width),
        name="next_states",
    )(where, *factors, b, c, x, dy)
    return by_piece(pieces, found)


def decay_of(tail):
    tail = tail.astype(F32)
    return tail[:1, :] + tail[TAIL // 2 : TAIL // 2 + 1, :]


def put_decay(ref, first, factor):
    high = factor.astype(BF16).astype(F32)
    shape = (TAIL, factor.shape[1])
    both = jnp.where(iota(shape, 0) < TAIL // 2, high, factor - high)
    ref[first:, :] = both.astype(BF16)


def sent_order(parts):
    return [parts[0], *parts[:0:-1]]


def in_order(group, forward):
    return list(range(group)) if forward else list(range(group - 1, -1, -1))


def side_rows(state, forward):
    return slice(0, state) if forward else slice(state, 2 * state)


def totals_kernel(state, levels, where, *refs):
    group = GROUP
    blocks, outs, sums = sent_order(refs[:group]), refs[-1 - levels : -1], refs[-1]
    for here in range(group):

        @pl.when(place_of(where) == here)
        def _(here=here):
            decays = [decay_of(blocks[q ^ here][2 * state :, :]) for q in range(group)]
            for forward in (True, False):
                rows, value = side_rows(state, forward), None
                for q in in_order(group, forward):
                    piece = blocks[q ^ here][rows, :].astype(F32)
                    value = piece if value is None else decays[q] * value + piece
                sums[rows, :] = value.astype(BF16)

    factor = decay_of(blocks[0][2 * state :, :])
    for block in blocks[1:]:
        factor = factor * decay_of(block[2 * state :, :])
    if not levels:
        put_decay(sums, 2 * state, factor)
    for level, out in enumerate(outs):
        put_decay(out, state, factor)
        for forward in (True, False):

            @pl.when(bit_of(where, level) != forward)
            def _(out=out, forward=forward):
                out[:state, :] = sums[side_rows(state, forward), :]


def totals(state, levels, where, blocks, after):
    part = blocks[0].shape[1]
    outs = [jax.ShapeDtypeStruct((state + TAIL, part), BF16)] * levels
    if not levels:
        outs = [jax.ShapeDtypeStruct(blocks[0].shape, BF16)]
    return pl.pallas_call(
        functools.partial(totals_kernel, state, levels),
        out_shape=outs,
        in_specs=[SMEM] + whole(len(blocks)) + [ANY] * len(after),
        out_specs=whole(len(outs)),
        scratch_shapes=[pltpu.VMEM((2 * state, part), BF16)] if levels else [],
        compiler_params=params(4),
        cost_estimate=cost(8 * blocks[0].size, 10 * blocks[0].size),
        name="totals",
    )(where, *sent_order(blocks), *after)


def merged_kernel(state, level, last, where, own, received, *refs):
    out = refs[-1]
    d_own, d_other = decay_of(own[2 * state :, :]), decay_of(received[2 * state :, :])
    upper = bit_of(where, level)
    later = bit_of(where, level + 1)
    for is_upper in (False, True):
        for forward in (True, False):
            chosen = upper == is_upper
            if last:
                chosen = chosen & (later != forward)

            @pl.when(chosen)
            def _(is_upper=is_upper, forward=forward):
                rows = side_rows(state, forward)
                mine, other = own[rows, :].astype(F32), received[rows, :].astype(F32)
                value = mine + d_own * other if is_upper == forward else other + d_other * mine
                out[slice(0, state) if last else rows, :] = value.astype(BF16)

    if not last:
        put_decay(out, 2 * state, d_own * d_other)


def merged(state, level, last, where, own, received, after):
    rows = state if last else own.shape[0]
    return pl.pallas_call(
        functools.partial(merged_kernel, state, level, last),
        out_shape=pltpu.VMEM((rows, own.shape[1]), BF16),
        in_specs=[SMEM] + whole(2) + [ANY] * len(after),
        out_specs=whole(1)[0],
        compiler_params=params(4),
        cost_estimate=cost(4 * own.size, 6 * own.size),
        name="merged",
    )(where, own, received, *after)


def put_direct(state, groups, number, received, entry):
    for mine in range(groups):

        @pl.when(number == mine)
        def _(mine=mine):
            for forward in (True, False):
                rows = side_rows(state, forward)
                others = range(mine - 1, -1, -1) if forward else range(mine + 1, groups)
                value, factor = jnp.zeros((state, entry.shape[1]), F32), None
                for other in others:
                    r = received[(mine ^ other) - 1]
                    piece = r[:state, :].astype(F32)
                    value = piece if factor is None else value + factor * piece
                    d = decay_of(r[state:, :])
                    factor = d if factor is None else factor * d
                entry[rows, :] = value


def put_rounds(state, where, received, entry):
    for forward in (True, False):
        value, factor = None, 1.0
        for level, r in enumerate(received):
            gets = bit_of(where, level) == forward
            both = r.shape[0] > 2 * state
            rows = side_rows(state, forward) if both else slice(0, state)
            piece = r[rows, :].astype(F32) * jnp.where(gets, 1.0, 0.0)
            value = piece if value is None else value + factor * piece
            if both:
                factor = factor * jnp.where(gets, decay_of(r[2 * state :, :]), 1.0)
        entry[side_rows(state, forward), :] = value


def members_kernel(state, direct, n_received, where, *refs):
    received, refs = refs[:n_received], refs[n_received:]
    group = GROUP
    blocks, outs, entry = refs[:group], refs[-1 - group : -1], refs[-1]
    if direct:
        put_direct(state, n_received + 1, where[0] // group, received, entry)
    else:
        put_rounds(state, where, received, entry)
    for here in range(group):

        @pl.when(place_of(where) == here)
        def _(here=here):
            decays = [decay_of(blocks[q ^ here][2 * state :, :]) for q in range(group)]
            for forward in (True, False):
                rows, order = side_rows(state, forward), in_order(group, forward)
                value = entry[rows, :]
                for q in order:
                    outs[q ^ here][rows, :] = value.astype(BF16)
                    if q != order[-1]:
                        value = decays[q] * value + blocks[q ^ here][rows, :].astype(F32)


def member_entries(state, direct, where, blocks, received, after):
    group, part = len(blocks), blocks[0].shape[1]
    return pl.pallas_call(
        functools.partial(members_kernel, state, direct, len(received)),
        out_shape=[jax.ShapeDtypeStruct((2 * state, part), BF16)] * group,
        in_specs=[SMEM] + whole(group + len(received)) + [ANY] * len(after),
        out_specs=whole(group),
        scratch_shapes=[pltpu.VMEM((2 * state, part), F32)],
        compiler_params=params(4),
        cost_estimate=cost(12 * blocks[0].size, 16 * blocks[0].size),
        name="member_entries",
    )(where, *received, *blocks, *after)


def exchange(parts):
    count = lax.axis_size("seq")
    out = list(parts)
    for k in range(len(parts) - 1, 0, -1):
        out[k] = lax.ppermute(parts[k], "seq", [(s, s ^ k) for s in range(count)])
    return out


def split_pairs(first, count):
    if count == 1:
        return []
    middle = first + count // 2
    return (
        [(first, middle, first + count)]
        + split_pairs(first, middle - first)
        + split_pairs(middle, first + count - middle)
    )


def grouped_cuts(pieces):
    groups = {}
    for cut in split_pairs(0, pieces):
        groups.setdefault((cut[1] - cut[0], cut[2] - cut[1]), []).append(cut)
    return list(groups.items())


def rows_of(first, end, piece):
    return slice(first * piece, end * piece)


def setup_kernel(piece, ld, b, c, *refs):
    near, cum_terms = refs[-2:]
    heads, length = ld.shape
    rows, other = iota((length, length), 0), iota((length, length), 1)
    mask = jnp.where(other <= rows, 1.0, 0.0).astype(BF16)
    cum = summed(mask, three(ld[...] * LOG2E))
    lane = iota(cum.shape, 1)
    in_slots = jnp.where(lane < SLOT, cum, 0.0)
    in_slots = in_slots + pltpu.roll(in_slots, SLOT, 1) + pltpu.roll(in_slots, 2 * SLOT, 1)
    high, mid, low = three(in_slots)
    cum_terms[...] = jnp.where(lane < SLOT, high, jnp.where(lane < 2 * SLOT, mid, low))
    keep = iota((piece, piece), 0) <= iota((piece, piece), 1)
    pieces = length // piece
    for n in range(pieces):
        here = rows_of(n, n + 1, piece)
        near[here, :] = jnp.where(keep, dot(b[here, :], c[here, :], NT), 0.0).astype(BF16)
    cuts = [cut for _, same in grouped_cuts(pieces) for cut in same]
    for (lo, mid_, hi), far in zip(cuts, refs):
        left, right = rows_of(lo, mid_, piece), rows_of(mid_, hi, piece)
        far[...] = dot(b[left, :], c[right, :], NT).astype(BF16)


def inner_setup(piece, ld, b, c, after):
    length = b.shape[0]
    cuts = [cut for _, same in grouped_cuts(length // piece) for cut in same]
    outs = [
        jax.ShapeDtypeStruct(((mid - lo) * piece, (hi - mid) * piece), BF16) for lo, mid, hi in cuts
    ]
    outs.append(jax.ShapeDtypeStruct((length, piece), BF16))
    outs.append(jax.ShapeDtypeStruct((length, LANES), BF16))
    return pl.pallas_call(
        functools.partial(setup_kernel_after, piece, len(after)),
        out_shape=outs,
        in_specs=whole(3) + [ANY] * len(after),
        out_specs=whole(len(outs)),
        compiler_params=params(4),
        cost_estimate=cost(8 * b.size * length, 8 * b.size),
        name="inner_setup",
    )(ld, b, c, *after)


def setup_kernel_after(piece, n_after, ld, b, c, *refs):
    setup_kernel(piece, ld, b, c, *refs[n_after:])


def inner_kernel(head_dim, worked, n_before, n_after, b, c, x, dy, *refs):
    length, width = x.shape
    piece = head_dim
    pieces = length // piece
    groups = grouped_cuts(pieces)
    n_cuts = sum(len(same) for _, same in groups)
    fars, (near, cum_terms), refs = refs[:n_cuts], refs[n_cuts : n_cuts + 2], refs[n_cuts + 2 :]
    before, refs = refs[:n_before], refs[n_before + n_after :]
    dx_outs, (db_out, dc_out, x_near, dy_near, *scratch) = refs[: len(worked)], refs[len(worked) :]
    lefts, rights = scratch[: len(groups)], scratch[len(groups) :]
    part = dx_outs[0].shape[1]
    difference = row_less_head(head_dim, part, SLOT)

    for at, (chunk, m) in enumerate(worked):
        owned = m * (width // GROUP) + chunk * part
        lanes, here = slice(owned, owned + part), slice(at * part, (at + 1) * part)
        cum = dot(cum_terms[...], head_of_lane(difference, owned // head_dim), NN)
        dx = []
        for n in range(pieces):
            rows = rows_of(n, n + 1, piece)
            middle = cum[n * piece + piece // 2 : n * piece + piece // 2 + 1, :]
            gap = middle - cum[rows, :]
            down, up = jnp.exp2(gap), jnp.exp2(-gap)
            x_near[rows, here] = (x[rows, lanes].astype(F32) * down).astype(BF16)
            dy_piece = (dy[rows, lanes].astype(F32) * up).astype(BF16)
            dy_near[rows, here] = dy_piece
            dx.append(down * dot(near[rows, :], dy_piece, NN))
        far_of = iter(fars)
        for (_, same), left_ref, right_ref in zip(groups, lefts, rights):
            for g, (lo, mid, hi) in enumerate(same):
                left, right = rows_of(lo, mid, piece), rows_of(mid, hi, piece)
                edge = cum[mid * piece - 1 : mid * piece, :]
                to_edge = jnp.exp2(edge - cum[left, :])
                from_edge = jnp.exp2(cum[right, :] - edge)
                x_left = (x[left, lanes].astype(F32) * to_edge).astype(BF16)
                dy_right = (dy[right, lanes].astype(F32) * from_edge).astype(BF16)
                left_ref[rows_of(g, g + 1, (mid - lo) * piece), here] = x_left
                right_ref[rows_of(g, g + 1, (hi - mid) * piece), here] = dy_right
                far = to_edge * dot(next(far_of)[...], dy_right, NN)
                for n in range(lo, mid):
                    dx[n] = dx[n] + far[rows_of(n - lo, n - lo + 1, piece), :]
        for n in range(pieces):
            dx_outs[at][rows_of(n, n + 1, piece), :] = dx[n].astype(BF16)

    if before:
        db_out[...] = before[0][...]
        dc_out[...] = before[1][...]
    else:
        db_out[...] = jnp.zeros_like(db_out)
        dc_out[...] = jnp.zeros_like(dc_out)
    batch = 4
    for first in range(0, pieces, batch):
        rows = rows_of(first, min(first + batch, pieces), piece)
        total = dot(x_near[rows, :], dy_near[rows, :], NT)
        row, col = iota(total.shape, 0), iota(total.shape, 1)
        keep = (split_of(row, piece) == split_of(col, piece)) & (row <= col)
        weighted = jnp.where(keep, total, 0.0).astype(BF16)
        db_out[rows, :] += dot(weighted, c[rows, :], NN)
        dc_out[rows, :] += dot(weighted, b[rows, :], TN)
    for ((n_left, n_right), same), left_ref, right_ref in zip(groups, lefts, rights):
        total = dot(left_ref[...], right_ref[...], NT)
        if len(same) > 1:
            row, col = iota(total.shape, 0), iota(total.shape, 1)
            same_cut = split_of(row, n_left * piece) == split_of(col, n_right * piece)
            total = jnp.where(same_cut, total, 0.0)
        weighted = total.astype(BF16)
        b_left = jnp.concatenate([b[rows_of(lo, mid, piece), :] for lo, mid, _ in same], axis=0)
        c_right = jnp.concatenate([c[rows_of(mid, hi, piece), :] for _, mid, hi in same], axis=0)
        db = dot(weighted, c_right, NN)
        dc = dot(weighted, b_left, TN)
        for g, (lo, mid, hi) in enumerate(same):
            db_out[rows_of(lo, mid, piece), :] += db[rows_of(g, g + 1, n_left * piece), :]
            dc_out[rows_of(mid, hi, piece), :] += dc[rows_of(g, g + 1, n_right * piece), :]


def inner_terms(head_dim, worked, setup, b, c, x, dy, before, after):
    (length, state), width = b.shape, x.shape[1]
    part = width // (GROUP * chunk_count(width))
    used = part * len(worked)
    groups = grouped_cuts(length // head_dim)
    sizes = [[len(same) * n * head_dim for n in halves] for halves, same in groups]
    found = pl.pallas_call(
        functools.partial(inner_kernel, head_dim, worked, len(before), len(after)),
        out_shape=[jax.ShapeDtypeStruct((length, part), BF16)] * len(worked)
        + [jax.ShapeDtypeStruct((length, state), F32)] * 2,
        in_specs=whole(4 + len(setup) + len(before)) + [ANY] * len(after),
        out_specs=whole(len(worked) + 2),
        scratch_shapes=[pltpu.VMEM((length, used), BF16)] * 2
        + [pltpu.VMEM((left, used), BF16) for left, _ in sizes]
        + [pltpu.VMEM((right, used), BF16) for _, right in sizes],
        compiler_params=params(16),
        cost_estimate=cost(8 * x.size * state, 4 * x.size, 2 * x.size),
        name="inner_terms",
    )(b, c, x, dy, *setup, *before, *after)
    return dict(zip(worked, found)), list(found[-2:])


def parts_kernel(last, db_before, dc_before, *refs):
    scaled, refs = refs[: 2 * GROUP], refs[2 * GROUP :]
    entries, outs = sent_order(refs[:GROUP]), refs[-1 if last else -2 :]
    length, state = db_before.shape
    db, dc = db_before[...], dc_before[...]
    for k, entry in enumerate(entries):
        db = db + dot(scaled[2 * k][...], entry[state:, :], NT)
        dc = dc + dot(scaled[2 * k + 1][...], entry[:state, :], NT)
    if last:
        outs[0][:length, :] = db.astype(BF16)
        outs[0][length:, :] = dc.astype(BF16)
    else:
        outs[0][...] = db
        outs[1][...] = dc


def entry_parts(last, scaled, db_before, dc_before, entries, after):
    length, state = db_before.shape
    one = jax.ShapeDtypeStruct((length, state), F32)
    outs = [jax.ShapeDtypeStruct((2 * length, state), BF16)] if last else [one, one]
    return pl.pallas_call(
        functools.partial(parts_kernel, last),
        out_shape=outs,
        in_specs=whole(2 + 3 * GROUP) + [ANY] * len(after),
        out_specs=whole(len(outs)),
        compiler_params=params(8),
        cost_estimate=cost(8 * scaled[0].size * state, 8 * scaled[0].size),
        name="entry_parts",
    )(db_before, dc_before, *scaled, *sent_order(entries), *after)


def put_values(where, spread, b, local_parts, dx_local, entries, put):
    state, part = b.shape[1], entries[0].shape[1]
    for m, one in enumerate(local_parts):
        dx_local[:, m * part : (m + 1) * part] = one[...]
    for k, entry in enumerate(entries):
        here = slice(k * part, (k + 1) * part)
        local = dx_local[:, pl.ds(pl.multiple_of((place_of(where) ^ k) * part, part), part)]
        far = spread[k][...].astype(F32) * dot(b[...], entry[state:, :], NN)
        put(k, here, (local.astype(F32) + far).astype(BF16))


def values_kernel(where, b, *refs):
    local_parts, spread = refs[:GROUP], refs[GROUP : 2 * GROUP]
    entries, (out, dx_local) = sent_order(refs[2 * GROUP : 3 * GROUP]), refs[-2:]

    def put(k, here, value):
        out[:, here] = value

    put_values(where, spread, b, local_parts, dx_local, entries, put)


def last_values_kernel(chunks, where, b, *refs):
    local_parts, spread, refs = refs[:GROUP], refs[GROUP : 2 * GROUP], refs[2 * GROUP :]
    entries, before = sent_order(refs[:GROUP]), refs[GROUP : GROUP + chunks - 1]
    out, dx, dx_local, sems = refs[-4:]
    part = entries[0].shape[1]
    stores = []

    def store(chunk, k, source):
        lanes = chunk_lanes(where, k, chunk, part, out.shape[1])
        at = sems.at[chunk * GROUP + k]
        stores.append(pltpu.make_async_copy(source, out.at[:, lanes], at))
        stores[-1].start()

    for chunk, values in enumerate(before):
        for k in range(GROUP):
            store(chunk, k, values.at[:, pl.ds(k * part, part)])

    def put(k, here, value):
        dx[k] = value
        store(chunks - 1, k, dx.at[k])

    put_values(where, spread, b, local_parts, dx_local, entries, put)
    for one in stores:
        one.wait()


def entry_values(chunk, chunks, where, spread, b, local_parts, entries, before):
    length, part = b.shape[0], entries[0].shape[1]
    last = chunk == chunks - 1
    estimate = cost(8 * local_parts[0].size * b.shape[1], 16 * local_parts[0].size)
    operands = [where, b, *local_parts, *spread, *sent_order(entries)]
    if not last:
        return pl.pallas_call(
            values_kernel,
            out_shape=jax.ShapeDtypeStruct((length, GROUP * part), BF16),
            in_specs=[SMEM] + whole(1 + 3 * GROUP),
            out_specs=whole(1)[0],
            scratch_shapes=[pltpu.VMEM((length, GROUP * part), BF16)],
            compiler_params=params(8),
            cost_estimate=estimate,
            name="entry_values",
        )(*operands)
    return pl.pallas_call(
        functools.partial(last_values_kernel, chunks),
        out_shape=pltpu.HBM((length, chunks * GROUP * part), BF16),
        in_specs=[SMEM] + whole(1 + 3 * GROUP + len(before)),
        out_specs=HBM,
        scratch_shapes=[
            pltpu.VMEM((GROUP, length, part), BF16),
            pltpu.VMEM((length, GROUP * part), BF16),
            pltpu.SemaphoreType.DMA((chunks * GROUP,)),
        ],
        compiler_params=params(8),
        cost_estimate=estimate,
        name="last_values",
    )(*operands, *before)


def over_heads(part):
    count = lax.axis_size("head")
    total = part.astype(F32)
    for shift in range(1, count):
        pairs = [(s, (s + shift) % count) for s in range(count)]
        total = total + lax.ppermute(part, "head", pairs).astype(F32)
    return total.astype(BF16)


def shards(token_values, b_inputs, c_inputs, log_decay, grad_out):
    head_dim = token_values.shape[1] // log_decay.shape[0]
    length, state = b_inputs.shape
    count, group = lax.axis_size("seq"), GROUP
    chunks = chunk_count(token_values.shape[1])
    levels = (count // group).bit_length() - 1
    where = lax.axis_index("seq").astype(jnp.int32)[None]
    inputs = (log_decay, b_inputs, c_inputs, token_values, grad_out)
    order = [(chunk, k) for chunk in range(chunks) for k in range(group - 1, -1, -1)]
    kept, states = first_states(head_dim, order[: group - 1], where, inputs)
    ld, b, c, x, dy, *factors = kept
    late = order[group:] + order[group - 1 : group]
    states.update(next_states(head_dim, late, where, factors, b, c, x, dy))
    blocks = [
        exchange([states[chunk, k][3] for k in range(group)]) for chunk in range(chunks)
    ]
    setup = inner_setup(head_dim, ld, b, c, [states[late[-1]][0]])

    def to_group(block, k):
        return lax.ppermute(block, "seq", [(s, s ^ (k * group)) for s in range(count)])

    every = [(chunk, m) for chunk in range(chunks) for m in range(group)]
    worked = [every[:3]] + [every[chunk * group :][:2] for chunk in range(1, chunks)]
    rest = [one for one in every if not any(one in some for some in worked)]
    entries, inner, sums = [], {}, []

    def add_inner(some, after):
        found, sums[:] = inner_terms(head_dim, some, setup, b, c, x, dy, sums, after)
        inner.update(found)

    for chunk in range(chunks):
        (own,) = totals(state, 0, where, blocks[chunk], setup[-1:] if chunk == 0 else [])
        received = [to_group(own, 1)]
        for level in range(levels - 1):
            last = level == levels - 2
            own = merged(state, level, last, where, own, received[level], [])
            received.append(to_group(own, 2 << level))
        add_inner(worked[chunk], [own])
        found = member_entries(state, False, where, blocks[chunk], received, sums[:1])
        entries.append(exchange(found))
    add_inner(rest, found[:1])

    values = []
    for chunk in range(chunks):
        last = chunk == chunks - 1
        ours = [states[chunk, k] for k in range(group)]
        scaled = [one for k in range(group) for one in ours[k][:2]]
        spread = [one[2] for one in ours]
        sums = entry_parts(last, scaled, *sums, entries[chunk], values)
        local = [inner[chunk, m] for m in range(group)]
        values.append(
            entry_values(chunk, chunks, where, spread, b, local, entries[chunk], values)
        )
    both = over_heads(sums[0])
    return values[-1], both[:length], both[length:]


def solution(mesh):
    in_specs = (
        P("seq", "head"),
        P("seq", None),
        P("seq", None),
        P("head", "seq"),
        P("seq", "head"),
    )
    out_specs = (P("seq", "head"), P("seq", None), P("seq", None))
    return jax.shard_map(shards, mesh=mesh, in_specs=in_specs, out_specs=out_specs, check_vma=False)
```

```python
import functools

import jax
import jax.numpy as jnp
from jax import lax
from jax.experimental import pallas as pl
from jax.experimental.pallas import tpu as pltpu
from jax.sharding import PartitionSpec as P

BF16 = jnp.bfloat16
F32 = jnp.float32
LANES = 128
GROUP = 4
TAIL = 16
LOG2E = 1.4426950408889634
MIB = 1024 * 1024

NN = (((1,), (0,)), ((), ()))
NT = (((1,), (1,)), ((), ()))
TN = (((0,), (0,)), ((), ()))


def dot(a, b, dims):
    return lax.dot_general(a, b, dims, preferred_element_type=F32)


def iota(shape, dim):
    return lax.broadcasted_iota(jnp.int32, shape, dim)


def three(values):
    high = values.astype(BF16)
    rest = values - high.astype(F32)
    mid = rest.astype(BF16)
    return high, mid, (rest - mid.astype(F32)).astype(BF16)


SLOT = LANES // 4


def summed(mask, terms):
    heads, length = terms[0].shape
    gap = [] if heads == SLOT else [jnp.zeros((SLOT - heads, length), BF16)]
    rows = [r for t in terms for r in [t] + gap] + [jnp.zeros((SLOT, length), BF16)]
    each = dot(mask, jnp.concatenate(rows, axis=0), NT)
    return each + pltpu.roll(each, LANES - SLOT, 1) + pltpu.roll(each, LANES - 2 * SLOT, 1)


def split_of(index, size):
    shift = size.bit_length() - 1
    return lax.shift_right_logical(index, shift) if size == 1 << shift else index // size


def row_less_head(head_dim, width, rows=LANES):
    shape = (LANES, width)
    row = iota(shape, 0)
    if rows < LANES:
        row = row & (rows - 1)
    return row - split_of(iota(shape, 1), head_dim)


def head_of_lane(difference, first):
    return jnp.where(difference == first, 1.0, 0.0).astype(BF16)


def whole(count):
    return [pl.BlockSpec(memory_space=pltpu.VMEM)] * count


def in_hbm(*arrays):
    return [pltpu.with_memory_space_constraint(a, pltpu.HBM) for a in arrays]


SMEM = pl.BlockSpec(memory_space=pltpu.SMEM)
HBM = pl.BlockSpec(memory_space=pltpu.HBM)
ANY = pl.BlockSpec(memory_space=pl.ANY)


def params(mib):
    return pltpu.CompilerParams(vmem_limit_bytes=mib * MIB)


def cost(flops, size, transcendentals=0):
    return pl.CostEstimate(flops=flops, bytes_accessed=size, transcendentals=transcendentals)


def place_of(where):
    return where[0] & (GROUP - 1)


def bit_of(where, level):
    return (where[0] >> (level + GROUP.bit_length() - 1)) & 1 == 1


def chunk_count(width):
    return 2 if (width // GROUP) % (2 * LANES) == 0 else 1


def chunk_lanes(where, k, chunk, part, width):
    start = (place_of(where) ^ k) * (width // GROUP) + chunk * part
    return pl.ds(pl.multiple_of(start, part), part)


def masks_of(length):
    rows, other = iota((length, length), 0), iota((length, length), 1)
    after = jnp.where(other > rows, 1.0, 0.0).astype(BF16)
    return after, jnp.where(other <= rows, 1.0, 0.0).astype(BF16)


def factors_of(ld, after, until):
    length = ld.shape[1]
    terms = three(ld)
    into_end = jnp.exp(summed(after, terms)).astype(BF16)
    from_start = jnp.exp(summed(until, terms)).astype(BF16)
    total = jnp.exp(summed(jnp.ones((TAIL, length), BF16), terms))
    high = total.astype(BF16).astype(F32)
    halves = jnp.where(iota(total.shape, 0) < TAIL // 2, high, total - high).astype(BF16)
    return into_end, from_start, halves


def put_states(head_dim, pieces, where, operands, outs, ready):
    into_end, from_start, halves, b, c, x, dy = operands
    state, width = b.shape[1], x.shape[1]
    chunks = chunk_count(width)
    part = width // (GROUP * chunks)
    difference = row_less_head(head_dim, part)
    for side, (factors, proj, cols) in enumerate([(into_end, b, x), (from_start, c, dy)]):
        ready(side)
        turned = proj[...].T
        for n, (chunk, k) in enumerate(pieces):
            x_scaled, dy_scaled, spread, send = outs[4 * n : 4 * n + 4]
            lanes = chunk_lanes(where, k, chunk, part, width)
            first_head = ((place_of(where) ^ k) * chunks + chunk) * (part // head_dim)
            hot = head_of_lane(difference, first_head)
            wide = dot(factors, hot, NN).astype(BF16)
            if side == 0:
                spread[...] = wide
                send[2 * state :, :] = dot(halves, hot, NN).astype(BF16)
            piece = cols[:, lanes] * wide
            (dy_scaled if side else x_scaled)[...] = piece
            send[side * state : (side + 1) * state, :] = dot(turned, piece, NN).astype(BF16)


def first_states_kernel(head_dim, pieces, where, ld_in, b_in, c_in, x_in, dy_in, *refs):
    ld, b, c, x, dy, into_end, from_start, halves = refs[:8]
    outs, sems = refs[8:-1], refs[-1]
    pairs = [(ld_in, ld), (b_in, b), (x_in, x), (c_in, c), (dy_in, dy)]
    copies = [pltpu.make_async_copy(i, o, sems.at[n]) for n, (i, o) in enumerate(pairs)]
    for copy in copies:
        copy.start()
    masks = masks_of(ld.shape[1])
    copies[0].wait()
    factors = factors_of(ld[...], *masks)
    for ref, value in zip((into_end, from_start, halves), factors):
        ref[...] = value

    def ready(side):
        copies[1 + 2 * side].wait()
        copies[2 + 2 * side].wait()

    put_states(head_dim, pieces, where, (*factors, b, c, x, dy), outs, ready)


def next_states_kernel(head_dim, pieces, where, into_end, from_start, halves, *refs):
    operands = (into_end[...], from_start[...], halves[...], *refs[:4])
    outs = refs[-4 * len(pieces) :]
    put_states(head_dim, pieces, where, operands, outs, lambda side: None)


def states_shapes(n_parts, length, width, state):
    part = width // (GROUP * chunk_count(width))
    scaled = jax.ShapeDtypeStruct((length, part), BF16)
    send = jax.ShapeDtypeStruct((2 * state + TAIL, part), BF16)
    return [scaled, scaled, scaled, send] * n_parts


def by_piece(pieces, outs):
    return {piece: outs[4 * n : 4 * n + 4] for n, piece in enumerate(pieces)}


def first_states(head_dim, pieces, where, inputs):
    ld, b, c, x, dy = inputs
    (length, width), state = x.shape, b.shape[1]
    kept = [jax.ShapeDtypeStruct(a.shape, a.dtype) for a in inputs]
    kept += [jax.ShapeDtypeStruct((rows, LANES), BF16) for rows in (length, length, TAIL)]
    outs = kept + states_shapes(len(pieces), length, width, state)
    found = pl.pallas_call(
        functools.partial(first_states_kernel, head_dim, pieces),
        out_shape=outs,
        in_specs=[SMEM] + [HBM] * 5,
        out_specs=whole(len(outs)),
        scratch_shapes=[pltpu.SemaphoreType.DMA((5,))],
        compiler_params=params(8),
        cost_estimate=cost(2 * length * width * (state + LANES), 8 * length * width),
        name="first_states",
    )(where, *in_hbm(*inputs))
    return found[:8], by_piece(pieces, found[8:])


def next_states(head_dim, pieces, where, factors, b, c, x, dy):
    (length, width), state = x.shape, b.shape[1]
    outs = states_shapes(len(pieces), length, width, state)
    found = pl.pallas_call(
        functools.partial(next_states_kernel, head_dim, pieces),
        out_shape=outs,
        in_specs=[SMEM] + whole(7),
        out_specs=whole(len(outs)),
        compiler_params=params(8),
        cost_estimate=cost(2 * length * width * (state + LANES), 4 * length * width),
        name="next_states",
    )(where, *factors, b, c, x, dy)
    return by_piece(pieces, found)


def decay_of(tail):
    tail = tail.astype(F32)
    return tail[:1, :] + tail[TAIL // 2 : TAIL // 2 + 1, :]


def put_decay(ref, first, factor):
    high = factor.astype(BF16).astype(F32)
    shape = (TAIL, factor.shape[1])
    both = jnp.where(iota(shape, 0) < TAIL // 2, high, factor - high)
    ref[first:, :] = both.astype(BF16)


def sent_order(parts):
    return [parts[0], *parts[:0:-1]]


def in_order(group, forward):
    return list(range(group)) if forward else list(range(group - 1, -1, -1))


def side_rows(state, forward):
    return slice(0, state) if forward else slice(state, 2 * state)


def totals_kernel(state, levels, where, *refs):
    group = GROUP
    blocks, outs, sums = sent_order(refs[:group]), refs[-1 - levels : -1], refs[-1]
    for here in range(group):

        @pl.when(place_of(where) == here)
        def _(here=here):
            decays = [decay_of(blocks[q ^ here][2 * state :, :]) for q in range(group)]
            for forward in (True, False):
                rows, value = side_rows(state, forward), None
                for q in in_order(group, forward):
                    piece = blocks[q ^ here][rows, :].astype(F32)
                    value = piece if value is None else decays[q] * value + piece
                sums[rows, :] = value.astype(BF16)

    factor = decay_of(blocks[0][2 * state :, :])
    for block in blocks[1:]:
        factor = factor * decay_of(block[2 * state :, :])
    if not levels:
        put_decay(sums, 2 * state, factor)
    for level, out in enumerate(outs):
        put_decay(out, state, factor)
        for forward in (True, False):

            @pl.when(bit_of(where, level) != forward)
            def _(out=out, forward=forward):
                out[:state, :] = sums[side_rows(state, forward), :]


def totals(state, levels, where, blocks, after):
    part = blocks[0].shape[1]
    outs = [jax.ShapeDtypeStruct((state + TAIL, part), BF16)] * levels
    if not levels:
        outs = [jax.ShapeDtypeStruct(blocks[0].shape, BF16)]
    return pl.pallas_call(
        functools.partial(totals_kernel, state, levels),
        out_shape=outs,
        in_specs=[SMEM] + whole(len(blocks)) + [ANY] * len(after),
        out_specs=whole(len(outs)),
        scratch_shapes=[pltpu.VMEM((2 * state, part), BF16)] if levels else [],
        compiler_params=params(4),
        cost_estimate=cost(8 * blocks[0].size, 10 * blocks[0].size),
        name="totals",
    )(where, *sent_order(blocks), *after)


def merged_kernel(state, level, last, where, own, received, *refs):
    out = refs[-1]
    d_own, d_other = decay_of(own[2 * state :, :]), decay_of(received[2 * state :, :])
    upper = bit_of(where, level)
    later = bit_of(where, level + 1)
    for is_upper in (False, True):
        for forward in (True, False):
            chosen = upper == is_upper
            if last:
                chosen = chosen & (later != forward)

            @pl.when(chosen)
            def _(is_upper=is_upper, forward=forward):
                rows = side_rows(state, forward)
                mine, other = own[rows, :].astype(F32), received[rows, :].astype(F32)
                value = mine + d_own * other if is_upper == forward else other + d_other * mine
                out[slice(0, state) if last else rows, :] = value.astype(BF16)

    if not last:
        put_decay(out, 2 * state, d_own * d_other)


def merged(state, level, last, where, own, received, after):
    rows = state if last else own.shape[0]
    return pl.pallas_call(
        functools.partial(merged_kernel, state, level, last),
        out_shape=pltpu.VMEM((rows, own.shape[1]), BF16),
        in_specs=[SMEM] + whole(2) + [ANY] * len(after),
        out_specs=whole(1)[0],
        compiler_params=params(4),
        cost_estimate=cost(4 * own.size, 6 * own.size),
        name="merged",
    )(where, own, received, *after)


def put_direct(state, groups, number, received, entry):
    for mine in range(groups):

        @pl.when(number == mine)
        def _(mine=mine):
            for forward in (True, False):
                rows = side_rows(state, forward)
                others = range(mine - 1, -1, -1) if forward else range(mine + 1, groups)
                value, factor = jnp.zeros((state, entry.shape[1]), F32), None
                for other in others:
                    r = received[(mine ^ other) - 1]
                    piece = r[:state, :].astype(F32)
                    value = piece if factor is None else value + factor * piece
                    d = decay_of(r[state:, :])
                    factor = d if factor is None else factor * d
                entry[rows, :] = value


def put_rounds(state, where, received, entry):
    for forward in (True, False):
        value, factor = None, 1.0
        for level, r in enumerate(received):
            gets = bit_of(where, level) == forward
            both = r.shape[0] > 2 * state
            rows = side_rows(state, forward) if both else slice(0, state)
            piece = r[rows, :].astype(F32) * jnp.where(gets, 1.0, 0.0)
            value = piece if value is None else value + factor * piece
            if both:
                factor = factor * jnp.where(gets, decay_of(r[2 * state :, :]), 1.0)
        entry[side_rows(state, forward), :] = value


def members_kernel(state, direct, n_received, where, *refs):
    received, refs = refs[:n_received], refs[n_received:]
    group = GROUP
    blocks, outs, entry = refs[:group], refs[-1 - group : -1], refs[-1]
    if direct:
        put_direct(state, n_received + 1, where[0] // group, received, entry)
    else:
        put_rounds(state, where, received, entry)
    for here in range(group):

        @pl.when(place_of(where) == here)
        def _(here=here):
            decays = [decay_of(blocks[q ^ here][2 * state :, :]) for q in range(group)]
            for forward in (True, False):
                rows, order = side_rows(state, forward), in_order(group, forward)
                value = entry[rows, :]
                for q in order:
                    outs[q ^ here][rows, :] = value.astype(BF16)
                    if q != order[-1]:
                        value = decays[q] * value + blocks[q ^ here][rows, :].astype(F32)


def member_entries(state, direct, where, blocks, received, after):
    group, part = len(blocks), blocks[0].shape[1]
    return pl.pallas_call(
        functools.partial(members_kernel, state, direct, len(received)),
        out_shape=[jax.ShapeDtypeStruct((2 * state, part), BF16)] * group,
        in_specs=[SMEM] + whole(group + len(received)) + [ANY] * len(after),
        out_specs=whole(group),
        scratch_shapes=[pltpu.VMEM((2 * state, part), F32)],
        compiler_params=params(4),
        cost_estimate=cost(12 * blocks[0].size, 16 * blocks[0].size),
        name="member_entries",
    )(where, *received, *blocks, *after)


def exchange(parts):
    count = lax.axis_size("seq")
    out = list(parts)
    for k in range(len(parts) - 1, 0, -1):
        out[k] = lax.ppermute(parts[k], "seq", [(s, s ^ k) for s in range(count)])
    return out


def split_pairs(first, count):
    if count == 1:
        return []
    middle = first + count // 2
    return (
        [(first, middle, first + count)]
        + split_pairs(first, middle - first)
        + split_pairs(middle, first + count - middle)
    )


def grouped_cuts(pieces):
    groups = {}
    for cut in split_pairs(0, pieces):
        groups.setdefault((cut[1] - cut[0], cut[2] - cut[1]), []).append(cut)
    return list(groups.items())


def rows_of(first, end, piece):
    return slice(first * piece, end * piece)


def setup_kernel(piece, ld, b, c, *refs):
    near, cum_terms = refs[-2:]
    heads, length = ld.shape
    rows, other = iota((length, length), 0), iota((length, length), 1)
    mask = jnp.where(other <= rows, 1.0, 0.0).astype(BF16)
    cum = summed(mask, three(ld[...] * LOG2E))
    lane = iota(cum.shape, 1)
    in_slots = jnp.where(lane < SLOT, cum, 0.0)
    in_slots = in_slots + pltpu.roll(in_slots, SLOT, 1) + pltpu.roll(in_slots, 2 * SLOT, 1)
    high, mid, low = three(in_slots)
    cum_terms[...] = jnp.where(lane < SLOT, high, jnp.where(lane < 2 * SLOT, mid, low))
    keep = iota((piece, piece), 0) <= iota((piece, piece), 1)
    pieces = length // piece
    for n in range(pieces):
        here = rows_of(n, n + 1, piece)
        near[here, :] = jnp.where(keep, dot(b[here, :], c[here, :], NT), 0.0).astype(BF16)
    cuts = [cut for _, same in grouped_cuts(pieces) for cut in same]
    for (lo, mid_, hi), far in zip(cuts, refs):
        left, right = rows_of(lo, mid_, piece), rows_of(mid_, hi, piece)
        far[...] = dot(b[left, :], c[right, :], NT).astype(BF16)


def inner_setup(piece, ld, b, c, after):
    length = b.shape[0]
    cuts = [cut for _, same in grouped_cuts(length // piece) for cut in same]
    outs = [
        jax.ShapeDtypeStruct(((mid - lo) * piece, (hi - mid) * piece), BF16) for lo, mid, hi in cuts
    ]
    outs.append(jax.ShapeDtypeStruct((length, piece), BF16))
    outs.append(jax.ShapeDtypeStruct((length, LANES), BF16))
    return pl.pallas_call(
        functools.partial(setup_kernel_after, piece, len(after)),
        out_shape=outs,
        in_specs=whole(3) + [ANY] * len(after),
        out_specs=whole(len(outs)),
        compiler_params=params(4),
        cost_estimate=cost(8 * b.size * length, 8 * b.size),
        name="inner_setup",
    )(ld, b, c, *after)


def setup_kernel_after(piece, n_after, ld, b, c, *refs):
    setup_kernel(piece, ld, b, c, *refs[n_after:])


def inner_kernel(head_dim, worked, n_before, n_after, b, c, x, dy, *refs):
    length, width = x.shape
    piece = head_dim
    pieces = length // piece
    groups = grouped_cuts(pieces)
    n_cuts = sum(len(same) for _, same in groups)
    fars, (near, cum_terms), refs = refs[:n_cuts], refs[n_cuts : n_cuts + 2], refs[n_cuts + 2 :]
    before, refs = refs[:n_before], refs[n_before + n_after :]
    dx_outs, (db_out, dc_out, x_near, dy_near, *scratch) = refs[: len(worked)], refs[len(worked) :]
    lefts, rights = scratch[: len(groups)], scratch[len(groups) :]
    part = dx_outs[0].shape[1]
    difference = row_less_head(head_dim, part, SLOT)

    for at, (chunk, m) in enumerate(worked):
        owned = m * (width // GROUP) + chunk * part
        lanes, here = slice(owned, owned + part), slice(at * part, (at + 1) * part)
        cum = dot(cum_terms[...], head_of_lane(difference, owned // head_dim), NN)
        dx = []
        for n in range(pieces):
            rows = rows_of(n, n + 1, piece)
            middle = cum[n * piece + piece // 2 : n * piece + piece // 2 + 1, :]
            gap = middle - cum[rows, :]
            down, up = jnp.exp2(gap), jnp.exp2(-gap)
            x_near[rows, here] = (x[rows, lanes].astype(F32) * down).astype(BF16)
            dy_piece = (dy[rows, lanes].astype(F32) * up).astype(BF16)
            dy_near[rows, here] = dy_piece
            dx.append(down * dot(near[rows, :], dy_piece, NN))
        far_of = iter(fars)
        for (_, same), left_ref, right_ref in zip(groups, lefts, rights):
            for g, (lo, mid, hi) in enumerate(same):
                left, right = rows_of(lo, mid, piece), rows_of(mid, hi, piece)
                edge = cum[mid * piece - 1 : mid * piece, :]
                to_edge = jnp.exp2(edge - cum[left, :])
                from_edge = jnp.exp2(cum[right, :] - edge)
                x_left = (x[left, lanes].astype(F32) * to_edge).astype(BF16)
                dy_right = (dy[right, lanes].astype(F32) * from_edge).astype(BF16)
                left_ref[rows_of(g, g + 1, (mid - lo) * piece), here] = x_left
                right_ref[rows_of(g, g + 1, (hi - mid) * piece), here] = dy_right
                far = to_edge * dot(next(far_of)[...], dy_right, NN)
                for n in range(lo, mid):
                    dx[n] = dx[n] + far[rows_of(n - lo, n - lo + 1, piece), :]
        for n in range(pieces):
            dx_outs[at][rows_of(n, n + 1, piece), :] = dx[n].astype(BF16)

    if before:
        db_out[...] = before[0][...]
        dc_out[...] = before[1][...]
    else:
        db_out[...] = jnp.zeros_like(db_out)
        dc_out[...] = jnp.zeros_like(dc_out)
    batch = 4
    for first in range(0, pieces, batch):
        rows = rows_of(first, min(first + batch, pieces), piece)
        total = dot(x_near[rows, :], dy_near[rows, :], NT)
        row, col = iota(total.shape, 0), iota(total.shape, 1)
        keep = (split_of(row, piece) == split_of(col, piece)) & (row <= col)
        weighted = jnp.where(keep, total, 0.0).astype(BF16)
        db_out[rows, :] += dot(weighted, c[rows, :], NN)
        dc_out[rows, :] += dot(weighted, b[rows, :], TN)
    for ((n_left, n_right), same), left_ref, right_ref in zip(groups, lefts, rights):
        total = dot(left_ref[...], right_ref[...], NT)
        if len(same) > 1:
            row, col = iota(total.shape, 0), iota(total.shape, 1)
            same_cut = split_of(row, n_left * piece) == split_of(col, n_right * piece)
            total = jnp.where(same_cut, total, 0.0)
        weighted = total.astype(BF16)
        b_left = jnp.concatenate([b[rows_of(lo, mid, piece), :] for lo, mid, _ in same], axis=0)
        c_right = jnp.concatenate([c[rows_of(mid, hi, piece), :] for _, mid, hi in same], axis=0)
        db = dot(weighted, c_right, NN)
        dc = dot(weighted, b_left, TN)
        for g, (lo, mid, hi) in enumerate(same):
            db_out[rows_of(lo, mid, piece), :] += db[rows_of(g, g + 1, n_left * piece), :]
            dc_out[rows_of(mid, hi, piece), :] += dc[rows_of(g, g + 1, n_right * piece), :]


def inner_terms(head_dim, worked, setup, b, c, x, dy, before, after, hides=True):
    (length, state), width = b.shape, x.shape[1]
    part = width // (GROUP * chunk_count(width))
    used = part * len(worked)
    groups = grouped_cuts(length // head_dim)
    sizes = [[len(same) * n * head_dim for n in halves] for halves, same in groups]
    found = pl.pallas_call(
        functools.partial(inner_kernel, head_dim, worked, len(before), len(after)),
        out_shape=[jax.ShapeDtypeStruct((length, part), BF16)] * len(worked)
        + [jax.ShapeDtypeStruct((length, state), F32)] * 2,
        in_specs=whole(4 + len(setup) + len(before)) + [ANY] * len(after),
        out_specs=whole(len(worked) + 2),
        scratch_shapes=[pltpu.VMEM((length, used), BF16)] * 2
        + [pltpu.VMEM((left, used), BF16) for left, _ in sizes]
        + [pltpu.VMEM((right, used), BF16) for _, right in sizes],
        compiler_params=params(16),
        cost_estimate=cost(8 * x.size * state, 4 * x.size, 2 * x.size) if hides else cost(1, 1),
        name="inner_terms",
    )(b, c, x, dy, *setup, *before, *after)
    return dict(zip(worked, found)), list(found[-2:])


def parts_kernel(last, db_before, dc_before, *refs):
    scaled, refs = refs[: 2 * GROUP], refs[2 * GROUP :]
    entries, outs = sent_order(refs[:GROUP]), refs[-1 if last else -2 :]
    length, state = db_before.shape
    db, dc = db_before[...], dc_before[...]
    for k, entry in enumerate(entries):
        db = db + dot(scaled[2 * k][...], entry[state:, :], NT)
        dc = dc + dot(scaled[2 * k + 1][...], entry[:state, :], NT)
    if last:
        outs[0][:length, :] = db.astype(BF16)
        outs[0][length:, :] = dc.astype(BF16)
    else:
        outs[0][...] = db
        outs[1][...] = dc


def entry_parts(last, scaled, db_before, dc_before, entries, after):
    length, state = db_before.shape
    one = jax.ShapeDtypeStruct((length, state), F32)
    outs = [jax.ShapeDtypeStruct((2 * length, state), BF16)] if last else [one, one]
    return pl.pallas_call(
        functools.partial(parts_kernel, last),
        out_shape=outs,
        in_specs=whole(2 + 3 * GROUP) + [ANY] * len(after),
        out_specs=whole(len(outs)),
        compiler_params=params(8),
        cost_estimate=cost(8 * scaled[0].size * state, 8 * scaled[0].size),
        name="entry_parts",
    )(db_before, dc_before, *scaled, *sent_order(entries), *after)


def put_values(where, spread, b, local_parts, dx_local, entries, put):
    state, part = b.shape[1], entries[0].shape[1]
    for m, one in enumerate(local_parts):
        dx_local[:, m * part : (m + 1) * part] = one[...]
    for k, entry in enumerate(entries):
        here = slice(k * part, (k + 1) * part)
        local = dx_local[:, pl.ds(pl.multiple_of((place_of(where) ^ k) * part, part), part)]
        far = spread[k][...].astype(F32) * dot(b[...], entry[state:, :], NN)
        put(k, here, (local.astype(F32) + far).astype(BF16))


def values_kernel(where, b, *refs):
    local_parts, spread = refs[:GROUP], refs[GROUP : 2 * GROUP]
    entries, (out, dx_local) = sent_order(refs[2 * GROUP : 3 * GROUP]), refs[-2:]

    def put(k, here, value):
        out[:, here] = value

    put_values(where, spread, b, local_parts, dx_local, entries, put)


def last_values_kernel(chunks, where, b, *refs):
    local_parts, spread, refs = refs[:GROUP], refs[GROUP : 2 * GROUP], refs[2 * GROUP :]
    entries, before = sent_order(refs[:GROUP]), refs[GROUP : GROUP + chunks - 1]
    out, dx, dx_local, sems = refs[-4:]
    part = entries[0].shape[1]
    stores = []

    def store(chunk, k, source):
        lanes = chunk_lanes(where, k, chunk, part, out.shape[1])
        at = sems.at[chunk * GROUP + k]
        stores.append(pltpu.make_async_copy(source, out.at[:, lanes], at))
        stores[-1].start()

    for chunk, values in enumerate(before):
        for k in range(GROUP):
            store(chunk, k, values.at[:, pl.ds(k * part, part)])

    def put(k, here, value):
        dx[k] = value
        store(chunks - 1, k, dx.at[k])

    put_values(where, spread, b, local_parts, dx_local, entries, put)
    for one in stores:
        one.wait()


def entry_values(chunk, chunks, where, spread, b, local_parts, entries, before):
    length, part = b.shape[0], entries[0].shape[1]
    last = chunk == chunks - 1
    estimate = cost(8 * local_parts[0].size * b.shape[1], 16 * local_parts[0].size)
    operands = [where, b, *local_parts, *spread, *sent_order(entries)]
    if not last:
        return pl.pallas_call(
            values_kernel,
            out_shape=jax.ShapeDtypeStruct((length, GROUP * part), BF16),
            in_specs=[SMEM] + whole(1 + 3 * GROUP),
            out_specs=whole(1)[0],
            scratch_shapes=[pltpu.VMEM((length, GROUP * part), BF16)],
            compiler_params=params(8),
            cost_estimate=estimate,
            name="entry_values",
        )(*operands)
    return pl.pallas_call(
        functools.partial(last_values_kernel, chunks),
        out_shape=pltpu.HBM((length, chunks * GROUP * part), BF16),
        in_specs=[SMEM] + whole(1 + 3 * GROUP + len(before)),
        out_specs=HBM,
        scratch_shapes=[
            pltpu.VMEM((GROUP, length, part), BF16),
            pltpu.VMEM((length, GROUP * part), BF16),
            pltpu.SemaphoreType.DMA((chunks * GROUP,)),
        ],
        compiler_params=params(8),
        cost_estimate=estimate,
        name="last_values",
    )(*operands, *before)


def over_heads(part):
    count = lax.axis_size("head")
    total = part.astype(F32)
    for shift in range(1, count):
        pairs = [(s, (s + shift) % count) for s in range(count)]
        total = total + lax.ppermute(part, "head", pairs).astype(F32)
    return total.astype(BF16)


def shards(token_values, b_inputs, c_inputs, log_decay, grad_out):
    head_dim = token_values.shape[1] // log_decay.shape[0]
    length, state = b_inputs.shape
    count, group = lax.axis_size("seq"), GROUP
    chunks = chunk_count(token_values.shape[1])
    levels = (count // group).bit_length() - 1
    where = lax.axis_index("seq").astype(jnp.int32)[None]
    inputs = (log_decay, b_inputs, c_inputs, token_values, grad_out)
    order = [(chunk, k) for chunk in range(chunks) for k in range(group - 1, -1, -1)]
    kept, states = first_states(head_dim, order[: group - 1], where, inputs)
    ld, b, c, x, dy, *factors = kept
    late = order[group:] + order[group - 1 : group]
    states.update(next_states(head_dim, late, where, factors, b, c, x, dy))
    blocks = [
        exchange([states[chunk, k][3] for k in range(group)]) for chunk in range(chunks)
    ]
    setup = inner_setup(head_dim, ld, b, c, [states[late[-1]][0]])

    def to_group(block, k):
        return lax.ppermute(block, "seq", [(s, s ^ (k * group)) for s in range(count)])

    every = [(chunk, m) for chunk in range(chunks) for m in range(group)]
    worked = [every[1:3]] + [every[chunk * group :][:2] for chunk in range(1, chunks)]
    rest = [one for one in every[1:] if not any(one in some for some in worked)]
    entries, inner, sums = [], {}, []

    def add_inner(some, after, hides=True):
        found, sums[:] = inner_terms(head_dim, some, setup, b, c, x, dy, sums, after, hides)
        inner.update(found)

    own = [totals(state, 0, where, blocks[0], setup[-1:])]
    add_inner(every[:1], own[0], False)
    own += [totals(state, 0, where, blocks[chunk], sums[:1]) for chunk in range(1, chunks)]
    for chunk in range(chunks):
        (total,) = own[chunk]
        received = [to_group(total, 1)]
        for level in range(levels - 1):
            last = level == levels - 2
            total = merged(state, level, last, where, total, received[level], [])
            received.append(to_group(total, 2 << level))
        add_inner(worked[chunk], [total])
        found = member_entries(state, False, where, blocks[chunk], received, sums[:1])
        entries.append(exchange(found))
    add_inner(rest, found[:1])

    values = []
    for chunk in range(chunks):
        last = chunk == chunks - 1
        ours = [states[chunk, k] for k in range(group)]
        scaled = [one for k in range(group) for one in ours[k][:2]]
        spread = [one[2] for one in ours]
        sums = entry_parts(last, scaled, *sums, entries[chunk], values)
        local = [inner[chunk, m] for m in range(group)]
        values.append(
            entry_values(chunk, chunks, where, spread, b, local, entries[chunk], values)
        )
    both = over_heads(sums[0])
    return values[-1], both[:length], both[length:]


def solution(mesh):
    in_specs = (
        P("seq", "head"),
        P("seq", None),
        P("seq", None),
        P("head", "seq"),
        P("seq", "head"),
    )
    out_specs = (P("seq", "head"), P("seq", None), P("seq", None))
    return jax.shard_map(shards, mesh=mesh, in_specs=in_specs, out_specs=out_specs, check_vma=False)
```

```python
import functools

import jax
import jax.numpy as jnp
from jax import lax
from jax.experimental import pallas as pl
from jax.experimental.pallas import tpu as pltpu
from jax.sharding import PartitionSpec as P

BF16 = jnp.bfloat16
F32 = jnp.float32
LANES = 128
GROUP = 4
TAIL = 16
LOG2E = 1.4426950408889634
MIB = 1024 * 1024

NN = (((1,), (0,)), ((), ()))
NT = (((1,), (1,)), ((), ()))
TN = (((0,), (0,)), ((), ()))


def dot(a, b, dims):
    return lax.dot_general(a, b, dims, preferred_element_type=F32)


def iota(shape, dim):
    return lax.broadcasted_iota(jnp.int32, shape, dim)


def three(values):
    high = values.astype(BF16)
    rest = values - high.astype(F32)
    mid = rest.astype(BF16)
    return high, mid, (rest - mid.astype(F32)).astype(BF16)


SLOT = LANES // 4


def summed(mask, terms):
    heads, length = terms[0].shape
    gap = [] if heads == SLOT else [jnp.zeros((SLOT - heads, length), BF16)]
    rows = [r for t in terms for r in [t] + gap] + [jnp.zeros((SLOT, length), BF16)]
    each = dot(mask, jnp.concatenate(rows, axis=0), NT)
    return each + pltpu.roll(each, LANES - SLOT, 1) + pltpu.roll(each, LANES - 2 * SLOT, 1)


def split_of(index, size):
    shift = size.bit_length() - 1
    return lax.shift_right_logical(index, shift) if size == 1 << shift else index // size


def row_less_head(head_dim, width, rows=LANES):
    shape = (LANES, width)
    row = iota(shape, 0)
    if rows < LANES:
        row = row & (rows - 1)
    return row - split_of(iota(shape, 1), head_dim)


def head_of_lane(difference, first):
    return jnp.where(difference == first, 1.0, 0.0).astype(BF16)


def whole(count):
    return [pl.BlockSpec(memory_space=pltpu.VMEM)] * count


def in_hbm(*arrays):
    return [pltpu.with_memory_space_constraint(a, pltpu.HBM) for a in arrays]


SMEM = pl.BlockSpec(memory_space=pltpu.SMEM)
HBM = pl.BlockSpec(memory_space=pltpu.HBM)
ANY = pl.BlockSpec(memory_space=pl.ANY)


def params(mib):
    return pltpu.CompilerParams(vmem_limit_bytes=mib * MIB)


def cost(flops, size, transcendentals=0):
    return pl.CostEstimate(flops=flops, bytes_accessed=size, transcendentals=transcendentals)


def place_of(where):
    return where[0] & (GROUP - 1)


def bit_of(where, level):
    return (where[0] >> (level + GROUP.bit_length() - 1)) & 1 == 1


def chunk_count(width):
    return 2 if (width // GROUP) % (2 * LANES) == 0 else 1


def chunk_lanes(where, k, chunk, part, width):
    start = (place_of(where) ^ k) * (width // GROUP) + chunk * part
    return pl.ds(pl.multiple_of(start, part), part)


def masks_of(length):
    rows, other = iota((length, length), 0), iota((length, length), 1)
    after = jnp.where(other > rows, 1.0, 0.0).astype(BF16)
    return after, jnp.where(other <= rows, 1.0, 0.0).astype(BF16)


def factors_of(ld, after, until):
    length = ld.shape[1]
    terms = three(ld)
    into_end = jnp.exp(summed(after, terms)).astype(BF16)
    from_start = jnp.exp(summed(until, terms)).astype(BF16)
    total = jnp.exp(summed(jnp.ones((TAIL, length), BF16), terms))
    high = total.astype(BF16).astype(F32)
    halves = jnp.where(iota(total.shape, 0) < TAIL // 2, high, total - high).astype(BF16)
    return into_end, from_start, halves


def put_states(head_dim, pieces, where, operands, outs, ready):
    into_end, from_start, halves, b, c, x, dy = operands
    state, width = b.shape[1], x.shape[1]
    chunks = chunk_count(width)
    part = width // (GROUP * chunks)
    difference = row_less_head(head_dim, part)
    for side, (factors, proj, cols) in enumerate([(into_end, b, x), (from_start, c, dy)]):
        ready(side)
        turned = proj[...].T
        for n, (chunk, k) in enumerate(pieces):
            x_scaled, dy_scaled, spread, send = outs[4 * n : 4 * n + 4]
            lanes = chunk_lanes(where, k, chunk, part, width)
            first_head = ((place_of(where) ^ k) * chunks + chunk) * (part // head_dim)
            hot = head_of_lane(difference, first_head)
            wide = dot(factors, hot, NN).astype(BF16)
            if side == 0:
                spread[...] = wide
                send[2 * state :, :] = dot(halves, hot, NN).astype(BF16)
            piece = cols[:, lanes] * wide
            (dy_scaled if side else x_scaled)[...] = piece
            send[side * state : (side + 1) * state, :] = dot(turned, piece, NN).astype(BF16)


def first_states_kernel(head_dim, pieces, where, ld_in, b_in, c_in, x_in, dy_in, *refs):
    ld, b, c, x, dy, into_end, from_start, halves = refs[:8]
    outs, sems = refs[8:-1], refs[-1]
    pairs = [(ld_in, ld), (b_in, b), (x_in, x), (c_in, c), (dy_in, dy)]
    copies = [pltpu.make_async_copy(i, o, sems.at[n]) for n, (i, o) in enumerate(pairs)]
    for copy in copies[:3]:
        copy.start()
    masks = masks_of(ld.shape[1])
    copies[0].wait()
    for copy in copies[3:]:
        copy.start()
    factors = factors_of(ld[...], *masks)
    for ref, value in zip((into_end, from_start, halves), factors):
        ref[...] = value

    def ready(side):
        copies[1 + 2 * side].wait()
        copies[2 + 2 * side].wait()

    put_states(head_dim, pieces, where, (*factors, b, c, x, dy), outs, ready)


def next_states_kernel(head_dim, pieces, where, into_end, from_start, halves, *refs):
    operands = (into_end[...], from_start[...], halves[...], *refs[:4])
    outs = refs[-4 * len(pieces) :]
    put_states(head_dim, pieces, where, operands, outs, lambda side: None)


def states_shapes(n_parts, length, width, state):
    part = width // (GROUP * chunk_count(width))
    scaled = jax.ShapeDtypeStruct((length, part), BF16)
    send = jax.ShapeDtypeStruct((2 * state + TAIL, part), BF16)
    return [scaled, scaled, scaled, send] * n_parts


def by_piece(pieces, outs):
    return {piece: outs[4 * n : 4 * n + 4] for n, piece in enumerate(pieces)}


def first_states(head_dim, pieces, where, inputs):
    ld, b, c, x, dy = inputs
    (length, width), state = x.shape, b.shape[1]
    kept = [jax.ShapeDtypeStruct(a.shape, a.dtype) for a in inputs]
    kept += [jax.ShapeDtypeStruct((rows, LANES), BF16) for rows in (length, length, TAIL)]
    outs = kept + states_shapes(len(pieces), length, width, state)
    found = pl.pallas_call(
        functools.partial(first_states_kernel, head_dim, pieces),
        out_shape=outs,
        in_specs=[SMEM] + [HBM] * 5,
        out_specs=whole(len(outs)),
        scratch_shapes=[pltpu.SemaphoreType.DMA((5,))],
        compiler_params=params(8),
        cost_estimate=cost(2 * length * width * (state + LANES), 8 * length * width),
        name="first_states",
    )(where, *in_hbm(*inputs))
    return found[:8], by_piece(pieces, found[8:])


def next_states(head_dim, pieces, where, factors, b, c, x, dy):
    (length, width), state = x.shape, b.shape[1]
    outs = states_shapes(len(pieces), length, width, state)
    found = pl.pallas_call(
        functools.partial(next_states_kernel, head_dim, pieces),
        out_shape=outs,
        in_specs=[SMEM] + whole(7),
        out_specs=whole(len(outs)),
        compiler_params=params(8),
        cost_estimate=cost(2 * length * width * (state + LANES), 4 * length * width),
        name="next_states",
    )(where, *factors, b, c, x, dy)
    return by_piece(pieces, found)


def decay_of(tail):
    tail = tail.astype(F32)
    return tail[:1, :] + tail[TAIL // 2 : TAIL // 2 + 1, :]


def put_decay(ref, first, factor):
    high = factor.astype(BF16).astype(F32)
    shape = (TAIL, factor.shape[1])
    both = jnp.where(iota(shape, 0) < TAIL // 2, high, factor - high)
    ref[first:, :] = both.astype(BF16)


def sent_order(parts):
    return [parts[0], *parts[:0:-1]]


def in_order(group, forward):
    return list(range(group)) if forward else list(range(group - 1, -1, -1))


def side_rows(state, forward):
    return slice(0, state) if forward else slice(state, 2 * state)


def totals_kernel(state, levels, where, *refs):
    group = GROUP
    blocks, outs, sums = sent_order(refs[:group]), refs[-1 - levels : -1], refs[-1]
    for here in range(group):

        @pl.when(place_of(where) == here)
        def _(here=here):
            decays = [decay_of(blocks[q ^ here][2 * state :, :]) for q in range(group)]
            for forward in (True, False):
                rows, value = side_rows(state, forward), None
                for q in in_order(group, forward):
                    piece = blocks[q ^ here][rows, :].astype(F32)
                    value = piece if value is None else decays[q] * value + piece
                sums[rows, :] = value.astype(BF16)

    factor = decay_of(blocks[0][2 * state :, :])
    for block in blocks[1:]:
        factor = factor * decay_of(block[2 * state :, :])
    if not levels:
        put_decay(sums, 2 * state, factor)
    for level, out in enumerate(outs):
        put_decay(out, state, factor)
        for forward in (True, False):

            @pl.when(bit_of(where, level) != forward)
            def _(out=out, forward=forward):
                out[:state, :] = sums[side_rows(state, forward), :]


def totals(state, levels, where, blocks, after):
    part = blocks[0].shape[1]
    outs = [jax.ShapeDtypeStruct((state + TAIL, part), BF16)] * levels
    if not levels:
        outs = [jax.ShapeDtypeStruct(blocks[0].shape, BF16)]
    return pl.pallas_call(
        functools.partial(totals_kernel, state, levels),
        out_shape=outs,
        in_specs=[SMEM] + whole(len(blocks)) + [ANY] * len(after),
        out_specs=whole(len(outs)),
        scratch_shapes=[pltpu.VMEM((2 * state, part), BF16)] if levels else [],
        compiler_params=params(4),
        cost_estimate=cost(8 * blocks[0].size, 10 * blocks[0].size),
        name="totals",
    )(where, *sent_order(blocks), *after)


def merged_kernel(state, level, last, where, own, received, *refs):
    out = refs[-1]
    d_own, d_other = decay_of(own[2 * state :, :]), decay_of(received[2 * state :, :])
    upper = bit_of(where, level)
    later = bit_of(where, level + 1)
    for is_upper in (False, True):
        for forward in (True, False):
            chosen = upper == is_upper
            if last:
                chosen = chosen & (later != forward)

            @pl.when(chosen)
            def _(is_upper=is_upper, forward=forward):
                rows = side_rows(state, forward)
                mine, other = own[rows, :].astype(F32), received[rows, :].astype(F32)
                value = mine + d_own * other if is_upper == forward else other + d_other * mine
                out[slice(0, state) if last else rows, :] = value.astype(BF16)

    if not last:
        put_decay(out, 2 * state, d_own * d_other)


def merged(state, level, last, where, own, received, after):
    rows = state if last else own.shape[0]
    return pl.pallas_call(
        functools.partial(merged_kernel, state, level, last),
        out_shape=pltpu.VMEM((rows, own.shape[1]), BF16),
        in_specs=[SMEM] + whole(2) + [ANY] * len(after),
        out_specs=whole(1)[0],
        compiler_params=params(4),
        cost_estimate=cost(4 * own.size, 6 * own.size),
        name="merged",
    )(where, own, received, *after)


def put_direct(state, groups, number, received, entry):
    for mine in range(groups):

        @pl.when(number == mine)
        def _(mine=mine):
            for forward in (True, False):
                rows = side_rows(state, forward)
                others = range(mine - 1, -1, -1) if forward else range(mine + 1, groups)
                value, factor = jnp.zeros((state, entry.shape[1]), F32), None
                for other in others:
                    r = received[(mine ^ other) - 1]
                    piece = r[:state, :].astype(F32)
                    value = piece if factor is None else value + factor * piece
                    d = decay_of(r[state:, :])
                    factor = d if factor is None else factor * d
                entry[rows, :] = value


def put_rounds(state, where, received, entry):
    for forward in (True, False):
        value, factor = None, 1.0
        for level, r in enumerate(received):
            gets = bit_of(where, level) == forward
            both = r.shape[0] > 2 * state
            rows = side_rows(state, forward) if both else slice(0, state)
            piece = r[rows, :].astype(F32) * jnp.where(gets, 1.0, 0.0)
            value = piece if value is None else value + factor * piece
            if both:
                factor = factor * jnp.where(gets, decay_of(r[2 * state :, :]), 1.0)
        entry[side_rows(state, forward), :] = value


def members_kernel(state, direct, n_received, where, *refs):
    received, refs = refs[:n_received], refs[n_received:]
    group = GROUP
    blocks, outs, entry = refs[:group], refs[-1 - group : -1], refs[-1]
    if direct:
        put_direct(state, n_received + 1, where[0] // group, received, entry)
    else:
        put_rounds(state, where, received, entry)
    for here in range(group):

        @pl.when(place_of(where) == here)
        def _(here=here):
            decays = [decay_of(blocks[q ^ here][2 * state :, :]) for q in range(group)]
            for forward in (True, False):
                rows, order = side_rows(state, forward), in_order(group, forward)
                value = entry[rows, :]
                for q in order:
                    outs[q ^ here][rows, :] = value.astype(BF16)
                    if q != order[-1]:
                        value = decays[q] * value + blocks[q ^ here][rows, :].astype(F32)


def member_entries(state, direct, where, blocks, received, after):
    group, part = len(blocks), blocks[0].shape[1]
    return pl.pallas_call(
        functools.partial(members_kernel, state, direct, len(received)),
        out_shape=[jax.ShapeDtypeStruct((2 * state, part), BF16)] * group,
        in_specs=[SMEM] + whole(group + len(received)) + [ANY] * len(after),
        out_specs=whole(group),
        scratch_shapes=[pltpu.VMEM((2 * state, part), F32)],
        compiler_params=params(4),
        cost_estimate=cost(12 * blocks[0].size, 16 * blocks[0].size),
        name="member_entries",
    )(where, *received, *blocks, *after)


def exchange(parts):
    count = lax.axis_size("seq")
    out = list(parts)
    for k in range(len(parts) - 1, 0, -1):
        out[k] = lax.ppermute(parts[k], "seq", [(s, s ^ k) for s in range(count)])
    return out


def split_pairs(first, count):
    if count == 1:
        return []
    middle = first + count // 2
    return (
        [(first, middle, first + count)]
        + split_pairs(first, middle - first)
        + split_pairs(middle, first + count - middle)
    )


def grouped_cuts(pieces):
    groups = {}
    for cut in split_pairs(0, pieces):
        groups.setdefault((cut[1] - cut[0], cut[2] - cut[1]), []).append(cut)
    return list(groups.items())


def rows_of(first, end, piece):
    return slice(first * piece, end * piece)


def setup_kernel(piece, ld, b, c, *refs):
    near, cum_terms = refs[-2:]
    heads, length = ld.shape
    rows, other = iota((length, length), 0), iota((length, length), 1)
    mask = jnp.where(other <= rows, 1.0, 0.0).astype(BF16)
    cum = summed(mask, three(ld[...] * LOG2E))
    lane = iota(cum.shape, 1)
    in_slots = jnp.where(lane < SLOT, cum, 0.0)
    in_slots = in_slots + pltpu.roll(in_slots, SLOT, 1) + pltpu.roll(in_slots, 2 * SLOT, 1)
    high, mid, low = three(in_slots)
    cum_terms[...] = jnp.where(lane < SLOT, high, jnp.where(lane < 2 * SLOT, mid, low))
    keep = iota((piece, piece), 0) <= iota((piece, piece), 1)
    pieces = length // piece
    for n in range(pieces):
        here = rows_of(n, n + 1, piece)
        near[here, :] = jnp.where(keep, dot(b[here, :], c[here, :], NT), 0.0).astype(BF16)
    cuts = [cut for _, same in grouped_cuts(pieces) for cut in same]
    for (lo, mid_, hi), far in zip(cuts, refs):
        left, right = rows_of(lo, mid_, piece), rows_of(mid_, hi, piece)
        far[...] = dot(b[left, :], c[right, :], NT).astype(BF16)


def inner_setup(piece, ld, b, c, after):
    length = b.shape[0]
    cuts = [cut for _, same in grouped_cuts(length // piece) for cut in same]
    outs = [
        jax.ShapeDtypeStruct(((mid - lo) * piece, (hi - mid) * piece), BF16) for lo, mid, hi in cuts
    ]
    outs.append(jax.ShapeDtypeStruct((length, piece), BF16))
    outs.append(jax.ShapeDtypeStruct((length, LANES), BF16))
    return pl.pallas_call(
        functools.partial(setup_kernel_after, piece, len(after)),
        out_shape=outs,
        in_specs=whole(3) + [ANY] * len(after),
        out_specs=whole(len(outs)),
        compiler_params=params(4),
        cost_estimate=cost(8 * b.size * length, 8 * b.size),
        name="inner_setup",
    )(ld, b, c, *after)


def setup_kernel_after(piece, n_after, ld, b, c, *refs):
    setup_kernel(piece, ld, b, c, *refs[n_after:])


def inner_kernel(head_dim, worked, n_before, n_after, b, c, x, dy, *refs):
    length, width = x.shape
    piece = head_dim
    pieces = length // piece
    groups = grouped_cuts(pieces)
    n_cuts = sum(len(same) for _, same in groups)
    fars, (near, cum_terms), refs = refs[:n_cuts], refs[n_cuts : n_cuts + 2], refs[n_cuts + 2 :]
    before, refs = refs[:n_before], refs[n_before + n_after :]
    dx_outs, (db_out, dc_out, x_near, dy_near, *scratch) = refs[: len(worked)], refs[len(worked) :]
    lefts, rights = scratch[: len(groups)], scratch[len(groups) :]
    part = dx_outs[0].shape[1]
    difference = row_less_head(head_dim, part, SLOT)

    for at, (chunk, m) in enumerate(worked):
        owned = m * (width // GROUP) + chunk * part
        lanes, here = slice(owned, owned + part), slice(at * part, (at + 1) * part)
        cum = dot(cum_terms[...], head_of_lane(difference, owned // head_dim), NN)
        dx = []
        for n in range(pieces):
            rows = rows_of(n, n + 1, piece)
            middle = cum[n * piece + piece // 2 : n * piece + piece // 2 + 1, :]
            gap = middle - cum[rows, :]
            down, up = jnp.exp2(gap), jnp.exp2(-gap)
            x_near[rows, here] = (x[rows, lanes].astype(F32) * down).astype(BF16)
            dy_piece = (dy[rows, lanes].astype(F32) * up).astype(BF16)
            dy_near[rows, here] = dy_piece
            dx.append(down * dot(near[rows, :], dy_piece, NN))
        far_of = iter(fars)
        for (_, same), left_ref, right_ref in zip(groups, lefts, rights):
            for g, (lo, mid, hi) in enumerate(same):
                left, right = rows_of(lo, mid, piece), rows_of(mid, hi, piece)
                edge = cum[mid * piece - 1 : mid * piece, :]
                to_edge = jnp.exp2(edge - cum[left, :])
                from_edge = jnp.exp2(cum[right, :] - edge)
                x_left = (x[left, lanes].astype(F32) * to_edge).astype(BF16)
                dy_right = (dy[right, lanes].astype(F32) * from_edge).astype(BF16)
                left_ref[rows_of(g, g + 1, (mid - lo) * piece), here] = x_left
                right_ref[rows_of(g, g + 1, (hi - mid) * piece), here] = dy_right
                far = to_edge * dot(next(far_of)[...], dy_right, NN)
                for n in range(lo, mid):
                    dx[n] = dx[n] + far[rows_of(n - lo, n - lo + 1, piece), :]
        for n in range(pieces):
            dx_outs[at][rows_of(n, n + 1, piece), :] = dx[n].astype(BF16)

    if before:
        db_out[...] = before[0][...]
        dc_out[...] = before[1][...]
    else:
        db_out[...] = jnp.zeros_like(db_out)
        dc_out[...] = jnp.zeros_like(dc_out)
    batch = 4
    for first in range(0, pieces, batch):
        rows = rows_of(first, min(first + batch, pieces), piece)
        total = dot(x_near[rows, :], dy_near[rows, :], NT)
        row, col = iota(total.shape, 0), iota(total.shape, 1)
        keep = (split_of(row, piece) == split_of(col, piece)) & (row <= col)
        weighted = jnp.where(keep, total, 0.0).astype(BF16)
        db_out[rows, :] += dot(weighted, c[rows, :], NN)
        dc_out[rows, :] += dot(weighted, b[rows, :], TN)
    for ((n_left, n_right), same), left_ref, right_ref in zip(groups, lefts, rights):
        total = dot(left_ref[...], right_ref[...], NT)
        if len(same) > 1:
            row, col = iota(total.shape, 0), iota(total.shape, 1)
            same_cut = split_of(row, n_left * piece) == split_of(col, n_right * piece)
            total = jnp.where(same_cut, total, 0.0)
        weighted = total.astype(BF16)
        b_left = jnp.concatenate([b[rows_of(lo, mid, piece), :] for lo, mid, _ in same], axis=0)
        c_right = jnp.concatenate([c[rows_of(mid, hi, piece), :] for _, mid, hi in same], axis=0)
        db = dot(weighted, c_right, NN)
        dc = dot(weighted, b_left, TN)
        for g, (lo, mid, hi) in enumerate(same):
            db_out[rows_of(lo, mid, piece), :] += db[rows_of(g, g + 1, n_left * piece), :]
            dc_out[rows_of(mid, hi, piece), :] += dc[rows_of(g, g + 1, n_right * piece), :]


def inner_terms(head_dim, worked, setup, b, c, x, dy, before, after, hides=True):
    (length, state), width = b.shape, x.shape[1]
    part = width // (GROUP * chunk_count(width))
    used = part * len(worked)
    groups = grouped_cuts(length // head_dim)
    sizes = [[len(same) * n * head_dim for n in halves] for halves, same in groups]
    found = pl.pallas_call(
        functools.partial(inner_kernel, head_dim, worked, len(before), len(after)),
        out_shape=[jax.ShapeDtypeStruct((length, part), BF16)] * len(worked)
        + [jax.ShapeDtypeStruct((length, state), F32)] * 2,
        in_specs=whole(4 + len(setup) + len(before)) + [ANY] * len(after),
        out_specs=whole(len(worked) + 2),
        scratch_shapes=[pltpu.VMEM((length, used), BF16)] * 2
        + [pltpu.VMEM((left, used), BF16) for left, _ in sizes]
        + [pltpu.VMEM((right, used), BF16) for _, right in sizes],
        compiler_params=params(16),
        cost_estimate=cost(8 * x.size * state, 4 * x.size, 2 * x.size) if hides else cost(1, 1),
        name="inner_terms",
    )(b, c, x, dy, *setup, *before, *after)
    return dict(zip(worked, found)), list(found[-2:])


def parts_kernel(last, ks, db_before, dc_before, *refs):
    scaled, refs = refs[: 2 * len(ks)], refs[2 * len(ks) :]
    entries, outs = refs[: len(ks)], refs[-1 if last else -2 :]
    length, state = db_before.shape
    db, dc = db_before[...], dc_before[...]
    for n, entry in enumerate(entries):
        db = db + dot(scaled[2 * n][...], entry[state:, :], NT)
        dc = dc + dot(scaled[2 * n + 1][...], entry[:state, :], NT)
    if last:
        outs[0][:length, :] = db.astype(BF16)
        outs[0][length:, :] = dc.astype(BF16)
    else:
        outs[0][...] = db
        outs[1][...] = dc


def entry_parts(last, ks, scaled, db_before, dc_before, entries, after):
    length, state = db_before.shape
    one = jax.ShapeDtypeStruct((length, state), F32)
    outs = [jax.ShapeDtypeStruct((2 * length, state), BF16)] if last else [one, one]
    operands = [one for k in ks for one in scaled[k]] + [entries[k] for k in ks]
    return pl.pallas_call(
        functools.partial(parts_kernel, last, ks),
        out_shape=outs,
        in_specs=whole(2 + len(operands)) + [ANY] * len(after),
        out_specs=whole(len(outs)),
        compiler_params=params(8),
        cost_estimate=cost(2 * len(operands) * scaled[0][0].size * state, scaled[0][0].size),
        name="entry_parts",
    )(db_before, dc_before, *operands, *after)


def put_values(where, spread, b, local_parts, dx_local, entries, put):
    state, part = b.shape[1], entries[0].shape[1]
    for m, one in enumerate(local_parts):
        dx_local[:, m * part : (m + 1) * part] = one[...]
    for k, entry in enumerate(entries):
        here = slice(k * part, (k + 1) * part)
        local = dx_local[:, pl.ds(pl.multiple_of((place_of(where) ^ k) * part, part), part)]
        far = spread[k][...].astype(F32) * dot(b[...], entry[state:, :], NN)
        put(k, here, (local.astype(F32) + far).astype(BF16))


def values_kernel(where, b, *refs):
    local_parts, spread = refs[:GROUP], refs[GROUP : 2 * GROUP]
    entries, (out, dx_local) = sent_order(refs[2 * GROUP : 3 * GROUP]), refs[-2:]

    def put(k, here, value):
        out[:, here] = value

    put_values(where, spread, b, local_parts, dx_local, entries, put)


def last_values_kernel(chunks, where, b, *refs):
    local_parts, spread, refs = refs[:GROUP], refs[GROUP : 2 * GROUP], refs[2 * GROUP :]
    entries, before = sent_order(refs[:GROUP]), refs[GROUP : GROUP + chunks - 1]
    out, dx, dx_local, sems = refs[-4:]
    part = entries[0].shape[1]
    stores = []

    def store(chunk, k, source):
        lanes = chunk_lanes(where, k, chunk, part, out.shape[1])
        at = sems.at[chunk * GROUP + k]
        stores.append(pltpu.make_async_copy(source, out.at[:, lanes], at))
        stores[-1].start()

    for chunk, values in enumerate(before):
        for k in range(GROUP):
            store(chunk, k, values.at[:, pl.ds(k * part, part)])

    def put(k, here, value):
        dx[k] = value
        store(chunks - 1, k, dx.at[k])

    put_values(where, spread, b, local_parts, dx_local, entries, put)
    for one in stores:
        one.wait()


def entry_values(chunk, chunks, where, spread, b, local_parts, entries, before):
    length, part = b.shape[0], entries[0].shape[1]
    last = chunk == chunks - 1
    estimate = cost(8 * local_parts[0].size * b.shape[1], 16 * local_parts[0].size)
    operands = [where, b, *local_parts, *spread, *sent_order(entries)]
    if not last:
        return pl.pallas_call(
            values_kernel,
            out_shape=jax.ShapeDtypeStruct((length, GROUP * part), BF16),
            in_specs=[SMEM] + whole(1 + 3 * GROUP),
            out_specs=whole(1)[0],
            scratch_shapes=[pltpu.VMEM((length, GROUP * part), BF16)],
            compiler_params=params(8),
            cost_estimate=estimate,
            name="entry_values",
        )(*operands)
    return pl.pallas_call(
        functools.partial(last_values_kernel, chunks),
        out_shape=pltpu.HBM((length, chunks * GROUP * part), BF16),
        in_specs=[SMEM] + whole(1 + 3 * GROUP + len(before)),
        out_specs=HBM,
        scratch_shapes=[
            pltpu.VMEM((GROUP, length, part), BF16),
            pltpu.VMEM((length, GROUP * part), BF16),
            pltpu.SemaphoreType.DMA((chunks * GROUP,)),
        ],
        compiler_params=params(8),
        cost_estimate=estimate,
        name="last_values",
    )(*operands, *before)


def sum_kernel(*refs):
    parts, (db, dc) = refs[:-2], refs[-2:]
    length = db.shape[0]
    for out, rows in ((db, slice(0, length)), (dc, slice(length, 2 * length))):
        total = parts[0][rows, :].astype(F32)
        for part in parts[1:]:
            total = total + part[rows, :].astype(F32)
        out[...] = total.astype(BF16)


def over_heads(part):
    count, (rows, state) = lax.axis_size("head"), part.shape
    parts = [part]
    for shift in range(1, count):
        pairs = [(s, (s + shift) % count) for s in range(count)]
        parts.append(lax.ppermute(part, "head", pairs))
    return pl.pallas_call(
        sum_kernel,
        out_shape=[jax.ShapeDtypeStruct((rows // 2, state), BF16)] * 2,
        in_specs=whole(count),
        out_specs=whole(2),
        compiler_params=params(4),
        cost_estimate=cost(count * part.size, 2 * count * part.size),
        name="sum_over_heads",
    )(*parts)


def shards(token_values, b_inputs, c_inputs, log_decay, grad_out):
    head_dim = token_values.shape[1] // log_decay.shape[0]
    state = b_inputs.shape[1]
    count, group = lax.axis_size("seq"), GROUP
    chunks = chunk_count(token_values.shape[1])
    levels = (count // group).bit_length() - 1
    where = lax.axis_index("seq").astype(jnp.int32)[None]
    inputs = (log_decay, b_inputs, c_inputs, token_values, grad_out)
    order = [(chunk, k) for chunk in range(chunks) for k in range(group - 1, -1, -1)]
    kept, states = first_states(head_dim, order[: group - 1], where, inputs)
    ld, b, c, x, dy, *factors = kept
    late = order[group:] + order[group - 1 : group]
    states.update(next_states(head_dim, late, where, factors, b, c, x, dy))
    blocks = [
        exchange([states[chunk, k][3] for k in range(group)]) for chunk in range(chunks)
    ]
    setup = inner_setup(head_dim, ld, b, c, [states[late[-1]][0]])

    def to_group(block, k):
        return lax.ppermute(block, "seq", [(s, s ^ (k * group)) for s in range(count)])

    every = [(chunk, m) for chunk in range(chunks) for m in range(group)]
    worked = [every[1:4]] + [every[chunk * group :][:2] for chunk in range(1, chunks)]
    rest = [one for one in every[1:] if not any(one in some for some in worked)]
    entries, inner, sums = [], {}, []

    def add_inner(some, after, hides=True):
        found, sums[:] = inner_terms(head_dim, some, setup, b, c, x, dy, sums, after, hides)
        inner.update(found)

    own = [totals(state, 0, where, blocks[0], setup[-1:])]
    add_inner(every[:1], own[0], False)
    own += [totals(state, 0, where, blocks[chunk], sums[:1]) for chunk in range(1, chunks)]
    for chunk in range(chunks):
        (total,) = own[chunk]
        received = [to_group(total, 1)]
        for level in range(levels - 1):
            last = level == levels - 2
            total = merged(state, level, last, where, total, received[level], [])
            received.append(to_group(total, 2 << level))
        add_inner(worked[chunk], [total])
        found = member_entries(state, False, where, blocks[chunk], received, sums[:1])
        entries.append(exchange(found))
    if rest:
        add_inner(rest, found[:1])

    values = []
    for chunk in range(chunks):
        last = chunk == chunks - 1
        ours = [states[chunk, k] for k in range(group)]
        scaled = [one[:2] for one in ours]
        spread = [one[2] for one in ours]
        if last:
            sums = entry_parts(False, (0, 3), scaled, *sums, entries[chunk], values)
        ks = (2, 1) if last else (0, 3, 2, 1)
        sums = entry_parts(last, ks, scaled, *sums, entries[chunk], [])
        local = [inner[chunk, m] for m in range(group)]
        values.append(
            entry_values(chunk, chunks, where, spread, b, local, entries[chunk], values)
        )
    return (values[-1], *over_heads(sums[0]))


def solution(mesh):
    in_specs = (
        P("seq", "head"),
        P("seq", None),
        P("seq", None),
        P("head", "seq"),
        P("seq", "head"),
    )
    out_specs = (P("seq", "head"), P("seq", None), P("seq", None))
    return jax.shard_map(shards, mesh=mesh, in_specs=in_specs, out_specs=out_specs, check_vma=False)
```

```python
import functools

import jax
import jax.numpy as jnp
from jax import lax
from jax.experimental import pallas as pl
from jax.experimental.pallas import tpu as pltpu
from jax.sharding import PartitionSpec as P

BF16 = jnp.bfloat16
F32 = jnp.float32
LANES = 128
GROUP = 4
TAIL = 16
LOG2E = 1.4426950408889634
MIB = 1024 * 1024

NN = (((1,), (0,)), ((), ()))
NT = (((1,), (1,)), ((), ()))
TN = (((0,), (0,)), ((), ()))


def dot(a, b, dims):
    return lax.dot_general(a, b, dims, preferred_element_type=F32)


def iota(shape, dim):
    return lax.broadcasted_iota(jnp.int32, shape, dim)


def three(values):
    high = values.astype(BF16)
    rest = values - high.astype(F32)
    mid = rest.astype(BF16)
    return high, mid, (rest - mid.astype(F32)).astype(BF16)


SLOT = LANES // 4


def summed(mask, terms):
    heads, length = terms[0].shape
    gap = [] if heads == SLOT else [jnp.zeros((SLOT - heads, length), BF16)]
    rows = [r for t in terms for r in [t] + gap] + [jnp.zeros((SLOT, length), BF16)]
    each = dot(mask, jnp.concatenate(rows, axis=0), NT)
    return each + pltpu.roll(each, LANES - SLOT, 1) + pltpu.roll(each, LANES - 2 * SLOT, 1)


def split_of(index, size):
    shift = size.bit_length() - 1
    return lax.shift_right_logical(index, shift) if size == 1 << shift else index // size


def row_less_head(head_dim, width, rows=LANES):
    shape = (LANES, width)
    row = iota(shape, 0)
    if rows < LANES:
        row = row & (rows - 1)
    return row - split_of(iota(shape, 1), head_dim)


def head_of_lane(difference, first):
    return jnp.where(difference == first, 1.0, 0.0).astype(BF16)


def whole(count):
    return [pl.BlockSpec(memory_space=pltpu.VMEM)] * count


def in_hbm(*arrays):
    return [pltpu.with_memory_space_constraint(a, pltpu.HBM) for a in arrays]


SMEM = pl.BlockSpec(memory_space=pltpu.SMEM)
HBM = pl.BlockSpec(memory_space=pltpu.HBM)
ANY = pl.BlockSpec(memory_space=pl.ANY)


def params(mib):
    return pltpu.CompilerParams(vmem_limit_bytes=mib * MIB)


def cost(flops, size, transcendentals=0):
    return pl.CostEstimate(flops=flops, bytes_accessed=size, transcendentals=transcendentals)


def place_of(where):
    return where[0] & (GROUP - 1)


def bit_of(where, level):
    return (where[0] >> (level + GROUP.bit_length() - 1)) & 1 == 1


def chunk_count(width):
    return 2 if (width // GROUP) % (2 * LANES) == 0 else 1


def chunk_lanes(where, k, chunk, part, width):
    start = (place_of(where) ^ k) * (width // GROUP) + chunk * part
    return pl.ds(pl.multiple_of(start, part), part)


def masks_of(length):
    rows, other = iota((length, length), 0), iota((length, length), 1)
    after = jnp.where(other > rows, 1.0, 0.0).astype(BF16)
    return after, jnp.where(other <= rows, 1.0, 0.0).astype(BF16)


def factors_of(ld, after, until):
    length = ld.shape[1]
    terms = three(ld)
    into_end = jnp.exp(summed(after, terms)).astype(BF16)
    from_start = jnp.exp(summed(until, terms)).astype(BF16)
    total = jnp.exp(summed(jnp.ones((TAIL, length), BF16), terms))
    high = total.astype(BF16).astype(F32)
    halves = jnp.where(iota(total.shape, 0) < TAIL // 2, high, total - high).astype(BF16)
    return into_end, from_start, halves


def put_states(head_dim, chunks, pieces, where, operands, outs, ready):
    into_end, from_start, halves, b, c, xs, dys = operands
    state, part = b.shape[1], xs[0].shape[1] // GROUP
    difference = row_less_head(head_dim, part)
    for side, (factors, proj, cols) in enumerate([(into_end, b, xs), (from_start, c, dys)]):
        turned = None
        for n, (chunk, k) in enumerate(pieces):
            if n == 0 or chunk != pieces[n - 1][0]:
                ready(side, chunk)
            if turned is None:
                turned = proj[...].T
            x_scaled, dy_scaled, spread, send = outs[4 * n : 4 * n + 4]
            member = place_of(where) ^ k
            first_head = (member * chunks + chunk) * (part // head_dim)
            hot = head_of_lane(difference, first_head)
            wide = dot(factors, hot, NN).astype(BF16)
            if side == 0:
                spread[...] = wide
                send[2 * state :, :] = dot(halves, hot, NN).astype(BF16)
            lanes = pl.ds(pl.multiple_of(member * part, part), part)
            piece = cols[chunk][:, lanes] * wide
            (dy_scaled if side else x_scaled)[...] = piece
            send[side * state : (side + 1) * state, :] = dot(turned, piece, NN).astype(BF16)


def load_chunk(chunk, chunks, source, target, sems, first):
    part = target.shape[1] // GROUP
    copies = []
    for m in range(GROUP):
        lanes = pl.ds((m * chunks + chunk) * part, part)
        at = target.at[:, pl.ds(m * part, part)]
        copies.append(pltpu.make_async_copy(source.at[:, lanes], at, sems.at[first + m]))
        copies[-1].start()
    return copies


def first_states_kernel(head_dim, chunks, pieces, where, ld_in, b_in, c_in, x_in, dy_in, *refs):
    ld, b, c, x, dy, into_end, from_start, halves = refs[:8]
    outs, sems = refs[8:-1], refs[-1]

    def load(n, source, target):
        copy = pltpu.make_async_copy(source, target, sems.at[n])
        copy.start()
        return copy

    first = load(0, ld_in, ld)
    copies = [
        [load(1, b_in, b), *load_chunk(0, chunks, x_in, x, sems, 3)],
        [load(2, c_in, c), *load_chunk(0, chunks, dy_in, dy, sems, 3 + GROUP)],
    ]
    masks = masks_of(ld.shape[1])
    first.wait()
    factors = factors_of(ld[...], *masks)
    for ref, value in zip((into_end, from_start, halves), factors):
        ref[...] = value

    def ready(side, chunk):
        for copy in copies[side]:
            copy.wait()

    operands = (*factors, b, c, {0: x}, {0: dy})
    put_states(head_dim, chunks, pieces, where, operands, outs, ready)


def next_states_kernel(head_dim, chunks, pieces, where, into_end, from_start, halves, *refs):
    b, c, x, dy, x_in, dy_in = refs[:6]
    outs, sems = refs[6:-1], refs[-1]
    kept, outs = outs[: 2 * (chunks - 1)], outs[2 * (chunks - 1) :]
    xs, dys, copies = {0: x}, {0: dy}, {}
    for chunk in range(1, chunks):
        xs[chunk], dys[chunk] = kept[2 * chunk - 2 : 2 * chunk]
        at = 2 * GROUP * (chunk - 1)
        copies[0, chunk] = load_chunk(chunk, chunks, x_in, xs[chunk], sems, at)
        copies[1, chunk] = load_chunk(chunk, chunks, dy_in, dys[chunk], sems, at + GROUP)

    def ready(side, chunk):
        for copy in copies.get((side, chunk), []):
            copy.wait()

    operands = (into_end[...], from_start[...], halves[...], b, c, xs, dys)
    put_states(head_dim, chunks, pieces, where, operands, outs, ready)


def states_shapes(n_parts, length, width, state):
    part = width // (GROUP * chunk_count(width))
    scaled = jax.ShapeDtypeStruct((length, part), BF16)
    send = jax.ShapeDtypeStruct((2 * state + TAIL, part), BF16)
    return [scaled, scaled, scaled, send] * n_parts


def by_piece(pieces, outs):
    return {piece: outs[4 * n : 4 * n + 4] for n, piece in enumerate(pieces)}


def first_states(head_dim, pieces, where, inputs):
    ld, b, c, x, dy = inputs
    (length, width), state = x.shape, b.shape[1]
    chunks = chunk_count(width)
    columns = jax.ShapeDtypeStruct((length, width // chunks), BF16)
    kept = [jax.ShapeDtypeStruct(a.shape, a.dtype) for a in (ld, b, c)] + [columns] * 2
    kept += [jax.ShapeDtypeStruct((rows, LANES), BF16) for rows in (length, length, TAIL)]
    outs = kept + states_shapes(len(pieces), length, width, state)
    found = pl.pallas_call(
        functools.partial(first_states_kernel, head_dim, chunks, pieces),
        out_shape=outs,
        in_specs=[SMEM] + [HBM] * 5,
        out_specs=whole(len(outs)),
        scratch_shapes=[pltpu.SemaphoreType.DMA((3 + 2 * GROUP,))],
        compiler_params=params(8),
        cost_estimate=cost(2 * length * width * (state + LANES), 8 * length * width),
        name="first_states",
    )(where, *in_hbm(*inputs))
    return found[:8], by_piece(pieces, found[8:])


def next_states(head_dim, pieces, where, factors, b, c, x_0, dy_0, x, dy):
    (length, width), state = x.shape, b.shape[1]
    chunks = chunk_count(width)
    n_kept = 2 * (chunks - 1)
    outs = [jax.ShapeDtypeStruct(x_0.shape, BF16)] * n_kept
    outs += states_shapes(len(pieces), length, width, state)
    found = pl.pallas_call(
        functools.partial(next_states_kernel, head_dim, chunks, pieces),
        out_shape=outs,
        in_specs=[SMEM] + whole(7) + [HBM] * 2,
        out_specs=whole(len(outs)),
        scratch_shapes=[pltpu.SemaphoreType.DMA((max(n_kept, 1) * GROUP,))],
        compiler_params=params(8),
        cost_estimate=cost(2 * length * width * (state + LANES), 4 * length * width),
        name="next_states",
    )(where, *factors, b, c, x_0, dy_0, *in_hbm(x, dy))
    return found[:n_kept], by_piece(pieces, found[n_kept:])


def decay_of(tail):
    tail = tail.astype(F32)
    return tail[:1, :] + tail[TAIL // 2 : TAIL // 2 + 1, :]


def put_decay(ref, first, factor):
    high = factor.astype(BF16).astype(F32)
    shape = (TAIL, factor.shape[1])
    both = jnp.where(iota(shape, 0) < TAIL // 2, high, factor - high)
    ref[first:, :] = both.astype(BF16)


def sent_order(parts):
    return [parts[0], *parts[:0:-1]]


def in_order(group, forward):
    return list(range(group)) if forward else list(range(group - 1, -1, -1))


def side_rows(state, forward):
    return slice(0, state) if forward else slice(state, 2 * state)


def totals_kernel(state, levels, where, *refs):
    group = GROUP
    blocks, outs, sums = sent_order(refs[:group]), refs[-1 - levels : -1], refs[-1]
    for here in range(group):

        @pl.when(place_of(where) == here)
        def _(here=here):
            decays = [decay_of(blocks[q ^ here][2 * state :, :]) for q in range(group)]
            for forward in (True, False):
                rows, value = side_rows(state, forward), None
                for q in in_order(group, forward):
                    piece = blocks[q ^ here][rows, :].astype(F32)
                    value = piece if value is None else decays[q] * value + piece
                sums[rows, :] = value.astype(BF16)

    factor = decay_of(blocks[0][2 * state :, :])
    for block in blocks[1:]:
        factor = factor * decay_of(block[2 * state :, :])
    if not levels:
        put_decay(sums, 2 * state, factor)
    for level, out in enumerate(outs):
        put_decay(out, state, factor)
        for forward in (True, False):

            @pl.when(bit_of(where, level) != forward)
            def _(out=out, forward=forward):
                out[:state, :] = sums[side_rows(state, forward), :]


def totals(state, levels, where, blocks, after):
    part = blocks[0].shape[1]
    outs = [jax.ShapeDtypeStruct((state + TAIL, part), BF16)] * levels
    if not levels:
        outs = [jax.ShapeDtypeStruct(blocks[0].shape, BF16)]
    return pl.pallas_call(
        functools.partial(totals_kernel, state, levels),
        out_shape=outs,
        in_specs=[SMEM] + whole(len(blocks)) + [ANY] * len(after),
        out_specs=whole(len(outs)),
        scratch_shapes=[pltpu.VMEM((2 * state, part), BF16)] if levels else [],
        compiler_params=params(4),
        cost_estimate=cost(8 * blocks[0].size, 10 * blocks[0].size),
        name="totals",
    )(where, *sent_order(blocks), *after)


def merged_kernel(state, level, last, where, own, received, *refs):
    out = refs[-1]
    d_own, d_other = decay_of(own[2 * state :, :]), decay_of(received[2 * state :, :])
    upper = bit_of(where, level)
    later = bit_of(where, level + 1)
    for is_upper in (False, True):
        for forward in (True, False):
            chosen = upper == is_upper
            if last:
                chosen = chosen & (later != forward)

            @pl.when(chosen)
            def _(is_upper=is_upper, forward=forward):
                rows = side_rows(state, forward)
                mine, other = own[rows, :].astype(F32), received[rows, :].astype(F32)
                value = mine + d_own * other if is_upper == forward else other + d_other * mine
                out[slice(0, state) if last else rows, :] = value.astype(BF16)

    if not last:
        put_decay(out, 2 * state, d_own * d_other)


def merged(state, level, last, where, own, received, after):
    rows = state if last else own.shape[0]
    return pl.pallas_call(
        functools.partial(merged_kernel, state, level, last),
        out_shape=pltpu.VMEM((rows, own.shape[1]), BF16),
        in_specs=[SMEM] + whole(2) + [ANY] * len(after),
        out_specs=whole(1)[0],
        compiler_params=params(4),
        cost_estimate=cost(4 * own.size, 6 * own.size),
        name="merged",
    )(where, own, received, *after)


def put_direct(state, groups, number, received, entry):
    for mine in range(groups):

        @pl.when(number == mine)
        def _(mine=mine):
            for forward in (True, False):
                rows = side_rows(state, forward)
                others = range(mine - 1, -1, -1) if forward else range(mine + 1, groups)
                value, factor = jnp.zeros((state, entry.shape[1]), F32), None
                for other in others:
                    r = received[(mine ^ other) - 1]
                    piece = r[:state, :].astype(F32)
                    value = piece if factor is None else value + factor * piece
                    d = decay_of(r[state:, :])
                    factor = d if factor is None else factor * d
                entry[rows, :] = value


def put_rounds(state, where, received, entry):
    for forward in (True, False):
        value, factor = None, 1.0
        for level, r in enumerate(received):
            gets = bit_of(where, level) == forward
            both = r.shape[0] > 2 * state
            rows = side_rows(state, forward) if both else slice(0, state)
            piece = r[rows, :].astype(F32) * jnp.where(gets, 1.0, 0.0)
            value = piece if value is None else value + factor * piece
            if both:
                factor = factor * jnp.where(gets, decay_of(r[2 * state :, :]), 1.0)
        entry[side_rows(state, forward), :] = value


def members_kernel(state, direct, n_received, where, *refs):
    received, refs = refs[:n_received], refs[n_received:]
    group = GROUP
    blocks, outs, entry = refs[:group], refs[-1 - group : -1], refs[-1]
    if direct:
        put_direct(state, n_received + 1, where[0] // group, received, entry)
    else:
        put_rounds(state, where, received, entry)
    for here in range(group):

        @pl.when(place_of(where) == here)
        def _(here=here):
            decays = [decay_of(blocks[q ^ here][2 * state :, :]) for q in range(group)]
            for forward in (True, False):
                rows, order = side_rows(state, forward), in_order(group, forward)
                value = entry[rows, :]
                for q in order:
                    outs[q ^ here][rows, :] = value.astype(BF16)
                    if q != order[-1]:
                        value = decays[q] * value + blocks[q ^ here][rows, :].astype(F32)


def member_entries(state, direct, where, blocks, received, after):
    group, part = len(blocks), blocks[0].shape[1]
    return pl.pallas_call(
        functools.partial(members_kernel, state, direct, len(received)),
        out_shape=[jax.ShapeDtypeStruct((2 * state, part), BF16)] * group,
        in_specs=[SMEM] + whole(group + len(received)) + [ANY] * len(after),
        out_specs=whole(group),
        scratch_shapes=[pltpu.VMEM((2 * state, part), F32)],
        compiler_params=params(4),
        cost_estimate=cost(12 * blocks[0].size, 16 * blocks[0].size),
        name="member_entries",
    )(where, *received, *blocks, *after)


def exchange(parts):
    count = lax.axis_size("seq")
    out = list(parts)
    for k in range(len(parts) - 1, 0, -1):
        out[k] = lax.ppermute(parts[k], "seq", [(s, s ^ k) for s in range(count)])
    return out


def split_pairs(first, count):
    if count == 1:
        return []
    middle = first + count // 2
    return (
        [(first, middle, first + count)]
        + split_pairs(first, middle - first)
        + split_pairs(middle, first + count - middle)
    )


def grouped_cuts(pieces):
    groups = {}
    for cut in split_pairs(0, pieces):
        groups.setdefault((cut[1] - cut[0], cut[2] - cut[1]), []).append(cut)
    return list(groups.items())


def rows_of(first, end, piece):
    return slice(first * piece, end * piece)


def setup_kernel(piece, ld, b, c, *refs):
    near, cum_terms = refs[-2:]
    heads, length = ld.shape
    rows, other = iota((length, length), 0), iota((length, length), 1)
    mask = jnp.where(other <= rows, 1.0, 0.0).astype(BF16)
    cum = summed(mask, three(ld[...] * LOG2E))
    lane = iota(cum.shape, 1)
    in_slots = jnp.where(lane < SLOT, cum, 0.0)
    in_slots = in_slots + pltpu.roll(in_slots, SLOT, 1) + pltpu.roll(in_slots, 2 * SLOT, 1)
    high, mid, low = three(in_slots)
    cum_terms[...] = jnp.where(lane < SLOT, high, jnp.where(lane < 2 * SLOT, mid, low))
    keep = iota((piece, piece), 0) <= iota((piece, piece), 1)
    pieces = length // piece
    for n in range(pieces):
        here = rows_of(n, n + 1, piece)
        near[here, :] = jnp.where(keep, dot(b[here, :], c[here, :], NT), 0.0).astype(BF16)
    cuts = [cut for _, same in grouped_cuts(pieces) for cut in same]
    for (lo, mid_, hi), far in zip(cuts, refs):
        left, right = rows_of(lo, mid_, piece), rows_of(mid_, hi, piece)
        far[...] = dot(b[left, :], c[right, :], NT).astype(BF16)


def inner_setup(piece, ld, b, c, after):
    length = b.shape[0]
    cuts = [cut for _, same in grouped_cuts(length // piece) for cut in same]
    outs = [
        jax.ShapeDtypeStruct(((mid - lo) * piece, (hi - mid) * piece), BF16) for lo, mid, hi in cuts
    ]
    outs.append(jax.ShapeDtypeStruct((length, piece), BF16))
    outs.append(jax.ShapeDtypeStruct((length, LANES), BF16))
    return pl.pallas_call(
        functools.partial(setup_kernel_after, piece, len(after)),
        out_shape=outs,
        in_specs=whole(3) + [ANY] * len(after),
        out_specs=whole(len(outs)),
        compiler_params=params(4),
        cost_estimate=cost(8 * b.size * length, 8 * b.size),
        name="inner_setup",
    )(ld, b, c, *after)


def setup_kernel_after(piece, n_after, ld, b, c, *refs):
    setup_kernel(piece, ld, b, c, *refs[n_after:])


def inner_kernel(head_dim, worked, chunks, n_before, n_after, b, c, *refs):
    xs, dys, refs = refs[:chunks], refs[chunks : 2 * chunks], refs[2 * chunks :]
    length, width = xs[0].shape
    piece = head_dim
    pieces = length // piece
    groups = grouped_cuts(pieces)
    n_cuts = sum(len(same) for _, same in groups)
    fars, (near, cum_terms), refs = refs[:n_cuts], refs[n_cuts : n_cuts + 2], refs[n_cuts + 2 :]
    before, refs = refs[:n_before], refs[n_before + n_after :]
    dx_outs, (db_out, dc_out, x_near, dy_near, *scratch) = refs[: len(worked)], refs[len(worked) :]
    lefts, rights = scratch[: len(groups)], scratch[len(groups) :]
    part = dx_outs[0].shape[1]
    difference = row_less_head(head_dim, part, SLOT)

    for at, (chunk, m) in enumerate(worked):
        x, dy, first_head = xs[chunk], dys[chunk], (m * chunks + chunk) * (part // head_dim)
        lanes, here = slice(m * part, (m + 1) * part), slice(at * part, (at + 1) * part)
        cum = dot(cum_terms[...], head_of_lane(difference, first_head), NN)
        dx = []
        for n in range(pieces):
            rows = rows_of(n, n + 1, piece)
            middle = cum[n * piece + piece // 2 : n * piece + piece // 2 + 1, :]
            gap = middle - cum[rows, :]
            down, up = jnp.exp2(gap), jnp.exp2(-gap)
            x_near[rows, here] = (x[rows, lanes].astype(F32) * down).astype(BF16)
            dy_piece = (dy[rows, lanes].astype(F32) * up).astype(BF16)
            dy_near[rows, here] = dy_piece
            dx.append(down * dot(near[rows, :], dy_piece, NN))
        far_of = iter(fars)
        for (_, same), left_ref, right_ref in zip(groups, lefts, rights):
            for g, (lo, mid, hi) in enumerate(same):
                left, right = rows_of(lo, mid, piece), rows_of(mid, hi, piece)
                edge = cum[mid * piece - 1 : mid * piece, :]
                to_edge = jnp.exp2(edge - cum[left, :])
                from_edge = jnp.exp2(cum[right, :] - edge)
                x_left = (x[left, lanes].astype(F32) * to_edge).astype(BF16)
                dy_right = (dy[right, lanes].astype(F32) * from_edge).astype(BF16)
                left_ref[rows_of(g, g + 1, (mid - lo) * piece), here] = x_left
                right_ref[rows_of(g, g + 1, (hi - mid) * piece), here] = dy_right
                far = to_edge * dot(next(far_of)[...], dy_right, NN)
                for n in range(lo, mid):
                    dx[n] = dx[n] + far[rows_of(n - lo, n - lo + 1, piece), :]
        for n in range(pieces):
            dx_outs[at][rows_of(n, n + 1, piece), :] = dx[n].astype(BF16)

    if before:
        db_out[...] = before[0][...]
        dc_out[...] = before[1][...]
    else:
        db_out[...] = jnp.zeros_like(db_out)
        dc_out[...] = jnp.zeros_like(dc_out)
    batch = 4
    for first in range(0, pieces, batch):
        rows = rows_of(first, min(first + batch, pieces), piece)
        total = dot(x_near[rows, :], dy_near[rows, :], NT)
        row, col = iota(total.shape, 0), iota(total.shape, 1)
        keep = (split_of(row, piece) == split_of(col, piece)) & (row <= col)
        weighted = jnp.where(keep, total, 0.0).astype(BF16)
        db_out[rows, :] += dot(weighted, c[rows, :], NN)
        dc_out[rows, :] += dot(weighted, b[rows, :], TN)
    for ((n_left, n_right), same), left_ref, right_ref in zip(groups, lefts, rights):
        total = dot(left_ref[...], right_ref[...], NT)
        if len(same) > 1:
            row, col = iota(total.shape, 0), iota(total.shape, 1)
            same_cut = split_of(row, n_left * piece) == split_of(col, n_right * piece)
            total = jnp.where(same_cut, total, 0.0)
        weighted = total.astype(BF16)
        b_left = jnp.concatenate([b[rows_of(lo, mid, piece), :] for lo, mid, _ in same], axis=0)
        c_right = jnp.concatenate([c[rows_of(mid, hi, piece), :] for _, mid, hi in same], axis=0)
        db = dot(weighted, c_right, NN)
        dc = dot(weighted, b_left, TN)
        for g, (lo, mid, hi) in enumerate(same):
            db_out[rows_of(lo, mid, piece), :] += db[rows_of(g, g + 1, n_left * piece), :]
            dc_out[rows_of(mid, hi, piece), :] += dc[rows_of(g, g + 1, n_right * piece), :]


def inner_terms(head_dim, worked, setup, b, c, xs, dys, before, after, hides=True):
    (length, state), columns, chunks = b.shape, xs[0].size, len(xs)
    part = xs[0].shape[1] // GROUP
    used = part * len(worked)
    groups = grouped_cuts(length // head_dim)
    sizes = [[len(same) * n * head_dim for n in halves] for halves, same in groups]
    found = pl.pallas_call(
        functools.partial(inner_kernel, head_dim, worked, chunks, len(before), len(after)),
        out_shape=[jax.ShapeDtypeStruct((length, part), BF16)] * len(worked)
        + [jax.ShapeDtypeStruct((length, state), F32)] * 2,
        in_specs=whole(2 + 2 * chunks + len(setup) + len(before)) + [ANY] * len(after),
        out_specs=whole(len(worked) + 2),
        scratch_shapes=[pltpu.VMEM((length, used), BF16)] * 2
        + [pltpu.VMEM((left, used), BF16) for left, _ in sizes]
        + [pltpu.VMEM((right, used), BF16) for _, right in sizes],
        compiler_params=params(16),
        cost_estimate=cost(16 * columns * state, 8 * columns, 4 * columns) if hides else cost(1, 1),
        name="inner_terms",
    )(b, c, *xs, *dys, *setup, *before, *after)
    return dict(zip(worked, found)), list(found[-2:])


def parts_kernel(last, ks, db_before, dc_before, *refs):
    scaled, refs = refs[: 2 * len(ks)], refs[2 * len(ks) :]
    entries, outs = refs[: len(ks)], refs[-1 if last else -2 :]
    length, state = db_before.shape
    db, dc = db_before[...], dc_before[...]
    for n, entry in enumerate(entries):
        db = db + dot(scaled[2 * n][...], entry[state:, :], NT)
        dc = dc + dot(scaled[2 * n + 1][...], entry[:state, :], NT)
    if last:
        outs[0][:length, :] = db.astype(BF16)
        outs[0][length:, :] = dc.astype(BF16)
    else:
        outs[0][...] = db
        outs[1][...] = dc


def entry_parts(last, ks, scaled, db_before, dc_before, entries, after):
    length, state = db_before.shape
    one = jax.ShapeDtypeStruct((length, state), F32)
    outs = [jax.ShapeDtypeStruct((2 * length, state), BF16)] if last else [one, one]
    operands = [one for k in ks for one in scaled[k]] + [entries[k] for k in ks]
    return pl.pallas_call(
        functools.partial(parts_kernel, last, ks),
        out_shape=outs,
        in_specs=whole(2 + len(operands)) + [ANY] * len(after),
        out_specs=whole(len(outs)),
        compiler_params=params(8),
        cost_estimate=cost(2 * len(operands) * scaled[0][0].size * state, scaled[0][0].size),
        name="entry_parts",
    )(db_before, dc_before, *operands, *after)


def put_values(where, spread, b, local_parts, dx_local, entries, put):
    state, part = b.shape[1], entries[0].shape[1]
    for m, one in enumerate(local_parts):
        dx_local[:, m * part : (m + 1) * part] = one[...]
    for k, entry in enumerate(entries):
        here = slice(k * part, (k + 1) * part)
        local = dx_local[:, pl.ds(pl.multiple_of((place_of(where) ^ k) * part, part), part)]
        far = spread[k][...].astype(F32) * dot(b[...], entry[state:, :], NN)
        put(k, here, (local.astype(F32) + far).astype(BF16))


def values_kernel(where, b, *refs):
    local_parts, spread = refs[:GROUP], refs[GROUP : 2 * GROUP]
    entries, (out, dx_local) = sent_order(refs[2 * GROUP : 3 * GROUP]), refs[-2:]

    def put(k, here, value):
        out[:, here] = value

    put_values(where, spread, b, local_parts, dx_local, entries, put)


def last_values_kernel(chunks, where, b, *refs):
    local_parts, spread, refs = refs[:GROUP], refs[GROUP : 2 * GROUP], refs[2 * GROUP :]
    entries, before = sent_order(refs[:GROUP]), refs[GROUP : GROUP + chunks - 1]
    out, dx, dx_local, sems = refs[-4:]
    part = entries[0].shape[1]
    stores = []

    def store(chunk, k, source):
        lanes = chunk_lanes(where, k, chunk, part, out.shape[1])
        at = sems.at[chunk * GROUP + k]
        stores.append(pltpu.make_async_copy(source, out.at[:, lanes], at))
        stores[-1].start()

    for chunk, values in enumerate(before):
        for k in range(GROUP):
            store(chunk, k, values.at[:, pl.ds(k * part, part)])

    def put(k, here, value):
        dx[k] = value
        store(chunks - 1, k, dx.at[k])

    put_values(where, spread, b, local_parts, dx_local, entries, put)
    for one in stores:
        one.wait()


def entry_values(chunk, chunks, where, spread, b, local_parts, entries, before):
    length, part = b.shape[0], entries[0].shape[1]
    last = chunk == chunks - 1
    estimate = cost(8 * local_parts[0].size * b.shape[1], 16 * local_parts[0].size)
    operands = [where, b, *local_parts, *spread, *sent_order(entries)]
    if not last:
        return pl.pallas_call(
            values_kernel,
            out_shape=jax.ShapeDtypeStruct((length, GROUP * part), BF16),
            in_specs=[SMEM] + whole(1 + 3 * GROUP),
            out_specs=whole(1)[0],
            scratch_shapes=[pltpu.VMEM((length, GROUP * part), BF16)],
            compiler_params=params(8),
            cost_estimate=estimate,
            name="entry_values",
        )(*operands)
    return pl.pallas_call(
        functools.partial(last_values_kernel, chunks),
        out_shape=pltpu.HBM((length, chunks * GROUP * part), BF16),
        in_specs=[SMEM] + whole(1 + 3 * GROUP + len(before)),
        out_specs=HBM,
        scratch_shapes=[
            pltpu.VMEM((GROUP, length, part), BF16),
            pltpu.VMEM((length, GROUP * part), BF16),
            pltpu.SemaphoreType.DMA((chunks * GROUP,)),
        ],
        compiler_params=params(8),
        cost_estimate=estimate,
        name="last_values",
    )(*operands, *before)


def sum_kernel(*refs):
    parts, (db, dc) = refs[:-2], refs[-2:]
    length = db.shape[0]
    for out, rows in ((db, slice(0, length)), (dc, slice(length, 2 * length))):
        total = parts[0][rows, :].astype(F32)
        for part in parts[1:]:
            total = total + part[rows, :].astype(F32)
        out[...] = total.astype(BF16)


def over_heads(part):
    count, (rows, state) = lax.axis_size("head"), part.shape
    parts = [part]
    for shift in range(1, count):
        pairs = [(s, (s + shift) % count) for s in range(count)]
        parts.append(lax.ppermute(part, "head", pairs))
    return pl.pallas_call(
        sum_kernel,
        out_shape=[jax.ShapeDtypeStruct((rows // 2, state), BF16)] * 2,
        in_specs=whole(count),
        out_specs=whole(2),
        compiler_params=params(4),
        cost_estimate=cost(count * part.size, 2 * count * part.size),
        name="sum_over_heads",
    )(*parts)


def shards(token_values, b_inputs, c_inputs, log_decay, grad_out):
    head_dim = token_values.shape[1] // log_decay.shape[0]
    state = b_inputs.shape[1]
    count, group = lax.axis_size("seq"), GROUP
    chunks = chunk_count(token_values.shape[1])
    levels = (count // group).bit_length() - 1
    where = lax.axis_index("seq").astype(jnp.int32)[None]
    inputs = (log_decay, b_inputs, c_inputs, token_values, grad_out)
    order = [(chunk, k) for chunk in range(chunks) for k in range(group - 1, -1, -1)]
    kept, states = first_states(head_dim, order[: group - 1], where, inputs)
    ld, b, c, x_0, dy_0, *factors = kept
    late = order[group - 1 :]
    columns = (x_0, dy_0, token_values, grad_out)
    more, found = next_states(head_dim, late, where, factors, b, c, *columns)
    states.update(found)
    xs, dys = [x_0, *more[::2]], [dy_0, *more[1::2]]
    blocks = [
        exchange([states[chunk, k][3] for k in range(group)]) for chunk in range(chunks)
    ]
    setup = inner_setup(head_dim, ld, b, c, [states[late[-1]][0]])

    def to_group(block, k):
        return lax.ppermute(block, "seq", [(s, s ^ (k * group)) for s in range(count)])

    every = [(chunk, m) for chunk in range(chunks) for m in range(group)]
    worked = [every[1:4]] + [every[chunk * group :][:2] for chunk in range(1, chunks)]
    rest = [one for one in every[1:] if not any(one in some for some in worked)]
    entries, inner, sums = [], {}, []

    def add_inner(some, after, hides=True):
        found, sums[:] = inner_terms(head_dim, some, setup, b, c, xs, dys, sums, after, hides)
        inner.update(found)

    own = [totals(state, 0, where, blocks[0], setup[-1:])]
    add_inner(every[:1], own[0], False)
    own += [totals(state, 0, where, blocks[chunk], sums[:1]) for chunk in range(1, chunks)]
    for chunk in range(chunks):
        (total,) = own[chunk]
        received = [to_group(total, 1)]
        for level in range(levels - 1):
            last = level == levels - 2
            total = merged(state, level, last, where, total, received[level], [])
            received.append(to_group(total, 2 << level))
        add_inner(worked[chunk], [total])
        found = member_entries(state, False, where, blocks[chunk], received, sums[:1])
        entries.append(exchange(found))
    if rest:
        add_inner(rest, found[:1])

    values = []
    for chunk in range(chunks):
        last = chunk == chunks - 1
        ours = [states[chunk, k] for k in range(group)]
        scaled = [one[:2] for one in ours]
        spread = [one[2] for one in ours]
        if last:
            sums = entry_parts(False, (0, 3), scaled, *sums, entries[chunk], values)
        ks = (2, 1) if last else (0, 3, 2, 1)
        sums = entry_parts(last, ks, scaled, *sums, entries[chunk], [])
        local = [inner[chunk, m] for m in range(group)]
        values.append(
            entry_values(chunk, chunks, where, spread, b, local, entries[chunk], values)
        )
    return (values[-1], *over_heads(sums[0]))


def solution(mesh):
    in_specs = (
        P("seq", "head"),
        P("seq", None),
        P("seq", None),
        P("head", "seq"),
        P("seq", "head"),
    )
    out_specs = (P("seq", "head"), P("seq", None), P("seq", None))
    return jax.shard_map(shards, mesh=mesh, in_specs=in_specs, out_specs=out_specs, check_vma=False)
```

```python
import functools

import jax
import jax.numpy as jnp
from jax import lax
from jax.experimental import pallas as pl
from jax.experimental.pallas import tpu as pltpu
from jax.sharding import PartitionSpec as P

BF16 = jnp.bfloat16
F32 = jnp.float32
LANES = 128
GROUP = 4
TAIL = 16
LOG2E = 1.4426950408889634
MIB = 1024 * 1024

NN = (((1,), (0,)), ((), ()))
NT = (((1,), (1,)), ((), ()))
TN = (((0,), (0,)), ((), ()))


def dot(a, b, dims):
    return lax.dot_general(a, b, dims, preferred_element_type=F32)


def iota(shape, dim):
    return lax.broadcasted_iota(jnp.int32, shape, dim)


def three(values):
    high = values.astype(BF16)
    rest = values - high.astype(F32)
    mid = rest.astype(BF16)
    return high, mid, (rest - mid.astype(F32)).astype(BF16)


SLOT = LANES // 4


def summed(mask, terms):
    heads, length = terms[0].shape
    gap = [] if heads == SLOT else [jnp.zeros((SLOT - heads, length), BF16)]
    rows = [r for t in terms for r in [t] + gap] + [jnp.zeros((SLOT, length), BF16)]
    each = dot(mask, jnp.concatenate(rows, axis=0), NT)
    return each + pltpu.roll(each, LANES - SLOT, 1) + pltpu.roll(each, LANES - 2 * SLOT, 1)


def split_of(index, size):
    shift = size.bit_length() - 1
    return lax.shift_right_logical(index, shift) if size == 1 << shift else index // size


def row_less_head(head_dim, width, rows=LANES):
    shape = (LANES, width)
    row = iota(shape, 0)
    if rows < LANES:
        row = row & (rows - 1)
    return row - split_of(iota(shape, 1), head_dim)


def head_of_lane(difference, first):
    return jnp.where(difference == first, 1.0, 0.0).astype(BF16)


def whole(count):
    return [pl.BlockSpec(memory_space=pltpu.VMEM)] * count


def in_hbm(*arrays):
    return [pltpu.with_memory_space_constraint(a, pltpu.HBM) for a in arrays]


SMEM = pl.BlockSpec(memory_space=pltpu.SMEM)
HBM = pl.BlockSpec(memory_space=pltpu.HBM)
ANY = pl.BlockSpec(memory_space=pl.ANY)


def params(mib):
    return pltpu.CompilerParams(vmem_limit_bytes=mib * MIB)


def cost(flops, size, transcendentals=0):
    return pl.CostEstimate(flops=flops, bytes_accessed=size, transcendentals=transcendentals)


def place_of(where):
    return where[0] & (GROUP - 1)


def bit_of(where, level):
    return (where[0] >> (level + GROUP.bit_length() - 1)) & 1 == 1


def chunk_count(width):
    return 2 if (width // GROUP) % (2 * LANES) == 0 else 1


def chunk_lanes(where, k, chunk, part):
    start = (chunk * GROUP + (place_of(where) ^ k)) * part
    return pl.ds(pl.multiple_of(start, part), part)


def masks_of(length):
    rows, other = iota((length, length), 0), iota((length, length), 1)
    after = jnp.where(other > rows, 1.0, 0.0).astype(BF16)
    return after, jnp.where(other <= rows, 1.0, 0.0).astype(BF16)


def factors_of(ld, after, until):
    length = ld.shape[1]
    terms = three(ld)
    into_end = jnp.exp(summed(after, terms)).astype(BF16)
    from_start = jnp.exp(summed(until, terms)).astype(BF16)
    total = jnp.exp(summed(jnp.ones((TAIL, length), BF16), terms))
    high = total.astype(BF16).astype(F32)
    halves = jnp.where(iota(total.shape, 0) < TAIL // 2, high, total - high).astype(BF16)
    return into_end, from_start, halves


def put_states(head_dim, chunks, pieces, where, operands, outs, ready):
    into_end, from_start, halves, b, c, xs, dys = operands
    state, part = b.shape[1], xs[0].shape[1] // GROUP
    difference = row_less_head(head_dim, part)
    for side, (factors, proj, cols) in enumerate([(into_end, b, xs), (from_start, c, dys)]):
        turned = None
        for n, (chunk, k) in enumerate(pieces):
            if n == 0 or chunk != pieces[n - 1][0]:
                ready(side, chunk)
            if turned is None:
                turned = proj[...].T
            x_scaled, dy_scaled, spread, send = outs[4 * n : 4 * n + 4]
            member = place_of(where) ^ k
            first_head = (chunk * GROUP + member) * (part // head_dim)
            hot = head_of_lane(difference, first_head)
            wide = dot(factors, hot, NN).astype(BF16)
            if side == 0:
                spread[...] = wide
                send[2 * state :, :] = dot(halves, hot, NN).astype(BF16)
            lanes = pl.ds(pl.multiple_of(member * part, part), part)
            piece = cols[chunk][:, lanes] * wide
            (dy_scaled if side else x_scaled)[...] = piece
            send[side * state : (side + 1) * state, :] = dot(turned, piece, NN).astype(BF16)


def load_chunk(chunk, source, target, sem):
    width = target.shape[1]
    copy = pltpu.make_async_copy(source.at[:, pl.ds(chunk * width, width)], target, sem)
    copy.start()
    return copy


def first_states_kernel(head_dim, chunks, pieces, where, ld_in, b_in, c_in, x_in, dy_in, *refs):
    ld, b, c, x, dy, into_end, from_start, halves = refs[:8]
    outs, sems = refs[8:-1], refs[-1]

    def load(n, source, target):
        copy = pltpu.make_async_copy(source, target, sems.at[n])
        copy.start()
        return copy

    first = load(0, ld_in, ld)
    copies = [
        [load(1, b_in, b), load_chunk(0, x_in, x, sems.at[3])],
        [load(2, c_in, c), load_chunk(0, dy_in, dy, sems.at[4])],
    ]
    masks = masks_of(ld.shape[1])
    first.wait()
    factors = factors_of(ld[...], *masks)
    for ref, value in zip((into_end, from_start, halves), factors):
        ref[...] = value

    def ready(side, chunk):
        for copy in copies[side]:
            copy.wait()

    operands = (*factors, b, c, {0: x}, {0: dy})
    put_states(head_dim, chunks, pieces, where, operands, outs, ready)


def next_states_kernel(head_dim, chunks, pieces, where, into_end, from_start, halves, *refs):
    b, c, x, dy, x_in, dy_in = refs[:6]
    outs, sems = refs[6:-1], refs[-1]
    kept, outs = outs[: 2 * (chunks - 1)], outs[2 * (chunks - 1) :]
    xs, dys, copies = {0: x}, {0: dy}, {}
    for chunk in range(1, chunks):
        xs[chunk], dys[chunk] = kept[2 * chunk - 2 : 2 * chunk]
        copies[0, chunk] = load_chunk(chunk, x_in, xs[chunk], sems.at[2 * chunk - 2])
        copies[1, chunk] = load_chunk(chunk, dy_in, dys[chunk], sems.at[2 * chunk - 1])

    def ready(side, chunk):
        if (side, chunk) in copies:
            copies[side, chunk].wait()

    operands = (into_end[...], from_start[...], halves[...], b, c, xs, dys)
    put_states(head_dim, chunks, pieces, where, operands, outs, ready)


def states_shapes(n_parts, length, width, state):
    part = width // (GROUP * chunk_count(width))
    scaled = jax.ShapeDtypeStruct((length, part), BF16)
    send = jax.ShapeDtypeStruct((2 * state + TAIL, part), BF16)
    return [scaled, scaled, scaled, send] * n_parts


def by_piece(pieces, outs):
    return {piece: outs[4 * n : 4 * n + 4] for n, piece in enumerate(pieces)}


def first_states(head_dim, pieces, where, inputs):
    ld, b, c, x, dy = inputs
    (length, width), state = x.shape, b.shape[1]
    chunks = chunk_count(width)
    columns = jax.ShapeDtypeStruct((length, width // chunks), BF16)
    kept = [jax.ShapeDtypeStruct(a.shape, a.dtype) for a in (ld, b, c)] + [columns] * 2
    kept += [jax.ShapeDtypeStruct((rows, LANES), BF16) for rows in (length, length, TAIL)]
    outs = kept + states_shapes(len(pieces), length, width, state)
    found = pl.pallas_call(
        functools.partial(first_states_kernel, head_dim, chunks, pieces),
        out_shape=outs,
        in_specs=[SMEM] + [HBM] * 5,
        out_specs=whole(len(outs)),
        scratch_shapes=[pltpu.SemaphoreType.DMA((5,))],
        compiler_params=params(8),
        cost_estimate=cost(2 * length * width * (state + LANES), 8 * length * width),
        name="first_states",
    )(where, *in_hbm(*inputs))
    return found[:8], by_piece(pieces, found[8:])


def next_states(head_dim, pieces, where, factors, b, c, x_0, dy_0, x, dy):
    (length, width), state = x.shape, b.shape[1]
    chunks = chunk_count(width)
    n_kept = 2 * (chunks - 1)
    outs = [jax.ShapeDtypeStruct(x_0.shape, BF16)] * n_kept
    outs += states_shapes(len(pieces), length, width, state)
    found = pl.pallas_call(
        functools.partial(next_states_kernel, head_dim, chunks, pieces),
        out_shape=outs,
        in_specs=[SMEM] + whole(7) + [HBM] * 2,
        out_specs=whole(len(outs)),
        scratch_shapes=[pltpu.SemaphoreType.DMA((max(n_kept, 1),))],
        compiler_params=params(8),
        cost_estimate=cost(2 * length * width * (state + LANES), 4 * length * width),
        name="next_states",
    )(where, *factors, b, c, x_0, dy_0, *in_hbm(x, dy))
    return found[:n_kept], by_piece(pieces, found[n_kept:])


def decay_of(tail):
    tail = tail.astype(F32)
    return tail[:1, :] + tail[TAIL // 2 : TAIL // 2 + 1, :]


def put_decay(ref, first, factor):
    high = factor.astype(BF16).astype(F32)
    shape = (TAIL, factor.shape[1])
    both = jnp.where(iota(shape, 0) < TAIL // 2, high, factor - high)
    ref[first:, :] = both.astype(BF16)


def sent_order(parts):
    return [parts[0], *parts[:0:-1]]


def in_order(group, forward):
    return list(range(group)) if forward else list(range(group - 1, -1, -1))


def side_rows(state, forward):
    return slice(0, state) if forward else slice(state, 2 * state)


def totals_kernel(state, levels, where, *refs):
    group = GROUP
    blocks, outs, sums = sent_order(refs[:group]), refs[-1 - levels : -1], refs[-1]
    for here in range(group):

        @pl.when(place_of(where) == here)
        def _(here=here):
            decays = [decay_of(blocks[q ^ here][2 * state :, :]) for q in range(group)]
            for forward in (True, False):
                rows, value = side_rows(state, forward), None
                for q in in_order(group, forward):
                    piece = blocks[q ^ here][rows, :].astype(F32)
                    value = piece if value is None else decays[q] * value + piece
                sums[rows, :] = value.astype(BF16)

    factor = decay_of(blocks[0][2 * state :, :])
    for block in blocks[1:]:
        factor = factor * decay_of(block[2 * state :, :])
    if not levels:
        put_decay(sums, 2 * state, factor)
    for level, out in enumerate(outs):
        put_decay(out, state, factor)
        for forward in (True, False):

            @pl.when(bit_of(where, level) != forward)
            def _(out=out, forward=forward):
                out[:state, :] = sums[side_rows(state, forward), :]


def totals(state, levels, where, blocks, after):
    part = blocks[0].shape[1]
    outs = [jax.ShapeDtypeStruct((state + TAIL, part), BF16)] * levels
    if not levels:
        outs = [jax.ShapeDtypeStruct(blocks[0].shape, BF16)]
    return pl.pallas_call(
        functools.partial(totals_kernel, state, levels),
        out_shape=outs,
        in_specs=[SMEM] + whole(len(blocks)) + [ANY] * len(after),
        out_specs=whole(len(outs)),
        scratch_shapes=[pltpu.VMEM((2 * state, part), BF16)] if levels else [],
        compiler_params=params(4),
        cost_estimate=cost(8 * blocks[0].size, 10 * blocks[0].size),
        name="totals",
    )(where, *sent_order(blocks), *after)


def merged_kernel(state, level, last, where, own, received, *refs):
    out = refs[-1]
    d_own, d_other = decay_of(own[2 * state :, :]), decay_of(received[2 * state :, :])
    upper = bit_of(where, level)
    later = bit_of(where, level + 1)
    for is_upper in (False, True):
        for forward in (True, False):
            chosen = upper == is_upper
            if last:
                chosen = chosen & (later != forward)

            @pl.when(chosen)
            def _(is_upper=is_upper, forward=forward):
                rows = side_rows(state, forward)
                mine, other = own[rows, :].astype(F32), received[rows, :].astype(F32)
                value = mine + d_own * other if is_upper == forward else other + d_other * mine
                out[slice(0, state) if last else rows, :] = value.astype(BF16)

    if not last:
        put_decay(out, 2 * state, d_own * d_other)


def merged(state, level, last, where, own, received, after):
    rows = state if last else own.shape[0]
    return pl.pallas_call(
        functools.partial(merged_kernel, state, level, last),
        out_shape=pltpu.VMEM((rows, own.shape[1]), BF16),
        in_specs=[SMEM] + whole(2) + [ANY] * len(after),
        out_specs=whole(1)[0],
        compiler_params=params(4),
        cost_estimate=cost(4 * own.size, 6 * own.size),
        name="merged",
    )(where, own, received, *after)


def put_direct(state, groups, number, received, entry):
    for mine in range(groups):

        @pl.when(number == mine)
        def _(mine=mine):
            for forward in (True, False):
                rows = side_rows(state, forward)
                others = range(mine - 1, -1, -1) if forward else range(mine + 1, groups)
                value, factor = jnp.zeros((state, entry.shape[1]), F32), None
                for other in others:
                    r = received[(mine ^ other) - 1]
                    piece = r[:state, :].astype(F32)
                    value = piece if factor is None else value + factor * piece
                    d = decay_of(r[state:, :])
                    factor = d if factor is None else factor * d
                entry[rows, :] = value


def put_rounds(state, where, received, entry):
    for forward in (True, False):
        value, factor = None, 1.0
        for level, r in enumerate(received):
            gets = bit_of(where, level) == forward
            both = r.shape[0] > 2 * state
            rows = side_rows(state, forward) if both else slice(0, state)
            piece = r[rows, :].astype(F32) * jnp.where(gets, 1.0, 0.0)
            value = piece if value is None else value + factor * piece
            if both:
                factor = factor * jnp.where(gets, decay_of(r[2 * state :, :]), 1.0)
        entry[side_rows(state, forward), :] = value


def members_kernel(state, direct, n_received, where, *refs):
    received, refs = refs[:n_received], refs[n_received:]
    group = GROUP
    blocks, outs, entry = refs[:group], refs[-1 - group : -1], refs[-1]
    if direct:
        put_direct(state, n_received + 1, where[0] // group, received, entry)
    else:
        put_rounds(state, where, received, entry)
    for here in range(group):

        @pl.when(place_of(where) == here)
        def _(here=here):
            decays = [decay_of(blocks[q ^ here][2 * state :, :]) for q in range(group)]
            for forward in (True, False):
                rows, order = side_rows(state, forward), in_order(group, forward)
                value = entry[rows, :]
                for q in order:
                    outs[q ^ here][rows, :] = value.astype(BF16)
                    if q != order[-1]:
                        value = decays[q] * value + blocks[q ^ here][rows, :].astype(F32)


def member_entries(state, direct, where, blocks, received, after):
    group, part = len(blocks), blocks[0].shape[1]
    return pl.pallas_call(
        functools.partial(members_kernel, state, direct, len(received)),
        out_shape=[jax.ShapeDtypeStruct((2 * state, part), BF16)] * group,
        in_specs=[SMEM] + whole(group + len(received)) + [ANY] * len(after),
        out_specs=whole(group),
        scratch_shapes=[pltpu.VMEM((2 * state, part), F32)],
        compiler_params=params(4),
        cost_estimate=cost(12 * blocks[0].size, 16 * blocks[0].size),
        name="member_entries",
    )(where, *received, *blocks, *after)


def exchange(parts):
    count = lax.axis_size("seq")
    out = list(parts)
    for k in range(len(parts) - 1, 0, -1):
        out[k] = lax.ppermute(parts[k], "seq", [(s, s ^ k) for s in range(count)])
    return out


def split_pairs(first, count):
    if count == 1:
        return []
    middle = first + count // 2
    return (
        [(first, middle, first + count)]
        + split_pairs(first, middle - first)
        + split_pairs(middle, first + count - middle)
    )


def grouped_cuts(pieces):
    groups = {}
    for cut in split_pairs(0, pieces):
        groups.setdefault((cut[1] - cut[0], cut[2] - cut[1]), []).append(cut)
    return list(groups.items())


def rows_of(first, end, piece):
    return slice(first * piece, end * piece)


def setup_kernel(piece, ld, b, c, *refs):
    near, cum_terms = refs[-2:]
    heads, length = ld.shape
    rows, other = iota((length, length), 0), iota((length, length), 1)
    mask = jnp.where(other <= rows, 1.0, 0.0).astype(BF16)
    cum = summed(mask, three(ld[...] * LOG2E))
    lane = iota(cum.shape, 1)
    in_slots = jnp.where(lane < SLOT, cum, 0.0)
    in_slots = in_slots + pltpu.roll(in_slots, SLOT, 1) + pltpu.roll(in_slots, 2 * SLOT, 1)
    high, mid, low = three(in_slots)
    cum_terms[...] = jnp.where(lane < SLOT, high, jnp.where(lane < 2 * SLOT, mid, low))
    keep = iota((piece, piece), 0) <= iota((piece, piece), 1)
    pieces = length // piece
    for n in range(pieces):
        here = rows_of(n, n + 1, piece)
        near[here, :] = jnp.where(keep, dot(b[here, :], c[here, :], NT), 0.0).astype(BF16)
    cuts = [cut for _, same in grouped_cuts(pieces) for cut in same]
    for (lo, mid_, hi), far in zip(cuts, refs):
        left, right = rows_of(lo, mid_, piece), rows_of(mid_, hi, piece)
        far[...] = dot(b[left, :], c[right, :], NT).astype(BF16)


def inner_setup(piece, ld, b, c, after):
    length = b.shape[0]
    cuts = [cut for _, same in grouped_cuts(length // piece) for cut in same]
    outs = [
        jax.ShapeDtypeStruct(((mid - lo) * piece, (hi - mid) * piece), BF16) for lo, mid, hi in cuts
    ]
    outs.append(jax.ShapeDtypeStruct((length, piece), BF16))
    outs.append(jax.ShapeDtypeStruct((length, LANES), BF16))
    return pl.pallas_call(
        functools.partial(setup_kernel_after, piece, len(after)),
        out_shape=outs,
        in_specs=whole(3) + [ANY] * len(after),
        out_specs=whole(len(outs)),
        compiler_params=params(4),
        cost_estimate=cost(8 * b.size * length, 8 * b.size),
        name="inner_setup",
    )(ld, b, c, *after)


def setup_kernel_after(piece, n_after, ld, b, c, *refs):
    setup_kernel(piece, ld, b, c, *refs[n_after:])


def inner_kernel(head_dim, worked, chunks, n_before, n_after, b, c, *refs):
    xs, dys, refs = refs[:chunks], refs[chunks : 2 * chunks], refs[2 * chunks :]
    length, width = xs[0].shape
    piece = head_dim
    pieces = length // piece
    groups = grouped_cuts(pieces)
    n_cuts = sum(len(same) for _, same in groups)
    fars, (near, cum_terms), refs = refs[:n_cuts], refs[n_cuts : n_cuts + 2], refs[n_cuts + 2 :]
    before, refs = refs[:n_before], refs[n_before + n_after :]
    dx_outs, (db_out, dc_out, x_near, dy_near, *scratch) = refs[: len(worked)], refs[len(worked) :]
    lefts, rights = scratch[: len(groups)], scratch[len(groups) :]
    part = dx_outs[0].shape[1]
    difference = row_less_head(head_dim, part, SLOT)

    for at, (chunk, m) in enumerate(worked):
        x, dy, first_head = xs[chunk], dys[chunk], (chunk * GROUP + m) * (part // head_dim)
        lanes, here = slice(m * part, (m + 1) * part), slice(at * part, (at + 1) * part)
        cum = dot(cum_terms[...], head_of_lane(difference, first_head), NN)
        dx = []
        for n in range(pieces):
            rows = rows_of(n, n + 1, piece)
            middle = cum[n * piece + piece // 2 : n * piece + piece // 2 + 1, :]
            gap = middle - cum[rows, :]
            down, up = jnp.exp2(gap), jnp.exp2(-gap)
            x_near[rows, here] = (x[rows, lanes].astype(F32) * down).astype(BF16)
            dy_piece = (dy[rows, lanes].astype(F32) * up).astype(BF16)
            dy_near[rows, here] = dy_piece
            dx.append(down * dot(near[rows, :], dy_piece, NN))
        far_of = iter(fars)
        for (_, same), left_ref, right_ref in zip(groups, lefts, rights):
            for g, (lo, mid, hi) in enumerate(same):
                left, right = rows_of(lo, mid, piece), rows_of(mid, hi, piece)
                edge = cum[mid * piece - 1 : mid * piece, :]
                to_edge = jnp.exp2(edge - cum[left, :])
                from_edge = jnp.exp2(cum[right, :] - edge)
                x_left = (x[left, lanes].astype(F32) * to_edge).astype(BF16)
                dy_right = (dy[right, lanes].astype(F32) * from_edge).astype(BF16)
                left_ref[rows_of(g, g + 1, (mid - lo) * piece), here] = x_left
                right_ref[rows_of(g, g + 1, (hi - mid) * piece), here] = dy_right
                far = to_edge * dot(next(far_of)[...], dy_right, NN)
                for n in range(lo, mid):
                    dx[n] = dx[n] + far[rows_of(n - lo, n - lo + 1, piece), :]
        for n in range(pieces):
            dx_outs[at][rows_of(n, n + 1, piece), :] = dx[n].astype(BF16)

    if before:
        db_out[...] = before[0][...]
        dc_out[...] = before[1][...]
    else:
        db_out[...] = jnp.zeros_like(db_out)
        dc_out[...] = jnp.zeros_like(dc_out)
    batch = 4
    for first in range(0, pieces, batch):
        rows = rows_of(first, min(first + batch, pieces), piece)
        total = dot(x_near[rows, :], dy_near[rows, :], NT)
        row, col = iota(total.shape, 0), iota(total.shape, 1)
        keep = (split_of(row, piece) == split_of(col, piece)) & (row <= col)
        weighted = jnp.where(keep, total, 0.0).astype(BF16)
        db_out[rows, :] += dot(weighted, c[rows, :], NN)
        dc_out[rows, :] += dot(weighted, b[rows, :], TN)
    for ((n_left, n_right), same), left_ref, right_ref in zip(groups, lefts, rights):
        total = dot(left_ref[...], right_ref[...], NT)
        if len(same) > 1:
            row, col = iota(total.shape, 0), iota(total.shape, 1)
            same_cut = split_of(row, n_left * piece) == split_of(col, n_right * piece)
            total = jnp.where(same_cut, total, 0.0)
        weighted = total.astype(BF16)
        b_left = jnp.concatenate([b[rows_of(lo, mid, piece), :] for lo, mid, _ in same], axis=0)
        c_right = jnp.concatenate([c[rows_of(mid, hi, piece), :] for _, mid, hi in same], axis=0)
        db = dot(weighted, c_right, NN)
        dc = dot(weighted, b_left, TN)
        for g, (lo, mid, hi) in enumerate(same):
            db_out[rows_of(lo, mid, piece), :] += db[rows_of(g, g + 1, n_left * piece), :]
            dc_out[rows_of(mid, hi, piece), :] += dc[rows_of(g, g + 1, n_right * piece), :]


def inner_terms(head_dim, worked, setup, b, c, xs, dys, before, after, hides=True):
    (length, state), columns, chunks = b.shape, xs[0].size, len(xs)
    part = xs[0].shape[1] // GROUP
    used = part * len(worked)
    groups = grouped_cuts(length // head_dim)
    sizes = [[len(same) * n * head_dim for n in halves] for halves, same in groups]
    found = pl.pallas_call(
        functools.partial(inner_kernel, head_dim, worked, chunks, len(before), len(after)),
        out_shape=[jax.ShapeDtypeStruct((length, part), BF16)] * len(worked)
        + [jax.ShapeDtypeStruct((length, state), F32)] * 2,
        in_specs=whole(2 + 2 * chunks + len(setup) + len(before)) + [ANY] * len(after),
        out_specs=whole(len(worked) + 2),
        scratch_shapes=[pltpu.VMEM((length, used), BF16)] * 2
        + [pltpu.VMEM((left, used), BF16) for left, _ in sizes]
        + [pltpu.VMEM((right, used), BF16) for _, right in sizes],
        compiler_params=params(16),
        cost_estimate=cost(16 * columns * state, 8 * columns, 4 * columns) if hides else cost(1, 1),
        name="inner_terms",
    )(b, c, *xs, *dys, *setup, *before, *after)
    return dict(zip(worked, found)), list(found[-2:])


def parts_kernel(last, ks, db_before, dc_before, *refs):
    scaled, refs = refs[: 2 * len(ks)], refs[2 * len(ks) :]
    entries, outs = refs[: len(ks)], refs[-1 if last else -2 :]
    length, state = db_before.shape
    db, dc = db_before[...], dc_before[...]
    for n, entry in enumerate(entries):
        db = db + dot(scaled[2 * n][...], entry[state:, :], NT)
        dc = dc + dot(scaled[2 * n + 1][...], entry[:state, :], NT)
    if last:
        outs[0][:length, :] = db.astype(BF16)
        outs[0][length:, :] = dc.astype(BF16)
    else:
        outs[0][...] = db
        outs[1][...] = dc


def entry_parts(last, ks, scaled, db_before, dc_before, entries, after):
    length, state = db_before.shape
    one = jax.ShapeDtypeStruct((length, state), F32)
    outs = [jax.ShapeDtypeStruct((2 * length, state), BF16)] if last else [one, one]
    operands = [one for k in ks for one in scaled[k]] + [entries[k] for k in ks]
    return pl.pallas_call(
        functools.partial(parts_kernel, last, ks),
        out_shape=outs,
        in_specs=whole(2 + len(operands)) + [ANY] * len(after),
        out_specs=whole(len(outs)),
        compiler_params=params(8),
        cost_estimate=cost(2 * len(operands) * scaled[0][0].size * state, scaled[0][0].size),
        name="entry_parts",
    )(db_before, dc_before, *operands, *after)


def put_values(where, spread, b, local_parts, dx_local, entries, put):
    state, part = b.shape[1], entries[0].shape[1]
    for m, one in enumerate(local_parts):
        dx_local[:, m * part : (m + 1) * part] = one[...]
    for k, entry in enumerate(entries):
        here = slice(k * part, (k + 1) * part)
        local = dx_local[:, pl.ds(pl.multiple_of((place_of(where) ^ k) * part, part), part)]
        far = spread[k][...].astype(F32) * dot(b[...], entry[state:, :], NN)
        put(k, here, (local.astype(F32) + far).astype(BF16))


def values_kernel(where, b, *refs):
    local_parts, spread = refs[:GROUP], refs[GROUP : 2 * GROUP]
    entries, (out, dx_local) = sent_order(refs[2 * GROUP : 3 * GROUP]), refs[-2:]

    def put(k, here, value):
        out[:, here] = value

    put_values(where, spread, b, local_parts, dx_local, entries, put)


def last_values_kernel(chunks, where, b, *refs):
    local_parts, spread, refs = refs[:GROUP], refs[GROUP : 2 * GROUP], refs[2 * GROUP :]
    entries, before = sent_order(refs[:GROUP]), refs[GROUP : GROUP + chunks - 1]
    out, dx, dx_local, sems = refs[-4:]
    part = entries[0].shape[1]
    stores = []

    def store(chunk, k, source):
        lanes = chunk_lanes(where, k, chunk, part)
        at = sems.at[chunk * GROUP + k]
        stores.append(pltpu.make_async_copy(source, out.at[:, lanes], at))
        stores[-1].start()

    for chunk, values in enumerate(before):
        for k in range(GROUP):
            store(chunk, k, values.at[:, pl.ds(k * part, part)])

    def put(k, here, value):
        dx[k] = value
        store(chunks - 1, k, dx.at[k])

    put_values(where, spread, b, local_parts, dx_local, entries, put)
    for one in stores:
        one.wait()


def entry_values(chunk, chunks, where, spread, b, local_parts, entries, before):
    length, part = b.shape[0], entries[0].shape[1]
    last = chunk == chunks - 1
    estimate = cost(8 * local_parts[0].size * b.shape[1], 16 * local_parts[0].size)
    operands = [where, b, *local_parts, *spread, *sent_order(entries)]
    if not last:
        return pl.pallas_call(
            values_kernel,
            out_shape=jax.ShapeDtypeStruct((length, GROUP * part), BF16),
            in_specs=[SMEM] + whole(1 + 3 * GROUP),
            out_specs=whole(1)[0],
            scratch_shapes=[pltpu.VMEM((length, GROUP * part), BF16)],
            compiler_params=params(8),
            cost_estimate=estimate,
            name="entry_values",
        )(*operands)
    return pl.pallas_call(
        functools.partial(last_values_kernel, chunks),
        out_shape=pltpu.HBM((length, chunks * GROUP * part), BF16),
        in_specs=[SMEM] + whole(1 + 3 * GROUP + len(before)),
        out_specs=HBM,
        scratch_shapes=[
            pltpu.VMEM((GROUP, length, part), BF16),
            pltpu.VMEM((length, GROUP * part), BF16),
            pltpu.SemaphoreType.DMA((chunks * GROUP,)),
        ],
        compiler_params=params(8),
        cost_estimate=estimate,
        name="last_values",
    )(*operands, *before)


def sum_kernel(*refs):
    parts, (db, dc) = refs[:-2], refs[-2:]
    length = db.shape[0]
    for out, rows in ((db, slice(0, length)), (dc, slice(length, 2 * length))):
        total = parts[0][rows, :].astype(F32)
        for part in parts[1:]:
            total = total + part[rows, :].astype(F32)
        out[...] = total.astype(BF16)


def over_heads(part):
    count, (rows, state) = lax.axis_size("head"), part.shape
    parts = [part]
    for shift in range(1, count):
        pairs = [(s, (s + shift) % count) for s in range(count)]
        parts.append(lax.ppermute(part, "head", pairs))
    return pl.pallas_call(
        sum_kernel,
        out_shape=[jax.ShapeDtypeStruct((rows // 2, state), BF16)] * 2,
        in_specs=whole(count),
        out_specs=whole(2),
        compiler_params=params(4),
        cost_estimate=cost(count * part.size, 2 * count * part.size),
        name="sum_over_heads",
    )(*parts)


def shards(token_values, b_inputs, c_inputs, log_decay, grad_out):
    head_dim = token_values.shape[1] // log_decay.shape[0]
    state = b_inputs.shape[1]
    count, group = lax.axis_size("seq"), GROUP
    chunks = chunk_count(token_values.shape[1])
    levels = (count // group).bit_length() - 1
    where = lax.axis_index("seq").astype(jnp.int32)[None]
    inputs = (log_decay, b_inputs, c_inputs, token_values, grad_out)
    order = [(chunk, k) for chunk in range(chunks) for k in range(group - 1, -1, -1)]
    kept, states = first_states(head_dim, order[: group - 1], where, inputs)
    ld, b, c, x_0, dy_0, *factors = kept
    late = order[group - 1 :]
    columns = (x_0, dy_0, token_values, grad_out)
    more, found = next_states(head_dim, late, where, factors, b, c, *columns)
    states.update(found)
    xs, dys = [x_0, *more[::2]], [dy_0, *more[1::2]]
    blocks = [
        exchange([states[chunk, k][3] for k in range(group)]) for chunk in range(chunks)
    ]
    setup = inner_setup(head_dim, ld, b, c, [states[late[-1]][0]])

    def to_group(block, k):
        return lax.ppermute(block, "seq", [(s, s ^ (k * group)) for s in range(count)])

    every = [(chunk, m) for chunk in range(chunks) for m in range(group)]
    worked = [every[1:4]] + [every[chunk * group :][:2] for chunk in range(1, chunks)]
    rest = [one for one in every[1:] if not any(one in some for some in worked)]
    entries, inner, sums = [], {}, []

    def add_inner(some, after, hides=True):
        found, sums[:] = inner_terms(head_dim, some, setup, b, c, xs, dys, sums, after, hides)
        inner.update(found)

    own = [totals(state, 0, where, blocks[0], setup[-1:])]
    add_inner(every[:1], own[0], False)
    own += [totals(state, 0, where, blocks[chunk], sums[:1]) for chunk in range(1, chunks)]
    for chunk in range(chunks):
        (total,) = own[chunk]
        received = [to_group(total, 1)]
        for level in range(levels - 1):
            last = level == levels - 2
            total = merged(state, level, last, where, total, received[level], [])
            received.append(to_group(total, 2 << level))
        add_inner(worked[chunk], [total])
        found = member_entries(state, False, where, blocks[chunk], received, sums[:1])
        entries.append(exchange(found))
    if rest:
        add_inner(rest, found[:1])

    values = []
    for chunk in range(chunks):
        last = chunk == chunks - 1
        ours = [states[chunk, k] for k in range(group)]
        scaled = [one[:2] for one in ours]
        spread = [one[2] for one in ours]
        if last:
            sums = entry_parts(False, (0, 3), scaled, *sums, entries[chunk], values)
        ks = (2, 1) if last else (0, 3, 2, 1)
        sums = entry_parts(last, ks, scaled, *sums, entries[chunk], [])
        local = [inner[chunk, m] for m in range(group)]
        values.append(
            entry_values(chunk, chunks, where, spread, b, local, entries[chunk], values)
        )
    return (values[-1], *over_heads(sums[0]))


def solution(mesh):
    in_specs = (
        P("seq", "head"),
        P("seq", None),
        P("seq", None),
        P("head", "seq"),
        P("seq", "head"),
    )
    out_specs = (P("seq", "head"), P("seq", None), P("seq", None))
    return jax.shard_map(shards, mesh=mesh, in_specs=in_specs, out_specs=out_specs, check_vma=False)
```

```python
import functools

import jax
import jax.numpy as jnp
from jax import lax
from jax.experimental import pallas as pl
from jax.experimental.pallas import tpu as pltpu
from jax.sharding import PartitionSpec as P

BF16 = jnp.bfloat16
F32 = jnp.float32
LANES = 128
GROUP = 4
TAIL = 16
LOG2E = 1.4426950408889634
MIB = 1024 * 1024

NN = (((1,), (0,)), ((), ()))
NT = (((1,), (1,)), ((), ()))
TN = (((0,), (0,)), ((), ()))


def dot(a, b, dims):
    return lax.dot_general(a, b, dims, preferred_element_type=F32)


def iota(shape, dim):
    return lax.broadcasted_iota(jnp.int32, shape, dim)


def three(values):
    high = values.astype(BF16)
    rest = values - high.astype(F32)
    mid = rest.astype(BF16)
    return high, mid, (rest - mid.astype(F32)).astype(BF16)


SLOT = LANES // 4


def summed(mask, terms):
    heads, length = terms[0].shape
    gap = [] if heads == SLOT else [jnp.zeros((SLOT - heads, length), BF16)]
    rows = [r for t in terms for r in [t] + gap] + [jnp.zeros((SLOT, length), BF16)]
    each = dot(mask, jnp.concatenate(rows, axis=0), NT)
    return each + pltpu.roll(each, LANES - SLOT, 1) + pltpu.roll(each, LANES - 2 * SLOT, 1)


def split_of(index, size):
    shift = size.bit_length() - 1
    return lax.shift_right_logical(index, shift) if size == 1 << shift else index // size


def row_less_head(head_dim, width, rows=LANES):
    shape = (LANES, width)
    row = iota(shape, 0)
    if rows < LANES:
        row = row & (rows - 1)
    return row - split_of(iota(shape, 1), head_dim)


def head_of_lane(difference, first):
    return jnp.where(difference == first, 1.0, 0.0).astype(BF16)


def whole(count):
    return [pl.BlockSpec(memory_space=pltpu.VMEM)] * count


def in_hbm(*arrays):
    return [pltpu.with_memory_space_constraint(a, pltpu.HBM) for a in arrays]


SMEM = pl.BlockSpec(memory_space=pltpu.SMEM)
HBM = pl.BlockSpec(memory_space=pltpu.HBM)
ANY = pl.BlockSpec(memory_space=pl.ANY)


def params(mib):
    return pltpu.CompilerParams(vmem_limit_bytes=mib * MIB)


def cost(flops, size, transcendentals=0):
    return pl.CostEstimate(flops=flops, bytes_accessed=size, transcendentals=transcendentals)


def place_of(where):
    return where[0] & (GROUP - 1)


def bit_of(where, level):
    return (where[0] >> (level + GROUP.bit_length() - 1)) & 1 == 1


def chunk_count(width):
    return 2 if (width // GROUP) % (2 * LANES) == 0 else 1


def chunk_lanes(where, k, chunk, part):
    start = (chunk * GROUP + (place_of(where) ^ k)) * part
    return pl.ds(pl.multiple_of(start, part), part)


def masks_of(length):
    rows, other = iota((length, length), 0), iota((length, length), 1)
    after = jnp.where(other > rows, 1.0, 0.0).astype(BF16)
    return after, jnp.where(other <= rows, 1.0, 0.0).astype(BF16)


def factors_of(ld, after, until):
    length = ld.shape[1]
    terms = three(ld)
    into_end = jnp.exp(summed(after, terms)).astype(BF16)
    from_start = jnp.exp(summed(until, terms)).astype(BF16)
    total = jnp.exp(summed(jnp.ones((TAIL, length), BF16), terms))
    high = total.astype(BF16).astype(F32)
    halves = jnp.where(iota(total.shape, 0) < TAIL // 2, high, total - high).astype(BF16)
    return into_end, from_start, halves


def put_states(head_dim, pieces, where, operands, outs, ready):
    into_end, from_start, halves, b, c, xs, dys = operands
    state, part = b.shape[1], xs[0].shape[1] // GROUP
    difference = row_less_head(head_dim, part)
    for side, (factors, proj, cols) in enumerate([(into_end, b, xs), (from_start, c, dys)]):
        turned = None
        for n, (chunk, k) in enumerate(pieces):
            if n == 0 or chunk != pieces[n - 1][0]:
                ready(side, chunk)
            if turned is None:
                turned = proj[...].T
            x_scaled, dy_scaled, spread, send = outs[4 * n : 4 * n + 4]
            member = place_of(where) ^ k
            first_head = (chunk * GROUP + member) * (part // head_dim)
            hot = head_of_lane(difference, first_head)
            wide = dot(factors, hot, NN).astype(BF16)
            if side == 0:
                spread[...] = wide
                send[2 * state :, :] = dot(halves, hot, NN).astype(BF16)
            lanes = pl.ds(pl.multiple_of(member * part, part), part)
            piece = cols[chunk][:, lanes] * wide
            (dy_scaled if side else x_scaled)[...] = piece
            send[side * state : (side + 1) * state, :] = dot(turned, piece, NN).astype(BF16)


def load_chunk(chunk, source, target, sem):
    width = target.shape[1]
    copy = pltpu.make_async_copy(source.at[:, pl.ds(chunk * width, width)], target, sem)
    copy.start()
    return copy


def first_states_kernel(head_dim, pieces, where, ld_in, b_in, c_in, x_in, dy_in, *refs):
    ld, b, c, x, dy, into_end, from_start, halves = refs[:8]
    outs, sems = refs[8:-1], refs[-1]

    def load(n, source, target):
        copy = pltpu.make_async_copy(source, target, sems.at[n])
        copy.start()
        return copy

    first = load(0, ld_in, ld)
    copies = [
        [load(1, b_in, b), load_chunk(0, x_in, x, sems.at[3])],
        [load(2, c_in, c), load_chunk(0, dy_in, dy, sems.at[4])],
    ]
    masks = masks_of(ld.shape[1])
    first.wait()
    factors = factors_of(ld[...], *masks)
    for ref, value in zip((into_end, from_start, halves), factors):
        ref[...] = value

    def ready(side, chunk):
        for copy in copies[side]:
            copy.wait()

    operands = (*factors, b, c, {0: x}, {0: dy})
    put_states(head_dim, pieces, where, operands, outs, ready)


def next_states_kernel(head_dim, chunks, pieces, n_setup, where, into_end, from_start, halves, *refs):
    ld, b, c, x, dy, x_in, dy_in = refs[:7]
    setup, outs, sems = refs[7 : 7 + n_setup], refs[7 + n_setup : -1], refs[-1]
    kept, outs = outs[: 2 * (chunks - 1)], outs[2 * (chunks - 1) :]
    xs, dys, copies = {0: x}, {0: dy}, {}
    for chunk in range(1, chunks):
        xs[chunk], dys[chunk] = kept[2 * chunk - 2 : 2 * chunk]
        copies[0, chunk] = load_chunk(chunk, x_in, xs[chunk], sems.at[2 * chunk - 2])
        copies[1, chunk] = load_chunk(chunk, dy_in, dys[chunk], sems.at[2 * chunk - 1])

    def ready(side, chunk):
        if (side, chunk) in copies:
            copies[side, chunk].wait()

    put_setup(head_dim, ld, b, c, *setup)
    operands = (into_end[...], from_start[...], halves[...], b, c, xs, dys)
    put_states(head_dim, pieces[:1], where, operands, outs[:4], ready)
    put_states(head_dim, pieces[1:], where, operands, outs[4:], ready)


def states_shapes(n_parts, length, width, state):
    part = width // (GROUP * chunk_count(width))
    scaled = jax.ShapeDtypeStruct((length, part), BF16)
    send = jax.ShapeDtypeStruct((2 * state + TAIL, part), BF16)
    return [scaled, scaled, scaled, send] * n_parts


def by_piece(pieces, outs):
    return {piece: outs[4 * n : 4 * n + 4] for n, piece in enumerate(pieces)}


def first_states(head_dim, pieces, where, inputs):
    ld, b, c, x, dy = inputs
    (length, width), state = x.shape, b.shape[1]
    chunks = chunk_count(width)
    columns = jax.ShapeDtypeStruct((length, width // chunks), BF16)
    kept = [jax.ShapeDtypeStruct(a.shape, a.dtype) for a in (ld, b, c)] + [columns] * 2
    kept += [jax.ShapeDtypeStruct((rows, LANES), BF16) for rows in (length, length, TAIL)]
    outs = kept + states_shapes(len(pieces), length, width, state)
    found = pl.pallas_call(
        functools.partial(first_states_kernel, head_dim, pieces),
        out_shape=outs,
        in_specs=[SMEM] + [HBM] * 5,
        out_specs=whole(len(outs)),
        scratch_shapes=[pltpu.SemaphoreType.DMA((5,))],
        compiler_params=params(8),
        cost_estimate=cost(2 * length * width * (state + LANES), 8 * length * width),
        name="first_states",
    )(where, *in_hbm(*inputs))
    return found[:8], by_piece(pieces, found[8:])


def next_states(head_dim, pieces, where, factors, ld, b, c, x_0, dy_0, x, dy):
    (length, width), state = x.shape, b.shape[1]
    chunks = chunk_count(width)
    n_kept = 2 * (chunks - 1)
    setup = setup_shapes(head_dim, length)
    outs = setup + [jax.ShapeDtypeStruct(x_0.shape, BF16)] * n_kept
    outs += states_shapes(len(pieces), length, width, state)
    found = pl.pallas_call(
        functools.partial(next_states_kernel, head_dim, chunks, pieces, len(setup)),
        out_shape=outs,
        in_specs=[SMEM] + whole(8) + [HBM] * 2,
        out_specs=whole(len(outs)),
        scratch_shapes=[pltpu.SemaphoreType.DMA((max(n_kept, 1),))],
        compiler_params=params(8),
        cost_estimate=cost(2 * length * width * (state + LANES), 4 * length * width),
        name="next_states",
    )(where, *factors, ld, b, c, x_0, dy_0, *in_hbm(x, dy))
    setup, found = found[: len(setup)], found[len(setup) :]
    return setup, found[:n_kept], by_piece(pieces, found[n_kept:])


def decay_of(tail):
    tail = tail.astype(F32)
    return tail[:1, :] + tail[TAIL // 2 : TAIL // 2 + 1, :]


def put_decay(ref, first, factor):
    high = factor.astype(BF16).astype(F32)
    shape = (TAIL, factor.shape[1])
    both = jnp.where(iota(shape, 0) < TAIL // 2, high, factor - high)
    ref[first:, :] = both.astype(BF16)


def sent_order(parts):
    return [parts[0], *parts[:0:-1]]


def in_order(group, forward):
    return list(range(group)) if forward else list(range(group - 1, -1, -1))


def side_rows(state, forward):
    return slice(0, state) if forward else slice(state, 2 * state)


def totals_kernel(state, levels, where, *refs):
    group = GROUP
    blocks, outs, sums = sent_order(refs[:group]), refs[-1 - levels : -1], refs[-1]
    for here in range(group):

        @pl.when(place_of(where) == here)
        def _(here=here):
            decays = [decay_of(blocks[q ^ here][2 * state :, :]) for q in range(group)]
            for forward in (True, False):
                rows, value = side_rows(state, forward), None
                for q in in_order(group, forward):
                    piece = blocks[q ^ here][rows, :].astype(F32)
                    value = piece if value is None else decays[q] * value + piece
                sums[rows, :] = value.astype(BF16)

    factor = decay_of(blocks[0][2 * state :, :])
    for block in blocks[1:]:
        factor = factor * decay_of(block[2 * state :, :])
    if not levels:
        put_decay(sums, 2 * state, factor)
    for level, out in enumerate(outs):
        put_decay(out, state, factor)
        for forward in (True, False):

            @pl.when(bit_of(where, level) != forward)
            def _(out=out, forward=forward):
                out[:state, :] = sums[side_rows(state, forward), :]


def totals(state, levels, where, blocks, after):
    part = blocks[0].shape[1]
    outs = [jax.ShapeDtypeStruct((state + TAIL, part), BF16)] * levels
    if not levels:
        outs = [jax.ShapeDtypeStruct(blocks[0].shape, BF16)]
    return pl.pallas_call(
        functools.partial(totals_kernel, state, levels),
        out_shape=outs,
        in_specs=[SMEM] + whole(len(blocks)) + [ANY] * len(after),
        out_specs=whole(len(outs)),
        scratch_shapes=[pltpu.VMEM((2 * state, part), BF16)] if levels else [],
        compiler_params=params(4),
        cost_estimate=cost(8 * blocks[0].size, 10 * blocks[0].size),
        name="totals",
    )(where, *sent_order(blocks), *after)


def merged_kernel(state, level, last, where, own, received, *refs):
    out = refs[-1]
    d_own, d_other = decay_of(own[2 * state :, :]), decay_of(received[2 * state :, :])
    upper = bit_of(where, level)
    later = bit_of(where, level + 1)
    for is_upper in (False, True):
        for forward in (True, False):
            chosen = upper == is_upper
            if last:
                chosen = chosen & (later != forward)

            @pl.when(chosen)
            def _(is_upper=is_upper, forward=forward):
                rows = side_rows(state, forward)
                mine, other = own[rows, :].astype(F32), received[rows, :].astype(F32)
                value = mine + d_own * other if is_upper == forward else other + d_other * mine
                out[slice(0, state) if last else rows, :] = value.astype(BF16)

    if not last:
        put_decay(out, 2 * state, d_own * d_other)


def merged(state, level, last, where, own, received, after):
    rows = state if last else own.shape[0]
    return pl.pallas_call(
        functools.partial(merged_kernel, state, level, last),
        out_shape=pltpu.VMEM((rows, own.shape[1]), BF16),
        in_specs=[SMEM] + whole(2) + [ANY] * len(after),
        out_specs=whole(1)[0],
        compiler_params=params(4),
        cost_estimate=cost(4 * own.size, 6 * own.size),
        name="merged",
    )(where, own, received, *after)


def put_direct(state, groups, number, received, entry):
    for mine in range(groups):

        @pl.when(number == mine)
        def _(mine=mine):
            for forward in (True, False):
                rows = side_rows(state, forward)
                others = range(mine - 1, -1, -1) if forward else range(mine + 1, groups)
                value, factor = jnp.zeros((state, entry.shape[1]), F32), None
                for other in others:
                    r = received[(mine ^ other) - 1]
                    piece = r[:state, :].astype(F32)
                    value = piece if factor is None else value + factor * piece
                    d = decay_of(r[state:, :])
                    factor = d if factor is None else factor * d
                entry[rows, :] = value


def put_rounds(state, where, received, entry):
    for forward in (True, False):
        value, factor = None, 1.0
        for level, r in enumerate(received):
            gets = bit_of(where, level) == forward
            both = r.shape[0] > 2 * state
            rows = side_rows(state, forward) if both else slice(0, state)
            piece = r[rows, :].astype(F32) * jnp.where(gets, 1.0, 0.0)
            value = piece if value is None else value + factor * piece
            if both:
                factor = factor * jnp.where(gets, decay_of(r[2 * state :, :]), 1.0)
        entry[side_rows(state, forward), :] = value


def members_kernel(state, direct, n_received, where, *refs):
    received, refs = refs[:n_received], refs[n_received:]
    group = GROUP
    blocks, outs, entry = refs[:group], refs[-1 - group : -1], refs[-1]
    if direct:
        put_direct(state, n_received + 1, where[0] // group, received, entry)
    else:
        put_rounds(state, where, received, entry)
    for here in range(group):

        @pl.when(place_of(where) == here)
        def _(here=here):
            decays = [decay_of(blocks[q ^ here][2 * state :, :]) for q in range(group)]
            for forward in (True, False):
                rows, order = side_rows(state, forward), in_order(group, forward)
                value = entry[rows, :]
                for q in order:
                    outs[q ^ here][rows, :] = value.astype(BF16)
                    if q != order[-1]:
                        value = decays[q] * value + blocks[q ^ here][rows, :].astype(F32)


def member_entries(state, direct, where, blocks, received, after):
    group, part = len(blocks), blocks[0].shape[1]
    return pl.pallas_call(
        functools.partial(members_kernel, state, direct, len(received)),
        out_shape=[jax.ShapeDtypeStruct((2 * state, part), BF16)] * group,
        in_specs=[SMEM] + whole(group + len(received)) + [ANY] * len(after),
        out_specs=whole(group),
        scratch_shapes=[pltpu.VMEM((2 * state, part), F32)],
        compiler_params=params(4),
        cost_estimate=cost(12 * blocks[0].size, 16 * blocks[0].size),
        name="member_entries",
    )(where, *received, *blocks, *after)


def exchange(parts):
    count = lax.axis_size("seq")
    out = list(parts)
    for k in range(len(parts) - 1, 0, -1):
        out[k] = lax.ppermute(parts[k], "seq", [(s, s ^ k) for s in range(count)])
    return out


def split_pairs(first, count):
    if count == 1:
        return []
    middle = first + count // 2
    return (
        [(first, middle, first + count)]
        + split_pairs(first, middle - first)
        + split_pairs(middle, first + count - middle)
    )


def grouped_cuts(pieces):
    groups = {}
    for cut in split_pairs(0, pieces):
        groups.setdefault((cut[1] - cut[0], cut[2] - cut[1]), []).append(cut)
    return list(groups.items())


def rows_of(first, end, piece):
    return slice(first * piece, end * piece)


def put_setup(piece, ld, b, c, *refs):
    near, cum_terms = refs[-2:]
    heads, length = ld.shape
    rows, other = iota((length, length), 0), iota((length, length), 1)
    mask = jnp.where(other <= rows, 1.0, 0.0).astype(BF16)
    cum = summed(mask, three(ld[...] * LOG2E))
    lane = iota(cum.shape, 1)
    in_slots = jnp.where(lane < SLOT, cum, 0.0)
    in_slots = in_slots + pltpu.roll(in_slots, SLOT, 1) + pltpu.roll(in_slots, 2 * SLOT, 1)
    high, mid, low = three(in_slots)
    cum_terms[...] = jnp.where(lane < SLOT, high, jnp.where(lane < 2 * SLOT, mid, low))
    keep = iota((piece, piece), 0) <= iota((piece, piece), 1)
    pieces = length // piece
    for n in range(pieces):
        here = rows_of(n, n + 1, piece)
        near[here, :] = jnp.where(keep, dot(b[here, :], c[here, :], NT), 0.0).astype(BF16)
    cuts = [cut for _, same in grouped_cuts(pieces) for cut in same]
    for (lo, mid_, hi), far in zip(cuts, refs):
        left, right = rows_of(lo, mid_, piece), rows_of(mid_, hi, piece)
        far[...] = dot(b[left, :], c[right, :], NT).astype(BF16)


def setup_shapes(piece, length):
    cuts = [cut for _, same in grouped_cuts(length // piece) for cut in same]
    sizes = [((mid - lo) * piece, (hi - mid) * piece) for lo, mid, hi in cuts]
    sizes += [(length, piece), (length, LANES)]
    return [jax.ShapeDtypeStruct(size, BF16) for size in sizes]


def inner_kernel(head_dim, worked, chunks, n_before, n_after, b, c, *refs):
    xs, dys, refs = refs[:chunks], refs[chunks : 2 * chunks], refs[2 * chunks :]
    length, width = xs[0].shape
    piece = head_dim
    pieces = length // piece
    groups = grouped_cuts(pieces)
    n_cuts = sum(len(same) for _, same in groups)
    fars, (near, cum_terms), refs = refs[:n_cuts], refs[n_cuts : n_cuts + 2], refs[n_cuts + 2 :]
    before, refs = refs[:n_before], refs[n_before + n_after :]
    dx_outs, (db_out, dc_out, x_near, dy_near, *scratch) = refs[: len(worked)], refs[len(worked) :]
    lefts, rights = scratch[: len(groups)], scratch[len(groups) :]
    part = dx_outs[0].shape[1]
    difference = row_less_head(head_dim, part, SLOT)

    for at, (chunk, m) in enumerate(worked):
        x, dy, first_head = xs[chunk], dys[chunk], (chunk * GROUP + m) * (part // head_dim)
        lanes, here = slice(m * part, (m + 1) * part), slice(at * part, (at + 1) * part)
        cum = dot(cum_terms[...], head_of_lane(difference, first_head), NN)
        dx = []
        for n in range(pieces):
            rows = rows_of(n, n + 1, piece)
            middle = cum[n * piece + piece // 2 : n * piece + piece // 2 + 1, :]
            gap = middle - cum[rows, :]
            down, up = jnp.exp2(gap), jnp.exp2(-gap)
            x_near[rows, here] = (x[rows, lanes].astype(F32) * down).astype(BF16)
            dy_piece = (dy[rows, lanes].astype(F32) * up).astype(BF16)
            dy_near[rows, here] = dy_piece
            dx.append(down * dot(near[rows, :], dy_piece, NN))
        far_of = iter(fars)
        for (_, same), left_ref, right_ref in zip(groups, lefts, rights):
            for g, (lo, mid, hi) in enumerate(same):
                left, right = rows_of(lo, mid, piece), rows_of(mid, hi, piece)
                edge = cum[mid * piece - 1 : mid * piece, :]
                to_edge = jnp.exp2(edge - cum[left, :])
                from_edge = jnp.exp2(cum[right, :] - edge)
                x_left = (x[left, lanes].astype(F32) * to_edge).astype(BF16)
                dy_right = (dy[right, lanes].astype(F32) * from_edge).astype(BF16)
                left_ref[rows_of(g, g + 1, (mid - lo) * piece), here] = x_left
                right_ref[rows_of(g, g + 1, (hi - mid) * piece), here] = dy_right
                far = to_edge * dot(next(far_of)[...], dy_right, NN)
                for n in range(lo, mid):
                    dx[n] = dx[n] + far[rows_of(n - lo, n - lo + 1, piece), :]
        for n in range(pieces):
            dx_outs[at][rows_of(n, n + 1, piece), :] = dx[n].astype(BF16)

    if before:
        db_out[...] = before[0][...]
        dc_out[...] = before[1][...]
    else:
        db_out[...] = jnp.zeros_like(db_out)
        dc_out[...] = jnp.zeros_like(dc_out)
    batch = 4
    for first in range(0, pieces, batch):
        rows = rows_of(first, min(first + batch, pieces), piece)
        total = dot(x_near[rows, :], dy_near[rows, :], NT)
        row, col = iota(total.shape, 0), iota(total.shape, 1)
        keep = (split_of(row, piece) == split_of(col, piece)) & (row <= col)
        weighted = jnp.where(keep, total, 0.0).astype(BF16)
        db_out[rows, :] += dot(weighted, c[rows, :], NN)
        dc_out[rows, :] += dot(weighted, b[rows, :], TN)
    for ((n_left, n_right), same), left_ref, right_ref in zip(groups, lefts, rights):
        total = dot(left_ref[...], right_ref[...], NT)
        if len(same) > 1:
            row, col = iota(total.shape, 0), iota(total.shape, 1)
            same_cut = split_of(row, n_left * piece) == split_of(col, n_right * piece)
            total = jnp.where(same_cut, total, 0.0)
        weighted = total.astype(BF16)
        b_left = jnp.concatenate([b[rows_of(lo, mid, piece), :] for lo, mid, _ in same], axis=0)
        c_right = jnp.concatenate([c[rows_of(mid, hi, piece), :] for _, mid, hi in same], axis=0)
        db = dot(weighted, c_right, NN)
        dc = dot(weighted, b_left, TN)
        for g, (lo, mid, hi) in enumerate(same):
            db_out[rows_of(lo, mid, piece), :] += db[rows_of(g, g + 1, n_left * piece), :]
            dc_out[rows_of(mid, hi, piece), :] += dc[rows_of(g, g + 1, n_right * piece), :]


def inner_terms(head_dim, worked, setup, b, c, xs, dys, before, after, hides=True):
    (length, state), columns, chunks = b.shape, xs[0].size, len(xs)
    part = xs[0].shape[1] // GROUP
    used = part * len(worked)
    groups = grouped_cuts(length // head_dim)
    sizes = [[len(same) * n * head_dim for n in halves] for halves, same in groups]
    found = pl.pallas_call(
        functools.partial(inner_kernel, head_dim, worked, chunks, len(before), len(after)),
        out_shape=[jax.ShapeDtypeStruct((length, part), BF16)] * len(worked)
        + [jax.ShapeDtypeStruct((length, state), F32)] * 2,
        in_specs=whole(2 + 2 * chunks + len(setup) + len(before)) + [ANY] * len(after),
        out_specs=whole(len(worked) + 2),
        scratch_shapes=[pltpu.VMEM((length, used), BF16)] * 2
        + [pltpu.VMEM((left, used), BF16) for left, _ in sizes]
        + [pltpu.VMEM((right, used), BF16) for _, right in sizes],
        compiler_params=params(16),
        cost_estimate=cost(16 * columns * state, 8 * columns, 4 * columns) if hides else cost(1, 1),
        name="inner_terms",
    )(b, c, *xs, *dys, *setup, *before, *after)
    return dict(zip(worked, found)), list(found[-2:])


def parts_kernel(last, ks, db_before, dc_before, *refs):
    scaled, refs = refs[: 2 * len(ks)], refs[2 * len(ks) :]
    entries, outs = refs[: len(ks)], refs[-1 if last else -2 :]
    length, state = db_before.shape
    db, dc = db_before[...], dc_before[...]
    for n, entry in enumerate(entries):
        db = db + dot(scaled[2 * n][...], entry[state:, :], NT)
        dc = dc + dot(scaled[2 * n + 1][...], entry[:state, :], NT)
    if last:
        outs[0][:length, :] = db.astype(BF16)
        outs[0][length:, :] = dc.astype(BF16)
    else:
        outs[0][...] = db
        outs[1][...] = dc


def entry_parts(last, ks, scaled, db_before, dc_before, entries, after):
    length, state = db_before.shape
    one = jax.ShapeDtypeStruct((length, state), F32)
    outs = [jax.ShapeDtypeStruct((2 * length, state), BF16)] if last else [one, one]
    operands = [one for k in ks for one in scaled[k]] + [entries[k] for k in ks]
    return pl.pallas_call(
        functools.partial(parts_kernel, last, ks),
        out_shape=outs,
        in_specs=whole(2 + len(operands)) + [ANY] * len(after),
        out_specs=whole(len(outs)),
        compiler_params=params(8),
        cost_estimate=cost(2 * len(operands) * scaled[0][0].size * state, scaled[0][0].size),
        name="entry_parts",
    )(db_before, dc_before, *operands, *after)


def put_values(where, spread, b, local_parts, dx_local, entries, put):
    state, part = b.shape[1], entries[0].shape[1]
    for m, one in enumerate(local_parts):
        dx_local[:, m * part : (m + 1) * part] = one[...]
    for k, entry in enumerate(entries):
        here = slice(k * part, (k + 1) * part)
        local = dx_local[:, pl.ds(pl.multiple_of((place_of(where) ^ k) * part, part), part)]
        far = spread[k][...].astype(F32) * dot(b[...], entry[state:, :], NN)
        put(k, here, (local.astype(F32) + far).astype(BF16))


def values_kernel(where, b, *refs):
    local_parts, spread = refs[:GROUP], refs[GROUP : 2 * GROUP]
    entries, (out, dx_local) = sent_order(refs[2 * GROUP : 3 * GROUP]), refs[-2:]

    def put(k, here, value):
        out[:, here] = value

    put_values(where, spread, b, local_parts, dx_local, entries, put)


def last_values_kernel(chunks, where, b, *refs):
    local_parts, spread, refs = refs[:GROUP], refs[GROUP : 2 * GROUP], refs[2 * GROUP :]
    entries, before = sent_order(refs[:GROUP]), refs[GROUP : GROUP + chunks - 1]
    out, dx, dx_local, sems = refs[-4:]
    part = entries[0].shape[1]
    stores = []

    def store(chunk, k, source):
        lanes = chunk_lanes(where, k, chunk, part)
        at = sems.at[chunk * GROUP + k]
        stores.append(pltpu.make_async_copy(source, out.at[:, lanes], at))
        stores[-1].start()

    for chunk, values in enumerate(before):
        for k in range(GROUP):
            store(chunk, k, values.at[:, pl.ds(k * part, part)])

    def put(k, here, value):
        dx[k] = value
        store(chunks - 1, k, dx.at[k])

    put_values(where, spread, b, local_parts, dx_local, entries, put)
    for one in stores:
        one.wait()


def entry_values(chunk, chunks, where, spread, b, local_parts, entries, before):
    length, part = b.shape[0], entries[0].shape[1]
    last = chunk == chunks - 1
    estimate = cost(8 * local_parts[0].size * b.shape[1], 16 * local_parts[0].size)
    operands = [where, b, *local_parts, *spread, *sent_order(entries)]
    if not last:
        return pl.pallas_call(
            values_kernel,
            out_shape=jax.ShapeDtypeStruct((length, GROUP * part), BF16),
            in_specs=[SMEM] + whole(1 + 3 * GROUP),
            out_specs=whole(1)[0],
            scratch_shapes=[pltpu.VMEM((length, GROUP * part), BF16)],
            compiler_params=params(8),
            cost_estimate=estimate,
            name="entry_values",
        )(*operands)
    return pl.pallas_call(
        functools.partial(last_values_kernel, chunks),
        out_shape=pltpu.HBM((length, chunks * GROUP * part), BF16),
        in_specs=[SMEM] + whole(1 + 3 * GROUP + len(before)),
        out_specs=HBM,
        scratch_shapes=[
            pltpu.VMEM((GROUP, length, part), BF16),
            pltpu.VMEM((length, GROUP * part), BF16),
            pltpu.SemaphoreType.DMA((chunks * GROUP,)),
        ],
        compiler_params=params(8),
        cost_estimate=estimate,
        name="last_values",
    )(*operands, *before)


def sum_kernel(*refs):
    parts, (db, dc) = refs[:-2], refs[-2:]
    length = db.shape[0]
    for out, rows in ((db, slice(0, length)), (dc, slice(length, 2 * length))):
        total = parts[0][rows, :].astype(F32)
        for part in parts[1:]:
            total = total + part[rows, :].astype(F32)
        out[...] = total.astype(BF16)


def over_heads(part):
    count, (rows, state) = lax.axis_size("head"), part.shape
    parts = [part]
    for shift in range(1, count):
        pairs = [(s, (s + shift) % count) for s in range(count)]
        parts.append(lax.ppermute(part, "head", pairs))
    return pl.pallas_call(
        sum_kernel,
        out_shape=[jax.ShapeDtypeStruct((rows // 2, state), BF16)] * 2,
        in_specs=whole(count),
        out_specs=whole(2),
        compiler_params=params(4),
        cost_estimate=cost(count * part.size, 2 * count * part.size),
        name="sum_over_heads",
    )(*parts)


def shards(token_values, b_inputs, c_inputs, log_decay, grad_out):
    head_dim = token_values.shape[1] // log_decay.shape[0]
    state = b_inputs.shape[1]
    count, group = lax.axis_size("seq"), GROUP
    chunks = chunk_count(token_values.shape[1])
    levels = (count // group).bit_length() - 1
    where = lax.axis_index("seq").astype(jnp.int32)[None]
    inputs = (log_decay, b_inputs, c_inputs, token_values, grad_out)
    order = [(chunk, k) for chunk in range(chunks) for k in range(group - 1, -1, -1)]
    kept, states = first_states(head_dim, order[: group - 1], where, inputs)
    ld, b, c, x_0, dy_0, *factors = kept
    late = order[group - 1 :]
    columns = (x_0, dy_0, token_values, grad_out)
    setup, more, found = next_states(head_dim, late, where, factors, ld, b, c, *columns)
    states.update(found)
    xs, dys = [x_0, *more[::2]], [dy_0, *more[1::2]]
    blocks = [
        exchange([states[chunk, k][3] for k in range(group)]) for chunk in range(chunks)
    ]

    def to_group(block, k):
        return lax.ppermute(block, "seq", [(s, s ^ (k * group)) for s in range(count)])

    every = [(chunk, m) for chunk in range(chunks) for m in range(group)]
    worked = [every[1:4]] + [every[chunk * group :][:2] for chunk in range(1, chunks)]
    rest = [one for one in every[1:] if not any(one in some for some in worked)]
    entries, inner, sums = [], {}, []

    def add_inner(some, after, hides=True):
        found, sums[:] = inner_terms(head_dim, some, setup, b, c, xs, dys, sums, after, hides)
        inner.update(found)

    own = [totals(state, 0, where, blocks[0], setup[-1:])]
    add_inner(every[:1], own[0], False)
    own += [totals(state, 0, where, blocks[chunk], sums[:1]) for chunk in range(1, chunks)]
    for chunk in range(chunks):
        (total,) = own[chunk]
        received = [to_group(total, 1)]
        for level in range(levels - 1):
            last = level == levels - 2
            total = merged(state, level, last, where, total, received[level], [])
            received.append(to_group(total, 2 << level))
        add_inner(worked[chunk], [total])
        found = member_entries(state, False, where, blocks[chunk], received, sums[:1])
        entries.append(exchange(found))
    if rest:
        add_inner(rest, found[:1])

    values = []
    for chunk in range(chunks):
        last = chunk == chunks - 1
        ours = [states[chunk, k] for k in range(group)]
        scaled = [one[:2] for one in ours]
        spread = [one[2] for one in ours]
        if last:
            sums = entry_parts(False, (0, 3), scaled, *sums, entries[chunk], values)
        ks = (2, 1) if last else (0, 3, 2, 1)
        sums = entry_parts(last, ks, scaled, *sums, entries[chunk], [])
        local = [inner[chunk, m] for m in range(group)]
        values.append(
            entry_values(chunk, chunks, where, spread, b, local, entries[chunk], values)
        )
    return (values[-1], *over_heads(sums[0]))


def solution(mesh):
    in_specs = (
        P("seq", "head"),
        P("seq", None),
        P("seq", None),
        P("head", "seq"),
        P("seq", "head"),
    )
    out_specs = (P("seq", "head"), P("seq", None), P("seq", None))
    return jax.shard_map(shards, mesh=mesh, in_specs=in_specs, out_specs=out_specs, check_vma=False)
```

```python
import functools

import jax
import jax.numpy as jnp
from jax import lax
from jax.experimental import pallas as pl
from jax.experimental.pallas import tpu as pltpu
from jax.sharding import PartitionSpec as P

BF16 = jnp.bfloat16
F32 = jnp.float32
LANES = 128
GROUP = 4
TAIL = 16
LOG2E = 1.4426950408889634
MIB = 1024 * 1024

NN = (((1,), (0,)), ((), ()))
NT = (((1,), (1,)), ((), ()))
TN = (((0,), (0,)), ((), ()))


def dot(a, b, dims):
    return lax.dot_general(a, b, dims, preferred_element_type=F32)


def iota(shape, dim):
    return lax.broadcasted_iota(jnp.int32, shape, dim)


def three(values):
    high = values.astype(BF16)
    rest = values - high.astype(F32)
    mid = rest.astype(BF16)
    return high, mid, (rest - mid.astype(F32)).astype(BF16)


SLOT = LANES // 4


def summed(mask, terms):
    heads, length = terms[0].shape
    gap = [] if heads == SLOT else [jnp.zeros((SLOT - heads, length), BF16)]
    rows = [r for t in terms for r in [t] + gap] + [jnp.zeros((SLOT, length), BF16)]
    each = dot(mask, jnp.concatenate(rows, axis=0), NT)
    return each + pltpu.roll(each, LANES - SLOT, 1) + pltpu.roll(each, LANES - 2 * SLOT, 1)


def split_of(index, size):
    shift = size.bit_length() - 1
    return lax.shift_right_logical(index, shift) if size == 1 << shift else index // size


def row_less_head(head_dim, width, rows=LANES):
    shape = (LANES, width)
    row = iota(shape, 0)
    if rows < LANES:
        row = row & (rows - 1)
    return row - split_of(iota(shape, 1), head_dim)


def head_of_lane(difference, first):
    return jnp.where(difference == first, 1.0, 0.0).astype(BF16)


def whole(count):
    return [pl.BlockSpec(memory_space=pltpu.VMEM)] * count


def in_hbm(*arrays):
    return [pltpu.with_memory_space_constraint(a, pltpu.HBM) for a in arrays]


SMEM = pl.BlockSpec(memory_space=pltpu.SMEM)
HBM = pl.BlockSpec(memory_space=pltpu.HBM)
ANY = pl.BlockSpec(memory_space=pl.ANY)


def params(mib):
    return pltpu.CompilerParams(vmem_limit_bytes=mib * MIB)


def cost(flops, size, transcendentals=0):
    return pl.CostEstimate(flops=flops, bytes_accessed=size, transcendentals=transcendentals)


def place_of(where):
    return where[0] & (GROUP - 1)


def bit_of(where, level):
    return (where[0] >> (level + GROUP.bit_length() - 1)) & 1 == 1


def chunk_count(width):
    return 2 if (width // GROUP) % (2 * LANES) == 0 else 1


def chunk_lanes(where, k, chunk, part):
    start = (chunk * GROUP + (place_of(where) ^ k)) * part
    return pl.ds(pl.multiple_of(start, part), part)


def masks_of(length):
    rows, other = iota((length, length), 0), iota((length, length), 1)
    after = jnp.where(other > rows, 1.0, 0.0).astype(BF16)
    return after, jnp.where(other <= rows, 1.0, 0.0).astype(BF16)


def factors_of(ld, after, until):
    length = ld.shape[1]
    terms = three(ld)
    into_end = jnp.exp(summed(after, terms)).astype(BF16)
    from_start = jnp.exp(summed(until, terms)).astype(BF16)
    total = jnp.exp(summed(jnp.ones((TAIL, length), BF16), terms))
    high = total.astype(BF16).astype(F32)
    halves = jnp.where(iota(total.shape, 0) < TAIL // 2, high, total - high).astype(BF16)
    return into_end, from_start, halves


def put_states(head_dim, chunks, pieces, where, operands, outs, ready):
    into_end, from_start, halves, b, c, xs, dys = operands
    state, part = b.shape[1], xs[0].shape[1] // GROUP
    difference = row_less_head(head_dim, part)
    for side, (factors, proj, cols) in enumerate([(into_end, b, xs), (from_start, c, dys)]):
        turned = None
        for n, (chunk, k) in enumerate(pieces):
            if n == 0 or chunk != pieces[n - 1][0]:
                ready(side, chunk)
            if turned is None:
                turned = proj[...].T
            x_scaled, dy_scaled, spread, send = outs[4 * n : 4 * n + 4]
            member = place_of(where) ^ k
            first_head = (chunk * GROUP + member) * (part // head_dim)
            hot = head_of_lane(difference, first_head)
            wide = dot(factors, hot, NN).astype(BF16)
            if side == 0:
                spread[...] = wide
                send[2 * state :, :] = dot(halves, hot, NN).astype(BF16)
            lanes = pl.ds(pl.multiple_of(member * part, part), part)
            piece = cols[chunk][:, lanes] * wide
            (dy_scaled if side else x_scaled)[...] = piece
            send[side * state : (side + 1) * state, :] = dot(turned, piece, NN).astype(BF16)


def load_chunk(chunk, source, target, sem):
    width = target.shape[1]
    copy = pltpu.make_async_copy(source.at[:, pl.ds(chunk * width, width)], target, sem)
    copy.start()
    return copy


def first_states_kernel(head_dim, chunks, pieces, where, ld_in, b_in, c_in, x_in, dy_in, *refs):
    ld, b, c, x, dy, into_end, from_start, halves = refs[:8]
    outs, sems = refs[8:-1], refs[-1]

    def load(n, source, target):
        copy = pltpu.make_async_copy(source, target, sems.at[n])
        copy.start()
        return copy

    first = load(0, ld_in, ld)
    copies = [
        [load(1, b_in, b), load_chunk(0, x_in, x, sems.at[3])],
        [load(2, c_in, c), load_chunk(0, dy_in, dy, sems.at[4])],
    ]
    masks = masks_of(ld.shape[1])
    first.wait()
    factors = factors_of(ld[...], *masks)
    for ref, value in zip((into_end, from_start, halves), factors):
        ref[...] = value

    def ready(side, chunk):
        for copy in copies[side]:
            copy.wait()

    operands = (*factors, b, c, {0: x}, {0: dy})
    put_states(head_dim, chunks, pieces, where, operands, outs, ready)


def next_states_kernel(head_dim, chunks, pieces, where, into_end, from_start, halves, *refs):
    b, c, x, dy, x_in, dy_in = refs[:6]
    outs, sems = refs[6:-1], refs[-1]
    kept, outs = outs[: 2 * (chunks - 1)], outs[2 * (chunks - 1) :]
    xs, dys, copies = {0: x}, {0: dy}, {}
    for chunk in range(1, chunks):
        xs[chunk], dys[chunk] = kept[2 * chunk - 2 : 2 * chunk]
        copies[0, chunk] = load_chunk(chunk, x_in, xs[chunk], sems.at[2 * chunk - 2])
        copies[1, chunk] = load_chunk(chunk, dy_in, dys[chunk], sems.at[2 * chunk - 1])

    def ready(side, chunk):
        if (side, chunk) in copies:
            copies[side, chunk].wait()

    operands = (into_end[...], from_start[...], halves[...], b, c, xs, dys)
    put_states(head_dim, chunks, pieces, where, operands, outs, ready)


def states_shapes(n_parts, length, width, state):
    part = width // (GROUP * chunk_count(width))
    scaled = jax.ShapeDtypeStruct((length, part), BF16)
    send = jax.ShapeDtypeStruct((2 * state + TAIL, part), BF16)
    return [scaled, scaled, scaled, send] * n_parts


def by_piece(pieces, outs):
    return {piece: outs[4 * n : 4 * n + 4] for n, piece in enumerate(pieces)}


def first_states(head_dim, pieces, where, inputs):
    ld, b, c, x, dy = inputs
    (length, width), state = x.shape, b.shape[1]
    chunks = chunk_count(width)
    columns = jax.ShapeDtypeStruct((length, width // chunks), BF16)
    kept = [jax.ShapeDtypeStruct(a.shape, a.dtype) for a in (ld, b, c)] + [columns] * 2
    kept += [jax.ShapeDtypeStruct((rows, LANES), BF16) for rows in (length, length, TAIL)]
    outs = kept + states_shapes(len(pieces), length, width, state)
    found = pl.pallas_call(
        functools.partial(first_states_kernel, head_dim, chunks, pieces),
        out_shape=outs,
        in_specs=[SMEM] + [HBM] * 5,
        out_specs=whole(len(outs)),
        scratch_shapes=[pltpu.SemaphoreType.DMA((5,))],
        compiler_params=params(8),
        cost_estimate=cost(2 * length * width * (state + LANES), 8 * length * width),
        name="first_states",
    )(where, *in_hbm(*inputs))
    return found[:8], by_piece(pieces, found[8:])


def next_states(head_dim, pieces, where, factors, b, c, x_0, dy_0, x, dy):
    (length, width), state = x.shape, b.shape[1]
    chunks = chunk_count(width)
    n_kept = 2 * (chunks - 1)
    outs = [jax.ShapeDtypeStruct(x_0.shape, BF16)] * n_kept
    outs += states_shapes(len(pieces), length, width, state)
    found = pl.pallas_call(
        functools.partial(next_states_kernel, head_dim, chunks, pieces),
        out_shape=outs,
        in_specs=[SMEM] + whole(7) + [HBM] * 2,
        out_specs=whole(len(outs)),
        scratch_shapes=[pltpu.SemaphoreType.DMA((max(n_kept, 1),))],
        compiler_params=params(8),
        cost_estimate=cost(2 * length * width * (state + LANES), 4 * length * width),
        name="next_states",
    )(where, *factors, b, c, x_0, dy_0, *in_hbm(x, dy))
    return found[:n_kept], by_piece(pieces, found[n_kept:])


def decay_of(tail):
    tail = tail.astype(F32)
    return tail[:1, :] + tail[TAIL // 2 : TAIL // 2 + 1, :]


def put_decay(ref, first, factor):
    high = factor.astype(BF16).astype(F32)
    shape = (TAIL, factor.shape[1])
    both = jnp.where(iota(shape, 0) < TAIL // 2, high, factor - high)
    ref[first:, :] = both.astype(BF16)


def sent_order(parts):
    return [parts[0], *parts[:0:-1]]


def in_order(group, forward):
    return list(range(group)) if forward else list(range(group - 1, -1, -1))


def side_rows(state, forward):
    return slice(0, state) if forward else slice(state, 2 * state)


def totals_kernel(state, levels, where, *refs):
    group = GROUP
    blocks, outs, sums = sent_order(refs[:group]), refs[-1 - levels : -1], refs[-1]
    for here in range(group):

        @pl.when(place_of(where) == here)
        def _(here=here):
            decays = [decay_of(blocks[q ^ here][2 * state :, :]) for q in range(group)]
            for forward in (True, False):
                rows, value = side_rows(state, forward), None
                for q in in_order(group, forward):
                    piece = blocks[q ^ here][rows, :].astype(F32)
                    value = piece if value is None else decays[q] * value + piece
                sums[rows, :] = value.astype(BF16)

    factor = decay_of(blocks[0][2 * state :, :])
    for block in blocks[1:]:
        factor = factor * decay_of(block[2 * state :, :])
    if not levels:
        put_decay(sums, 2 * state, factor)
    for level, out in enumerate(outs):
        put_decay(out, state, factor)
        for forward in (True, False):

            @pl.when(bit_of(where, level) != forward)
            def _(out=out, forward=forward):
                out[:state, :] = sums[side_rows(state, forward), :]


def totals(state, levels, where, blocks, after):
    part = blocks[0].shape[1]
    outs = [jax.ShapeDtypeStruct((state + TAIL, part), BF16)] * levels
    if not levels:
        outs = [jax.ShapeDtypeStruct(blocks[0].shape, BF16)]
    return pl.pallas_call(
        functools.partial(totals_kernel, state, levels),
        out_shape=outs,
        in_specs=[SMEM] + whole(len(blocks)) + [ANY] * len(after),
        out_specs=whole(len(outs)),
        scratch_shapes=[pltpu.VMEM((2 * state, part), BF16)] if levels else [],
        compiler_params=params(4),
        cost_estimate=cost(8 * blocks[0].size, 10 * blocks[0].size),
        name="totals",
    )(where, *sent_order(blocks), *after)


def merged_kernel(state, level, last, where, own, received, *refs):
    out = refs[-1]
    d_own, d_other = decay_of(own[2 * state :, :]), decay_of(received[2 * state :, :])
    upper = bit_of(where, level)
    later = bit_of(where, level + 1)
    for is_upper in (False, True):
        for forward in (True, False):
            chosen = upper == is_upper
            if last:
                chosen = chosen & (later != forward)

            @pl.when(chosen)
            def _(is_upper=is_upper, forward=forward):
                rows = side_rows(state, forward)
                mine, other = own[rows, :].astype(F32), received[rows, :].astype(F32)
                value = mine + d_own * other if is_upper == forward else other + d_other * mine
                out[slice(0, state) if last else rows, :] = value.astype(BF16)

    if not last:
        put_decay(out, 2 * state, d_own * d_other)


def merged(state, level, last, where, own, received, after):
    rows = state if last else own.shape[0]
    return pl.pallas_call(
        functools.partial(merged_kernel, state, level, last),
        out_shape=pltpu.VMEM((rows, own.shape[1]), BF16),
        in_specs=[SMEM] + whole(2) + [ANY] * len(after),
        out_specs=whole(1)[0],
        compiler_params=params(4),
        cost_estimate=cost(4 * own.size, 6 * own.size),
        name="merged",
    )(where, own, received, *after)


def put_direct(state, groups, number, received, entry):
    for mine in range(groups):

        @pl.when(number == mine)
        def _(mine=mine):
            for forward in (True, False):
                rows = side_rows(state, forward)
                others = range(mine - 1, -1, -1) if forward else range(mine + 1, groups)
                value, factor = jnp.zeros((state, entry.shape[1]), F32), None
                for other in others:
                    r = received[(mine ^ other) - 1]
                    piece = r[:state, :].astype(F32)
                    value = piece if factor is None else value + factor * piece
                    d = decay_of(r[state:, :])
                    factor = d if factor is None else factor * d
                entry[rows, :] = value


def put_rounds(state, where, received, entry):
    for forward in (True, False):
        value, factor = None, 1.0
        for level, r in enumerate(received):
            gets = bit_of(where, level) == forward
            both = r.shape[0] > 2 * state
            rows = side_rows(state, forward) if both else slice(0, state)
            piece = r[rows, :].astype(F32) * jnp.where(gets, 1.0, 0.0)
            value = piece if value is None else value + factor * piece
            if both:
                factor = factor * jnp.where(gets, decay_of(r[2 * state :, :]), 1.0)
        entry[side_rows(state, forward), :] = value


def members_kernel(state, direct, n_received, where, *refs):
    received, refs = refs[:n_received], refs[n_received:]
    group = GROUP
    blocks, outs, entry = refs[:group], refs[-1 - group : -1], refs[-1]
    if direct:
        put_direct(state, n_received + 1, where[0] // group, received, entry)
    else:
        put_rounds(state, where, received, entry)
    for here in range(group):

        @pl.when(place_of(where) == here)
        def _(here=here):
            decays = [decay_of(blocks[q ^ here][2 * state :, :]) for q in range(group)]
            for forward in (True, False):
                rows, order = side_rows(state, forward), in_order(group, forward)
                value = entry[rows, :]
                for q in order:
                    outs[q ^ here][rows, :] = value.astype(BF16)
                    if q != order[-1]:
                        value = decays[q] * value + blocks[q ^ here][rows, :].astype(F32)


def member_entries(state, direct, where, blocks, received, after):
    group, part = len(blocks), blocks[0].shape[1]
    return pl.pallas_call(
        functools.partial(members_kernel, state, direct, len(received)),
        out_shape=[jax.ShapeDtypeStruct((2 * state, part), BF16)] * group,
        in_specs=[SMEM] + whole(group + len(received)) + [ANY] * len(after),
        out_specs=whole(group),
        scratch_shapes=[pltpu.VMEM((2 * state, part), F32)],
        compiler_params=params(4),
        cost_estimate=cost(12 * blocks[0].size, 16 * blocks[0].size),
        name="member_entries",
    )(where, *received, *blocks, *after)


def exchange(parts):
    count = lax.axis_size("seq")
    out = list(parts)
    for k in range(len(parts) - 1, 0, -1):
        out[k] = lax.ppermute(parts[k], "seq", [(s, s ^ k) for s in range(count)])
    return out


def split_pairs(first, count):
    if count == 1:
        return []
    middle = first + count // 2
    return (
        [(first, middle, first + count)]
        + split_pairs(first, middle - first)
        + split_pairs(middle, first + count - middle)
    )


def grouped_cuts(pieces):
    groups = {}
    for cut in split_pairs(0, pieces):
        groups.setdefault((cut[1] - cut[0], cut[2] - cut[1]), []).append(cut)
    return list(groups.items())


def rows_of(first, end, piece):
    return slice(first * piece, end * piece)


def setup_kernel(piece, ld, b, c, *refs):
    near, cum_terms = refs[-2:]
    heads, length = ld.shape
    rows, other = iota((length, length), 0), iota((length, length), 1)
    mask = jnp.where(other <= rows, 1.0, 0.0).astype(BF16)
    cum = summed(mask, three(ld[...] * LOG2E))
    lane = iota(cum.shape, 1)
    in_slots = jnp.where(lane < SLOT, cum, 0.0)
    in_slots = in_slots + pltpu.roll(in_slots, SLOT, 1) + pltpu.roll(in_slots, 2 * SLOT, 1)
    high, mid, low = three(in_slots)
    cum_terms[...] = jnp.where(lane < SLOT, high, jnp.where(lane < 2 * SLOT, mid, low))
    keep = iota((piece, piece), 0) <= iota((piece, piece), 1)
    pieces = length // piece
    for n in range(pieces):
        here = rows_of(n, n + 1, piece)
        near[here, :] = jnp.where(keep, dot(b[here, :], c[here, :], NT), 0.0).astype(BF16)
    cuts = [cut for _, same in grouped_cuts(pieces) for cut in same]
    for (lo, mid_, hi), far in zip(cuts, refs):
        left, right = rows_of(lo, mid_, piece), rows_of(mid_, hi, piece)
        far[...] = dot(b[left, :], c[right, :], NT).astype(BF16)


def inner_setup(piece, ld, b, c, after):
    length = b.shape[0]
    cuts = [cut for _, same in grouped_cuts(length // piece) for cut in same]
    outs = [
        jax.ShapeDtypeStruct(((mid - lo) * piece, (hi - mid) * piece), BF16) for lo, mid, hi in cuts
    ]
    outs.append(jax.ShapeDtypeStruct((length, piece), BF16))
    outs.append(jax.ShapeDtypeStruct((length, LANES), BF16))
    return pl.pallas_call(
        functools.partial(setup_kernel_after, piece, len(after)),
        out_shape=outs,
        in_specs=whole(3) + [ANY] * len(after),
        out_specs=whole(len(outs)),
        compiler_params=params(4),
        cost_estimate=cost(8 * b.size * length, 8 * b.size),
        name="inner_setup",
    )(ld, b, c, *after)


def setup_kernel_after(piece, n_after, ld, b, c, *refs):
    setup_kernel(piece, ld, b, c, *refs[n_after:])


def inner_kernel(head_dim, worked, chunks, n_before, n_after, b, c, *refs):
    xs, dys, refs = refs[:chunks], refs[chunks : 2 * chunks], refs[2 * chunks :]
    length, width = xs[0].shape
    piece = head_dim
    pieces = length // piece
    groups = grouped_cuts(pieces)
    n_cuts = sum(len(same) for _, same in groups)
    fars, (near, cum_terms), refs = refs[:n_cuts], refs[n_cuts : n_cuts + 2], refs[n_cuts + 2 :]
    before, refs = refs[:n_before], refs[n_before + n_after :]
    dx_outs, (db_out, dc_out, x_near, dy_near, *scratch) = refs[: len(worked)], refs[len(worked) :]
    lefts, rights = scratch[: len(groups)], scratch[len(groups) :]
    part = dx_outs[0].shape[1]
    difference = row_less_head(head_dim, part, SLOT)

    for at, (chunk, m) in enumerate(worked):
        x, dy, first_head = xs[chunk], dys[chunk], (chunk * GROUP + m) * (part // head_dim)
        lanes, here = slice(m * part, (m + 1) * part), slice(at * part, (at + 1) * part)
        cum = dot(cum_terms[...], head_of_lane(difference, first_head), NN)
        dx = []
        for n in range(pieces):
            rows = rows_of(n, n + 1, piece)
            middle = cum[n * piece + piece // 2 : n * piece + piece // 2 + 1, :]
            gap = middle - cum[rows, :]
            down, up = jnp.exp2(gap), jnp.exp2(-gap)
            x_near[rows, here] = (x[rows, lanes].astype(F32) * down).astype(BF16)
            dy_piece = (dy[rows, lanes].astype(F32) * up).astype(BF16)
            dy_near[rows, here] = dy_piece
            dx.append(down * dot(near[rows, :], dy_piece, NN))
        far_of = iter(fars)
        for (_, same), left_ref, right_ref in zip(groups, lefts, rights):
            for g, (lo, mid, hi) in enumerate(same):
                left, right = rows_of(lo, mid, piece), rows_of(mid, hi, piece)
                edge = cum[mid * piece - 1 : mid * piece, :]
                to_edge = jnp.exp2(edge - cum[left, :])
                from_edge = jnp.exp2(cum[right, :] - edge)
                x_left = (x[left, lanes].astype(F32) * to_edge).astype(BF16)
                dy_right = (dy[right, lanes].astype(F32) * from_edge).astype(BF16)
                left_ref[rows_of(g, g + 1, (mid - lo) * piece), here] = x_left
                right_ref[rows_of(g, g + 1, (hi - mid) * piece), here] = dy_right
                far = to_edge * dot(next(far_of)[...], dy_right, NN)
                for n in range(lo, mid):
                    dx[n] = dx[n] + far[rows_of(n - lo, n - lo + 1, piece), :]
        for n in range(pieces):
            dx_outs[at][rows_of(n, n + 1, piece), :] = dx[n].astype(BF16)

    if before:
        db_out[...] = before[0][...]
        dc_out[...] = before[1][...]
    else:
        db_out[...] = jnp.zeros_like(db_out)
        dc_out[...] = jnp.zeros_like(dc_out)
    batch = 4
    for first in range(0, pieces, batch):
        rows = rows_of(first, min(first + batch, pieces), piece)
        total = dot(x_near[rows, :], dy_near[rows, :], NT)
        row, col = iota(total.shape, 0), iota(total.shape, 1)
        keep = (split_of(row, piece) == split_of(col, piece)) & (row <= col)
        weighted = jnp.where(keep, total, 0.0).astype(BF16)
        db_out[rows, :] += dot(weighted, c[rows, :], NN)
        dc_out[rows, :] += dot(weighted, b[rows, :], TN)
    for ((n_left, n_right), same), left_ref, right_ref in zip(groups, lefts, rights):
        total = dot(left_ref[...], right_ref[...], NT)
        if len(same) > 1:
            row, col = iota(total.shape, 0), iota(total.shape, 1)
            same_cut = split_of(row, n_left * piece) == split_of(col, n_right * piece)
            total = jnp.where(same_cut, total, 0.0)
        weighted = total.astype(BF16)
        b_left = jnp.concatenate([b[rows_of(lo, mid, piece), :] for lo, mid, _ in same], axis=0)
        c_right = jnp.concatenate([c[rows_of(mid, hi, piece), :] for _, mid, hi in same], axis=0)
        db = dot(weighted, c_right, NN)
        dc = dot(weighted, b_left, TN)
        for g, (lo, mid, hi) in enumerate(same):
            db_out[rows_of(lo, mid, piece), :] += db[rows_of(g, g + 1, n_left * piece), :]
            dc_out[rows_of(mid, hi, piece), :] += dc[rows_of(g, g + 1, n_right * piece), :]


def inner_terms(head_dim, worked, setup, b, c, xs, dys, before, after, hides=True):
    (length, state), columns, chunks = b.shape, xs[0].size, len(xs)
    part = xs[0].shape[1] // GROUP
    used = part * len(worked)
    groups = grouped_cuts(length // head_dim)
    sizes = [[len(same) * n * head_dim for n in halves] for halves, same in groups]
    found = pl.pallas_call(
        functools.partial(inner_kernel, head_dim, worked, chunks, len(before), len(after)),
        out_shape=[jax.ShapeDtypeStruct((length, part), BF16)] * len(worked)
        + [jax.ShapeDtypeStruct((length, state), F32)] * 2,
        in_specs=whole(2 + 2 * chunks + len(setup) + len(before)) + [ANY] * len(after),
        out_specs=whole(len(worked) + 2),
        scratch_shapes=[pltpu.VMEM((length, used), BF16)] * 2
        + [pltpu.VMEM((left, used), BF16) for left, _ in sizes]
        + [pltpu.VMEM((right, used), BF16) for _, right in sizes],
        compiler_params=params(16),
        cost_estimate=cost(16 * columns * state, 8 * columns, 4 * columns) if hides else cost(1, 1),
        name="inner_terms",
    )(b, c, *xs, *dys, *setup, *before, *after)
    return dict(zip(worked, found)), list(found[-2:])


def parts_kernel(last, ks, db_before, dc_before, *refs):
    scaled, refs = refs[: 2 * len(ks)], refs[2 * len(ks) :]
    entries, outs = refs[: len(ks)], refs[-1 if last else -2 :]
    length, state = db_before.shape
    db, dc = db_before[...], dc_before[...]
    for n, entry in enumerate(entries):
        db = db + dot(scaled[2 * n][...], entry[state:, :], NT)
        dc = dc + dot(scaled[2 * n + 1][...], entry[:state, :], NT)
    if last:
        outs[0][:length, :] = db.astype(BF16)
        outs[0][length:, :] = dc.astype(BF16)
    else:
        outs[0][...] = db
        outs[1][...] = dc


def entry_parts(last, ks, scaled, db_before, dc_before, entries, after):
    length, state = db_before.shape
    one = jax.ShapeDtypeStruct((length, state), F32)
    outs = [jax.ShapeDtypeStruct((2 * length, state), BF16)] if last else [one, one]
    operands = [one for k in ks for one in scaled[k]] + [entries[k] for k in ks]
    return pl.pallas_call(
        functools.partial(parts_kernel, last, ks),
        out_shape=outs,
        in_specs=whole(2 + len(operands)) + [ANY] * len(after),
        out_specs=whole(len(outs)),
        compiler_params=params(8),
        cost_estimate=cost(2 * len(operands) * scaled[0][0].size * state, scaled[0][0].size),
        name="entry_parts",
    )(db_before, dc_before, *operands, *after)


def put_values(where, spread, b, local_parts, dx_local, entries, put):
    state, part = b.shape[1], entries[0].shape[1]
    for m, one in enumerate(local_parts):
        dx_local[:, m * part : (m + 1) * part] = one[...]
    for k, entry in enumerate(entries):
        lanes = pl.ds(pl.multiple_of((place_of(where) ^ k) * part, part), part)
        local = dx_local[:, lanes]
        far = spread[k][...].astype(F32) * dot(b[...], entry[state:, :], NN)
        put(k, lanes, (local.astype(F32) + far).astype(BF16))


def values_kernel(where, b, *refs):
    local_parts, spread = refs[:GROUP], refs[GROUP : 2 * GROUP]
    entries, (out, dx_local) = sent_order(refs[2 * GROUP : 3 * GROUP]), refs[-2:]

    def put(k, lanes, value):
        out[:, lanes] = value

    put_values(where, spread, b, local_parts, dx_local, entries, put)


def last_values_kernel(chunks, where, b, *refs):
    local_parts, spread, refs = refs[:GROUP], refs[GROUP : 2 * GROUP], refs[2 * GROUP :]
    entries, before = sent_order(refs[:GROUP]), refs[GROUP : GROUP + chunks - 1]
    out, dx, dx_local, sems = refs[-4:]
    part = entries[0].shape[1]
    stores = []

    def store(n, source, target):
        stores.append(pltpu.make_async_copy(source, target, sems.at[n]))
        stores[-1].start()

    for chunk, values in enumerate(before):
        store(GROUP + chunk, values, out.at[:, pl.ds(chunk * GROUP * part, GROUP * part)])

    def put(k, lanes, value):
        dx[k] = value
        store(k, dx.at[k], out.at[:, chunk_lanes(where, k, chunks - 1, part)])

    put_values(where, spread, b, local_parts, dx_local, entries, put)
    for one in stores:
        one.wait()


def entry_values(chunk, chunks, where, spread, b, local_parts, entries, before):
    length, part = b.shape[0], entries[0].shape[1]
    last = chunk == chunks - 1
    estimate = cost(8 * local_parts[0].size * b.shape[1], 16 * local_parts[0].size)
    operands = [where, b, *local_parts, *spread, *sent_order(entries)]
    if not last:
        return pl.pallas_call(
            values_kernel,
            out_shape=jax.ShapeDtypeStruct((length, GROUP * part), BF16),
            in_specs=[SMEM] + whole(1 + 3 * GROUP),
            out_specs=whole(1)[0],
            scratch_shapes=[pltpu.VMEM((length, GROUP * part), BF16)],
            compiler_params=params(8),
            cost_estimate=estimate,
            name="entry_values",
        )(*operands)
    return pl.pallas_call(
        functools.partial(last_values_kernel, chunks),
        out_shape=pltpu.HBM((length, chunks * GROUP * part), BF16),
        in_specs=[SMEM] + whole(1 + 3 * GROUP + len(before)),
        out_specs=HBM,
        scratch_shapes=[
            pltpu.VMEM((GROUP, length, part), BF16),
            pltpu.VMEM((length, GROUP * part), BF16),
            pltpu.SemaphoreType.DMA((GROUP + chunks - 1,)),
        ],
        compiler_params=params(8),
        cost_estimate=estimate,
        name="last_values",
    )(*operands, *before)


def sum_kernel(*refs):
    parts, (db, dc) = refs[:-2], refs[-2:]
    length = db.shape[0]
    for out, rows in ((db, slice(0, length)), (dc, slice(length, 2 * length))):
        total = parts[0][rows, :].astype(F32)
        for part in parts[1:]:
            total = total + part[rows, :].astype(F32)
        out[...] = total.astype(BF16)


def over_heads(part):
    count, (rows, state) = lax.axis_size("head"), part.shape
    parts = [part]
    for shift in range(1, count):
        pairs = [(s, (s + shift) % count) for s in range(count)]
        parts.append(lax.ppermute(part, "head", pairs))
    return pl.pallas_call(
        sum_kernel,
        out_shape=[jax.ShapeDtypeStruct((rows // 2, state), BF16)] * 2,
        in_specs=whole(count),
        out_specs=whole(2),
        compiler_params=params(4),
        cost_estimate=cost(count * part.size, 2 * count * part.size),
        name="sum_over_heads",
    )(*parts)


def shards(token_values, b_inputs, c_inputs, log_decay, grad_out):
    head_dim = token_values.shape[1] // log_decay.shape[0]
    state = b_inputs.shape[1]
    count, group = lax.axis_size("seq"), GROUP
    chunks = chunk_count(token_values.shape[1])
    levels = (count // group).bit_length() - 1
    where = lax.axis_index("seq").astype(jnp.int32)[None]
    inputs = (log_decay, b_inputs, c_inputs, token_values, grad_out)
    order = [(chunk, k) for chunk in range(chunks) for k in range(group - 1, -1, -1)]
    kept, states = first_states(head_dim, order[: group - 1], where, inputs)
    ld, b, c, x_0, dy_0, *factors = kept
    late = order[group - 1 :]
    columns = (x_0, dy_0, token_values, grad_out)
    more, found = next_states(head_dim, late, where, factors, b, c, *columns)
    states.update(found)
    xs, dys = [x_0, *more[::2]], [dy_0, *more[1::2]]
    blocks = [
        exchange([states[chunk, k][3] for k in range(group)]) for chunk in range(chunks)
    ]
    setup = inner_setup(head_dim, ld, b, c, [states[late[-1]][0]])

    def to_group(block, k):
        return lax.ppermute(block, "seq", [(s, s ^ (k * group)) for s in range(count)])

    every = [(chunk, m) for chunk in range(chunks) for m in range(group)]
    worked = [every[1:4]] + [every[chunk * group :][:2] for chunk in range(1, chunks)]
    rest = [one for one in every[1:] if not any(one in some for some in worked)]
    entries, inner, sums = [], {}, []

    def add_inner(some, after, hides=True):
        found, sums[:] = inner_terms(head_dim, some, setup, b, c, xs, dys, sums, after, hides)
        inner.update(found)

    own = [totals(state, 0, where, blocks[0], setup[-1:])]
    add_inner(every[:1], own[0], False)
    own += [totals(state, 0, where, blocks[chunk], sums[:1]) for chunk in range(1, chunks)]
    for chunk in range(chunks):
        (total,) = own[chunk]
        received = [to_group(total, 1)]
        for level in range(levels - 1):
            last = level == levels - 2
            total = merged(state, level, last, where, total, received[level], [])
            received.append(to_group(total, 2 << level))
        add_inner(worked[chunk], [total])
        found = member_entries(state, False, where, blocks[chunk], received, sums[:1])
        entries.append(exchange(found))
    if rest:
        add_inner(rest, found[:1])

    values = []
    for chunk in range(chunks):
        last = chunk == chunks - 1
        ours = [states[chunk, k] for k in range(group)]
        scaled = [one[:2] for one in ours]
        spread = [one[2] for one in ours]
        if last:
            sums = entry_parts(False, (0, 3), scaled, *sums, entries[chunk], values)
        ks = (2, 1) if last else (0, 3, 2, 1)
        sums = entry_parts(last, ks, scaled, *sums, entries[chunk], [])
        local = [inner[chunk, m] for m in range(group)]
        values.append(
            entry_values(chunk, chunks, where, spread, b, local, entries[chunk], values)
        )
    return (values[-1], *over_heads(sums[0]))


def solution(mesh):
    in_specs = (
        P("seq", "head"),
        P("seq", None),
        P("seq", None),
        P("head", "seq"),
        P("seq", "head"),
    )
    out_specs = (P("seq", "head"), P("seq", None), P("seq", None))
    return jax.shard_map(shards, mesh=mesh, in_specs=in_specs, out_specs=out_specs, check_vma=False)
```

```python
import functools

import jax
import jax.numpy as jnp
from jax import lax
from jax.experimental import pallas as pl
from jax.experimental.pallas import tpu as pltpu
from jax.sharding import PartitionSpec as P

BF16 = jnp.bfloat16
F32 = jnp.float32
LANES = 128
GROUP = 4
TAIL = 16
LOG2E = 1.4426950408889634
MIB = 1024 * 1024

NN = (((1,), (0,)), ((), ()))
NT = (((1,), (1,)), ((), ()))
TN = (((0,), (0,)), ((), ()))


def dot(a, b, dims):
    return lax.dot_general(a, b, dims, preferred_element_type=F32)


def iota(shape, dim):
    return lax.broadcasted_iota(jnp.int32, shape, dim)


def three(values):
    high = values.astype(BF16)
    rest = values - high.astype(F32)
    mid = rest.astype(BF16)
    return high, mid, (rest - mid.astype(F32)).astype(BF16)


SLOT = LANES // 4


def summed(mask, terms):
    heads, length = terms[0].shape
    gap = [] if heads == SLOT else [jnp.zeros((SLOT - heads, length), BF16)]
    rows = [r for t in terms for r in [t] + gap] + [jnp.zeros((SLOT, length), BF16)]
    each = dot(mask, jnp.concatenate(rows, axis=0), NT)
    return each + pltpu.roll(each, LANES - SLOT, 1) + pltpu.roll(each, LANES - 2 * SLOT, 1)


def split_of(index, size):
    shift = size.bit_length() - 1
    return lax.shift_right_logical(index, shift) if size == 1 << shift else index // size


def row_less_head(head_dim, width, rows=LANES):
    shape = (LANES, width)
    row = iota(shape, 0)
    if rows < LANES:
        row = row & (rows - 1)
    return row - split_of(iota(shape, 1), head_dim)


def head_of_lane(difference, first):
    return jnp.where(difference == first, 1.0, 0.0).astype(BF16)


def whole(count):
    return [pl.BlockSpec(memory_space=pltpu.VMEM)] * count


def in_hbm(*arrays):
    return [pltpu.with_memory_space_constraint(a, pltpu.HBM) for a in arrays]


SMEM = pl.BlockSpec(memory_space=pltpu.SMEM)
HBM = pl.BlockSpec(memory_space=pltpu.HBM)
ANY = pl.BlockSpec(memory_space=pl.ANY)


def params(mib):
    return pltpu.CompilerParams(vmem_limit_bytes=mib * MIB)


def cost(flops, size, transcendentals=0):
    return pl.CostEstimate(flops=flops, bytes_accessed=size, transcendentals=transcendentals)


def place_of(where):
    return where[0] & (GROUP - 1)


def bit_of(where, level):
    return (where[0] >> (level + GROUP.bit_length() - 1)) & 1 == 1


def chunk_count(width):
    return 2 if (width // GROUP) % (2 * LANES) == 0 else 1


def chunk_lanes(where, k, chunk, part):
    start = (chunk * GROUP + (place_of(where) ^ k)) * part
    return pl.ds(pl.multiple_of(start, part), part)


def masks_of(length):
    rows, other = iota((length, length), 0), iota((length, length), 1)
    after = jnp.where(other > rows, 1.0, 0.0).astype(BF16)
    return after, jnp.where(other <= rows, 1.0, 0.0).astype(BF16)


def factors_of(ld, after, until):
    length = ld.shape[1]
    terms = three(ld)
    into_end = jnp.exp(summed(after, terms)).astype(BF16)
    from_start = jnp.exp(summed(until, terms)).astype(BF16)
    total = jnp.exp(summed(jnp.ones((TAIL, length), BF16), terms))
    high = total.astype(BF16).astype(F32)
    halves = jnp.where(iota(total.shape, 0) < TAIL // 2, high, total - high).astype(BF16)
    return into_end, from_start, halves


def put_states(head_dim, chunks, pieces, where, operands, outs, ready):
    into_end, from_start, halves, b, c, xs, dys = operands
    state, part = b.shape[1], xs[0].shape[1] // GROUP
    difference = row_less_head(head_dim, part)
    for side, (factors, proj, cols) in enumerate([(into_end, b, xs), (from_start, c, dys)]):
        turned = None
        for n, (chunk, k) in enumerate(pieces):
            if n == 0 or chunk != pieces[n - 1][0]:
                ready(side, chunk)
            if turned is None:
                turned = proj[...].T
            x_scaled, dy_scaled, spread, send = outs[4 * n : 4 * n + 4]
            member = place_of(where) ^ k
            first_head = (chunk * GROUP + member) * (part // head_dim)
            hot = head_of_lane(difference, first_head)
            wide = dot(factors, hot, NN).astype(BF16)
            if side == 0:
                spread[...] = wide
                send[2 * state :, :] = dot(halves, hot, NN).astype(BF16)
            lanes = pl.ds(pl.multiple_of(member * part, part), part)
            piece = cols[chunk][:, lanes] * wide
            (dy_scaled if side else x_scaled)[...] = piece
            send[side * state : (side + 1) * state, :] = dot(turned, piece, NN).astype(BF16)


def load_chunk(chunk, source, target, sem):
    width = target.shape[1]
    copy = pltpu.make_async_copy(source.at[:, pl.ds(chunk * width, width)], target, sem)
    copy.start()
    return copy


def first_states_kernel(head_dim, chunks, pieces, where, ld_in, b_in, c_in, x_in, dy_in, *refs):
    ld, b, c, x, dy, into_end, from_start, halves = refs[:8]
    outs, sems = refs[8:-1], refs[-1]

    def load(n, source, target):
        copy = pltpu.make_async_copy(source, target, sems.at[n])
        copy.start()
        return copy

    first = load(0, ld_in, ld)
    copies = [
        [load(1, b_in, b), load_chunk(0, x_in, x, sems.at[3])],
        [load(2, c_in, c), load_chunk(0, dy_in, dy, sems.at[4])],
    ]
    masks = masks_of(ld.shape[1])
    first.wait()
    factors = factors_of(ld[...], *masks)
    for ref, value in zip((into_end, from_start, halves), factors):
        ref[...] = value

    def ready(side, chunk):
        for copy in copies[side]:
            copy.wait()

    operands = (*factors, b, c, {0: x}, {0: dy})
    put_states(head_dim, chunks, pieces, where, operands, outs, ready)


def next_states_kernel(head_dim, chunks, pieces, where, into_end, from_start, halves, *refs):
    b, c, x, dy, x_in, dy_in = refs[:6]
    outs, sems = refs[6:-1], refs[-1]
    kept, outs = outs[: 2 * (chunks - 1)], outs[2 * (chunks - 1) :]
    xs, dys, copies = {0: x}, {0: dy}, {}
    for chunk in range(1, chunks):
        xs[chunk], dys[chunk] = kept[2 * chunk - 2 : 2 * chunk]
        copies[0, chunk] = load_chunk(chunk, x_in, xs[chunk], sems.at[2 * chunk - 2])
        copies[1, chunk] = load_chunk(chunk, dy_in, dys[chunk], sems.at[2 * chunk - 1])

    def ready(side, chunk):
        if (side, chunk) in copies:
            copies[side, chunk].wait()

    operands = (into_end[...], from_start[...], halves[...], b, c, xs, dys)
    put_states(head_dim, chunks, pieces, where, operands, outs, ready)


def states_shapes(n_parts, length, width, state):
    part = width // (GROUP * chunk_count(width))
    scaled = jax.ShapeDtypeStruct((length, part), BF16)
    send = jax.ShapeDtypeStruct((2 * state + TAIL, part), BF16)
    return [scaled, scaled, scaled, send] * n_parts


def by_piece(pieces, outs):
    return {piece: outs[4 * n : 4 * n + 4] for n, piece in enumerate(pieces)}


def first_states(head_dim, pieces, where, inputs):
    ld, b, c, x, dy = inputs
    (length, width), state = x.shape, b.shape[1]
    chunks = chunk_count(width)
    columns = jax.ShapeDtypeStruct((length, width // chunks), BF16)
    kept = [jax.ShapeDtypeStruct(a.shape, a.dtype) for a in (ld, b, c)] + [columns] * 2
    kept += [jax.ShapeDtypeStruct((rows, LANES), BF16) for rows in (length, length, TAIL)]
    outs = kept + states_shapes(len(pieces), length, width, state)
    found = pl.pallas_call(
        functools.partial(first_states_kernel, head_dim, chunks, pieces),
        out_shape=outs,
        in_specs=[SMEM] + [HBM] * 5,
        out_specs=whole(len(outs)),
        scratch_shapes=[pltpu.SemaphoreType.DMA((5,))],
        compiler_params=params(8),
        cost_estimate=cost(2 * length * width * (state + LANES), 8 * length * width),
        name="first_states",
    )(where, *in_hbm(*inputs))
    return found[:8], by_piece(pieces, found[8:])


def next_states(head_dim, pieces, where, factors, b, c, x_0, dy_0, x, dy):
    (length, width), state = x.shape, b.shape[1]
    chunks = chunk_count(width)
    n_kept = 2 * (chunks - 1)
    outs = [jax.ShapeDtypeStruct(x_0.shape, BF16)] * n_kept
    outs += states_shapes(len(pieces), length, width, state)
    found = pl.pallas_call(
        functools.partial(next_states_kernel, head_dim, chunks, pieces),
        out_shape=outs,
        in_specs=[SMEM] + whole(7) + [HBM] * 2,
        out_specs=whole(len(outs)),
        scratch_shapes=[pltpu.SemaphoreType.DMA((max(n_kept, 1),))],
        compiler_params=params(8),
        cost_estimate=cost(2 * length * width * (state + LANES), 4 * length * width),
        name="next_states",
    )(where, *factors, b, c, x_0, dy_0, *in_hbm(x, dy))
    return found[:n_kept], by_piece(pieces, found[n_kept:])


def decay_of(tail):
    tail = tail.astype(F32)
    return tail[:1, :] + tail[TAIL // 2 : TAIL // 2 + 1, :]


def put_decay(ref, first, factor):
    high = factor.astype(BF16).astype(F32)
    shape = (TAIL, factor.shape[1])
    both = jnp.where(iota(shape, 0) < TAIL // 2, high, factor - high)
    ref[first:, :] = both.astype(BF16)


def sent_order(parts):
    return [parts[0], *parts[:0:-1]]


def in_order(group, forward):
    return list(range(group)) if forward else list(range(group - 1, -1, -1))


def side_rows(state, forward):
    return slice(0, state) if forward else slice(state, 2 * state)


def totals_kernel(state, levels, where, *refs):
    group = GROUP
    blocks, outs, sums = sent_order(refs[:group]), refs[-1 - levels : -1], refs[-1]
    for here in range(group):

        @pl.when(place_of(where) == here)
        def _(here=here):
            decays = [decay_of(blocks[q ^ here][2 * state :, :]) for q in range(group)]
            for forward in (True, False):
                rows, value = side_rows(state, forward), None
                for q in in_order(group, forward):
                    piece = blocks[q ^ here][rows, :].astype(F32)
                    value = piece if value is None else decays[q] * value + piece
                sums[rows, :] = value.astype(BF16)

    factor = decay_of(blocks[0][2 * state :, :])
    for block in blocks[1:]:
        factor = factor * decay_of(block[2 * state :, :])
    if not levels:
        put_decay(sums, 2 * state, factor)
    for level, out in enumerate(outs):
        put_decay(out, state, factor)
        for forward in (True, False):

            @pl.when(bit_of(where, level) != forward)
            def _(out=out, forward=forward):
                out[:state, :] = sums[side_rows(state, forward), :]


def totals(state, levels, where, blocks, after):
    part = blocks[0].shape[1]
    outs = [jax.ShapeDtypeStruct((state + TAIL, part), BF16)] * levels
    if not levels:
        outs = [jax.ShapeDtypeStruct(blocks[0].shape, BF16)]
    return pl.pallas_call(
        functools.partial(totals_kernel, state, levels),
        out_shape=outs,
        in_specs=[SMEM] + whole(len(blocks)) + [ANY] * len(after),
        out_specs=whole(len(outs)),
        scratch_shapes=[pltpu.VMEM((2 * state, part), BF16)] if levels else [],
        compiler_params=params(4),
        cost_estimate=cost(8 * blocks[0].size, 10 * blocks[0].size),
        name="totals",
    )(where, *sent_order(blocks), *after)


def merged_kernel(state, level, last, where, own, received, *refs):
    out = refs[-1]
    d_own, d_other = decay_of(own[2 * state :, :]), decay_of(received[2 * state :, :])
    upper = bit_of(where, level)
    later = bit_of(where, level + 1)
    for is_upper in (False, True):
        for forward in (True, False):
            chosen = upper == is_upper
            if last:
                chosen = chosen & (later != forward)

            @pl.when(chosen)
            def _(is_upper=is_upper, forward=forward):
                rows = side_rows(state, forward)
                mine, other = own[rows, :].astype(F32), received[rows, :].astype(F32)
                value = mine + d_own * other if is_upper == forward else other + d_other * mine
                out[slice(0, state) if last else rows, :] = value.astype(BF16)

    if not last:
        put_decay(out, 2 * state, d_own * d_other)


def merged(state, level, last, where, own, received, after):
    rows = state if last else own.shape[0]
    return pl.pallas_call(
        functools.partial(merged_kernel, state, level, last),
        out_shape=pltpu.VMEM((rows, own.shape[1]), BF16),
        in_specs=[SMEM] + whole(2) + [ANY] * len(after),
        out_specs=whole(1)[0],
        compiler_params=params(4),
        cost_estimate=cost(4 * own.size, 6 * own.size),
        name="merged",
    )(where, own, received, *after)


def put_direct(state, groups, number, received, entry):
    for mine in range(groups):

        @pl.when(number == mine)
        def _(mine=mine):
            for forward in (True, False):
                rows = side_rows(state, forward)
                others = range(mine - 1, -1, -1) if forward else range(mine + 1, groups)
                value, factor = jnp.zeros((state, entry.shape[1]), F32), None
                for other in others:
                    r = received[(mine ^ other) - 1]
                    piece = r[:state, :].astype(F32)
                    value = piece if factor is None else value + factor * piece
                    d = decay_of(r[state:, :])
                    factor = d if factor is None else factor * d
                entry[rows, :] = value


def put_rounds(state, where, received, entry):
    for forward in (True, False):
        value, factor = None, 1.0
        for level, r in enumerate(received):
            gets = bit_of(where, level) == forward
            both = r.shape[0] > 2 * state
            rows = side_rows(state, forward) if both else slice(0, state)
            piece = r[rows, :].astype(F32) * jnp.where(gets, 1.0, 0.0)
            value = piece if value is None else value + factor * piece
            if both:
                factor = factor * jnp.where(gets, decay_of(r[2 * state :, :]), 1.0)
        entry[side_rows(state, forward), :] = value


def members_kernel(state, direct, n_received, where, *refs):
    received, refs = refs[:n_received], refs[n_received:]
    group = GROUP
    blocks, outs, entry = refs[:group], refs[-1 - group : -1], refs[-1]
    if direct:
        put_direct(state, n_received + 1, where[0] // group, received, entry)
    else:
        put_rounds(state, where, received, entry)
    for here in range(group):

        @pl.when(place_of(where) == here)
        def _(here=here):
            decays = [decay_of(blocks[q ^ here][2 * state :, :]) for q in range(group)]
            for forward in (True, False):
                rows, order = side_rows(state, forward), in_order(group, forward)
                value = entry[rows, :]
                for q in order:
                    outs[q ^ here][rows, :] = value.astype(BF16)
                    if q != order[-1]:
                        value = decays[q] * value + blocks[q ^ here][rows, :].astype(F32)


def member_entries(state, direct, where, blocks, received, after):
    group, part = len(blocks), blocks[0].shape[1]
    return pl.pallas_call(
        functools.partial(members_kernel, state, direct, len(received)),
        out_shape=[jax.ShapeDtypeStruct((2 * state, part), BF16)] * group,
        in_specs=[SMEM] + whole(group + len(received)) + [ANY] * len(after),
        out_specs=whole(group),
        scratch_shapes=[pltpu.VMEM((2 * state, part), F32)],
        compiler_params=params(4),
        cost_estimate=cost(12 * blocks[0].size, 16 * blocks[0].size),
        name="member_entries",
    )(where, *received, *blocks, *after)


def exchange(parts):
    count = lax.axis_size("seq")
    out = list(parts)
    for k in range(len(parts) - 1, 0, -1):
        out[k] = lax.ppermute(parts[k], "seq", [(s, s ^ k) for s in range(count)])
    return out


def split_pairs(first, count):
    if count == 1:
        return []
    middle = first + count // 2
    return (
        [(first, middle, first + count)]
        + split_pairs(first, middle - first)
        + split_pairs(middle, first + count - middle)
    )


def grouped_cuts(pieces):
    groups = {}
    for cut in split_pairs(0, pieces):
        groups.setdefault((cut[1] - cut[0], cut[2] - cut[1]), []).append(cut)
    return list(groups.items())


def rows_of(first, end, piece):
    return slice(first * piece, end * piece)


def setup_kernel(piece, ld, b, c, *refs):
    near, cum_terms = refs[-2:]
    heads, length = ld.shape
    rows, other = iota((length, length), 0), iota((length, length), 1)
    mask = jnp.where(other <= rows, 1.0, 0.0).astype(BF16)
    cum = summed(mask, three(ld[...] * LOG2E))
    lane = iota(cum.shape, 1)
    in_slots = jnp.where(lane < SLOT, cum, 0.0)
    in_slots = in_slots + pltpu.roll(in_slots, SLOT, 1) + pltpu.roll(in_slots, 2 * SLOT, 1)
    high, mid, low = three(in_slots)
    cum_terms[...] = jnp.where(lane < SLOT, high, jnp.where(lane < 2 * SLOT, mid, low))
    keep = iota((piece, piece), 0) <= iota((piece, piece), 1)
    pieces = length // piece
    for n in range(pieces):
        here = rows_of(n, n + 1, piece)
        near[here, :] = jnp.where(keep, dot(b[here, :], c[here, :], NT), 0.0).astype(BF16)
    cuts = [cut for _, same in grouped_cuts(pieces) for cut in same]
    for (lo, mid_, hi), far in zip(cuts, refs):
        left, right = rows_of(lo, mid_, piece), rows_of(mid_, hi, piece)
        far[...] = dot(b[left, :], c[right, :], NT).astype(BF16)


def inner_setup(piece, ld, b, c, after):
    length = b.shape[0]
    cuts = [cut for _, same in grouped_cuts(length // piece) for cut in same]
    outs = [
        jax.ShapeDtypeStruct(((mid - lo) * piece, (hi - mid) * piece), BF16) for lo, mid, hi in cuts
    ]
    outs.append(jax.ShapeDtypeStruct((length, piece), BF16))
    outs.append(jax.ShapeDtypeStruct((length, LANES), BF16))
    return pl.pallas_call(
        functools.partial(setup_kernel_after, piece, len(after)),
        out_shape=outs,
        in_specs=whole(3) + [ANY] * len(after),
        out_specs=whole(len(outs)),
        compiler_params=params(4),
        cost_estimate=cost(8 * b.size * length, 8 * b.size),
        name="inner_setup",
    )(ld, b, c, *after)


def setup_kernel_after(piece, n_after, ld, b, c, *refs):
    setup_kernel(piece, ld, b, c, *refs[n_after:])


def inner_kernel(head_dim, worked, chunks, n_before, n_after, b, c, *refs):
    xs, dys, refs = refs[:chunks], refs[chunks : 2 * chunks], refs[2 * chunks :]
    length, width = xs[0].shape
    piece = head_dim
    pieces = length // piece
    groups = grouped_cuts(pieces)
    n_cuts = sum(len(same) for _, same in groups)
    fars, (near, cum_terms), refs = refs[:n_cuts], refs[n_cuts : n_cuts + 2], refs[n_cuts + 2 :]
    before, refs = refs[:n_before], refs[n_before + n_after :]
    dx_outs, (db_out, dc_out, x_near, dy_near, *scratch) = refs[: len(worked)], refs[len(worked) :]
    lefts, rights = scratch[: len(groups)], scratch[len(groups) :]
    part = dx_outs[0].shape[1]
    difference = row_less_head(head_dim, part, SLOT)

    for at, (chunk, m) in enumerate(worked):
        x, dy, first_head = xs[chunk], dys[chunk], (chunk * GROUP + m) * (part // head_dim)
        lanes, here = slice(m * part, (m + 1) * part), slice(at * part, (at + 1) * part)
        cum = dot(cum_terms[...], head_of_lane(difference, first_head), NN)
        dx = []
        for n in range(pieces):
            rows = rows_of(n, n + 1, piece)
            middle = cum[n * piece + piece // 2 : n * piece + piece // 2 + 1, :]
            gap = middle - cum[rows, :]
            down, up = jnp.exp2(gap), jnp.exp2(-gap)
            x_near[rows, here] = (x[rows, lanes].astype(F32) * down).astype(BF16)
            dy_piece = (dy[rows, lanes].astype(F32) * up).astype(BF16)
            dy_near[rows, here] = dy_piece
            dx.append(down * dot(near[rows, :], dy_piece, NN))
        far_of = iter(fars)
        for (_, same), left_ref, right_ref in zip(groups, lefts, rights):
            for g, (lo, mid, hi) in enumerate(same):
                left, right = rows_of(lo, mid, piece), rows_of(mid, hi, piece)
                edge = cum[mid * piece - 1 : mid * piece, :]
                to_edge = jnp.exp2(edge - cum[left, :])
                from_edge = jnp.exp2(cum[right, :] - edge)
                x_left = (x[left, lanes].astype(F32) * to_edge).astype(BF16)
                dy_right = (dy[right, lanes].astype(F32) * from_edge).astype(BF16)
                left_ref[rows_of(g, g + 1, (mid - lo) * piece), here] = x_left
                right_ref[rows_of(g, g + 1, (hi - mid) * piece), here] = dy_right
                far = to_edge * dot(next(far_of)[...], dy_right, NN)
                for n in range(lo, mid):
                    dx[n] = dx[n] + far[rows_of(n - lo, n - lo + 1, piece), :]
        for n in range(pieces):
            dx_outs[at][rows_of(n, n + 1, piece), :] = dx[n].astype(BF16)

    if before:
        db_out[...] = before[0][...]
        dc_out[...] = before[1][...]
    else:
        db_out[...] = jnp.zeros_like(db_out)
        dc_out[...] = jnp.zeros_like(dc_out)
    batch = 4
    for first in range(0, pieces, batch):
        rows = rows_of(first, min(first + batch, pieces), piece)
        total = dot(x_near[rows, :], dy_near[rows, :], NT)
        row, col = iota(total.shape, 0), iota(total.shape, 1)
        keep = (split_of(row, piece) == split_of(col, piece)) & (row <= col)
        weighted = jnp.where(keep, total, 0.0).astype(BF16)
        db_out[rows, :] += dot(weighted, c[rows, :], NN)
        dc_out[rows, :] += dot(weighted, b[rows, :], TN)
    for ((n_left, n_right), same), left_ref, right_ref in zip(groups, lefts, rights):
        total = dot(left_ref[...], right_ref[...], NT)
        if len(same) > 1:
            row, col = iota(total.shape, 0), iota(total.shape, 1)
            same_cut = split_of(row, n_left * piece) == split_of(col, n_right * piece)
            total = jnp.where(same_cut, total, 0.0)
        weighted = total.astype(BF16)
        b_left = jnp.concatenate([b[rows_of(lo, mid, piece), :] for lo, mid, _ in same], axis=0)
        c_right = jnp.concatenate([c[rows_of(mid, hi, piece), :] for _, mid, hi in same], axis=0)
        db = dot(weighted, c_right, NN)
        dc = dot(weighted, b_left, TN)
        for g, (lo, mid, hi) in enumerate(same):
            db_out[rows_of(lo, mid, piece), :] += db[rows_of(g, g + 1, n_left * piece), :]
            dc_out[rows_of(mid, hi, piece), :] += dc[rows_of(g, g + 1, n_right * piece), :]


def inner_terms(head_dim, worked, setup, b, c, xs, dys, before, after, hides=True):
    (length, state), columns, chunks = b.shape, xs[0].size, len(xs)
    part = xs[0].shape[1] // GROUP
    used = part * len(worked)
    groups = grouped_cuts(length // head_dim)
    sizes = [[len(same) * n * head_dim for n in halves] for halves, same in groups]
    found = pl.pallas_call(
        functools.partial(inner_kernel, head_dim, worked, chunks, len(before), len(after)),
        out_shape=[jax.ShapeDtypeStruct((length, part), BF16)] * len(worked)
        + [jax.ShapeDtypeStruct((length, state), F32)] * 2,
        in_specs=whole(2 + 2 * chunks + len(setup) + len(before)) + [ANY] * len(after),
        out_specs=whole(len(worked) + 2),
        scratch_shapes=[pltpu.VMEM((length, used), BF16)] * 2
        + [pltpu.VMEM((left, used), BF16) for left, _ in sizes]
        + [pltpu.VMEM((right, used), BF16) for _, right in sizes],
        compiler_params=params(16),
        cost_estimate=cost(16 * columns * state, 8 * columns, 4 * columns) if hides else cost(1, 1),
        name="inner_terms",
    )(b, c, *xs, *dys, *setup, *before, *after)
    return dict(zip(worked, found)), list(found[-2:])


def parts_kernel(last, ks, db_before, dc_before, *refs):
    scaled, refs = refs[: 2 * len(ks)], refs[2 * len(ks) :]
    entries, outs = refs[: len(ks)], refs[-1 if last else -2 :]
    length, state = db_before.shape
    db, dc = db_before[...], dc_before[...]
    for n, entry in enumerate(entries):
        db = db + dot(scaled[2 * n][...], entry[state:, :], NT)
        dc = dc + dot(scaled[2 * n + 1][...], entry[:state, :], NT)
    if last:
        outs[0][:length, :] = db.astype(BF16)
        outs[0][length:, :] = dc.astype(BF16)
    else:
        outs[0][...] = db
        outs[1][...] = dc


def entry_parts(last, ks, scaled, db_before, dc_before, entries, after):
    length, state = db_before.shape
    one = jax.ShapeDtypeStruct((length, state), F32)
    outs = [jax.ShapeDtypeStruct((2 * length, state), BF16)] if last else [one, one]
    operands = [one for k in ks for one in scaled[k]] + [entries[k] for k in ks]
    return pl.pallas_call(
        functools.partial(parts_kernel, last, ks),
        out_shape=outs,
        in_specs=whole(2 + len(operands)) + [ANY] * len(after),
        out_specs=whole(len(outs)),
        compiler_params=params(8),
        cost_estimate=cost(2 * len(operands) * scaled[0][0].size * state, scaled[0][0].size),
        name="entry_parts",
    )(db_before, dc_before, *operands, *after)


def put_values(where, spread, b, local_parts, dx_local, entries, put):
    state, part = b.shape[1], entries[0].shape[1]
    for m, one in enumerate(local_parts):
        dx_local[:, m * part : (m + 1) * part] = one[...]
    for k, entry in enumerate(entries):
        lanes = pl.ds(pl.multiple_of((place_of(where) ^ k) * part, part), part)
        local = dx_local[:, lanes]
        far = spread[k][...].astype(F32) * dot(b[...], entry[state:, :], NN)
        put(k, lanes, (local.astype(F32) + far).astype(BF16))


def values_kernel(where, b, *refs):
    local_parts, spread = refs[:GROUP], refs[GROUP : 2 * GROUP]
    entries, (out, dx_local) = sent_order(refs[2 * GROUP : 3 * GROUP]), refs[-2:]

    def put(k, lanes, value):
        out[:, lanes] = value

    put_values(where, spread, b, local_parts, dx_local, entries, put)


def last_values_kernel(chunks, where, b, *refs):
    local_parts, spread, refs = refs[:GROUP], refs[GROUP : 2 * GROUP], refs[2 * GROUP :]
    entries, before = sent_order(refs[:GROUP]), refs[GROUP : GROUP + chunks - 1]
    out, dx, dx_local, sems = refs[-4:]
    part = entries[0].shape[1]
    stores = []

    def store(n, source, target):
        stores.append(pltpu.make_async_copy(source, target, sems.at[n]))
        stores[-1].start()

    for chunk, values in enumerate(before):
        store(GROUP + chunk, values, out.at[:, pl.ds(chunk * GROUP * part, GROUP * part)])

    def put(k, lanes, value):
        dx[k] = value
        store(k, dx.at[k], out.at[:, chunk_lanes(where, k, chunks - 1, part)])

    put_values(where, spread, b, local_parts, dx_local, entries, put)
    for one in stores:
        one.wait()


def entry_values(chunk, chunks, where, spread, b, local_parts, entries, before):
    length, part = b.shape[0], entries[0].shape[1]
    last = chunk == chunks - 1
    estimate = cost(8 * local_parts[0].size * b.shape[1], 16 * local_parts[0].size)
    operands = [where, b, *local_parts, *spread, *sent_order(entries)]
    if not last:
        return pl.pallas_call(
            values_kernel,
            out_shape=jax.ShapeDtypeStruct((length, GROUP * part), BF16),
            in_specs=[SMEM] + whole(1 + 3 * GROUP),
            out_specs=whole(1)[0],
            scratch_shapes=[pltpu.VMEM((length, GROUP * part), BF16)],
            compiler_params=params(8),
            cost_estimate=estimate,
            name="entry_values",
        )(*operands)
    return pl.pallas_call(
        functools.partial(last_values_kernel, chunks),
        out_shape=pltpu.HBM((length, chunks * GROUP * part), BF16),
        in_specs=[SMEM] + whole(1 + 3 * GROUP + len(before)),
        out_specs=HBM,
        scratch_shapes=[
            pltpu.VMEM((GROUP, length, part), BF16),
            pltpu.VMEM((length, GROUP * part), BF16),
            pltpu.SemaphoreType.DMA((GROUP + chunks - 1,)),
        ],
        compiler_params=params(8),
        cost_estimate=estimate,
        name="last_values",
    )(*operands, *before)


def sum_kernel(*refs):
    parts, (db, dc) = refs[:-2], refs[-2:]
    length = db.shape[0]
    for out, rows in ((db, slice(0, length)), (dc, slice(length, 2 * length))):
        total = parts[0][rows, :].astype(F32)
        for part in parts[1:]:
            total = total + part[rows, :].astype(F32)
        out[...] = total.astype(BF16)


def over_heads(part):
    count, (rows, state) = lax.axis_size("head"), part.shape
    parts = [part]
    for shift in range(1, count):
        pairs = [(s, (s + shift) % count) for s in range(count)]
        parts.append(lax.ppermute(part, "head", pairs))
    return pl.pallas_call(
        sum_kernel,
        out_shape=[jax.ShapeDtypeStruct((rows // 2, state), BF16)] * 2,
        in_specs=whole(count),
        out_specs=whole(2),
        compiler_params=params(4),
        cost_estimate=cost(count * part.size, 2 * count * part.size),
        name="sum_over_heads",
    )(*parts)


def shards(token_values, b_inputs, c_inputs, log_decay, grad_out):
    head_dim = token_values.shape[1] // log_decay.shape[0]
    state = b_inputs.shape[1]
    count, group = lax.axis_size("seq"), GROUP
    chunks = chunk_count(token_values.shape[1])
    levels = (count // group).bit_length() - 1
    where = lax.axis_index("seq").astype(jnp.int32)[None]
    inputs = (log_decay, b_inputs, c_inputs, token_values, grad_out)
    order = [(chunk, k) for chunk in range(chunks) for k in range(group - 1, -1, -1)]
    kept, states = first_states(head_dim, order[: group - 1], where, inputs)
    ld, b, c, x_0, dy_0, *factors = kept
    late = order[group - 1 :]
    columns = (x_0, dy_0, token_values, grad_out)
    more, found = next_states(head_dim, late, where, factors, b, c, *columns)
    states.update(found)
    xs, dys = [x_0, *more[::2]], [dy_0, *more[1::2]]
    blocks = [
        exchange([states[chunk, k][3] for k in range(group)]) for chunk in range(chunks)
    ]
    setup = inner_setup(head_dim, ld, b, c, [states[late[-1]][0]])

    def to_group(block, k):
        return lax.ppermute(block, "seq", [(s, s ^ (k * group)) for s in range(count)])

    every = [(chunk, m) for chunk in range(chunks) for m in range(group)]
    worked = [every[1:4]] + [every[chunk * group :][:1] for chunk in range(1, chunks)]
    rest = [one for one in every[1:] if not any(one in some for some in worked)]
    entries, inner, sums = [], {}, []

    def add_inner(some, after, hides=True):
        found, sums[:] = inner_terms(head_dim, some, setup, b, c, xs, dys, sums, after, hides)
        inner.update(found)

    own = [totals(state, 0, where, blocks[0], setup[-1:])]
    add_inner(every[:1], own[0], False)
    own += [totals(state, 0, where, blocks[chunk], sums[:1]) for chunk in range(1, chunks)]
    for chunk in range(chunks):
        (total,) = own[chunk]
        received = [to_group(total, 1)]
        for level in range(levels - 1):
            last = level == levels - 2
            total = merged(state, level, last, where, total, received[level], [])
            received.append(to_group(total, 2 << level))
        add_inner(worked[chunk], [total])
        found = member_entries(state, False, where, blocks[chunk], received, sums[:1])
        entries.append(exchange(found))
    if rest:
        add_inner(rest, found[:1])

    values = []
    for chunk in range(chunks):
        last = chunk == chunks - 1
        ours = [states[chunk, k] for k in range(group)]
        scaled = [one[:2] for one in ours]
        spread = [one[2] for one in ours]
        if last:
            sums = entry_parts(False, (0, 3), scaled, *sums, entries[chunk], values)
        ks = (2, 1) if last else (0, 3, 2, 1)
        sums = entry_parts(last, ks, scaled, *sums, entries[chunk], [])
        local = [inner[chunk, m] for m in range(group)]
        values.append(
            entry_values(chunk, chunks, where, spread, b, local, entries[chunk], values)
        )
    return (values[-1], *over_heads(sums[0]))


def solution(mesh):
    in_specs = (
        P("seq", "head"),
        P("seq", None),
        P("seq", None),
        P("head", "seq"),
        P("seq", "head"),
    )
    out_specs = (P("seq", "head"), P("seq", None), P("seq", None))
    return jax.shard_map(shards, mesh=mesh, in_specs=in_specs, out_specs=out_specs, check_vma=False)
```

```python
import functools

import jax
import jax.numpy as jnp
from jax import lax
from jax.experimental import pallas as pl
from jax.experimental.pallas import tpu as pltpu
from jax.sharding import PartitionSpec as P

BF16 = jnp.bfloat16
F32 = jnp.float32
LANES = 128
GROUP = 4
TAIL = 16
LOG2E = 1.4426950408889634
MIB = 1024 * 1024

NN = (((1,), (0,)), ((), ()))
NT = (((1,), (1,)), ((), ()))
TN = (((0,), (0,)), ((), ()))


def dot(a, b, dims):
    return lax.dot_general(a, b, dims, preferred_element_type=F32)


def iota(shape, dim):
    return lax.broadcasted_iota(jnp.int32, shape, dim)


def three(values):
    high = values.astype(BF16)
    rest = values - high.astype(F32)
    mid = rest.astype(BF16)
    return high, mid, (rest - mid.astype(F32)).astype(BF16)


SLOT = LANES // 4


def summed(mask, terms):
    heads, length = terms[0].shape
    gap = [] if heads == SLOT else [jnp.zeros((SLOT - heads, length), BF16)]
    rows = [r for t in terms for r in [t] + gap] + [jnp.zeros((SLOT, length), BF16)]
    each = dot(mask, jnp.concatenate(rows, axis=0), NT)
    return each + pltpu.roll(each, LANES - SLOT, 1) + pltpu.roll(each, LANES - 2 * SLOT, 1)


def split_of(index, size):
    shift = size.bit_length() - 1
    return lax.shift_right_logical(index, shift) if size == 1 << shift else index // size


def row_less_head(head_dim, width, rows=LANES):
    shape = (LANES, width)
    row = iota(shape, 0)
    if rows < LANES:
        row = row & (rows - 1)
    return row - split_of(iota(shape, 1), head_dim)


def head_of_lane(difference, first):
    return jnp.where(difference == first, 1.0, 0.0).astype(BF16)


def whole(count):
    return [pl.BlockSpec(memory_space=pltpu.VMEM)] * count


def in_hbm(*arrays):
    return [pltpu.with_memory_space_constraint(a, pltpu.HBM) for a in arrays]


SMEM = pl.BlockSpec(memory_space=pltpu.SMEM)
HBM = pl.BlockSpec(memory_space=pltpu.HBM)
ANY = pl.BlockSpec(memory_space=pl.ANY)


def params(mib):
    return pltpu.CompilerParams(vmem_limit_bytes=mib * MIB)


def cost(flops, size, transcendentals=0):
    return pl.CostEstimate(flops=flops, bytes_accessed=size, transcendentals=transcendentals)


def place_of(where):
    return where[0] & (GROUP - 1)


def bit_of(where, level):
    return (where[0] >> (level + GROUP.bit_length() - 1)) & 1 == 1


def chunk_count(width):
    return 2 if (width // GROUP) % (2 * LANES) == 0 else 1


def chunk_lanes(where, k, chunk, part):
    start = (chunk * GROUP + (place_of(where) ^ k)) * part
    return pl.ds(pl.multiple_of(start, part), part)


def masks_of(length):
    rows, other = iota((length, length), 0), iota((length, length), 1)
    after = jnp.where(other > rows, 1.0, 0.0).astype(BF16)
    return after, jnp.where(other <= rows, 1.0, 0.0).astype(BF16)


def factors_of(ld, after, until):
    length = ld.shape[1]
    terms = three(ld)
    into_end = jnp.exp(summed(after, terms)).astype(BF16)
    from_start = jnp.exp(summed(until, terms)).astype(BF16)
    total = jnp.exp(summed(jnp.ones((TAIL, length), BF16), terms))
    high = total.astype(BF16).astype(F32)
    halves = jnp.where(iota(total.shape, 0) < TAIL // 2, high, total - high).astype(BF16)
    return into_end, from_start, halves


def put_states(head_dim, chunks, pieces, where, operands, outs, ready):
    into_end, from_start, halves, b, c, xs, dys = operands
    state, part = b.shape[1], xs[0].shape[1] // GROUP
    difference = row_less_head(head_dim, part)
    for side, (factors, proj, cols) in enumerate([(into_end, b, xs), (from_start, c, dys)]):
        turned = None
        for n, (chunk, k) in enumerate(pieces):
            if n == 0 or chunk != pieces[n - 1][0]:
                ready(side, chunk)
            if turned is None:
                turned = proj[...].T
            x_scaled, dy_scaled, spread, send = outs[4 * n : 4 * n + 4]
            member = place_of(where) ^ k
            first_head = (chunk * GROUP + member) * (part // head_dim)
            hot = head_of_lane(difference, first_head)
            wide = dot(factors, hot, NN).astype(BF16)
            if side == 0:
                spread[...] = wide
                send[2 * state :, :] = dot(halves, hot, NN).astype(BF16)
            lanes = pl.ds(pl.multiple_of(member * part, part), part)
            piece = cols[chunk][:, lanes] * wide
            (dy_scaled if side else x_scaled)[...] = piece
            send[side * state : (side + 1) * state, :] = dot(turned, piece, NN).astype(BF16)


def load_chunk(chunk, source, target, sem):
    width = target.shape[1]
    copy = pltpu.make_async_copy(source.at[:, pl.ds(chunk * width, width)], target, sem)
    copy.start()
    return copy


def first_states_kernel(head_dim, chunks, pieces, where, ld_in, b_in, c_in, x_in, dy_in, *refs):
    ld, b, c, x, dy, into_end, from_start, halves = refs[:8]
    outs, sems = refs[8:-1], refs[-1]

    def load(n, source, target):
        copy = pltpu.make_async_copy(source, target, sems.at[n])
        copy.start()
        return copy

    first = load(0, ld_in, ld)
    copies = [
        [load(1, b_in, b), load_chunk(0, x_in, x, sems.at[3])],
        [load(2, c_in, c), load_chunk(0, dy_in, dy, sems.at[4])],
    ]
    masks = masks_of(ld.shape[1])
    first.wait()
    factors = factors_of(ld[...], *masks)
    for ref, value in zip((into_end, from_start, halves), factors):
        ref[...] = value

    def ready(side, chunk):
        for copy in copies[side]:
            copy.wait()

    operands = (*factors, b, c, {0: x}, {0: dy})
    put_states(head_dim, chunks, pieces, where, operands, outs, ready)


def next_states_kernel(head_dim, chunks, pieces, where, into_end, from_start, halves, *refs):
    b, c, x, dy, x_in, dy_in = refs[:6]
    outs, sems = refs[6:-1], refs[-1]
    kept, outs = outs[: 2 * (chunks - 1)], outs[2 * (chunks - 1) :]
    xs, dys, copies = {0: x}, {0: dy}, {}
    for chunk in range(1, chunks):
        xs[chunk], dys[chunk] = kept[2 * chunk - 2 : 2 * chunk]
        copies[0, chunk] = load_chunk(chunk, x_in, xs[chunk], sems.at[2 * chunk - 2])
        copies[1, chunk] = load_chunk(chunk, dy_in, dys[chunk], sems.at[2 * chunk - 1])

    def ready(side, chunk):
        if (side, chunk) in copies:
            copies[side, chunk].wait()

    operands = (into_end[...], from_start[...], halves[...], b, c, xs, dys)
    put_states(head_dim, chunks, pieces, where, operands, outs, ready)


def states_shapes(n_parts, length, width, state):
    part = width // (GROUP * chunk_count(width))
    scaled = jax.ShapeDtypeStruct((length, part), BF16)
    send = jax.ShapeDtypeStruct((2 * state + TAIL, part), BF16)
    return [scaled, scaled, scaled, send] * n_parts


def by_piece(pieces, outs):
    return {piece: outs[4 * n : 4 * n + 4] for n, piece in enumerate(pieces)}


def first_states(head_dim, pieces, where, inputs):
    ld, b, c, x, dy = inputs
    (length, width), state = x.shape, b.shape[1]
    chunks = chunk_count(width)
    columns = jax.ShapeDtypeStruct((length, width // chunks), BF16)
    kept = [jax.ShapeDtypeStruct(a.shape, a.dtype) for a in (ld, b, c)] + [columns] * 2
    kept += [jax.ShapeDtypeStruct((rows, LANES), BF16) for rows in (length, length, TAIL)]
    outs = kept + states_shapes(len(pieces), length, width, state)
    found = pl.pallas_call(
        functools.partial(first_states_kernel, head_dim, chunks, pieces),
        out_shape=outs,
        in_specs=[SMEM] + [HBM] * 5,
        out_specs=whole(len(outs)),
        scratch_shapes=[pltpu.SemaphoreType.DMA((5,))],
        compiler_params=params(8),
        cost_estimate=cost(2 * length * width * (state + LANES), 8 * length * width),
        name="first_states",
    )(where, *in_hbm(*inputs))
    return found[:8], by_piece(pieces, found[8:])


def next_states(head_dim, pieces, where, factors, b, c, x_0, dy_0, x, dy):
    (length, width), state = x.shape, b.shape[1]
    chunks = chunk_count(width)
    n_kept = 2 * (chunks - 1)
    outs = [jax.ShapeDtypeStruct(x_0.shape, BF16)] * n_kept
    outs += states_shapes(len(pieces), length, width, state)
    found = pl.pallas_call(
        functools.partial(next_states_kernel, head_dim, chunks, pieces),
        out_shape=outs,
        in_specs=[SMEM] + whole(7) + [HBM] * 2,
        out_specs=whole(len(outs)),
        scratch_shapes=[pltpu.SemaphoreType.DMA((max(n_kept, 1),))],
        compiler_params=params(8),
        cost_estimate=cost(2 * length * width * (state + LANES), 4 * length * width),
        name="next_states",
    )(where, *factors, b, c, x_0, dy_0, *in_hbm(x, dy))
    return found[:n_kept], by_piece(pieces, found[n_kept:])


def decay_of(tail):
    tail = tail.astype(F32)
    return tail[:1, :] + tail[TAIL // 2 : TAIL // 2 + 1, :]


def put_decay(ref, first, factor):
    high = factor.astype(BF16).astype(F32)
    shape = (TAIL, factor.shape[1])
    both = jnp.where(iota(shape, 0) < TAIL // 2, high, factor - high)
    ref[first:, :] = both.astype(BF16)


def sent_order(parts):
    return [parts[0], *parts[:0:-1]]


def in_order(group, forward):
    return list(range(group)) if forward else list(range(group - 1, -1, -1))


def side_rows(state, forward):
    return slice(0, state) if forward else slice(state, 2 * state)


def totals_kernel(state, levels, where, *refs):
    group = GROUP
    blocks, outs, sums = sent_order(refs[:group]), refs[-1 - levels : -1], refs[-1]
    for here in range(group):

        @pl.when(place_of(where) == here)
        def _(here=here):
            decays = [decay_of(blocks[q ^ here][2 * state :, :]) for q in range(group)]
            for forward in (True, False):
                rows, value = side_rows(state, forward), None
                for q in in_order(group, forward):
                    piece = blocks[q ^ here][rows, :].astype(F32)
                    value = piece if value is None else decays[q] * value + piece
                sums[rows, :] = value.astype(BF16)

    factor = decay_of(blocks[0][2 * state :, :])
    for block in blocks[1:]:
        factor = factor * decay_of(block[2 * state :, :])
    if not levels:
        put_decay(sums, 2 * state, factor)
    for level, out in enumerate(outs):
        put_decay(out, state, factor)
        for forward in (True, False):

            @pl.when(bit_of(where, level) != forward)
            def _(out=out, forward=forward):
                out[:state, :] = sums[side_rows(state, forward), :]


def totals(state, levels, where, blocks, after):
    part = blocks[0].shape[1]
    outs = [jax.ShapeDtypeStruct((state + TAIL, part), BF16)] * levels
    if not levels:
        outs = [jax.ShapeDtypeStruct(blocks[0].shape, BF16)]
    return pl.pallas_call(
        functools.partial(totals_kernel, state, levels),
        out_shape=outs,
        in_specs=[SMEM] + whole(len(blocks)) + [ANY] * len(after),
        out_specs=whole(len(outs)),
        scratch_shapes=[pltpu.VMEM((2 * state, part), BF16)] if levels else [],
        compiler_params=params(4),
        cost_estimate=cost(8 * blocks[0].size, 10 * blocks[0].size),
        name="totals",
    )(where, *sent_order(blocks), *after)


def merged_kernel(state, level, last, where, own, received, *refs):
    out = refs[-1]
    d_own, d_other = decay_of(own[2 * state :, :]), decay_of(received[2 * state :, :])
    upper = bit_of(where, level)
    later = bit_of(where, level + 1)
    for is_upper in (False, True):
        for forward in (True, False):
            chosen = upper == is_upper
            if last:
                chosen = chosen & (later != forward)

            @pl.when(chosen)
            def _(is_upper=is_upper, forward=forward):
                rows = side_rows(state, forward)
                mine, other = own[rows, :].astype(F32), received[rows, :].astype(F32)
                value = mine + d_own * other if is_upper == forward else other + d_other * mine
                out[slice(0, state) if last else rows, :] = value.astype(BF16)

    if not last:
        put_decay(out, 2 * state, d_own * d_other)


def merged(state, level, last, where, own, received, after):
    rows = state if last else own.shape[0]
    return pl.pallas_call(
        functools.partial(merged_kernel, state, level, last),
        out_shape=pltpu.VMEM((rows, own.shape[1]), BF16),
        in_specs=[SMEM] + whole(2) + [ANY] * len(after),
        out_specs=whole(1)[0],
        compiler_params=params(4),
        cost_estimate=cost(4 * own.size, 6 * own.size),
        name="merged",
    )(where, own, received, *after)


def put_direct(state, groups, number, received, entry):
    for mine in range(groups):

        @pl.when(number == mine)
        def _(mine=mine):
            for forward in (True, False):
                rows = side_rows(state, forward)
                others = range(mine - 1, -1, -1) if forward else range(mine + 1, groups)
                value, factor = jnp.zeros((state, entry.shape[1]), F32), None
                for other in others:
                    r = received[(mine ^ other) - 1]
                    piece = r[:state, :].astype(F32)
                    value = piece if factor is None else value + factor * piece
                    d = decay_of(r[state:, :])
                    factor = d if factor is None else factor * d
                entry[rows, :] = value


def put_rounds(state, where, received, entry):
    for forward in (True, False):
        value, factor = None, 1.0
        for level, r in enumerate(received):
            gets = bit_of(where, level) == forward
            both = r.shape[0] > 2 * state
            rows = side_rows(state, forward) if both else slice(0, state)
            piece = r[rows, :].astype(F32) * jnp.where(gets, 1.0, 0.0)
            value = piece if value is None else value + factor * piece
            if both:
                factor = factor * jnp.where(gets, decay_of(r[2 * state :, :]), 1.0)
        entry[side_rows(state, forward), :] = value


def members_kernel(state, direct, n_received, where, *refs):
    received, refs = refs[:n_received], refs[n_received:]
    group = GROUP
    blocks, outs, entry = refs[:group], refs[-1 - group : -1], refs[-1]
    if direct:
        put_direct(state, n_received + 1, where[0] // group, received, entry)
    else:
        put_rounds(state, where, received, entry)
    for here in range(group):

        @pl.when(place_of(where) == here)
        def _(here=here):
            decays = [decay_of(blocks[q ^ here][2 * state :, :]) for q in range(group)]
            for forward in (True, False):
                rows, order = side_rows(state, forward), in_order(group, forward)
                value = entry[rows, :]
                for q in order:
                    outs[q ^ here][rows, :] = value.astype(BF16)
                    if q != order[-1]:
                        value = decays[q] * value + blocks[q ^ here][rows, :].astype(F32)


def member_entries(state, direct, where, blocks, received, after):
    group, part = len(blocks), blocks[0].shape[1]
    return pl.pallas_call(
        functools.partial(members_kernel, state, direct, len(received)),
        out_shape=[jax.ShapeDtypeStruct((2 * state, part), BF16)] * group,
        in_specs=[SMEM] + whole(group + len(received)) + [ANY] * len(after),
        out_specs=whole(group),
        scratch_shapes=[pltpu.VMEM((2 * state, part), F32)],
        compiler_params=params(4),
        cost_estimate=cost(12 * blocks[0].size, 16 * blocks[0].size),
        name="member_entries",
    )(where, *received, *blocks, *after)


def exchange(parts):
    count = lax.axis_size("seq")
    out = list(parts)
    for k in range(len(parts) - 1, 0, -1):
        out[k] = lax.ppermute(parts[k], "seq", [(s, s ^ k) for s in range(count)])
    return out


def split_pairs(first, count):
    if count == 1:
        return []
    middle = first + count // 2
    return (
        [(first, middle, first + count)]
        + split_pairs(first, middle - first)
        + split_pairs(middle, first + count - middle)
    )


def grouped_cuts(pieces):
    groups = {}
    for cut in split_pairs(0, pieces):
        groups.setdefault((cut[1] - cut[0], cut[2] - cut[1]), []).append(cut)
    return list(groups.items())


def rows_of(first, end, piece):
    return slice(first * piece, end * piece)


def setup_kernel(piece, ld, b, c, *refs):
    near, cum_terms = refs[-2:]
    heads, length = ld.shape
    rows, other = iota((length, length), 0), iota((length, length), 1)
    mask = jnp.where(other <= rows, 1.0, 0.0).astype(BF16)
    cum = summed(mask, three(ld[...] * LOG2E))
    lane = iota(cum.shape, 1)
    in_slots = jnp.where(lane < SLOT, cum, 0.0)
    in_slots = in_slots + pltpu.roll(in_slots, SLOT, 1) + pltpu.roll(in_slots, 2 * SLOT, 1)
    high, mid, low = three(in_slots)
    cum_terms[...] = jnp.where(lane < SLOT, high, jnp.where(lane < 2 * SLOT, mid, low))
    keep = iota((piece, piece), 0) <= iota((piece, piece), 1)
    pieces = length // piece
    for n in range(pieces):
        here = rows_of(n, n + 1, piece)
        near[here, :] = jnp.where(keep, dot(b[here, :], c[here, :], NT), 0.0).astype(BF16)
    cuts = [cut for _, same in grouped_cuts(pieces) for cut in same]
    for (lo, mid_, hi), far in zip(cuts, refs):
        left, right = rows_of(lo, mid_, piece), rows_of(mid_, hi, piece)
        far[...] = dot(b[left, :], c[right, :], NT).astype(BF16)


def inner_setup(piece, ld, b, c, after):
    length = b.shape[0]
    cuts = [cut for _, same in grouped_cuts(length // piece) for cut in same]
    outs = [
        jax.ShapeDtypeStruct(((mid - lo) * piece, (hi - mid) * piece), BF16) for lo, mid, hi in cuts
    ]
    outs.append(jax.ShapeDtypeStruct((length, piece), BF16))
    outs.append(jax.ShapeDtypeStruct((length, LANES), BF16))
    return pl.pallas_call(
        functools.partial(setup_kernel_after, piece, len(after)),
        out_shape=outs,
        in_specs=whole(3) + [ANY] * len(after),
        out_specs=whole(len(outs)),
        compiler_params=params(4),
        cost_estimate=cost(8 * b.size * length, 8 * b.size),
        name="inner_setup",
    )(ld, b, c, *after)


def setup_kernel_after(piece, n_after, ld, b, c, *refs):
    setup_kernel(piece, ld, b, c, *refs[n_after:])


def inner_kernel(head_dim, worked, chunks, n_before, n_after, b, c, *refs):
    xs, dys, refs = refs[:chunks], refs[chunks : 2 * chunks], refs[2 * chunks :]
    length, width = xs[0].shape
    piece = head_dim
    pieces = length // piece
    groups = grouped_cuts(pieces)
    n_cuts = sum(len(same) for _, same in groups)
    fars, (near, cum_terms), refs = refs[:n_cuts], refs[n_cuts : n_cuts + 2], refs[n_cuts + 2 :]
    before, refs = refs[:n_before], refs[n_before + n_after :]
    dx_outs, (db_out, dc_out, x_near, dy_near, *scratch) = refs[: len(worked)], refs[len(worked) :]
    lefts, rights = scratch[: len(groups)], scratch[len(groups) :]
    part = dx_outs[0].shape[1]
    difference = row_less_head(head_dim, part, SLOT)

    for at, (chunk, m) in enumerate(worked):
        x, dy, first_head = xs[chunk], dys[chunk], (chunk * GROUP + m) * (part // head_dim)
        lanes, here = slice(m * part, (m + 1) * part), slice(at * part, (at + 1) * part)
        cum = dot(cum_terms[...], head_of_lane(difference, first_head), NN)
        dx = []
        for n in range(pieces):
            rows = rows_of(n, n + 1, piece)
            middle = cum[n * piece + piece // 2 : n * piece + piece // 2 + 1, :]
            gap = middle - cum[rows, :]
            down, up = jnp.exp2(gap), jnp.exp2(-gap)
            x_near[rows, here] = (x[rows, lanes].astype(F32) * down).astype(BF16)
            dy_piece = (dy[rows, lanes].astype(F32) * up).astype(BF16)
            dy_near[rows, here] = dy_piece
            dx.append(down * dot(near[rows, :], dy_piece, NN))
        far_of = iter(fars)
        for (_, same), left_ref, right_ref in zip(groups, lefts, rights):
            for g, (lo, mid, hi) in enumerate(same):
                left, right = rows_of(lo, mid, piece), rows_of(mid, hi, piece)
                edge = cum[mid * piece - 1 : mid * piece, :]
                to_edge = jnp.exp2(edge - cum[left, :])
                from_edge = jnp.exp2(cum[right, :] - edge)
                x_left = (x[left, lanes].astype(F32) * to_edge).astype(BF16)
                dy_right = (dy[right, lanes].astype(F32) * from_edge).astype(BF16)
                left_ref[rows_of(g, g + 1, (mid - lo) * piece), here] = x_left
                right_ref[rows_of(g, g + 1, (hi - mid) * piece), here] = dy_right
                far = to_edge * dot(next(far_of)[...], dy_right, NN)
                for n in range(lo, mid):
                    dx[n] = dx[n] + far[rows_of(n - lo, n - lo + 1, piece), :]
        for n in range(pieces):
            dx_outs[at][rows_of(n, n + 1, piece), :] = dx[n].astype(BF16)

    if before:
        db_out[...] = before[0][...]
        dc_out[...] = before[1][...]
    else:
        db_out[...] = jnp.zeros_like(db_out)
        dc_out[...] = jnp.zeros_like(dc_out)
    batch = 4
    for first in range(0, pieces, batch):
        rows = rows_of(first, min(first + batch, pieces), piece)
        total = dot(x_near[rows, :], dy_near[rows, :], NT)
        row, col = iota(total.shape, 0), iota(total.shape, 1)
        keep = (split_of(row, piece) == split_of(col, piece)) & (row <= col)
        weighted = jnp.where(keep, total, 0.0).astype(BF16)
        db_out[rows, :] += dot(weighted, c[rows, :], NN)
        dc_out[rows, :] += dot(weighted, b[rows, :], TN)
    for ((n_left, n_right), same), left_ref, right_ref in zip(groups, lefts, rights):
        total = dot(left_ref[...], right_ref[...], NT)
        if len(same) > 1:
            row, col = iota(total.shape, 0), iota(total.shape, 1)
            same_cut = split_of(row, n_left * piece) == split_of(col, n_right * piece)
            total = jnp.where(same_cut, total, 0.0)
        weighted = total.astype(BF16)
        b_left = jnp.concatenate([b[rows_of(lo, mid, piece), :] for lo, mid, _ in same], axis=0)
        c_right = jnp.concatenate([c[rows_of(mid, hi, piece), :] for _, mid, hi in same], axis=0)
        db = dot(weighted, c_right, NN)
        dc = dot(weighted, b_left, TN)
        for g, (lo, mid, hi) in enumerate(same):
            db_out[rows_of(lo, mid, piece), :] += db[rows_of(g, g + 1, n_left * piece), :]
            dc_out[rows_of(mid, hi, piece), :] += dc[rows_of(g, g + 1, n_right * piece), :]


def inner_terms(head_dim, worked, setup, b, c, xs, dys, before, after, hides=True):
    (length, state), columns, chunks = b.shape, xs[0].size, len(xs)
    part = xs[0].shape[1] // GROUP
    used = part * len(worked)
    groups = grouped_cuts(length // head_dim)
    sizes = [[len(same) * n * head_dim for n in halves] for halves, same in groups]
    found = pl.pallas_call(
        functools.partial(inner_kernel, head_dim, worked, chunks, len(before), len(after)),
        out_shape=[jax.ShapeDtypeStruct((length, part), BF16)] * len(worked)
        + [jax.ShapeDtypeStruct((length, state), F32)] * 2,
        in_specs=whole(2 + 2 * chunks + len(setup) + len(before)) + [ANY] * len(after),
        out_specs=whole(len(worked) + 2),
        scratch_shapes=[pltpu.VMEM((length, used), BF16)] * 2
        + [pltpu.VMEM((left, used), BF16) for left, _ in sizes]
        + [pltpu.VMEM((right, used), BF16) for _, right in sizes],
        compiler_params=params(16),
        cost_estimate=cost(16 * columns * state, 8 * columns, 4 * columns) if hides else cost(1, 1),
        name="inner_terms",
    )(b, c, *xs, *dys, *setup, *before, *after)
    return dict(zip(worked, found)), list(found[-2:])


def parts_kernel(last, ks, db_before, dc_before, *refs):
    scaled, refs = refs[: 2 * len(ks)], refs[2 * len(ks) :]
    entries, outs = refs[: len(ks)], refs[-1 if last else -2 :]
    length, state = db_before.shape
    db, dc = db_before[...], dc_before[...]
    for n, entry in enumerate(entries):
        db = db + dot(scaled[2 * n][...], entry[state:, :], NT)
        dc = dc + dot(scaled[2 * n + 1][...], entry[:state, :], NT)
    if last:
        outs[0][:length, :] = db.astype(BF16)
        outs[0][length:, :] = dc.astype(BF16)
    else:
        outs[0][...] = db
        outs[1][...] = dc


def entry_parts(last, ks, scaled, db_before, dc_before, entries, after):
    length, state = db_before.shape
    one = jax.ShapeDtypeStruct((length, state), F32)
    outs = [jax.ShapeDtypeStruct((2 * length, state), BF16)] if last else [one, one]
    operands = [one for k in ks for one in scaled[k]] + [entries[k] for k in ks]
    return pl.pallas_call(
        functools.partial(parts_kernel, last, ks),
        out_shape=outs,
        in_specs=whole(2 + len(operands)) + [ANY] * len(after),
        out_specs=whole(len(outs)),
        compiler_params=params(8),
        cost_estimate=cost(2 * len(operands) * scaled[0][0].size * state, scaled[0][0].size),
        name="entry_parts",
    )(db_before, dc_before, *operands, *after)


def put_values(where, spread, b, local_parts, dx_local, entries, put):
    state, part = b.shape[1], entries[0].shape[1]
    for m, one in enumerate(local_parts):
        dx_local[:, m * part : (m + 1) * part] = one[...]
    for k, entry in enumerate(entries):
        lanes = pl.ds(pl.multiple_of((place_of(where) ^ k) * part, part), part)
        local = dx_local[:, lanes]
        far = spread[k][...].astype(F32) * dot(b[...], entry[state:, :], NN)
        put(k, lanes, (local.astype(F32) + far).astype(BF16))


def values_kernel(where, b, *refs):
    local_parts, spread = refs[:GROUP], refs[GROUP : 2 * GROUP]
    entries, (out, dx_local) = sent_order(refs[2 * GROUP : 3 * GROUP]), refs[-2:]

    def put(k, lanes, value):
        out[:, lanes] = value

    put_values(where, spread, b, local_parts, dx_local, entries, put)


def last_values_kernel(chunks, where, b, *refs):
    local_parts, spread, refs = refs[:GROUP], refs[GROUP : 2 * GROUP], refs[2 * GROUP :]
    entries, before = sent_order(refs[:GROUP]), refs[GROUP : GROUP + chunks - 1]
    out, dx, dx_local, sems = refs[-4:]
    part = entries[0].shape[1]
    stores = []

    def store(n, source, target):
        stores.append(pltpu.make_async_copy(source, target, sems.at[n]))
        stores[-1].start()

    for chunk, values in enumerate(before):
        store(GROUP + chunk, values, out.at[:, pl.ds(chunk * GROUP * part, GROUP * part)])

    def put(k, lanes, value):
        dx[k] = value
        store(k, dx.at[k], out.at[:, chunk_lanes(where, k, chunks - 1, part)])

    put_values(where, spread, b, local_parts, dx_local, entries, put)
    for one in stores:
        one.wait()


def entry_values(chunk, chunks, where, spread, b, local_parts, entries, before):
    length, part = b.shape[0], entries[0].shape[1]
    last = chunk == chunks - 1
    estimate = cost(8 * local_parts[0].size * b.shape[1], 16 * local_parts[0].size)
    operands = [where, b, *local_parts, *spread, *sent_order(entries)]
    if not last:
        return pl.pallas_call(
            values_kernel,
            out_shape=jax.ShapeDtypeStruct((length, GROUP * part), BF16),
            in_specs=[SMEM] + whole(1 + 3 * GROUP),
            out_specs=whole(1)[0],
            scratch_shapes=[pltpu.VMEM((length, GROUP * part), BF16)],
            compiler_params=params(8),
            cost_estimate=estimate,
            name="entry_values",
        )(*operands)
    return pl.pallas_call(
        functools.partial(last_values_kernel, chunks),
        out_shape=pltpu.HBM((length, chunks * GROUP * part), BF16),
        in_specs=[SMEM] + whole(1 + 3 * GROUP + len(before)),
        out_specs=HBM,
        scratch_shapes=[
            pltpu.VMEM((GROUP, length, part), BF16),
            pltpu.VMEM((length, GROUP * part), BF16),
            pltpu.SemaphoreType.DMA((GROUP + chunks - 1,)),
        ],
        compiler_params=params(8),
        cost_estimate=estimate,
        name="last_values",
    )(*operands, *before)


def sum_kernel(*refs):
    parts, (db, dc) = refs[:-2], refs[-2:]
    length = db.shape[0]
    for out, rows in ((db, slice(0, length)), (dc, slice(length, 2 * length))):
        total = parts[0][rows, :].astype(F32)
        for part in parts[1:]:
            total = total + part[rows, :].astype(F32)
        out[...] = total.astype(BF16)


def over_heads(part):
    count, (rows, state) = lax.axis_size("head"), part.shape
    parts = [part]
    for shift in range(1, count):
        pairs = [(s, (s + shift) % count) for s in range(count)]
        parts.append(lax.ppermute(part, "head", pairs))
    return pl.pallas_call(
        sum_kernel,
        out_shape=[jax.ShapeDtypeStruct((rows // 2, state), BF16)] * 2,
        in_specs=whole(count),
        out_specs=whole(2),
        compiler_params=params(4),
        cost_estimate=cost(count * part.size, 2 * count * part.size),
        name="sum_over_heads",
    )(*parts)


def shards(token_values, b_inputs, c_inputs, log_decay, grad_out):
    head_dim = token_values.shape[1] // log_decay.shape[0]
    state = b_inputs.shape[1]
    count, group = lax.axis_size("seq"), GROUP
    chunks = chunk_count(token_values.shape[1])
    levels = (count // group).bit_length() - 1
    where = lax.axis_index("seq").astype(jnp.int32)[None]
    inputs = (log_decay, b_inputs, c_inputs, token_values, grad_out)
    order = [(chunk, k) for chunk in range(chunks) for k in range(group - 1, -1, -1)]
    kept, states = first_states(head_dim, order[: group - 1], where, inputs)
    ld, b, c, x_0, dy_0, *factors = kept
    late = order[group - 1 :]
    columns = (x_0, dy_0, token_values, grad_out)
    more, found = next_states(head_dim, late, where, factors, b, c, *columns)
    states.update(found)
    xs, dys = [x_0, *more[::2]], [dy_0, *more[1::2]]
    blocks = [
        exchange([states[chunk, k][3] for k in range(group)]) for chunk in range(chunks)
    ]
    setup = inner_setup(head_dim, ld, b, c, [states[late[-1]][0]])

    def to_group(block, k):
        return lax.ppermute(block, "seq", [(s, s ^ (k * group)) for s in range(count)])

    every = [(chunk, m) for chunk in range(chunks) for m in range(group)]
    early, rest = every[:2], every[2:]
    worked = [rest[:3]] + [[one for one in rest[3:] if one[0] == n][:1] for n in range(1, chunks)]
    rest = [one for one in rest if not any(one in some for some in worked)]
    entries, inner, sums = [], {}, []

    def add_inner(some, after, hides=True):
        found, sums[:] = inner_terms(head_dim, some, setup, b, c, xs, dys, sums, after, hides)
        inner.update(found)

    own = [totals(state, 0, where, blocks[0], setup[-1:])]
    add_inner(early, own[0], False)
    own += [totals(state, 0, where, blocks[chunk], sums[:1]) for chunk in range(1, chunks)]
    for chunk in range(chunks):
        (total,) = own[chunk]
        received = [to_group(total, 1)]
        for level in range(levels - 1):
            last = level == levels - 2
            total = merged(state, level, last, where, total, received[level], [])
            received.append(to_group(total, 2 << level))
        add_inner(worked[chunk], [total])
        found = member_entries(state, False, where, blocks[chunk], received, sums[:1])
        entries.append(exchange(found))
    if rest:
        add_inner(rest, found[:1])

    values = []
    for chunk in range(chunks):
        last = chunk == chunks - 1
        ours = [states[chunk, k] for k in range(group)]
        scaled = [one[:2] for one in ours]
        spread = [one[2] for one in ours]
        if last:
            sums = entry_parts(False, (0, 3), scaled, *sums, entries[chunk], values)
        ks = (2, 1) if last else (0, 3, 2, 1)
        sums = entry_parts(last, ks, scaled, *sums, entries[chunk], [])
        local = [inner[chunk, m] for m in range(group)]
        values.append(
            entry_values(chunk, chunks, where, spread, b, local, entries[chunk], values)
        )
    return (values[-1], *over_heads(sums[0]))


def solution(mesh):
    in_specs = (
        P("seq", "head"),
        P("seq", None),
        P("seq", None),
        P("head", "seq"),
        P("seq", "head"),
    )
    out_specs = (P("seq", "head"), P("seq", None), P("seq", None))
    return jax.shard_map(shards, mesh=mesh, in_specs=in_specs, out_specs=out_specs, check_vma=False)
```

```python
import functools

import jax
import jax.numpy as jnp
from jax import lax
from jax.experimental import pallas as pl
from jax.experimental.pallas import tpu as pltpu
from jax.sharding import PartitionSpec as P

BF16 = jnp.bfloat16
F32 = jnp.float32
LANES = 128
GROUP = 4
TAIL = 16
LOG2E = 1.4426950408889634
MIB = 1024 * 1024

NN = (((1,), (0,)), ((), ()))
NT = (((1,), (1,)), ((), ()))
TN = (((0,), (0,)), ((), ()))


def dot(a, b, dims):
    return lax.dot_general(a, b, dims, preferred_element_type=F32)


def iota(shape, dim):
    return lax.broadcasted_iota(jnp.int32, shape, dim)


def three(values):
    high = values.astype(BF16)
    rest = values - high.astype(F32)
    mid = rest.astype(BF16)
    return high, mid, (rest - mid.astype(F32)).astype(BF16)


SLOT = LANES // 4


def summed(mask, terms):
    heads, length = terms[0].shape
    gap = [] if heads == SLOT else [jnp.zeros((SLOT - heads, length), BF16)]
    rows = [r for t in terms for r in [t] + gap] + [jnp.zeros((SLOT, length), BF16)]
    each = dot(mask, jnp.concatenate(rows, axis=0), NT)
    return each + pltpu.roll(each, LANES - SLOT, 1) + pltpu.roll(each, LANES - 2 * SLOT, 1)


def split_of(index, size):
    shift = size.bit_length() - 1
    return lax.shift_right_logical(index, shift) if size == 1 << shift else index // size


def row_less_head(head_dim, width, rows=LANES):
    shape = (LANES, width)
    row = iota(shape, 0)
    if rows < LANES:
        row = row & (rows - 1)
    return row - split_of(iota(shape, 1), head_dim)


def head_of_lane(difference, first):
    return jnp.where(difference == first, 1.0, 0.0).astype(BF16)


def whole(count):
    return [pl.BlockSpec(memory_space=pltpu.VMEM)] * count


def in_hbm(*arrays):
    return [pltpu.with_memory_space_constraint(a, pltpu.HBM) for a in arrays]


SMEM = pl.BlockSpec(memory_space=pltpu.SMEM)
HBM = pl.BlockSpec(memory_space=pltpu.HBM)
ANY = pl.BlockSpec(memory_space=pl.ANY)


def params(mib):
    return pltpu.CompilerParams(vmem_limit_bytes=mib * MIB)


def cost(flops, size, transcendentals=0):
    return pl.CostEstimate(flops=flops, bytes_accessed=size, transcendentals=transcendentals)


def place_of(where):
    return where[0] & (GROUP - 1)


def bit_of(where, level):
    return (where[0] >> (level + GROUP.bit_length() - 1)) & 1 == 1


def chunk_count(width):
    return 2 if (width // GROUP) % (2 * LANES) == 0 else 1


def chunk_lanes(where, k, chunk, part):
    start = (chunk * GROUP + (place_of(where) ^ k)) * part
    return pl.ds(pl.multiple_of(start, part), part)


def masks_of(length):
    rows, other = iota((length, length), 0), iota((length, length), 1)
    after = jnp.where(other > rows, 1.0, 0.0).astype(BF16)
    return after, jnp.where(other <= rows, 1.0, 0.0).astype(BF16)


def factors_of(ld, after, until):
    length = ld.shape[1]
    terms = three(ld)
    into_end = jnp.exp(summed(after, terms)).astype(BF16)
    from_start = jnp.exp(summed(until, terms)).astype(BF16)
    total = jnp.exp(summed(jnp.ones((TAIL, length), BF16), terms))
    high = total.astype(BF16).astype(F32)
    halves = jnp.where(iota(total.shape, 0) < TAIL // 2, high, total - high).astype(BF16)
    return into_end, from_start, halves


def put_states(head_dim, chunks, pieces, where, operands, outs, ready):
    into_end, from_start, halves, b, c, xs, dys = operands
    state, part = b.shape[1], xs[0].shape[1] // GROUP
    difference = row_less_head(head_dim, part)
    for side, (factors, proj, cols) in enumerate([(into_end, b, xs), (from_start, c, dys)]):
        turned = None
        for n, (chunk, k) in enumerate(pieces):
            if n == 0 or chunk != pieces[n - 1][0]:
                ready(side, chunk)
            if turned is None:
                turned = proj[...].T
            x_scaled, dy_scaled, spread, send = outs[4 * n : 4 * n + 4]
            member = place_of(where) ^ k
            first_head = (chunk * GROUP + member) * (part // head_dim)
            hot = head_of_lane(difference, first_head)
            wide = dot(factors, hot, NN).astype(BF16)
            if side == 0:
                spread[...] = wide
                send[2 * state :, :] = dot(halves, hot, NN).astype(BF16)
            lanes = pl.ds(pl.multiple_of(member * part, part), part)
            piece = cols[chunk][:, lanes] * wide
            (dy_scaled if side else x_scaled)[...] = piece
            send[side * state : (side + 1) * state, :] = dot(turned, piece, NN).astype(BF16)


def load_chunk(chunk, source, target, sem):
    width = target.shape[1]
    copy = pltpu.make_async_copy(source.at[:, pl.ds(chunk * width, width)], target, sem)
    copy.start()
    return copy


def first_states_kernel(head_dim, chunks, pieces, where, ld_in, b_in, c_in, x_in, dy_in, *refs):
    ld, b, c, x, dy, into_end, from_start, halves = refs[:8]
    outs, sems = refs[8:-1], refs[-1]

    def load(n, source, target):
        copy = pltpu.make_async_copy(source, target, sems.at[n])
        copy.start()
        return copy

    first = load(0, ld_in, ld)
    copies = [
        [load(1, b_in, b), load_chunk(0, x_in, x, sems.at[3])],
        [load(2, c_in, c), load_chunk(0, dy_in, dy, sems.at[4])],
    ]
    masks = masks_of(ld.shape[1])
    first.wait()
    factors = factors_of(ld[...], *masks)
    for ref, value in zip((into_end, from_start, halves), factors):
        ref[...] = value

    def ready(side, chunk):
        for copy in copies[side]:
            copy.wait()

    operands = (*factors, b, c, {0: x}, {0: dy})
    put_states(head_dim, chunks, pieces, where, operands, outs, ready)


def next_states_kernel(head_dim, chunks, pieces, where, into_end, from_start, halves, *refs):
    b, c, x, dy, x_in, dy_in = refs[:6]
    outs, sems = refs[6:-1], refs[-1]
    kept, outs = outs[: 2 * (chunks - 1)], outs[2 * (chunks - 1) :]
    xs, dys, copies = {0: x}, {0: dy}, {}
    for chunk in range(1, chunks):
        xs[chunk], dys[chunk] = kept[2 * chunk - 2 : 2 * chunk]
        copies[0, chunk] = load_chunk(chunk, x_in, xs[chunk], sems.at[2 * chunk - 2])
        copies[1, chunk] = load_chunk(chunk, dy_in, dys[chunk], sems.at[2 * chunk - 1])

    def ready(side, chunk):
        if (side, chunk) in copies:
            copies[side, chunk].wait()

    operands = (into_end[...], from_start[...], halves[...], b, c, xs, dys)
    put_states(head_dim, chunks, pieces, where, operands, outs, ready)


def states_shapes(n_parts, length, width, state):
    part = width // (GROUP * chunk_count(width))
    scaled = jax.ShapeDtypeStruct((length, part), BF16)
    send = jax.ShapeDtypeStruct((2 * state + TAIL, part), BF16)
    return [scaled, scaled, scaled, send] * n_parts


def by_piece(pieces, outs):
    return {piece: outs[4 * n : 4 * n + 4] for n, piece in enumerate(pieces)}


def first_states(head_dim, pieces, where, inputs):
    ld, b, c, x, dy = inputs
    (length, width), state = x.shape, b.shape[1]
    chunks = chunk_count(width)
    columns = jax.ShapeDtypeStruct((length, width // chunks), BF16)
    kept = [jax.ShapeDtypeStruct(a.shape, a.dtype) for a in (ld, b, c)] + [columns] * 2
    kept += [jax.ShapeDtypeStruct((rows, LANES), BF16) for rows in (length, length, TAIL)]
    outs = kept + states_shapes(len(pieces), length, width, state)
    found = pl.pallas_call(
        functools.partial(first_states_kernel, head_dim, chunks, pieces),
        out_shape=outs,
        in_specs=[SMEM] + [HBM] * 5,
        out_specs=whole(len(outs)),
        scratch_shapes=[pltpu.SemaphoreType.DMA((5,))],
        compiler_params=params(8),
        cost_estimate=cost(2 * length * width * (state + LANES), 8 * length * width),
        name="first_states",
    )(where, *in_hbm(*inputs))
    return found[:8], by_piece(pieces, found[8:])


def next_states(head_dim, pieces, where, factors, b, c, x_0, dy_0, x, dy):
    (length, width), state = x.shape, b.shape[1]
    chunks = chunk_count(width)
    n_kept = 2 * (chunks - 1)
    outs = [jax.ShapeDtypeStruct(x_0.shape, BF16)] * n_kept
    outs += states_shapes(len(pieces), length, width, state)
    found = pl.pallas_call(
        functools.partial(next_states_kernel, head_dim, chunks, pieces),
        out_shape=outs,
        in_specs=[SMEM] + whole(7) + [HBM] * 2,
        out_specs=whole(len(outs)),
        scratch_shapes=[pltpu.SemaphoreType.DMA((max(n_kept, 1),))],
        compiler_params=params(8),
        cost_estimate=cost(2 * length * width * (state + LANES), 4 * length * width),
        name="next_states",
    )(where, *factors, b, c, x_0, dy_0, *in_hbm(x, dy))
    return found[:n_kept], by_piece(pieces, found[n_kept:])


def decay_of(tail):
    tail = tail.astype(F32)
    return tail[:1, :] + tail[TAIL // 2 : TAIL // 2 + 1, :]


def put_decay(ref, first, factor):
    high = factor.astype(BF16).astype(F32)
    shape = (TAIL, factor.shape[1])
    both = jnp.where(iota(shape, 0) < TAIL // 2, high, factor - high)
    ref[first:, :] = both.astype(BF16)


def sent_order(parts):
    return [parts[0], *parts[:0:-1]]


def in_order(group, forward):
    return list(range(group)) if forward else list(range(group - 1, -1, -1))


def side_rows(state, forward):
    return slice(0, state) if forward else slice(state, 2 * state)


def totals_kernel(state, levels, where, *refs):
    group = GROUP
    blocks, outs, sums = sent_order(refs[:group]), refs[-1 - levels : -1], refs[-1]
    for here in range(group):

        @pl.when(place_of(where) == here)
        def _(here=here):
            decays = [decay_of(blocks[q ^ here][2 * state :, :]) for q in range(group)]
            for forward in (True, False):
                rows, value = side_rows(state, forward), None
                for q in in_order(group, forward):
                    piece = blocks[q ^ here][rows, :].astype(F32)
                    value = piece if value is None else decays[q] * value + piece
                sums[rows, :] = value.astype(BF16)

    factor = decay_of(blocks[0][2 * state :, :])
    for block in blocks[1:]:
        factor = factor * decay_of(block[2 * state :, :])
    if not levels:
        put_decay(sums, 2 * state, factor)
    for level, out in enumerate(outs):
        put_decay(out, state, factor)
        for forward in (True, False):

            @pl.when(bit_of(where, level) != forward)
            def _(out=out, forward=forward):
                out[:state, :] = sums[side_rows(state, forward), :]


def totals(state, levels, where, blocks, after):
    part = blocks[0].shape[1]
    outs = [jax.ShapeDtypeStruct((state + TAIL, part), BF16)] * levels
    if not levels:
        outs = [jax.ShapeDtypeStruct(blocks[0].shape, BF16)]
    return pl.pallas_call(
        functools.partial(totals_kernel, state, levels),
        out_shape=outs,
        in_specs=[SMEM] + whole(len(blocks)) + [ANY] * len(after),
        out_specs=whole(len(outs)),
        scratch_shapes=[pltpu.VMEM((2 * state, part), BF16)] if levels else [],
        compiler_params=params(4),
        cost_estimate=cost(8 * blocks[0].size, 10 * blocks[0].size),
        name="totals",
    )(where, *sent_order(blocks), *after)


def merged_kernel(state, level, last, where, own, received, *refs):
    out = refs[-1]
    d_own, d_other = decay_of(own[2 * state :, :]), decay_of(received[2 * state :, :])
    upper = bit_of(where, level)
    later = bit_of(where, level + 1)
    for is_upper in (False, True):
        for forward in (True, False):
            chosen = upper == is_upper
            if last:
                chosen = chosen & (later != forward)

            @pl.when(chosen)
            def _(is_upper=is_upper, forward=forward):
                rows = side_rows(state, forward)
                mine, other = own[rows, :].astype(F32), received[rows, :].astype(F32)
                value = mine + d_own * other if is_upper == forward else other + d_other * mine
                out[slice(0, state) if last else rows, :] = value.astype(BF16)

    if not last:
        put_decay(out, 2 * state, d_own * d_other)


def merged(state, level, last, where, own, received, after):
    rows = state if last else own.shape[0]
    return pl.pallas_call(
        functools.partial(merged_kernel, state, level, last),
        out_shape=pltpu.VMEM((rows, own.shape[1]), BF16),
        in_specs=[SMEM] + whole(2) + [ANY] * len(after),
        out_specs=whole(1)[0],
        compiler_params=params(4),
        cost_estimate=cost(4 * own.size, 6 * own.size),
        name="merged",
    )(where, own, received, *after)


def put_direct(state, groups, number, received, entry):
    for mine in range(groups):

        @pl.when(number == mine)
        def _(mine=mine):
            for forward in (True, False):
                rows = side_rows(state, forward)
                others = range(mine - 1, -1, -1) if forward else range(mine + 1, groups)
                value, factor = jnp.zeros((state, entry.shape[1]), F32), None
                for other in others:
                    r = received[(mine ^ other) - 1]
                    piece = r[:state, :].astype(F32)
                    value = piece if factor is None else value + factor * piece
                    d = decay_of(r[state:, :])
                    factor = d if factor is None else factor * d
                entry[rows, :] = value


def put_rounds(state, where, received, entry):
    for forward in (True, False):
        value, factor = None, 1.0
        for level, r in enumerate(received):
            gets = bit_of(where, level) == forward
            both = r.shape[0] > 2 * state
            rows = side_rows(state, forward) if both else slice(0, state)
            piece = r[rows, :].astype(F32) * jnp.where(gets, 1.0, 0.0)
            value = piece if value is None else value + factor * piece
            if both:
                factor = factor * jnp.where(gets, decay_of(r[2 * state :, :]), 1.0)
        entry[side_rows(state, forward), :] = value


def members_kernel(state, direct, n_received, where, *refs):
    received, refs = refs[:n_received], refs[n_received:]
    group = GROUP
    blocks, outs, entry = refs[:group], refs[-1 - group : -1], refs[-1]
    if direct:
        put_direct(state, n_received + 1, where[0] // group, received, entry)
    else:
        put_rounds(state, where, received, entry)
    for here in range(group):

        @pl.when(place_of(where) == here)
        def _(here=here):
            decays = [decay_of(blocks[q ^ here][2 * state :, :]) for q in range(group)]
            for forward in (True, False):
                rows, order = side_rows(state, forward), in_order(group, forward)
                value = entry[rows, :]
                for q in order:
                    outs[q ^ here][rows, :] = value.astype(BF16)
                    if q != order[-1]:
                        value = decays[q] * value + blocks[q ^ here][rows, :].astype(F32)


def member_entries(state, direct, where, blocks, received, after):
    group, part = len(blocks), blocks[0].shape[1]
    return pl.pallas_call(
        functools.partial(members_kernel, state, direct, len(received)),
        out_shape=[jax.ShapeDtypeStruct((2 * state, part), BF16)] * group,
        in_specs=[SMEM] + whole(group + len(received)) + [ANY] * len(after),
        out_specs=whole(group),
        scratch_shapes=[pltpu.VMEM((2 * state, part), F32)],
        compiler_params=params(4),
        cost_estimate=cost(12 * blocks[0].size, 16 * blocks[0].size),
        name="member_entries",
    )(where, *received, *blocks, *after)


def exchange(parts):
    count = lax.axis_size("seq")
    out = list(parts)
    for k in range(len(parts) - 1, 0, -1):
        out[k] = lax.ppermute(parts[k], "seq", [(s, s ^ k) for s in range(count)])
    return out


def split_pairs(first, count):
    if count == 1:
        return []
    middle = first + count // 2
    return (
        [(first, middle, first + count)]
        + split_pairs(first, middle - first)
        + split_pairs(middle, first + count - middle)
    )


def grouped_cuts(pieces):
    groups = {}
    for cut in split_pairs(0, pieces):
        groups.setdefault((cut[1] - cut[0], cut[2] - cut[1]), []).append(cut)
    return list(groups.items())


def rows_of(first, end, piece):
    return slice(first * piece, end * piece)


def setup_kernel(piece, ld, b, c, *refs):
    near, cum_terms = refs[-2:]
    heads, length = ld.shape
    rows, other = iota((length, length), 0), iota((length, length), 1)
    mask = jnp.where(other <= rows, 1.0, 0.0).astype(BF16)
    cum = summed(mask, three(ld[...] * LOG2E))
    lane = iota(cum.shape, 1)
    in_slots = jnp.where(lane < SLOT, cum, 0.0)
    in_slots = in_slots + pltpu.roll(in_slots, SLOT, 1) + pltpu.roll(in_slots, 2 * SLOT, 1)
    high, mid, low = three(in_slots)
    cum_terms[...] = jnp.where(lane < SLOT, high, jnp.where(lane < 2 * SLOT, mid, low))
    keep = iota((piece, piece), 0) <= iota((piece, piece), 1)
    pieces = length // piece
    for n in range(pieces):
        here = rows_of(n, n + 1, piece)
        near[here, :] = jnp.where(keep, dot(b[here, :], c[here, :], NT), 0.0).astype(BF16)
    cuts = [cut for _, same in grouped_cuts(pieces) for cut in same]
    for (lo, mid_, hi), far in zip(cuts, refs):
        left, right = rows_of(lo, mid_, piece), rows_of(mid_, hi, piece)
        far[...] = dot(b[left, :], c[right, :], NT).astype(BF16)


def inner_setup(piece, ld, b, c, after):
    length = b.shape[0]
    cuts = [cut for _, same in grouped_cuts(length // piece) for cut in same]
    outs = [
        jax.ShapeDtypeStruct(((mid - lo) * piece, (hi - mid) * piece), BF16) for lo, mid, hi in cuts
    ]
    outs.append(jax.ShapeDtypeStruct((length, piece), BF16))
    outs.append(jax.ShapeDtypeStruct((length, LANES), BF16))
    return pl.pallas_call(
        functools.partial(setup_kernel_after, piece, len(after)),
        out_shape=outs,
        in_specs=whole(3) + [ANY] * len(after),
        out_specs=whole(len(outs)),
        compiler_params=params(4),
        cost_estimate=cost(8 * b.size * length, 8 * b.size),
        name="inner_setup",
    )(ld, b, c, *after)


def setup_kernel_after(piece, n_after, ld, b, c, *refs):
    setup_kernel(piece, ld, b, c, *refs[n_after:])


def inner_kernel(head_dim, worked, chunks, n_before, n_after, b, c, *refs):
    xs, dys, refs = refs[:chunks], refs[chunks : 2 * chunks], refs[2 * chunks :]
    length, width = xs[0].shape
    piece = head_dim
    pieces = length // piece
    groups = grouped_cuts(pieces)
    n_cuts = sum(len(same) for _, same in groups)
    fars, (near, cum_terms), refs = refs[:n_cuts], refs[n_cuts : n_cuts + 2], refs[n_cuts + 2 :]
    before, refs = refs[:n_before], refs[n_before + n_after :]
    dx_outs, (db_out, dc_out, x_near, dy_near, *scratch) = refs[: len(worked)], refs[len(worked) :]
    lefts, rights = scratch[: len(groups)], scratch[len(groups) :]
    part = dx_outs[0].shape[1]
    difference = row_less_head(head_dim, part, SLOT)

    for at, (chunk, m) in enumerate(worked):
        x, dy, first_head = xs[chunk], dys[chunk], (chunk * GROUP + m) * (part // head_dim)
        lanes, here = slice(m * part, (m + 1) * part), slice(at * part, (at + 1) * part)
        cum = dot(cum_terms[...], head_of_lane(difference, first_head), NN)
        dx = []
        for n in range(pieces):
            rows = rows_of(n, n + 1, piece)
            middle = cum[n * piece + piece // 2 : n * piece + piece // 2 + 1, :]
            gap = middle - cum[rows, :]
            down, up = jnp.exp2(gap), jnp.exp2(-gap)
            x_near[rows, here] = (x[rows, lanes].astype(F32) * down).astype(BF16)
            dy_piece = (dy[rows, lanes].astype(F32) * up).astype(BF16)
            dy_near[rows, here] = dy_piece
            dx.append(down * dot(near[rows, :], dy_piece, NN))
        far_of = iter(fars)
        for (_, same), left_ref, right_ref in zip(groups, lefts, rights):
            for g, (lo, mid, hi) in enumerate(same):
                left, right = rows_of(lo, mid, piece), rows_of(mid, hi, piece)
                edge = cum[mid * piece - 1 : mid * piece, :]
                to_edge = jnp.exp2(edge - cum[left, :])
                from_edge = jnp.exp2(cum[right, :] - edge)
                x_left = (x[left, lanes].astype(F32) * to_edge).astype(BF16)
                dy_right = (dy[right, lanes].astype(F32) * from_edge).astype(BF16)
                left_ref[rows_of(g, g + 1, (mid - lo) * piece), here] = x_left
                right_ref[rows_of(g, g + 1, (hi - mid) * piece), here] = dy_right
                far = to_edge * dot(next(far_of)[...], dy_right, NN)
                for n in range(lo, mid):
                    dx[n] = dx[n] + far[rows_of(n - lo, n - lo + 1, piece), :]
        for n in range(pieces):
            dx_outs[at][rows_of(n, n + 1, piece), :] = dx[n].astype(BF16)

    if before:
        db_out[...] = before[0][...]
        dc_out[...] = before[1][...]
    else:
        db_out[...] = jnp.zeros_like(db_out)
        dc_out[...] = jnp.zeros_like(dc_out)
    batch = 4
    for first in range(0, pieces, batch):
        rows = rows_of(first, min(first + batch, pieces), piece)
        total = dot(x_near[rows, :], dy_near[rows, :], NT)
        row, col = iota(total.shape, 0), iota(total.shape, 1)
        keep = (split_of(row, piece) == split_of(col, piece)) & (row <= col)
        weighted = jnp.where(keep, total, 0.0).astype(BF16)
        db_out[rows, :] += dot(weighted, c[rows, :], NN)
        dc_out[rows, :] += dot(weighted, b[rows, :], TN)
    for ((n_left, n_right), same), left_ref, right_ref in zip(groups, lefts, rights):
        total = dot(left_ref[...], right_ref[...], NT)
        if len(same) > 1:
            row, col = iota(total.shape, 0), iota(total.shape, 1)
            same_cut = split_of(row, n_left * piece) == split_of(col, n_right * piece)
            total = jnp.where(same_cut, total, 0.0)
        weighted = total.astype(BF16)
        b_left = jnp.concatenate([b[rows_of(lo, mid, piece), :] for lo, mid, _ in same], axis=0)
        c_right = jnp.concatenate([c[rows_of(mid, hi, piece), :] for _, mid, hi in same], axis=0)
        db = dot(weighted, c_right, NN)
        dc = dot(weighted, b_left, TN)
        for g, (lo, mid, hi) in enumerate(same):
            db_out[rows_of(lo, mid, piece), :] += db[rows_of(g, g + 1, n_left * piece), :]
            dc_out[rows_of(mid, hi, piece), :] += dc[rows_of(g, g + 1, n_right * piece), :]


def inner_terms(head_dim, worked, setup, b, c, xs, dys, before, after, hides=True):
    (length, state), columns, chunks = b.shape, xs[0].size, len(xs)
    part = xs[0].shape[1] // GROUP
    used = part * len(worked)
    groups = grouped_cuts(length // head_dim)
    sizes = [[len(same) * n * head_dim for n in halves] for halves, same in groups]
    found = pl.pallas_call(
        functools.partial(inner_kernel, head_dim, worked, chunks, len(before), len(after)),
        out_shape=[jax.ShapeDtypeStruct((length, part), BF16)] * len(worked)
        + [jax.ShapeDtypeStruct((length, state), F32)] * 2,
        in_specs=whole(2 + 2 * chunks + len(setup) + len(before)) + [ANY] * len(after),
        out_specs=whole(len(worked) + 2),
        scratch_shapes=[pltpu.VMEM((length, used), BF16)] * 2
        + [pltpu.VMEM((left, used), BF16) for left, _ in sizes]
        + [pltpu.VMEM((right, used), BF16) for _, right in sizes],
        compiler_params=params(16),
        cost_estimate=cost(16 * columns * state, 8 * columns, 4 * columns) if hides else cost(1, 1),
        name="inner_terms",
    )(b, c, *xs, *dys, *setup, *before, *after)
    return dict(zip(worked, found)), list(found[-2:])


def parts_kernel(last, ks, db_before, dc_before, *refs):
    scaled, refs = refs[: 2 * len(ks)], refs[2 * len(ks) :]
    entries, outs = refs[: len(ks)], refs[-1 if last else -2 :]
    length, state = db_before.shape
    db, dc = db_before[...], dc_before[...]
    for n, entry in enumerate(entries):
        db = db + dot(scaled[2 * n][...], entry[state:, :], NT)
        dc = dc + dot(scaled[2 * n + 1][...], entry[:state, :], NT)
    if last:
        outs[0][:length, :] = db.astype(BF16)
        outs[0][length:, :] = dc.astype(BF16)
    else:
        outs[0][...] = db
        outs[1][...] = dc


def entry_parts(last, ks, scaled, db_before, dc_before, entries, after):
    length, state = db_before.shape
    one = jax.ShapeDtypeStruct((length, state), F32)
    outs = [jax.ShapeDtypeStruct((2 * length, state), BF16)] if last else [one, one]
    operands = [one for k in ks for one in scaled[k]] + [entries[k] for k in ks]
    return pl.pallas_call(
        functools.partial(parts_kernel, last, ks),
        out_shape=outs,
        in_specs=whole(2 + len(operands)) + [ANY] * len(after),
        out_specs=whole(len(outs)),
        compiler_params=params(8),
        cost_estimate=cost(2 * len(operands) * scaled[0][0].size * state, scaled[0][0].size),
        name="entry_parts",
    )(db_before, dc_before, *operands, *after)


def put_values(where, spread, b, local_parts, dx_local, entries, put):
    state, part = b.shape[1], entries[0].shape[1]
    for m, one in enumerate(local_parts):
        dx_local[:, m * part : (m + 1) * part] = one[...]
    for k, entry in enumerate(entries):
        lanes = pl.ds(pl.multiple_of((place_of(where) ^ k) * part, part), part)
        local = dx_local[:, lanes]
        far = spread[k][...].astype(F32) * dot(b[...], entry[state:, :], NN)
        put(k, lanes, (local.astype(F32) + far).astype(BF16))


def values_kernel(where, b, *refs):
    local_parts, spread = refs[:GROUP], refs[GROUP : 2 * GROUP]
    entries, (out, dx_local) = sent_order(refs[2 * GROUP : 3 * GROUP]), refs[-2:]

    def put(k, lanes, value):
        out[:, lanes] = value

    put_values(where, spread, b, local_parts, dx_local, entries, put)


def last_values_kernel(chunks, where, b, *refs):
    local_parts, spread, refs = refs[:GROUP], refs[GROUP : 2 * GROUP], refs[2 * GROUP :]
    entries, before = sent_order(refs[:GROUP]), refs[GROUP : GROUP + chunks - 1]
    out, dx, dx_local, sems = refs[-4:]
    part = entries[0].shape[1]
    stores = []

    def store(n, source, target):
        stores.append(pltpu.make_async_copy(source, target, sems.at[n]))
        stores[-1].start()

    for chunk, values in enumerate(before):
        store(GROUP + chunk, values, out.at[:, pl.ds(chunk * GROUP * part, GROUP * part)])

    def put(k, lanes, value):
        dx[k] = value
        store(k, dx.at[k], out.at[:, chunk_lanes(where, k, chunks - 1, part)])

    put_values(where, spread, b, local_parts, dx_local, entries, put)
    for one in stores:
        one.wait()


def entry_values(chunk, chunks, where, spread, b, local_parts, entries, before):
    length, part = b.shape[0], entries[0].shape[1]
    last = chunk == chunks - 1
    estimate = cost(8 * local_parts[0].size * b.shape[1], 16 * local_parts[0].size)
    operands = [where, b, *local_parts, *spread, *sent_order(entries)]
    if not last:
        return pl.pallas_call(
            values_kernel,
            out_shape=jax.ShapeDtypeStruct((length, GROUP * part), BF16),
            in_specs=[SMEM] + whole(1 + 3 * GROUP),
            out_specs=whole(1)[0],
            scratch_shapes=[pltpu.VMEM((length, GROUP * part), BF16)],
            compiler_params=params(8),
            cost_estimate=estimate,
            name="entry_values",
        )(*operands)
    return pl.pallas_call(
        functools.partial(last_values_kernel, chunks),
        out_shape=pltpu.HBM((length, chunks * GROUP * part), BF16),
        in_specs=[SMEM] + whole(1 + 3 * GROUP + len(before)),
        out_specs=HBM,
        scratch_shapes=[
            pltpu.VMEM((GROUP, length, part), BF16),
            pltpu.VMEM((length, GROUP * part), BF16),
            pltpu.SemaphoreType.DMA((GROUP + chunks - 1,)),
        ],
        compiler_params=params(8),
        cost_estimate=estimate,
        name="last_values",
    )(*operands, *before)


def sum_kernel(*refs):
    parts, (db, dc) = refs[:-2], refs[-2:]
    length = db.shape[0]
    for out, rows in ((db, slice(0, length)), (dc, slice(length, 2 * length))):
        total = parts[0][rows, :].astype(F32)
        for part in parts[1:]:
            total = total + part[rows, :].astype(F32)
        out[...] = total.astype(BF16)


def over_heads(part):
    count, (rows, state) = lax.axis_size("head"), part.shape
    parts = [part]
    for shift in range(1, count):
        pairs = [(s, (s + shift) % count) for s in range(count)]
        parts.append(lax.ppermute(part, "head", pairs))
    return pl.pallas_call(
        sum_kernel,
        out_shape=[jax.ShapeDtypeStruct((rows // 2, state), BF16)] * 2,
        in_specs=whole(count),
        out_specs=whole(2),
        compiler_params=params(4),
        cost_estimate=cost(count * part.size, 2 * count * part.size),
        name="sum_over_heads",
    )(*parts)


def shards(token_values, b_inputs, c_inputs, log_decay, grad_out):
    head_dim = token_values.shape[1] // log_decay.shape[0]
    state = b_inputs.shape[1]
    count, group = lax.axis_size("seq"), GROUP
    chunks = chunk_count(token_values.shape[1])
    levels = (count // group).bit_length() - 1
    where = lax.axis_index("seq").astype(jnp.int32)[None]
    inputs = (log_decay, b_inputs, c_inputs, token_values, grad_out)
    order = [(chunk, k) for chunk in range(chunks) for k in range(group - 1, -1, -1)]
    kept, states = first_states(head_dim, order[: group - 1], where, inputs)
    ld, b, c, x_0, dy_0, *factors = kept
    late = order[group - 1 :]
    columns = (x_0, dy_0, token_values, grad_out)
    more, found = next_states(head_dim, late, where, factors, b, c, *columns)
    states.update(found)
    xs, dys = [x_0, *more[::2]], [dy_0, *more[1::2]]
    blocks = [
        exchange([states[chunk, k][3] for k in range(group)]) for chunk in range(chunks)
    ]
    setup = inner_setup(head_dim, ld, b, c, [states[late[-1]][0]])

    def to_group(block, k):
        return lax.ppermute(block, "seq", [(s, s ^ (k * group)) for s in range(count)])

    every = [(chunk, m) for chunk in range(chunks) for m in range(group)]
    early, rest = every[:2], every[2:]
    worked = [rest[:3]] + [[]] * (chunks - 1)
    rest = [one for one in rest if not any(one in some for some in worked)]
    entries, inner, sums = [], {}, []

    def add_inner(some, after, hides=True):
        found, sums[:] = inner_terms(head_dim, some, setup, b, c, xs, dys, sums, after, hides)
        inner.update(found)

    own = [totals(state, 0, where, blocks[0], setup[-1:])]
    add_inner(early, own[0], False)
    own += [totals(state, 0, where, blocks[chunk], sums[:1]) for chunk in range(1, chunks)]
    for chunk in range(chunks):
        (total,) = own[chunk]
        received = [to_group(total, 1)]
        for level in range(levels - 1):
            last = level == levels - 2
            total = merged(state, level, last, where, total, received[level], [])
            received.append(to_group(total, 2 << level))
        if worked[chunk]:
            add_inner(worked[chunk], [total])
        found = member_entries(state, False, where, blocks[chunk], received, sums[:1])
        entries.append(exchange(found))
    if rest:
        add_inner(rest, found[:1])

    values = []
    for chunk in range(chunks):
        last = chunk == chunks - 1
        ours = [states[chunk, k] for k in range(group)]
        scaled = [one[:2] for one in ours]
        spread = [one[2] for one in ours]
        if last:
            sums = entry_parts(False, (0, 3), scaled, *sums, entries[chunk], values)
        ks = (2, 1) if last else (0, 3, 2, 1)
        sums = entry_parts(last, ks, scaled, *sums, entries[chunk], [])
        local = [inner[chunk, m] for m in range(group)]
        values.append(
            entry_values(chunk, chunks, where, spread, b, local, entries[chunk], values)
        )
    return (values[-1], *over_heads(sums[0]))


def solution(mesh):
    in_specs = (
        P("seq", "head"),
        P("seq", None),
        P("seq", None),
        P("head", "seq"),
        P("seq", "head"),
    )
    out_specs = (P("seq", "head"), P("seq", None), P("seq", None))
    return jax.shard_map(shards, mesh=mesh, in_specs=in_specs, out_specs=out_specs, check_vma=False)
```
